32 devices in a mesh: dp: 2 (over x), tensor: 4 (over y, core), blk: 4 (over z).
Axes of the slice: x: 2, y: 2, z: 4, core: 2. Of those that a mesh axis runs over, the one named last changes fastest.
Arguments:
- x_train: float32 [2, 1024, 768], P('dp', 'blk'), may hold values from -6 to 6
- x_quiz: float32 [4, 1024, 768], P('dp', 'blk'), may hold values from -6 to 6
- cot_train: float32 [2, 1024, 768], P('dp', 'blk'), may hold values from -6 to 6
- cot_quiz: float32 [4, 1024, 768], P('dp', 'blk'), may hold values from -6 to 6
- quiz_lengths: int32 [4], P('dp'), may hold values from 128 to 1024, as said below
- w_qkv: bfloat16 [3, 768, 768], P(None, None, 'tensor'), may hold values from -0.21875 to 0.21875
- b_qv: bfloat16 [2, 768], P(None, 'tensor'), may hold values from -3 to 3
- w_out: bfloat16 [768, 768], P('tensor'), may hold values from -3.5 to 3.5
- b_out: bfloat16 [768], replicated, may hold values from -3 to 3
- w_in: bfloat16 [768, 3072], P(None, 'tensor'), may hold values from -0.21875 to 0.21875
- b_in: bfloat16 [3072], P('tensor'), may hold values from -3 to 3
- w_back: bfloat16 [3072, 768], P('tensor'), may hold values from -0.109375 to 0.109375
- b_back: bfloat16 [768], replicated, may hold values from -3 to 3
- norm_gains: float32 [2, 768], replicated, may hold values from 0.25 to 1.75
- norm_shifts: float32 [2, 768], replicated, may hold values from -2 to 2
Outputs:
- out_train: float32 [2, 1024, 768], P('dp', 'blk')
- out_quiz: float32 [4, 1024, 768], P('dp', 'blk')
- grad_in_train: float32 [2, 1024, 768], P('dp', 'blk')
- grad_in_quiz: float32 [4, 1024, 768], P('dp', 'blk')
- grad_qkv: float32 [2, 3, 768, 768], P(None, None, None, 'tensor')
- grad_qv_bias: float32 [2, 2, 768], P(None, None, 'tensor')
- grad_out_w: float32 [2, 768, 768], P(None, 'tensor')
- grad_out_bias: float32 [2, 768], P(None, 'tensor')
- grad_in_w: float32 [2, 768, 3072], P(None, None, 'tensor')
- grad_in_bias: float32 [2, 3072], P(None, 'tensor')
- grad_back_w: float32 [2, 3072, 768], P(None, 'tensor')
- grad_back_bias: float32 [2, 768], P(None, 'tensor')
- grad_gains: float32 [2, 2, 768], P(None, None, 'tensor')
- grad_shifts: float32 [2, 2, 768], P(None, None, 'tensor')
The draws below stay inside these ranges and needn't reach their ends.
Inputs may be any that keep to these rules, and one draw needn't show every extreme that they name: `quiz_lengths`: among the 2 quiz sequences that one index of dp holds, one has the full length 1024.
All inputs are finite; a program needn't handle non-finite values.
Results may differ from the reference program's by a relative error of at most 0.039.
Values may be sent and summed in bfloat16 or wider, within the bound.
A program may use at most 192 MiB of HBM per device.

```python
import jax
import jax.numpy as jnp
from jax import lax

D = 768
HEAD_DIM = 64
FF = 3072
QUIZ_DEV = 2
SEQ_LEN = 1024
TRAIN = 2
QUIZ = 4


def draw_quiz_lengths(key, part):
    key = jax.random.fold_in(key, 7)
    first_key, second_key = jax.random.split(key)
    drawn = jax.random.randint(first_key, (QUIZ,), SEQ_LEN // 8, SEQ_LEN + 1)
    groups = QUIZ // QUIZ_DEV
    picked = jax.random.randint(second_key, (groups,), 0, QUIZ_DEV)
    slot_index = jnp.arange(QUIZ, dtype=jnp.int32) % QUIZ_DEV
    chosen = slot_index == jnp.repeat(picked, QUIZ_DEV)
    return jnp.where(chosen, SEQ_LEN, drawn).astype(jnp.int32)


def shard_levels(key, shape, cuts, low, high):
    def one(dim, parts):
        steps = jax.random.uniform(jax.random.fold_in(jax.random.fold_in(key, 6), dim), (parts,), jnp.float32, low / len(cuts), high / len(cuts))
        return jnp.repeat(jnp.exp(steps), shape[dim] // parts).reshape((-1,) + (1,) * (len(shape) - dim - 1))

    level = one(*cuts[0])
    for cut in cuts[1:]:
        level = level * one(*cut)
    return level


def noise(rng, extent, spread, reach, cuts=(), kind=jnp.bfloat16):
    entries = jax.random.normal(rng, extent, jnp.float32) * spread
    if len(cuts) > 0:
        entries = shard_levels(rng, extent, cuts, -0.22, 0.18) * entries
    return jnp.clip(entries, min=-reach, max=reach).astype(kind)


def setup_inputs(seed: int = 0) -> dict:
    arg_keys = jax.random.split(jax.random.key(seed), 16)
    x_train = noise(arg_keys[0], (TRAIN, SEQ_LEN, D), 1.0, 6.0, ((0, 2), (1, 4)), jnp.float32)
    x_quiz = noise(arg_keys[1], (QUIZ, SEQ_LEN, D), 1.0, 6.0, ((0, 2), (1, 4)), jnp.float32)
    cot_train = noise(arg_keys[2], (TRAIN, SEQ_LEN, D), 1.0, 6.0, ((0, 2), (1, 4)), jnp.float32)
    cot_quiz = noise(arg_keys[3], (QUIZ, SEQ_LEN, D), 1.0, 6.0, ((0, 2), (1, 4)), jnp.float32)
    quiz_lengths = draw_quiz_lengths(jax.random.fold_in(arg_keys[15], 71), 0)
    w_qkv = noise(arg_keys[5], (3, D, D), D ** -0.5, 0.21875, ((2, 4),))
    b_qv = noise(arg_keys[6], (2, D), 0.5, 3.0, ((1, 4),))
    w_out = noise(arg_keys[7], (D, D), (max(1, 4 * D // SEQ_LEN)) ** -0.5, 3.5, ((0, 4),))
    b_out = noise(arg_keys[8], (D,), 0.5, 3.0)
    w_in = noise(arg_keys[9], (D, FF), D ** -0.5, 0.21875, ((1, 4),))
    b_in = noise(arg_keys[10], (FF,), 0.5, 3.0, ((0, 4),))
    w_back = noise(arg_keys[11], (FF, D), FF ** -0.5, 0.109375, ((0, 4),))
    b_back = noise(arg_keys[12], (D,), 0.5, 3.0)
    norm_gains = jnp.clip(1.0 + 0.15 * jax.random.normal(arg_keys[13], (2, D), jnp.float32), 0.25, 1.75)
    norm_shifts = noise(arg_keys[14], (2, D), 0.3, 2.0, (), jnp.float32)
    return {"x_train": x_train, "x_quiz": x_quiz, "cot_train": cot_train, "cot_quiz": cot_quiz, "quiz_lengths": quiz_lengths, "w_qkv": w_qkv, "b_qv": b_qv, "w_out": w_out, "b_out": b_out, "w_in": w_in, "b_in": b_in, "w_back": w_back, "b_back": b_back, "norm_gains": norm_gains, "norm_shifts": norm_shifts}


@jax.custom_vjp
def low(v):
    return lax.optimization_barrier(v.astype(jnp.bfloat16)).astype(jnp.float32)

@jax.custom_vjp
def low_back(v):
    return v

def low_keep(v):
    return (low(v), None)

def low_pass(kept, grad):
    return (grad,)

def back_keep(v):
    return (v, None)

def back_low(kept, grad):
    return (low(grad),)
low.defvjp(low_keep, low_pass)
low_back.defvjp(back_keep, back_low)
EPSILON = 1e-12
ROOT_HALF = 0.7071067811865476

def matmul(left, right):
    return jnp.dot(left, right, precision=lax.Precision.HIGHEST)

def layer_norm(hidden, gain, shift):
    center = hidden - lax.optimization_barrier(jnp.mean(hidden, axis=-1, keepdims=True))
    inverse = lax.rsqrt(lax.optimization_barrier(jnp.mean(center * center, axis=-1, keepdims=True)) + EPSILON)
    return center * inverse * gain + shift

def gelu_exact(values):
    return 0.5 * values * (1.0 + lax.erf(values * ROOT_HALF))

def attend(query, key_rows, value_rows, length):
    heads = D // HEAD_DIM
    width = min(512, SEQ_LEN)
    key_heads = key_rows.reshape(SEQ_LEN, heads, HEAD_DIM)
    value_heads = value_rows.reshape(SEQ_LEN, heads, HEAD_DIM)
    visible = jnp.arange(SEQ_LEN, dtype=jnp.int32) < length

    def one_block(query_block):
        scores = jnp.einsum('qhd,khd->hqk', query_block, key_heads, precision=lax.Precision.HIGHEST) * HEAD_DIM ** (-0.5)
        scores = low_back(scores)
        scores = jnp.where(visible[None, None, :], scores, -1e+30)
        highest = lax.optimization_barrier(jnp.max(scores, axis=-1, keepdims=True))
        raised = jnp.exp(scores - highest)
        probs = low(raised / lax.optimization_barrier(jnp.sum(raised, axis=-1, keepdims=True)))
        return jnp.einsum('hqk,khd->qhd', probs, value_heads, precision=lax.Precision.HIGHEST)
    blocks = lax.map(jax.checkpoint(one_block), query.reshape(SEQ_LEN // width, width, heads, HEAD_DIM))
    return blocks.reshape(SEQ_LEN, D)

def sequence(params, tokens, length):
    w_qkv, b_qv, w_out, b_out, w_in, b_in, w_back, b_back, norm_gains, norm_shifts = params
    keep_rows = (jnp.arange(SEQ_LEN, dtype=jnp.int32) < length)[:, None]
    low_tokens = low(low_back(tokens))
    query = low(low_back(matmul(low_tokens, w_qkv[0]) + b_qv[0]))
    key_rows = low(low_back(matmul(low_tokens, w_qkv[1])))
    value_rows = low(low_back(matmul(low_tokens, w_qkv[2]) + b_qv[1]))
    mixed = low(low_back(attend(query, key_rows, value_rows, length)))
    attention = low_back(matmul(mixed, w_out) + b_out)
    normed = layer_norm(tokens + attention, norm_gains[0], norm_shifts[0])
    low_normed = low(low_back(normed))
    before = low_back(matmul(low_normed, w_in) + b_in)
    active = low(low_back(gelu_exact(before)))
    branch = low_back(matmul(active, w_back) + b_back)
    return jnp.where(keep_rows, layer_norm(normed + branch, norm_gains[1], norm_shifts[1]), 0.0)

def one_batch(params, inputs, cotangent, lengths):

    def whole(params_in, tokens_in):
        return lax.map(lambda item: sequence(params_in, item[0], item[1]), (tokens_in, lengths))
    outputs, pullback = jax.vjp(whole, params, inputs)
    grad_params, grad_inputs = pullback(cotangent)
    return (outputs, grad_inputs, grad_params)

def reference(x_train, x_quiz, cot_train, cot_quiz, quiz_lengths, w_qkv, b_qv, w_out, b_out, w_in, b_in, w_back, b_back, norm_gains, norm_shifts):
    params = tuple((item.astype(jnp.float32) for item in (w_qkv, b_qv, w_out, b_out, w_in, b_in, w_back, b_back, norm_gains, norm_shifts)))
    full_lengths = jnp.full((TRAIN,), SEQ_LEN, dtype=jnp.int32)
    out_train, grad_train, params_train = one_batch(params, x_train, cot_train, full_lengths)
    out_quiz, grad_quiz, params_quiz = one_batch(params, x_quiz, cot_quiz, quiz_lengths.astype(jnp.int32))
    stacked = [jnp.stack([first_grad, second_grad]) for first_grad, second_grad in zip(params_train, params_quiz)]
    return (out_train, out_quiz, grad_train, grad_quiz, stacked[0], stacked[1], stacked[2], stacked[3], stacked[4], stacked[5], stacked[6], stacked[7], stacked[8], stacked[9])
```

```python
import jax
import jax.numpy as jnp
from jax import lax
from jax.sharding import PartitionSpec as P

D = 768
HEAD_DIM = 64


EPSILON = 1e-12
ROOT_HALF = 0.7071067811865476
ROOT_TWO_PI = 2.5066282746310002
NEG_LARGE = -1e30


def layer_norm(hidden, gain, shift):
    center = hidden - jnp.mean(hidden, axis=-1, keepdims=True)
    inverse = lax.rsqrt(jnp.mean(center * center, axis=-1, keepdims=True) + EPSILON)
    normal = center * inverse
    return (normal * gain + shift, normal, inverse)


def norm_back(grad_out, normal, inverse, gain):
    scaled = grad_out * gain
    grad_in = inverse * (
        scaled
        - jnp.mean(scaled, axis=-1, keepdims=True)
        - normal * jnp.mean(scaled * normal, axis=-1, keepdims=True)
    )
    return (grad_in, jnp.sum(grad_out * normal, axis=0), jnp.sum(grad_out, axis=0))


def gelu_exact(values):
    return 0.5 * values * (1.0 + lax.erf(values * ROOT_HALF))


def gelu_slope(values):
    return (
        0.5 * (1.0 + lax.erf(values * ROOT_HALF))
        + values * jnp.exp(-0.5 * values * values) / ROOT_TWO_PI
    )


def across(left, right):
    return lax.dot_general(
        left, right, (((0,), (0,)), ((), ())), preferred_element_type=jnp.float32
    )


def against(left, right):
    return lax.dot_general(
        left, right, (((1,), (1,)), ((), ())), preferred_element_type=jnp.float32
    )


def rounded(values):
    return lax.optimization_barrier(values.astype(jnp.bfloat16)).astype(jnp.float32)


def crop(values, column, share):
    return lax.dynamic_slice_in_dim(values, column, share, axis=values.ndim - 1)


def pair_grads(query_heads, dout_heads, log_total, delta, key_heads, value_heads, visible):
    scale = query_heads.shape[-1] ** (-0.5)
    scores = (
        jnp.einsum("sqhe,skhe->shqk", query_heads, key_heads, preferred_element_type=jnp.float32)
        * scale
    )
    probs = jnp.where(visible[:, None, None, :], jnp.exp(scores - log_total[..., None]), 0.0)
    grad_value = jnp.einsum(
        "shqk,sqhe->skhe",
        probs.astype(jnp.bfloat16),
        dout_heads,
        preferred_element_type=jnp.float32,
    )
    grad_probs = jnp.einsum(
        "sqhe,skhe->shqk", dout_heads, value_heads, preferred_element_type=jnp.float32
    )
    grad_scores = (probs * (grad_probs - delta[..., None])).astype(jnp.bfloat16)
    grad_query = jnp.einsum(
        "shqk,skhe->sqhe", grad_scores, key_heads, preferred_element_type=jnp.float32
    )
    grad_key = jnp.einsum(
        "shqk,sqhe->skhe", grad_scores, query_heads, preferred_element_type=jnp.float32
    )
    return (grad_query, grad_key, grad_value)


def run(tokens, cotangent, lengths, first_row, weights):
    w_qkv, b_qv, w_out, b_out, w_in, b_in, w_back, b_back, norm_gains, norm_shifts = weights
    seq_count, row_count, width = tokens.shape
    seq_len = row_count * lax.axis_size("blk")
    span = min(512, seq_len)
    block_count = seq_len // span
    flat_tokens = tokens.reshape(seq_count * row_count, width)
    low_tokens = flat_tokens.astype(jnp.bfloat16)
    projected = jnp.einsum("nd,tde->tne", low_tokens, w_qkv, preferred_element_type=jnp.float32)
    qv_bias = b_qv.astype(jnp.float32)
    query = (projected[0] + qv_bias[0]).astype(jnp.bfloat16)
    key_rows = projected[1].astype(jnp.bfloat16)
    value_rows = (projected[2] + qv_bias[1]).astype(jnp.bfloat16)
    share = key_rows.shape[-1]
    heads = share // HEAD_DIM
    scale = HEAD_DIM ** (-0.5)
    head_shape = (seq_count, row_count, heads, HEAD_DIM)
    query_heads = query.reshape(head_shape)
    key_three = key_rows.reshape(seq_count, row_count, share)
    value_three = value_rows.reshape(seq_count, row_count, share)
    running_max = jnp.full((seq_count, heads, row_count), NEG_LARGE, jnp.float32)
    running_out = jnp.zeros(head_shape, jnp.float32)
    key_piece = lax.all_gather(key_three, "blk", axis=1, tiled=True)
    value_piece = lax.all_gather(value_three, "blk", axis=1, tiled=True)
    piece_rows = key_piece.shape[1]
    key_heads = key_piece.reshape(seq_count, piece_rows, heads, HEAD_DIM)
    value_heads = value_piece.reshape(seq_count, piece_rows, heads, HEAD_DIM)
    scores = (
        jnp.einsum("sqhe,skhe->shqk", query_heads, key_heads, preferred_element_type=jnp.float32)
        * scale
    )
    visible = (jnp.arange(piece_rows, dtype=jnp.int32)[None, :] < lengths[:, None])[
        :, None, None, :
    ]
    scores = jnp.where(visible, scores, NEG_LARGE)
    new_max = jnp.maximum(running_max, jnp.max(scores, axis=-1))
    factor = jnp.exp(running_max - new_max)
    raised = jnp.where(visible, jnp.exp(scores - new_max[..., None]), 0.0)
    new_sum = jnp.sum(raised, axis=-1)
    added = jnp.einsum(
        "shqk,skhe->sqhe",
        raised.astype(jnp.bfloat16),
        value_heads,
        preferred_element_type=jnp.float32,
    )
    new_out = running_out * jnp.swapaxes(factor, 1, 2)[..., None] + added
    mixed_heads = new_out / jnp.swapaxes(new_sum, 1, 2)[..., None]
    log_total = new_max + jnp.log(new_sum)
    mixed_low = mixed_heads.reshape(seq_count * row_count, share).astype(jnp.bfloat16)
    attention = lax.psum(
        jnp.dot(mixed_low, w_out, preferred_element_type=jnp.float32).astype(jnp.bfloat16), "tensor"
    ).astype(jnp.float32) + b_out.astype(jnp.float32)
    normed, unit_one, inverse_one = layer_norm(
        flat_tokens + attention, norm_gains[0], norm_shifts[0]
    )
    normed_low = normed.astype(jnp.bfloat16)
    before = jnp.dot(normed_low, w_in, preferred_element_type=jnp.float32) + b_in.astype(
        jnp.float32
    )
    active_low = gelu_exact(before).astype(jnp.bfloat16)
    branch = lax.psum(
        jnp.dot(active_low, w_back, preferred_element_type=jnp.float32).astype(jnp.bfloat16),
        "tensor",
    ).astype(jnp.float32) + b_back.astype(jnp.float32)
    final, unit_two, inverse_two = layer_norm(normed + branch, norm_gains[1], norm_shifts[1])
    positions = first_row + jnp.arange(row_count, dtype=jnp.int32)
    keep_rows = (
        (positions[None, :] < lengths[:, None])
        .reshape(seq_count * row_count, 1)
        .astype(jnp.float32)
    )
    outputs = (keep_rows * final).reshape(tokens.shape)
    grad_final = keep_rows * cotangent.reshape(seq_count * row_count, width)
    grad_mid, grad_gain_two, grad_shift_two = norm_back(
        grad_final, unit_two, inverse_two, norm_gains[1]
    )
    grad_branch = grad_mid.astype(jnp.bfloat16)
    grad_b_back = jnp.sum(grad_branch.astype(jnp.float32), axis=0)
    grad_w_back = across(active_low, grad_branch)
    grad_active = against(grad_branch, w_back).astype(jnp.bfloat16).astype(jnp.float32)
    grad_before = (grad_active * gelu_slope(before)).astype(jnp.bfloat16)
    grad_b_in = jnp.sum(grad_before.astype(jnp.float32), axis=0)
    grad_w_in = across(normed_low, grad_before)
    grad_normed = grad_mid + rounded(
        lax.psum(against(grad_before, w_in).astype(jnp.bfloat16), "tensor").astype(jnp.float32)
    )
    grad_hidden, grad_gain_one, grad_shift_one = norm_back(
        grad_normed, unit_one, inverse_one, norm_gains[0]
    )
    grad_attention = grad_hidden.astype(jnp.bfloat16)
    grad_b_out = jnp.sum(grad_attention.astype(jnp.float32), axis=0)
    grad_w_out = across(mixed_low, grad_attention)
    grad_mixed = against(grad_attention, w_out).astype(jnp.bfloat16)
    dout_heads = grad_mixed.reshape(head_shape)
    delta = jnp.swapaxes(jnp.sum(dout_heads.astype(jnp.float32) * mixed_heads, axis=-1), 1, 2)
    key_all, value_all = key_piece, value_piece
    key_blocks = jnp.moveaxis(key_all.reshape(seq_count, block_count, span, heads, HEAD_DIM), 1, 0)
    value_blocks = jnp.moveaxis(
        value_all.reshape(seq_count, block_count, span, heads, HEAD_DIM), 1, 0
    )
    visible_all = jnp.arange(seq_len, dtype=jnp.int32)[None, :] < lengths[:, None]
    visible_blocks = jnp.moveaxis(visible_all.reshape(seq_count, block_count, span), 1, 0)

    def sweep_keys(grad_query, item):
        key_block, value_block, visible_block = item
        part_query, part_key, part_value = pair_grads(
            query_heads, dout_heads, log_total, delta, key_block, value_block, visible_block
        )
        return (grad_query + part_query, (part_key, part_value))

    grad_query, (key_terms, value_terms) = lax.scan(
        sweep_keys, jnp.zeros(head_shape, jnp.float32), (key_blocks, value_blocks, visible_blocks)
    )
    key_terms = jnp.moveaxis(key_terms, 0, 1).reshape(seq_count, seq_len, share)
    value_terms = jnp.moveaxis(value_terms, 0, 1).reshape(seq_count, seq_len, share)
    key_sum, value_sum = (
        lax.psum_scatter(
            key_terms.astype(jnp.bfloat16), "blk", scatter_dimension=1, tiled=True
        ).astype(jnp.float32),
        lax.psum_scatter(
            value_terms.astype(jnp.bfloat16), "blk", scatter_dimension=1, tiled=True
        ).astype(jnp.float32),
    )
    grad_query_low = (grad_query * scale).reshape(seq_count * row_count, share).astype(jnp.bfloat16)
    grad_key_low = (key_sum * scale).reshape(seq_count * row_count, share).astype(jnp.bfloat16)
    grad_value_low = value_sum.reshape(seq_count * row_count, share).astype(jnp.bfloat16)
    grad_stack = jnp.stack([grad_query_low, grad_key_low, grad_value_low])
    grad_w_qkv = jnp.einsum(
        "nd,tne->tde", low_tokens, grad_stack, preferred_element_type=jnp.float32
    )
    grad_b_qv = jnp.stack(
        [
            jnp.sum(grad_query_low.astype(jnp.float32), axis=0),
            jnp.sum(grad_value_low.astype(jnp.float32), axis=0),
        ]
    )
    grad_through = lax.psum(
        jnp.einsum("tne,tde->nd", grad_stack, w_qkv, preferred_element_type=jnp.float32).astype(
            jnp.bfloat16
        ),
        "tensor",
    ).astype(jnp.float32)
    grad_tokens = (grad_hidden + rounded(grad_through)).reshape(tokens.shape)
    grad_gains = jnp.stack([grad_gain_one, grad_gain_two])
    grad_shifts = jnp.stack([grad_shift_one, grad_shift_two])
    grads = (
        grad_w_qkv,
        grad_b_qv,
        grad_w_out,
        grad_b_out,
        grad_w_in,
        grad_b_in,
        grad_w_back,
        grad_b_back,
        grad_gains,
        grad_shifts,
    )
    return (outputs, grad_tokens, grads)


def shards(
    x_train,
    x_quiz,
    cot_train,
    cot_quiz,
    quiz_lengths,
    w_qkv,
    b_qv,
    w_out,
    b_out,
    w_in,
    b_in,
    w_back,
    b_back,
    norm_gains,
    norm_shifts,
):
    row_count = x_train.shape[1]
    seq_len = row_count * lax.axis_size("blk")
    first_row = lax.axis_index("blk") * row_count
    share = D // lax.axis_size("tensor")
    column = lax.axis_index("tensor") * share
    weights = (w_qkv, b_qv, w_out, b_out, w_in, b_in, w_back, b_back, norm_gains, norm_shifts)
    full_lengths = jnp.full((x_train.shape[0],), seq_len, jnp.int32)
    out_train, grad_in_train, train_grads = run(
        x_train, cot_train, full_lengths, first_row, weights
    )
    out_quiz, grad_in_quiz, quiz_grads = run(x_quiz, cot_quiz, quiz_lengths, first_row, weights)
    def total(grads):
        pieces = (
            grads[0],
            grads[1],
            grads[2],
            crop(grads[3], column, share),
            grads[4],
            grads[5],
            grads[6],
            crop(grads[7], column, share),
            crop(grads[8], column, share),
            crop(grads[9], column, share),
        )
        low = tuple(piece.astype(jnp.bfloat16) for piece in pieces)
        return tuple(
            piece.astype(jnp.float32) for piece in lax.psum(low, ("dp", "blk"))
        )

    summed = [jnp.stack(pair) for pair in zip(total(train_grads), total(quiz_grads))]
    return (
        out_train,
        out_quiz,
        grad_in_train,
        grad_in_quiz,
        summed[0],
        summed[1],
        summed[2],
        summed[3],
        summed[4],
        summed[5],
        summed[6],
        summed[7],
        summed[8],
        summed[9],
    )


def solution(mesh):
    placed = (
        P("dp", "blk", None),
        P("dp", "blk", None),
        P("dp", "blk", None),
        P("dp", "blk", None),
        P("dp"),
        P(None, None, "tensor"),
        P(None, "tensor"),
        P("tensor", None),
        P(),
        P(None, "tensor"),
        P("tensor"),
        P("tensor", None),
        P(),
        P(),
        P(),
    )
    return jax.shard_map(
        shards,
        mesh=mesh,
        in_specs=placed,
        out_specs=(
            P("dp", "blk", None),
            P("dp", "blk", None),
            P("dp", "blk", None),
            P("dp", "blk", None),
            P(None, None, None, "tensor"),
            P(None, None, "tensor"),
            P(None, "tensor", None),
            P(None, "tensor"),
            P(None, None, "tensor"),
            P(None, "tensor"),
            P(None, "tensor", None),
            P(None, "tensor"),
            P(None, None, "tensor"),
            P(None, None, "tensor"),
        ),
        check_vma=False,
    )
```

```python
import functools

import jax
import jax.numpy as jnp
from jax import lax
from jax.experimental import pallas as pl
from jax.experimental.pallas import tpu as pltpu
from jax.sharding import PartitionSpec as P

D = 768
HEAD_DIM = 64


EPSILON = 1e-12
ROOT_HALF = 0.7071067811865476
ROOT_TWO_PI = 2.5066282746310002
NEG_LARGE = -1e30


def layer_norm(hidden, gain, shift):
    center = hidden - jnp.mean(hidden, axis=-1, keepdims=True)
    inverse = lax.rsqrt(jnp.mean(center * center, axis=-1, keepdims=True) + EPSILON)
    normal = center * inverse
    return (normal * gain + shift, normal, inverse)


def norm_back(grad_out, normal, inverse, gain):
    scaled = grad_out * gain
    grad_in = inverse * (
        scaled
        - jnp.mean(scaled, axis=-1, keepdims=True)
        - normal * jnp.mean(scaled * normal, axis=-1, keepdims=True)
    )
    return (grad_in, jnp.sum(grad_out * normal, axis=0), jnp.sum(grad_out, axis=0))


def gelu_exact(values):
    return 0.5 * values * (1.0 + lax.erf(values * ROOT_HALF))


def gelu_slope(values):
    return (
        0.5 * (1.0 + lax.erf(values * ROOT_HALF))
        + values * jnp.exp(-0.5 * values * values) / ROOT_TWO_PI
    )


def across(left, right):
    return lax.dot_general(
        left, right, (((0,), (0,)), ((), ())), preferred_element_type=jnp.float32
    )


def against(left, right):
    return lax.dot_general(
        left, right, (((1,), (1,)), ((), ())), preferred_element_type=jnp.float32
    )


def rounded(values):
    return lax.optimization_barrier(values.astype(jnp.bfloat16)).astype(jnp.float32)


def crop(values, column, share):
    return lax.dynamic_slice_in_dim(values, column, share, axis=values.ndim - 1)


def pair_grads(query_heads, dout_heads, log_total, delta, key_heads, value_heads, visible):
    scale = query_heads.shape[-1] ** (-0.5)
    scores = (
        jnp.einsum("sqhe,skhe->shqk", query_heads, key_heads, preferred_element_type=jnp.float32)
        * scale
    )
    probs = jnp.where(visible[:, None, None, :], jnp.exp(scores - log_total[..., None]), 0.0)
    grad_value = jnp.einsum(
        "shqk,sqhe->skhe",
        probs.astype(jnp.bfloat16),
        dout_heads,
        preferred_element_type=jnp.float32,
    )
    grad_probs = jnp.einsum(
        "sqhe,skhe->shqk", dout_heads, value_heads, preferred_element_type=jnp.float32
    )
    grad_scores = (probs * (grad_probs - delta[..., None])).astype(jnp.bfloat16)
    grad_query = jnp.einsum(
        "shqk,skhe->sqhe", grad_scores, key_heads, preferred_element_type=jnp.float32
    )
    grad_key = jnp.einsum(
        "shqk,sqhe->skhe", grad_scores, query_heads, preferred_element_type=jnp.float32
    )
    return (grad_query, grad_key, grad_value)


def run(tokens, cotangent, lengths, first_row, weights):
    w_qkv, b_qv, w_out, b_out, w_in, b_in, w_back, b_back, norm_gains, norm_shifts = weights
    seq_count, row_count, width = tokens.shape
    seq_len = row_count * lax.axis_size("blk")
    span = min(512, seq_len)
    block_count = seq_len // span
    flat_tokens = tokens.reshape(seq_count * row_count, width)
    low_tokens = flat_tokens.astype(jnp.bfloat16)
    projected = jnp.einsum("nd,tde->tne", low_tokens, w_qkv, preferred_element_type=jnp.float32)
    qv_bias = b_qv.astype(jnp.float32)
    query = (projected[0] + qv_bias[0]).astype(jnp.bfloat16)
    key_rows = projected[1].astype(jnp.bfloat16)
    value_rows = (projected[2] + qv_bias[1]).astype(jnp.bfloat16)
    share = key_rows.shape[-1]
    heads = share // HEAD_DIM
    scale = HEAD_DIM ** (-0.5)
    head_shape = (seq_count, row_count, heads, HEAD_DIM)
    query_heads = query.reshape(head_shape)
    key_three = key_rows.reshape(seq_count, row_count, share)
    value_three = value_rows.reshape(seq_count, row_count, share)
    running_max = jnp.full((seq_count, heads, row_count), NEG_LARGE, jnp.float32)
    running_out = jnp.zeros(head_shape, jnp.float32)
    key_piece = lax.all_gather(key_three, "blk", axis=1, tiled=True)
    value_piece = lax.all_gather(value_three, "blk", axis=1, tiled=True)
    piece_rows = key_piece.shape[1]
    key_heads = key_piece.reshape(seq_count, piece_rows, heads, HEAD_DIM)
    value_heads = value_piece.reshape(seq_count, piece_rows, heads, HEAD_DIM)
    scores = (
        jnp.einsum("sqhe,skhe->shqk", query_heads, key_heads, preferred_element_type=jnp.float32)
        * scale
    )
    visible = (jnp.arange(piece_rows, dtype=jnp.int32)[None, :] < lengths[:, None])[
        :, None, None, :
    ]
    scores = jnp.where(visible, scores, NEG_LARGE)
    new_max = jnp.maximum(running_max, jnp.max(scores, axis=-1))
    factor = jnp.exp(running_max - new_max)
    raised = jnp.where(visible, jnp.exp(scores - new_max[..., None]), 0.0)
    new_sum = jnp.sum(raised, axis=-1)
    added = jnp.einsum(
        "shqk,skhe->sqhe",
        raised.astype(jnp.bfloat16),
        value_heads,
        preferred_element_type=jnp.float32,
    )
    new_out = running_out * jnp.swapaxes(factor, 1, 2)[..., None] + added
    mixed_heads = new_out / jnp.swapaxes(new_sum, 1, 2)[..., None]
    log_total = new_max + jnp.log(new_sum)
    mixed_low = mixed_heads.reshape(seq_count * row_count, share).astype(jnp.bfloat16)
    attention = lax.psum(
        jnp.dot(mixed_low, w_out, preferred_element_type=jnp.float32).astype(jnp.bfloat16), "tensor"
    ).astype(jnp.float32) + b_out.astype(jnp.float32)
    normed, unit_one, inverse_one = layer_norm(
        flat_tokens + attention, norm_gains[0], norm_shifts[0]
    )
    normed_low = normed.astype(jnp.bfloat16)
    before = jnp.dot(normed_low, w_in, preferred_element_type=jnp.float32) + b_in.astype(
        jnp.float32
    )
    active_low = gelu_exact(before).astype(jnp.bfloat16)
    branch = lax.psum(
        jnp.dot(active_low, w_back, preferred_element_type=jnp.float32).astype(jnp.bfloat16),
        "tensor",
    ).astype(jnp.float32) + b_back.astype(jnp.float32)
    final, unit_two, inverse_two = layer_norm(normed + branch, norm_gains[1], norm_shifts[1])
    positions = first_row + jnp.arange(row_count, dtype=jnp.int32)
    keep_rows = (
        (positions[None, :] < lengths[:, None])
        .reshape(seq_count * row_count, 1)
        .astype(jnp.float32)
    )
    outputs = (keep_rows * final).reshape(tokens.shape)
    grad_final = keep_rows * cotangent.reshape(seq_count * row_count, width)
    grad_mid, grad_gain_two, grad_shift_two = norm_back(
        grad_final, unit_two, inverse_two, norm_gains[1]
    )
    grad_branch = grad_mid.astype(jnp.bfloat16)
    grad_b_back = jnp.sum(grad_branch.astype(jnp.float32), axis=0)
    grad_w_back = across(active_low, grad_branch)
    grad_active = against(grad_branch, w_back).astype(jnp.bfloat16).astype(jnp.float32)
    grad_before = (grad_active * gelu_slope(before)).astype(jnp.bfloat16)
    grad_b_in = jnp.sum(grad_before.astype(jnp.float32), axis=0)
    grad_w_in = across(normed_low, grad_before)
    grad_normed = grad_mid + rounded(
        lax.psum(against(grad_before, w_in).astype(jnp.bfloat16), "tensor").astype(jnp.float32)
    )
    grad_hidden, grad_gain_one, grad_shift_one = norm_back(
        grad_normed, unit_one, inverse_one, norm_gains[0]
    )
    grad_attention = grad_hidden.astype(jnp.bfloat16)
    grad_b_out = jnp.sum(grad_attention.astype(jnp.float32), axis=0)
    grad_w_out = across(mixed_low, grad_attention)
    grad_mixed = against(grad_attention, w_out).astype(jnp.bfloat16)
    dout_heads = grad_mixed.reshape(head_shape)
    delta = jnp.swapaxes(jnp.sum(dout_heads.astype(jnp.float32) * mixed_heads, axis=-1), 1, 2)
    key_all, value_all = key_piece, value_piece
    key_blocks = jnp.moveaxis(key_all.reshape(seq_count, block_count, span, heads, HEAD_DIM), 1, 0)
    value_blocks = jnp.moveaxis(
        value_all.reshape(seq_count, block_count, span, heads, HEAD_DIM), 1, 0
    )
    visible_all = jnp.arange(seq_len, dtype=jnp.int32)[None, :] < lengths[:, None]
    visible_blocks = jnp.moveaxis(visible_all.reshape(seq_count, block_count, span), 1, 0)

    def sweep_keys(grad_query, item):
        key_block, value_block, visible_block = item
        part_query, part_key, part_value = pair_grads(
            query_heads, dout_heads, log_total, delta, key_block, value_block, visible_block
        )
        return (grad_query + part_query, (part_key, part_value))

    grad_query, (key_terms, value_terms) = lax.scan(
        sweep_keys, jnp.zeros(head_shape, jnp.float32), (key_blocks, value_blocks, visible_blocks)
    )
    key_terms = jnp.moveaxis(key_terms, 0, 1).reshape(seq_count, seq_len, share)
    value_terms = jnp.moveaxis(value_terms, 0, 1).reshape(seq_count, seq_len, share)
    key_sum, value_sum = (
        lax.psum_scatter(
            key_terms.astype(jnp.bfloat16), "blk", scatter_dimension=1, tiled=True
        ).astype(jnp.float32),
        lax.psum_scatter(
            value_terms.astype(jnp.bfloat16), "blk", scatter_dimension=1, tiled=True
        ).astype(jnp.float32),
    )
    grad_query_low = (grad_query * scale).reshape(seq_count * row_count, share).astype(jnp.bfloat16)
    grad_key_low = (key_sum * scale).reshape(seq_count * row_count, share).astype(jnp.bfloat16)
    grad_value_low = value_sum.reshape(seq_count * row_count, share).astype(jnp.bfloat16)
    grad_stack = jnp.stack([grad_query_low, grad_key_low, grad_value_low])
    grad_w_qkv = jnp.einsum(
        "nd,tne->tde", low_tokens, grad_stack, preferred_element_type=jnp.float32
    )
    grad_b_qv = jnp.stack(
        [
            jnp.sum(grad_query_low.astype(jnp.float32), axis=0),
            jnp.sum(grad_value_low.astype(jnp.float32), axis=0),
        ]
    )
    grad_through = lax.psum(
        jnp.einsum("tne,tde->nd", grad_stack, w_qkv, preferred_element_type=jnp.float32).astype(
            jnp.bfloat16
        ),
        "tensor",
    ).astype(jnp.float32)
    grad_tokens = (grad_hidden + rounded(grad_through)).reshape(tokens.shape)
    grad_gains = jnp.stack([grad_gain_one, grad_gain_two])
    grad_shifts = jnp.stack([grad_shift_one, grad_shift_two])
    grads = (
        grad_w_qkv,
        grad_b_qv,
        grad_w_out,
        grad_b_out,
        grad_w_in,
        grad_b_in,
        grad_w_back,
        grad_b_back,
        grad_gains,
        grad_shifts,
    )
    return (outputs, grad_tokens, grads)


def shards(
    x_train,
    x_quiz,
    cot_train,
    cot_quiz,
    quiz_lengths,
    w_qkv,
    b_qv,
    w_out,
    b_out,
    w_in,
    b_in,
    w_back,
    b_back,
    norm_gains,
    norm_shifts,
):
    row_count = x_train.shape[1]
    seq_len = row_count * lax.axis_size("blk")
    first_row = lax.axis_index("blk") * row_count
    share = D // lax.axis_size("tensor")
    column = lax.axis_index("tensor") * share
    weights = (w_qkv, b_qv, w_out, b_out, w_in, b_in, w_back, b_back, norm_gains, norm_shifts)
    full_lengths = jnp.full((x_train.shape[0],), seq_len, jnp.int32)
    out_train, grad_in_train, train_grads = run(
        x_train, cot_train, full_lengths, first_row, weights
    )
    out_quiz, grad_in_quiz, quiz_grads = run(x_quiz, cot_quiz, quiz_lengths, first_row, weights)
    def total(grads):
        pieces = (
            grads[0],
            grads[1],
            grads[2],
            crop(grads[3], column, share),
            grads[4],
            grads[5],
            grads[6],
            crop(grads[7], column, share),
            crop(grads[8], column, share),
            crop(grads[9], column, share),
        )
        low = tuple(piece.astype(jnp.bfloat16) for piece in pieces)
        return tuple(
            piece.astype(jnp.float32) for piece in lax.psum(low, ("dp", "blk"))
        )

    summed = [jnp.stack(pair) for pair in zip(total(train_grads), total(quiz_grads))]
    return (
        out_train,
        out_quiz,
        grad_in_train,
        grad_in_quiz,
        summed[0],
        summed[1],
        summed[2],
        summed[3],
        summed[4],
        summed[5],
        summed[6],
        summed[7],
        summed[8],
        summed[9],
    )


MESH_ID = pl.DeviceIdType.MESH
F32 = jnp.float32
BF16 = jnp.bfloat16
SMALL = 32
BACK_KINDS = "xwxzxz"
IN_KINDS = "xxxxxx"
OUT_KINDS = "x"
QKV_KINDS = "xxwxxw"
INV_ROOT_TWO_PI = 1.0 / ROOT_TWO_PI
SETTLE_AGE = 100
WEIGHT_TILE = 256


def nn(left, right):
    return jnp.dot(left, right, preferred_element_type=F32)


def tile_loop(count, tile, body):
    def step(index, carry):
        body(pl.multiple_of(index * tile, tile))
        return carry

    lax.fori_loop(0, count // tile, step, 0)


def tiles(count, tile, body):
    for start in range(0, count, tile):
        body(start)


def sum_rows(value):
    return jnp.sum(value, axis=0, keepdims=True)


def lanes(count):
    return (count // 128 + 1) * 128


class Sizes:
    def __init__(self, nt, nq, rows, blocks, share, width, hidden):
        self.nt, self.nq, self.rows, self.blocks = nt, nq, rows, blocks
        self.share, self.width, self.hidden = share, width, hidden
        self.ns = nt + nq
        self.quarter = rows // 4
        self.seq_len = rows * blocks
        self.heads = share // HEAD_DIM
        self.back0 = 0
        self.in0 = hidden
        self.out0 = hidden + width
        self.qkv0 = self.out0 + share
        self.small0 = self.qkv0 + 3 * share
        self.total = self.small0 + SMALL
        half = self.quarter // 2
        self.streams = tuple((s, part * half, half) for s in range(nt) for part in range(2))
        self.streams += tuple((s, 0, self.quarter) for s in range(nt, self.ns))
        self.streams += tuple((s, 0, self.quarter) for s in range(nt))
        self.chunks = self.plan()
        self.first_half, self.first_zone, half, zone = [], [], 0, 0
        for _, count, kind in self.chunks:
            self.first_half.append(half)
            self.first_zone.append(zone)
            half += count // 2
            zone += count // 2 if kind == "x" else count
        self.half_rows, self.zone_rows = half, zone

    def plan(self):
        pieces = []
        for first, count, kinds in (
            (self.back0, self.hidden, BACK_KINDS),
            (self.in0, self.width, IN_KINDS),
            (self.out0, self.share, OUT_KINDS),
            (self.qkv0, 3 * self.share, QKV_KINDS),
        ):
            size = count // len(kinds)
            for index, kind in enumerate(kinds):
                pieces.append((first + index * size, size, kind))
        first, count, kind = pieces[-1]
        pieces[-1] = (first, count + SMALL, kind)
        return tuple(pieces)

    def scratch(self):
        ns, rows, share, width = self.ns, self.rows, self.share, self.width
        q, blocks, seq = self.quarter, self.blocks, self.seq_len
        dma = pltpu.SemaphoreType.DMA
        nc, nu = len(self.chunks), len(self.streams)
        return dict(
            xown=pltpu.VMEM((ns, q, width), F32),
            cown=pltpu.VMEM((ns, q, width), F32),
            vec=pltpu.VMEM((16, width), F32),
            xg=pltpu.VMEM((ns, seq, width), BF16),
            wqkv=pltpu.VMEM((3, share, width), BF16),
            wout=pltpu.VMEM((share, width), BF16),
            win=pltpu.VMEM((width, self.hidden), BF16),
            wback=pltpu.VMEM((self.hidden, width), BF16),
            qb=pltpu.VMEM((ns, rows, share), BF16),
            kb=pltpu.VMEM((ns, seq, share), BF16),
            vb=pltpu.VMEM((ns, seq, lanes(share)), BF16),
            probs=pltpu.VMEM((ns, self.heads, rows, seq), BF16),
            of=pltpu.VMEM((rows, lanes(share)), F32),
            invl=pltpu.VMEM((ns, rows, share), F32),
            orb=pltpu.VMEM((ns, rows, share), BF16),
            unit1=pltpu.VMEM((ns, q, width), F32),
            inv1=pltpu.VMEM((ns, q, 128), F32),
            n1r=pltpu.VMEM((ns, 4, q, width), BF16),
            dzr=pltpu.VMEM((ns, 4, q, width), BF16),
            dar=pltpu.VMEM((ns, 4, q, width), BF16),
            act=pltpu.VMEM((ns, 4, q, self.hidden), BF16),
            slope=pltpu.VMEM((ns, 4, q, self.hidden), BF16),
            work=pltpu.VMEM((rows, max(seq, width)), F32),
            dsb=pltpu.VMEM((rows, seq), BF16),
            dqb=pltpu.VMEM((ns, rows, share), BF16),
            dkvt=pltpu.VMEM((ns, 2, share, seq), BF16),
            tq=pltpu.VMEM((share, rows), BF16),
            tm=pltpu.VMEM((share, rows), BF16),
            gm=pltpu.VMEM((rows, share), BF16),
            delta=pltpu.VMEM((rows, 128), F32),
            part=pltpu.VMEM((ns, 2, 2, q, width), BF16),
            crecv=pltpu.VMEM((3, ns, 2, q, width), BF16),
            yrecv=pltpu.VMEM((3, ns, q, width), BF16),
            part4=pltpu.VMEM((ns, blocks, 2, 2, q, width), BF16),
            crecv4=pltpu.VMEM((ns, blocks, 2, q, width), BF16),
            yrecv4=pltpu.VMEM((ns, blocks, q, width), BF16),
            zrecv4=pltpu.VMEM((ns, 2, blocks - 1, q, width), BF16),
            outq=pltpu.VMEM((ns, q, width), BF16),
            ginq=pltpu.VMEM((ns, q, width), BF16),
            gb=pltpu.VMEM((2, self.total, width), BF16),
            xrecv=pltpu.VMEM((2, self.half_rows, width), BF16),
            zr1=pltpu.VMEM((2, self.zone_rows, width), BF16),
            zr2=pltpu.VMEM((2, self.half_rows, width), BF16),
            small=pltpu.VMEM((2, SMALL, width), F32),
            smallc=pltpu.VMEM((2, 8, width), F32),
            smalls=pltpu.VMEM((2, 8, width), F32),
            smally=pltpu.VMEM((2, 8, width), F32),
            load_sem=dma((2 * ns + 5,)),
            xz_s=dma((nu, 2, blocks - 1)),
            xz_r=dma((nu, 2, blocks - 1)),
            xc_s=dma((nu, 2, blocks - 1, 3)),
            xc_r=dma((nu, 2, blocks - 1, 3)),
            ex_s=dma((3, nu, 5)),
            ex_r=dma((3, nu, 5)),
            d4_s=dma((ns, 2)),
            d4_r=dma((ns, 2)),
            z4_s=dma((ns, 2, blocks - 1)),
            z4_r=dma((ns, 2, blocks - 1)),
            og_s=dma((2, ns, 3)),
            og_r=dma((2, ns, 3)),
            ol_s=dma((2, ns)),
            ar_s=dma((2, nc, 13)),
            ar_r=dma((2, nc, 13)),
            al_s=dma((2, nc)),
            sm_s=dma((2, 2)),
            sm_r=dma((2, 2)),
        )


INPUTS = (
    "xt", "xq", "ct", "cq", "lens", "wqkv_in", "wout_in", "win_in", "wback_in",
    "b_out", "b_in", "b_back", "gains", "shifts", "b_qv",
)
OUTPUTS = ("out", "gin", "grad")


def layer_kernel(z_, *refs):
    names = INPUTS + OUTPUTS + tuple(z_.scratch())
    r = dict(zip(names, refs))
    nt, ns, rows, blocks = z_.nt, z_.ns, z_.rows, z_.blocks
    share, width, hidden, quarter = z_.share, z_.width, z_.hidden, z_.quarter
    seq_len, heads = z_.seq_len, z_.heads
    scale = HEAD_DIM ** (-0.5)
    batches = (tuple(range(nt)), tuple(range(nt, ns)))
    lens_ref = r["lens"]
    xg, work, part, gb = r["xg"], r["work"], r["part"], r["gb"]

    x = lax.axis_index("dp")
    t = lax.axis_index("tensor")
    z = lax.axis_index("blk")
    y = t // 2
    c = t % 2
    to_x = (1 - x, t, z)
    to_c = (x, t + 1 - 2 * c, z)
    to_y = (x, (t + 2) % 4, z)
    to_d = (x, 3 - t, z)
    to_right = (x, t, jnp.minimum(z + 1, blocks - 1))
    to_left = (x, t, jnp.maximum(z - 1, 0))
    has_left = z > 0
    has_right = z < blocks - 1
    corner = jnp.logical_or(z == 0, z == blocks - 1)
    interior = jnp.logical_and(z > 0, z < blocks - 1)
    to_inner = (x, t, jnp.where(z == 0, 1, blocks - 2))
    to_mirror = (x, t, blocks - 1 - z)
    to_outer = (x, t, jnp.where(z == 1, 0, blocks - 1))
    finals, sent, ages = [], [], []

    def settle(count=3, age=SETTLE_AGE):
        ages.append(len(sent))
        ready = ages[-age] if len(ages) >= age else 0
        for _ in range(min(count, ready - settled[0])):
            sent[settled[0]]()
            settled[0] += 1

    settled = [0]

    def when(cond, fn):
        if cond is None:
            fn()
        else:
            pl.when(cond)(fn)

    def remote(src, dst, ssem, rsem, dev):
        return pltpu.make_async_remote_copy(
            src_ref=src,
            dst_ref=dst,
            send_sem=ssem,
            recv_sem=rsem,
            device_id=dev,
            device_id_type=MESH_ID,
        )

    def send(src, dst, ssem, rsem, dev, cond=None, final=True):
        when(cond, lambda: remote(src, dst, ssem, rsem, dev).start())
        if final:
            sent.append(
                lambda: when(cond, lambda: remote(src, dst, ssem, rsem, dev).wait_send())
            )

    def arrived(dst, ssem, rsem, dev, cond=None):
        when(cond, lambda: remote(dst, dst, ssem, rsem, dev).wait_recv())

    def local(src, dst, sem):
        copy = pltpu.make_async_copy(src, dst, sem)
        copy.start()
        return copy

    mine = pl.ds(pl.multiple_of(t * quarter, quarter), quarter)
    facing = (t + 2) % 4

    def stream(u):
        s, first, count = z_.streams[u]
        return s, pl.ds(first, count)

    def flat(ref, s, lanes_=slice(None)):
        value = ref[s, :, :, lanes_]
        return value.reshape(rows, value.shape[-1])
    own_block = pl.ds(pl.multiple_of(z * rows, rows), rows)

    vec_ref = r["vec"]

    def vec(row, size=None):
        return vec_ref[row : row + 1, : (size or width)]

    def gather_vectors():
        for row, name in enumerate(("b_out", "b_in", "b_back")):
            vec_ref[row : row + 1, :] = r[name][...].astype(F32).reshape(1, width)
        vec_ref[3:5, :] = r["gains"][...]
        vec_ref[5:7, :] = r["shifts"][...]
        vec_ref[7:9, :share] = r["b_qv"][...].astype(F32)

    gather_vectors()
    loads = {}
    load_sem = r["load_sem"]
    x_src = [r["xt"].at[s] for s in range(nt)] + [r["xq"].at[s] for s in range(ns - nt)]
    c_src = [r["ct"].at[s] for s in range(nt)] + [r["cq"].at[s] for s in range(ns - nt)]
    for s in range(ns):
        loads["x", s] = local(x_src[s].at[mine], r["xown"].at[s], load_sem.at[s])
    for index, name in enumerate(("wqkv", "wout", "win", "wback")):
        loads[name] = local(r[name + "_in"], r[name], load_sem.at[ns + index])
    for s in range(ns):
        loads["c", s] = local(c_src[s].at[mine], r["cown"].at[s], load_sem.at[ns + 4 + s])

    barrier = pltpu.get_barrier_semaphore()

    def greet(dev, cond=None):
        when(
            cond,
            lambda: pl.semaphore_signal(
                barrier, inc=1, device_id=dev, device_id_type=MESH_ID
            ),
        )

    for dev in (to_x, to_c, to_y, to_d):
        greet(dev)
    greet(to_left, has_left)
    greet(to_right, has_right)
    when(corner, lambda: pl.semaphore_wait(barrier, 5))
    when(interior, lambda: pl.semaphore_wait(barrier, 6))

    def block_rows(j, q, within=pl.ds(0, quarter)):
        start = j * rows + q * quarter + within.start
        return pl.ds(pl.multiple_of(start, within.size), within.size)

    def side_valid(side, d):
        return z >= d if side == 0 else z <= blocks - 1 - d

    def side_block(side, d):
        return jnp.maximum(z - d, 0) if side == 0 else jnp.minimum(z + d, blocks - 1)

    xz_s, xz_r, xc_s, xc_r = r["xz_s"], r["xz_r"], r["xc_s"], r["xc_r"]

    def xa_start(u):
        s, within = stream(u)
        if within.start == 0:
            loads["x", s].wait()
        place = block_rows(z, t, within)
        xg[s, place, :] = r["xown"][s, within, :].astype(BF16)
        here = xg.at[s, place]
        send(here, here, xz_s.at[u, 0, 0], xz_r.at[u, 0, 0], to_right, has_right)
        send(here, here, xz_s.at[u, 1, 0], xz_r.at[u, 1, 0], to_left, has_left)

    def xa_step(u, d):
        s, within = stream(u)
        for side in range(2):
            valid = side_valid(side, d)
            here = xg.at[s, block_rows(side_block(side, d), t, within)]
            arrived(here, xz_s.at[u, side, d - 1], xz_r.at[u, side, d - 1], to_c, valid)
            if d < blocks - 1:
                more = has_right if side == 0 else has_left
                send(
                    here,
                    here,
                    xz_s.at[u, side, d],
                    xz_r.at[u, side, d],
                    to_right if side == 0 else to_left,
                    jnp.logical_and(valid, more),
                )
            for kind, dev in ((0, to_y), (1, to_c)):
                pair = xc_s.at[u, side, d - 1, kind], xc_r.at[u, side, d - 1, kind]
                send(here, here, *pair, dev, valid)

    def xa_forward(u, d):
        s, within = stream(u)
        for side in range(2):
            valid = side_valid(side, d)
            here = xg.at[s, block_rows(side_block(side, d), facing, within)]
            pair = xc_s.at[u, side, d - 1, 0], xc_r.at[u, side, d - 1, 0]
            arrived(here, *pair, to_c, valid)
            pair = xc_s.at[u, side, d - 1, 2], xc_r.at[u, side, d - 1, 2]
            send(here, here, *pair, to_c, valid)

    def xa_done(u, d):
        s, within = stream(u)
        for side in range(2):
            for kind in (1, 2):
                here = xg.at[s, block_rows(side_block(side, d), t, within)]
                pair = xc_s.at[u, side, d - 1, kind], xc_r.at[u, side, d - 1, kind]
                arrived(here, *pair, to_c, side_valid(side, d))

    def own_cast(s):
        copy = local(x_src[s], work.at[:, pl.ds(0, width)], load_sem.at[2 * ns + 4])
        copy.wait()
        for q in range(4):

            def cast(q=q):
                xg[s, block_rows(z, q), :] = work[
                    q * quarter : (q + 1) * quarter, :width
                ].astype(BF16)

            when(t != q, cast)

    padded = lanes(share)
    padded_head = lax.broadcasted_iota(jnp.int32, (1, padded), 1) // HEAD_DIM
    head_of_lane = lax.broadcasted_iota(jnp.int32, (1, share), 1) // HEAD_DIM
    invl = r["invl"]
    ex_s, ex_r, crecv, yrecv = r["ex_s"], r["ex_r"], r["crecv"], r["yrecv"]

    def rs_sends(k, u):
        s, within = stream(u)
        return (
            (
                part.at[s, :, 1 - c, within],
                crecv.at[k, s, :, within],
                ex_s.at[k, u, 0],
                ex_r.at[k, u, 0],
                to_c,
            ),
            (
                part.at[s, 1 - y, c, within],
                yrecv.at[k, s, within],
                ex_s.at[k, u, 1],
                ex_r.at[k, u, 1],
                to_y,
            ),
        )

    def rs_core(k, u):
        send(*rs_sends(k, u)[0], final=False)

    def rs_y(k, u):
        s, within = stream(u)
        arrived(*rs_sends(k, u)[0][1:])
        part[s, 1 - y, c, within] = (
            part[s, 1 - y, c, within].astype(F32) + crecv[k, s, 1 - y, within].astype(F32)
        ).astype(BF16)
        send(*rs_sends(k, u)[1], final=False)

    def rs_total(k, u):
        s, within = stream(u)
        arrived(*rs_sends(k, u)[1][1:])
        return (
            part[s, y, c, within].astype(F32)
            + crecv[k, s, y, within].astype(F32)
            + yrecv[k, s, within].astype(F32)
        )

    def rs_sent(k, u):
        for args in rs_sends(k, u):
            remote(*args).wait_send()

    def ag_start(k, u, full):
        s, within = stream(u)
        here = full.at[s, t, within]
        send(here, here, ex_s.at[k, u, 3], ex_r.at[k, u, 3], to_y)
        send(here, here, ex_s.at[k, u, 2], ex_r.at[k, u, 2], to_c)

    def ag_forward(k, u, full):
        s, within = stream(u)
        here = full.at[s, facing, within]
        arrived(here, ex_s.at[k, u, 3], ex_r.at[k, u, 3], to_y)
        send(here, here, ex_s.at[k, u, 4], ex_r.at[k, u, 4], to_c)

    def ag_done(k, u, full):
        s, within = stream(u)
        here = full.at[s, t, within]
        arrived(here, ex_s.at[k, u, 2], ex_r.at[k, u, 2], to_c)
        arrived(here, ex_s.at[k, u, 4], ex_r.at[k, u, 4], to_c)

    def publish(buf, s, target, kind):
        here = target.at[s, mine]
        og_s, og_r = r["og_s"], r["og_r"]
        devices = tuple(enumerate((to_c, to_y, to_d)))
        for index, dev in devices:
            sems = og_s.at[kind, s, index], og_r.at[kind, s, index]
            send(buf.at[s], here, *sems, dev)
        copy = local(buf.at[s], here, r["ol_s"].at[kind, s])
        finals.append(copy.wait)

        def landed():
            for index, dev in devices:
                arrived(here, og_s.at[kind, s, index], og_r.at[kind, s, index], dev)

        finals.append(landed)

    def batch_of(s):
        return 0 if s < nt else 1

    def length(s):
        return jnp.int32(seq_len) if s < nt else lens_ref[s - nt]

    def keep_rows(s, within):
        first = z * rows + t * quarter + within.start
        position = first + lax.broadcasted_iota(jnp.int32, (within.size, 1), 0)
        return jnp.where(position < length(s), 1.0, 0.0)

    qb, kb, vb, probs, of, orb = (r[n] for n in ("qb", "kb", "vb", "probs", "of", "orb"))
    wqkv, wout, win, wback = (r[n] for n in ("wqkv", "wout", "win", "wback"))
    unit1, inv1 = r["unit1"], r["inv1"]
    dh = r["xown"]
    n1r, dzr, dar, act, slope = (r[n] for n in ("n1r", "dzr", "dar", "act", "slope"))
    dsb, dqb, dkvt = (r[n] for n in ("dsb", "dqb", "dkvt"))
    small = r["small"]
    tq, tm, gm, delta = (r[n] for n in ("tq", "tm", "gm", "delta"))

    def add_small(s, row, value, size=None):
        place = (batch_of(s), slice(row, row + 1), slice(0, size or width))
        small[place] += value

    def project_query(s):
        low = (against(xg[s, own_block, :], wqkv[0]) + vec(7, share)).astype(BF16)
        qb[s] = low * jnp.array(scale, BF16)

    def project_block(s, start):
        lane = lax.broadcasted_iota(jnp.int32, (rows, padded - share), 1)
        place = pl.ds(start, rows)
        block = xg[s, place, :]
        kb[s, place, :] = against(block, wqkv[1]).astype(BF16)
        vb[s, place, :share] = (against(block, wqkv[2]) + vec(8, share)).astype(BF16)
        vb[s, place, share:] = jnp.where(lane == 0, 1.0, 0.0).astype(BF16)

    def project_own(s):
        project_block(s, pl.multiple_of(z * rows, rows))

    def project_rest(s):
        for j in range(1, blocks):
            project_block(s, pl.multiple_of(((z + j) % blocks) * rows, rows))

    def store_part(s, cols, value, within=pl.ds(0, quarter)):
        low = value.astype(BF16).reshape(2, 2, within.size, value.shape[-1])
        part[s, :, :, within, cols] = low

    key_tiles = tuple(slice(first, first + 256) for first in range(0, seq_len, 256))

    def folded_max(value, running):
        for first in range(0, value.shape[-1], 128):
            piece = value[:, first : first + 128]
            running = piece if running is None else jnp.maximum(running, piece)
        return running

    def attention(s, h):
        if h == 0:
            of[...] = jnp.zeros((rows, padded), F32)
            invl[s] = jnp.zeros((rows, share), F32)
        mask = head_of_lane == h
        query = jnp.where(mask, qb[s], jnp.zeros((), BF16))
        highest = None
        for tile in key_tiles:
            scores = against(query, kb[s, tile, :])
            if s >= nt:
                position = tile.start + lax.broadcasted_iota(jnp.int32, (1, 256), 1)
                scores += jnp.where(position < length(s), 0.0, NEG_LARGE)
            work[:, tile] = scores
            highest = folded_max(scores, highest)
        delta[...] = jnp.broadcast_to(
            jnp.max(highest, axis=-1, keepdims=True), (rows, 128)
        )

        top = delta[...]
        mixed = None
        for tile in key_tiles:
            for first in range(tile.start, tile.stop, 128):
                piece = slice(first, first + 128)
                probs[s, h, :, piece] = jnp.exp(work[:, piece] - top).astype(BF16)
            term = nn(probs[s, h, :, tile], vb[s, tile, :])
            mixed = term if mixed is None else mixed + term
        inverse = 1.0 / mixed[:, share : share + 1]
        of[...] = jnp.where(padded_head == h, mixed * inverse, of[...])
        invl[s] = jnp.where(mask, inverse, invl[s])

    def attention_out(s):
        orb[s] = of[:, :share].astype(BF16)

        def body(start):
            cols = pl.ds(start, 256)
            store_part(s, cols, nn(orb[s], wout[:, cols]))

        tiles(width, 256, body)

    def forward_rows(u):
        s, within = stream(u)
        summed = r["xown"][s, within] + (rs_total(0, u) + vec(0))
        center = summed - jnp.mean(summed, axis=-1, keepdims=True)
        inverse = lax.rsqrt(jnp.mean(center * center, axis=-1, keepdims=True) + EPSILON)
        normal = center * inverse
        unit1[s, within] = normal
        inv1[s, within] = jnp.broadcast_to(inverse, (within.size, 128))
        n1r[s, t, within] = (normal * vec(3) + vec(5)).astype(BF16)

    def feed_forward(u):
        s, within = stream(u)
        count = 4 * within.size

        def up(start):
            cols = pl.ds(start, 256)
            left = n1r[s, :, within, :].reshape(count, width)
            before = nn(left, win[:, cols]) + vec_ref[1:2, cols]
            phi = 0.5 * (1.0 + lax.erf(before * ROOT_HALF))
            low = (before * phi).astype(BF16)
            act[s, :, within, cols] = low.reshape(4, within.size, 256)
            bell = jnp.exp(-0.5 * before * before) * INV_ROOT_TWO_PI
            low = (phi + before * bell).astype(BF16)
            slope[s, :, within, cols] = low.reshape(4, within.size, 256)

        tiles(hidden, 256, up)
        rs_sent(0, u)

        def down(start):
            cols = pl.ds(start, 256)
            left = act[s, :, within, :].reshape(count, hidden)
            store_part(s, cols, nn(left, wback[:, cols]), within)

        tiles(width, 256, down)

    def norm_back_rows(grad_out, normal, inverse, gain):
        scaled = grad_out * gain
        return inverse * (
            scaled
            - jnp.mean(scaled, axis=-1, keepdims=True)
            - normal * jnp.mean(scaled * normal, axis=-1, keepdims=True)
        )

    def middle_rows(u):
        s, within = stream(u)
        normed = unit1[s, within] * vec(3) + vec(5)
        summed = normed + (rs_total(1, u) + vec(2))
        center = summed - jnp.mean(summed, axis=-1, keepdims=True)
        inverse = lax.rsqrt(jnp.mean(center * center, axis=-1, keepdims=True) + EPSILON)
        normal = center * inverse
        keep = keep_rows(s, within)
        r["outq"][s, within] = (keep * (normal * vec(4) + vec(6))).astype(BF16)
        grad_out = keep * r["cown"][s, within]
        grad = norm_back_rows(grad_out, normal, inverse, vec(4))
        dh[s, within] = grad
        low = grad.astype(BF16)
        dzr[s, t, within] = low
        add_small(s, 1, sum_rows(grad_out * normal))
        add_small(s, 3, sum_rows(grad_out))
        add_small(s, 5, sum_rows(low.astype(F32)))

    def backward_hidden(s):
        b = batch_of(s)

        def up(start):
            cols = pl.ds(start, 256)
            grad = against(flat(dzr, s), wback[cols, :]).astype(BF16).astype(F32)
            low = (grad * flat(slope, s, cols).astype(F32)).astype(BF16)
            slope[s, :, :, cols] = low.reshape(4, quarter, 256)
            small[b, 8:9, cols] += sum_rows(low.astype(F32))

        tiles(hidden, 256, up)
        for u, (sequence, first, count) in enumerate(z_.streams):
            if sequence == s and (s >= nt or count < quarter):
                rs_sent(1, u)

        def down(start):
            cols = pl.ds(start, 256)
            store_part(s, cols, against(flat(slope, s), win[cols, :]))

        tiles(width, 256, down)

    def weight_grad(b, base, first, count, left, right):
        def body(start):
            total = None
            for s in batches[b]:
                term = across(flat(left, s, pl.ds(first + start, WEIGHT_TILE)), flat(right, s))
                total = term if total is None else total + term
            place = pl.ds(base + first + start, WEIGHT_TILE)
            gb[b, place, :] = total.astype(BF16)

        tiles(count, WEIGHT_TILE, body)

    def backward_rows(u):
        s, within = stream(u)
        grad_out = dh[s] + rs_total(2, u).astype(BF16).astype(F32)
        normal = unit1[s]
        grad = norm_back_rows(grad_out, normal, inv1[s, :, 0:1], vec(3))
        dh[s] = grad
        low = grad.astype(BF16)
        dar[s, t] = low
        add_small(s, 0, sum_rows(grad_out * normal))
        add_small(s, 2, sum_rows(grad_out))
        add_small(s, 4, sum_rows(low.astype(F32)))

    def out_grad(b):
        total = None
        for s in batches[b]:
            term = across(orb[s], flat(dar, s))
            total = term if total is None else total + term
        gb[b, z_.out0 : z_.out0 + share, :] = total.astype(BF16)


    def mixed_back(s):
        grad_mixed = against(flat(dar, s), wout[...]).astype(BF16).astype(F32)
        grad_mixed = (grad_mixed * invl[s]).astype(BF16)
        gm[...] = grad_mixed
        tm[...] = grad_mixed.T
        tq[...] = qb[s].T
        of[:, :share] = grad_mixed.astype(F32) * orb[s].astype(F32)

    def attention_back(s, h):
        if h == 0:
            mixed_back(s)
        mask = head_of_lane == h
        summed = jnp.sum(jnp.where(mask, of[:, :share], 0.0), axis=-1, keepdims=True)
        grad_head = jnp.where(mask, gm[...], jnp.zeros((), BF16))
        for tile in key_tiles:
            grads = against(grad_head, vb[s, tile, :share]) - summed
            dsb[:, tile] = (probs[s, h, :, tile].astype(F32) * grads).astype(BF16)
        grad_query = (nn(dsb[...], kb[s]) * scale).astype(BF16)
        dqb[s] = grad_query if h == 0 else jnp.where(mask, grad_query, dqb[s])
        place = slice(h * HEAD_DIM, (h + 1) * HEAD_DIM)
        dkvt[s, 0, place, :] = nn(tq[place, :], dsb[...]).astype(BF16)
        dkvt[s, 1, place, :] = nn(tm[place, :], probs[s, h]).astype(BF16)

    def through_back(s):
        add_small(s, 9, sum_rows(dqb[s].astype(F32)), share)
        ones = jnp.ones((8, seq_len), BF16)
        add_small(s, 10, against(ones, dkvt[s, 1])[0:1], share)

        work[:, :width] = nn(dqb[s], wqkv[0])
        for j in range(blocks):
            terms = dkvt[s, :, :, j * rows : (j + 1) * rows].reshape(2 * share, rows)
            total = across(terms, wqkv[1:3].reshape(2 * share, width))
            total += jnp.where(j == z, work[:, :width], 0.0)
            r["part4"][s, j] = total.astype(BF16).reshape(2, 2, quarter, width)

    def qkv_grad(b):
        query = other = None
        for s in batches[b]:
            term = across(dqb[s], xg[s, own_block, :])
            query = term if query is None else query + term
            term = nn(dkvt[s].reshape(2 * share, seq_len), xg[s])
            other = term if other is None else other + term
        first = z_.qkv0
        gb[b, first : first + share, :] = query.astype(BF16)
        gb[b, first + share : first + 3 * share, :] = other.astype(BF16)

    part4, crecv4, yrecv4, zrecv4 = (r[n] for n in ("part4", "crecv4", "yrecv4", "zrecv4"))
    d4_s, d4_r, z4_s, z4_r = (r[n] for n in ("d4_s", "d4_r", "z4_s", "z4_r"))

    def dx_core(s):
        send(part4.at[s, :, :, 1 - c], crecv4.at[s], d4_s.at[s, 0], d4_r.at[s, 0], to_c)

        def clear(side):
            zrecv4[s, side] = jnp.zeros(zrecv4.shape[2:], BF16)

        when(z == 0, lambda: clear(0))
        when(z == blocks - 1, lambda: clear(1))

    def dx_y(s):
        arrived(crecv4.at[s], d4_s.at[s, 0], d4_r.at[s, 0], to_c)

        def body(j, carry):
            part4[s, j, 1 - y, c] = (
                part4[s, j, 1 - y, c].astype(F32) + crecv4[s, j, 1 - y].astype(F32)
            ).astype(BF16)
            return carry

        lax.fori_loop(0, blocks, body, 0)
        send(part4.at[s, :, 1 - y, c], yrecv4.at[s], d4_s.at[s, 1], d4_r.at[s, 1], to_y)

    def dx_partial(s, j):
        return (
            part4[s, j, y, c].astype(F32)
            + crecv4[s, j, y].astype(F32)
            + yrecv4[s, j].astype(F32)
        )

    def dx_arrived_y(s):
        arrived(yrecv4.at[s], d4_s.at[s, 1], d4_r.at[s, 1], to_y)

    def dx_relay(s, d):
        for side in range(2):
            target = z + d if side == 0 else z - d
            valid = target <= blocks - 1 if side == 0 else target >= 0
            block = jnp.clip(target, 0, blocks - 1)
            has_source = has_left if side == 0 else has_right
            dev = to_right if side == 0 else to_left

            def go(side=side, block=block, has_source=has_source):
                if d < blocks - 1:
                    arrived(
                        zrecv4.at[s, side, d],
                        z4_s.at[s, side, d],
                        z4_r.at[s, side, d],
                        to_c,
                        has_source,
                    )
                    value = dx_partial(s, block) + zrecv4[s, side, d].astype(F32)
                else:
                    value = dx_partial(s, block)
                part4[s, block, y, c] = value.astype(BF16)

            when(valid, go)
            send(
                part4.at[s, block, y, c],
                zrecv4.at[s, side, d - 1],
                z4_s.at[s, side, d - 1],
                z4_r.at[s, side, d - 1],
                dev,
                valid,
            )

    def dx_final(s):
        for side, has_source in ((0, has_left), (1, has_right)):
            arrived(
                zrecv4.at[s, side, 0],
                z4_s.at[s, side, 0],
                z4_r.at[s, side, 0],
                to_c,
                has_source,
            )
        total = (
            dx_partial(s, z)
            + zrecv4[s, 0, 0].astype(F32)
            + zrecv4[s, 1, 0].astype(F32)
        )
        r["ginq"][s] = (dh[s] + total.astype(BF16).astype(F32)).astype(BF16)
        publish(r["ginq"], s, r["gin"], 1)

    xrecv, zr1, zr2, grad_ref = r["xrecv"], r["zr1"], r["zr2"], r["grad"]
    ar_s, ar_r, al_s = r["ar_s"], r["ar_r"], r["al_s"]

    def ar_places(i):
        first, count, kind = z_.chunks[i]
        half = count // 2
        index = x if kind == "x" else jnp.where(z == 1, 0, 1)
        own = pl.ds(pl.multiple_of(first + index * half, 16), half)
        other = pl.ds(pl.multiple_of(first + (1 - index) * half, 16), half)
        return own, other, pl.ds(z_.first_half[i], half), pl.ds(z_.first_zone[i], half)

    def zone_places(i):
        first, count, kind = z_.chunks[i]
        half, base = count // 2, z_.first_zone[i]
        index = jnp.where(z == 1, 0, 1)
        own = pl.ds(pl.multiple_of(base + index * half, 16), half)
        other = pl.ds(pl.multiple_of(base + (1 - index) * half, 16), half)
        return own, other, pl.ds(base, count), pl.ds(first, count)

    def add_into(b, dst, dst_first, left, left_first, right, right_first, count):
        tile = next(size for size in (64, 48, 32, 16) if count % size == 0)

        def body(start):
            at = lambda first: pl.ds(pl.multiple_of(first + start, 16), tile)
            dst[b, at(dst_first), :] = (
                left[b, at(left_first), :].astype(F32)
                + right[b, at(right_first), :].astype(F32)
            ).astype(BF16)

        tile_loop(count, tile, body)

    def sems(b, i, index):
        return ar_s.at[b, i, index], ar_r.at[b, i, index]

    def x0(b, i):
        own, other, half, zone = ar_places(i)
        send(gb.at[b, other], xrecv.at[b, half], *sems(b, i, 0), to_x)

    def x1(b, i):
        own, other, half, zone = ar_places(i)
        arrived(xrecv.at[b, half], *sems(b, i, 0), to_x)
        add_into(b, gb, own.start, gb, own.start, xrecv, half.start, half.size)
        send(gb.at[b, own], zr1.at[b, zone], *sems(b, i, 1), to_inner, corner)

    def x2(b, i):
        own, other, half, zone = ar_places(i)

        def add():
            arrived(zr1.at[b, zone], *sems(b, i, 1), to_x)
            add_into(b, gb, own.start, gb, own.start, zr1, zone.start, half.size)

        when(interior, add)
        send(gb.at[b, own], zr2.at[b, half], *sems(b, i, 2), to_mirror, interior)

    def x_share(b, i, cond):
        own, other, half, zone = ar_places(i)
        src, dst = zr1.at[b, zone], grad_ref.at[b, own]
        send(src, dst, *sems(b, i, 4), to_x, cond, final=False)
        when(cond, lambda: pltpu.make_async_copy(src, dst, al_s.at[b, i]).start())

    def x3(b, i):
        own, other, half, zone = ar_places(i)

        def add():
            arrived(zr2.at[b, half], *sems(b, i, 2), to_x)
            add_into(b, zr1, zone.start, gb, own.start, zr2, half.start, half.size)

        when(interior, add)
        send(zr1.at[b, zone], zr1.at[b, zone], *sems(b, i, 3), to_outer, interior)
        x_share(b, i, interior)

    def x4(b, i):
        own, other, half, zone = ar_places(i)
        arrived(zr1.at[b, zone], *sems(b, i, 3), to_x, corner)
        x_share(b, i, corner)

    def x5(b, i):
        own, other, half, zone = ar_places(i)
        src, dst = zr1.at[b, zone], grad_ref.at[b, own]
        remote(src, dst, *sems(b, i, 4), to_x).wait_send()
        pltpu.make_async_copy(src, dst, al_s.at[b, i]).wait()
        arrived(grad_ref.at[b, other], *sems(b, i, 4), to_x)

    def z0(b, i):
        whole, rows_of = zone_places(i)[2:]
        send(gb.at[b, rows_of], zr1.at[b, whole], *sems(b, i, 0), to_inner, corner)

    def z1(b, i):
        own, other, half, zone = ar_places(i)
        whole, rows_of = zone_places(i)[2:]

        def add():
            arrived(zr1.at[b, whole], *sems(b, i, 0), to_x)
            add_into(b, gb, rows_of.start, gb, rows_of.start, zr1, whole.start, whole.size)

        when(interior, add)
        send(gb.at[b, other], zr2.at[b, half], *sems(b, i, 1), to_mirror, interior)

    def z2(b, i):
        own, other, half, zone = ar_places(i)

        def add():
            arrived(zr2.at[b, half], *sems(b, i, 1), to_x)
            add_into(b, gb, own.start, gb, own.start, zr2, half.start, half.size)

        when(interior, add)
        send(gb.at[b, own], xrecv.at[b, half], *sems(b, i, 2), to_x, interior)

    def z3(b, i):
        own, other, half, zone = ar_places(i)
        zone_own = zone_places(i)[0]

        def add():
            arrived(xrecv.at[b, half], *sems(b, i, 2), to_x)
            add_into(b, zr1, zone_own.start, gb, own.start, xrecv, half.start, half.size)

        when(interior, add)
        here = zr1.at[b, zone_own]
        send(here, here, *sems(b, i, 3), to_mirror, interior)
        send(here, here, *sems(b, i, 4), to_outer, interior)

    def z4(b, i):
        there = zr1.at[b, zone_places(i)[1]]
        arrived(there, *sems(b, i, 3), to_x, interior)
        send(there, there, *sems(b, i, 5), to_outer, interior)

    def z5(b, i):
        there = zr1.at[b, zone_places(i)[1]]
        arrived(there, *sems(b, i, 4), to_x, corner)
        arrived(there, *sems(b, i, 5), to_x, corner)
        z_copy(b, i)

    def z_copy(b, i):
        whole, rows_of = zone_places(i)[2:]
        pltpu.make_async_copy(
            zr1.at[b, whole], grad_ref.at[b, rows_of], al_s.at[b, i]
        ).start()

    def z6(b, i):
        whole, rows_of = zone_places(i)[2:]
        pltpu.make_async_copy(
            zr1.at[b, whole], grad_ref.at[b, rows_of], al_s.at[b, i]
        ).wait()

    def w_halves(i):
        first, count, kind = z_.chunks[i]
        half, base = count // 2, z_.first_zone[i]
        return (
            (pl.ds(first, half), pl.ds(base, half), blocks - 1 - z, to_left, to_right),
            (pl.ds(first + half, half), pl.ds(base + half, half), z, to_right, to_left),
        )

    def w_in(step):
        def go(b, i):
            for index, (here, zone, place, down, up) in enumerate(w_halves(i)):
                at = place == step
                into = sems(b, i, 2 * (step - 1) + index) if step else None

                def add(here=here, zone=zone, into=into):
                    arrived(zr1.at[b, zone], *into, to_x)
                    add_into(b, gb, here.start, gb, here.start, zr1, zone.start, zone.size)

                if step:
                    when(at, add)
                if step < blocks - 1:
                    send(gb.at[b, here], zr1.at[b, zone], *sems(b, i, 2 * step + index), down, at)
                else:
                    half = pl.ds(z_.first_half[i], here.size)
                    send(gb.at[b, here], xrecv.at[b, half], *sems(b, i, 6), to_x, at)

        return go

    def w_out(step):
        def go(b, i):
            for index, (here, zone, place, down, up) in enumerate(w_halves(i)):
                at = place == blocks - 1 - step
                into = sems(b, i, 7 + 2 * (step - 1) + index) if step else None

                def add(here=here, zone=zone):
                    half = pl.ds(z_.first_half[i], here.size)
                    arrived(xrecv.at[b, half], *sems(b, i, 6), to_x)
                    add_into(b, zr1, zone.start, gb, here.start, xrecv, half.start, half.size)

                if step:
                    arrived(zr1.at[b, zone], *into, to_x, at)
                else:
                    when(at, add)
                if step < blocks - 1:
                    src = zr1.at[b, zone]
                    send(src, src, *sems(b, i, 7 + 2 * step + index), up, at)

        return go

    def w7(b, i):
        w_out(3)(b, i)
        z_copy(b, i)

    stages = dict(
        x=(x0, x1, x2, x3, x4, x5),
        z=(z0, z1, z2, z3, z4, z5, z6),
        w=(w_in(0), w_in(1), w_in(2), w_in(3), w_out(0), w_out(1), w_out(2), w7, z6),
    )

    def ar(b, i, stage):
        stages[z_.chunks[i][2]][stage](b, i)

    smallc, smalls, smally = r["smallc"], r["smalls"], r["smally"]
    sm_s, sm_r = r["sm_s"], r["sm_r"]
    top = pl.ds(0, 8)

    def small_core(b):
        send(small.at[b, top], smallc.at[b], sm_s.at[b, 0], sm_r.at[b, 0], to_c)

    def small_y(b):
        arrived(smallc.at[b], sm_s.at[b, 0], sm_r.at[b, 0], to_c)
        smalls[b] = small[b, 0:8, :] + smallc[b]
        send(smalls.at[b], smally.at[b], sm_s.at[b, 1], sm_r.at[b, 1], to_y)

    def small_total(b):
        arrived(smally.at[b], sm_s.at[b, 1], sm_r.at[b, 1], to_y)
        first = z_.small0
        gb[b, first : first + 16, :] = jnp.concatenate(
            [smalls[b] + smally[b], small[b, 8:16, :]], axis=0
        ).astype(BF16)
        gb[b, first + 16 : first + SMALL, :] = jnp.zeros((SMALL - 16, width), BF16)

    small[...] = jnp.zeros(small.shape, F32)
    xa_start(0)
    settle()
    xa_start(1)
    settle()
    loads["wqkv"].wait()
    settle()
    loads["wout"].wait()
    settle()
    loads["win"].wait()
    loads["wback"].wait()
    for s in range(ns):
        loads["c", s].wait()
    settle()
    own_cast(0)
    settle()
    xa_start(2)
    settle()
    own_cast(1)
    settle()
    project_own(1)
    settle()
    xa_step(0, 1)
    settle()
    project_own(0)
    settle()
    project_query(1)
    settle()
    xa_step(1, 1)
    settle()
    project_query(0)
    settle()
    xa_step(2, 1)
    settle()
    xa_step(0, 2)
    settle()
    xa_forward(0, 1)
    settle()
    xa_step(1, 2)
    settle()
    xa_forward(1, 1)
    settle()
    xa_step(2, 2)
    settle()
    xa_step(0, 3)
    settle()
    xa_step(1, 3)
    settle()
    xa_start(3)
    settle()
    own_cast(2)
    settle()
    project_own(2)
    settle()
    project_query(2)
    settle()
    xa_step(2, 3)
    settle()
    xa_forward(2, 1)
    settle()
    xa_forward(0, 2)
    settle()
    xa_forward(0, 3)
    settle()
    xa_forward(1, 2)
    settle()
    xa_forward(1, 3)
    settle()
    xa_step(3, 1)
    settle()
    xa_done(0, 1)
    xa_done(0, 2)
    xa_done(0, 3)
    xa_done(1, 1)
    xa_done(1, 2)
    xa_done(1, 3)
    settle()
    project_rest(0)
    settle()
    attention(0, 0)
    settle()
    attention(0, 1)
    settle()
    attention(0, 2)
    settle()
    xa_step(3, 2)
    settle()
    attention_out(0)
    settle()
    rs_core(0, 1)
    settle()
    rs_core(0, 0)
    settle()
    xa_forward(2, 2)
    settle()
    xa_forward(2, 3)
    settle()
    xa_forward(3, 1)
    settle()
    rs_y(0, 0)
    settle()
    rs_y(0, 1)
    settle()
    xa_done(2, 1)
    xa_done(2, 2)
    xa_done(2, 3)
    settle()
    project_rest(1)
    settle()
    attention(1, 0)
    settle()
    attention(1, 1)
    settle()
    forward_rows(0)
    ag_start(0, 0, n1r)
    settle()
    attention(1, 2)
    settle()
    forward_rows(1)
    ag_start(0, 1, n1r)
    settle()
    xa_forward(3, 2)
    settle()
    xa_step(3, 3)
    settle()
    attention_out(1)
    settle()
    rs_core(0, 2)
    settle()
    ag_forward(0, 0, n1r)
    settle()
    rs_y(0, 2)
    settle()
    ag_done(0, 0, n1r)
    settle()
    feed_forward(0)
    settle()
    rs_core(1, 0)
    settle()
    ag_forward(0, 1, n1r)
    settle()
    ag_done(0, 1, n1r)
    settle()
    feed_forward(1)
    settle()
    rs_core(1, 1)
    settle()
    rs_y(1, 0)
    settle()
    xa_forward(3, 3)
    settle()
    rs_y(1, 1)
    settle()
    forward_rows(2)
    ag_start(0, 2, n1r)
    settle()
    xa_done(3, 1)
    xa_done(3, 2)
    xa_done(3, 3)
    settle()
    project_rest(2)
    settle()
    middle_rows(0)
    ag_start(1, 0, dzr)
    settle()
    attention(2, 0)
    settle()
    middle_rows(1)
    ag_start(1, 1, dzr)
    settle()
    attention(2, 1)
    settle()
    attention(2, 2)
    settle()
    attention_out(2)
    settle()
    rs_core(0, 3)
    settle()
    ag_forward(0, 2, n1r)
    settle()
    ag_forward(1, 0, dzr)
    settle()
    rs_y(0, 3)
    settle()
    ag_done(1, 0, dzr)
    settle()
    ag_forward(1, 1, dzr)
    settle()
    ag_done(0, 2, n1r)
    settle()
    feed_forward(2)
    settle()
    rs_core(1, 2)
    settle()
    ag_done(1, 1, dzr)
    settle()
    weight_grad(0, z_.back0, 0, 256, act, dzr)
    settle()
    ar(0, 0, 0)
    settle()
    ar(0, 1, 0)
    settle()
    weight_grad(0, z_.back0, 256, 256, act, dzr)
    settle()
    ar(0, 2, 0)
    settle()
    ar(0, 3, 0)
    settle()
    weight_grad(0, z_.back0, 512, 256, act, dzr)
    settle()
    rs_y(1, 2)
    settle()
    ar(0, 4, 0)
    settle()
    ar(0, 5, 0)
    settle()
    backward_hidden(0)
    settle()
    weight_grad(0, z_.in0, 0, 256, n1r, slope)
    settle()
    ar(0, 6, 0)
    settle()
    ar(0, 7, 0)
    settle()
    weight_grad(0, z_.in0, 256, 256, n1r, slope)
    settle()
    ar(0, 8, 0)
    settle()
    weight_grad(0, z_.in0, 512, 256, n1r, slope)
    settle()
    ar(0, 9, 0)
    settle()
    ar(0, 10, 0)
    settle()
    ar(0, 11, 0)
    settle()
    rs_core(2, 4)
    settle()
    ar(0, 0, 1)
    settle()
    ar(0, 1, 1)
    settle()
    forward_rows(3)
    ag_start(0, 3, n1r)
    settle()
    middle_rows(2)
    ag_start(1, 2, dzr)
    settle()
    rs_y(2, 4)
    settle()
    ar(0, 2, 1)
    settle()
    ar(0, 1, 2)
    settle()
    ar(0, 3, 1)
    settle()
    ar(0, 4, 1)
    settle()
    ag_forward(0, 3, n1r)
    settle()
    ag_done(0, 3, n1r)
    settle()
    feed_forward(3)
    settle()
    ag_forward(1, 2, dzr)
    settle()
    rs_core(1, 3)
    settle()
    ar(0, 6, 1)
    settle()
    ar(0, 1, 3)
    settle()
    ar(0, 3, 2)
    settle()
    ag_done(1, 2, dzr)
    settle()
    ar(0, 5, 1)
    settle()
    rs_y(1, 3)
    settle()
    ar(0, 7, 1)
    settle()
    backward_rows(4)
    ag_start(2, 4, dar)
    settle()
    small_core(0)
    settle()
    backward_hidden(1)
    settle()
    ar(0, 0, 2)
    settle()
    small_y(0)
    settle()
    rs_core(2, 2)
    settle()
    ar(0, 8, 1)
    settle()
    ar(0, 5, 2)
    settle()
    ar(0, 2, 2)
    settle()
    rs_y(2, 2)
    settle()
    middle_rows(3)
    ag_start(1, 3, dzr)
    settle()
    ar(0, 9, 1)
    settle()
    ar(0, 0, 3)
    settle()
    ar(0, 4, 2)
    settle()
    ar(0, 10, 1)
    settle()
    ag_forward(2, 4, dar)
    settle()
    ar(0, 2, 3)
    settle()
    ar(0, 6, 2)
    settle()
    ag_done(2, 4, dar)
    settle()
    out_grad(0)
    settle()
    attention_back(0, 0)
    settle()
    ar(0, 3, 3)
    settle()
    ar(0, 4, 3)
    settle()
    ar(0, 7, 2)
    settle()
    ar(0, 0, 4)
    settle()
    backward_rows(2)
    ag_start(2, 2, dar)
    settle()
    ar(0, 1, 4)
    settle()
    ar(0, 12, 0)
    settle()
    ag_forward(1, 3, dzr)
    settle()
    ar(0, 11, 1)
    settle()
    attention_back(0, 1)
    settle()
    ar(0, 5, 3)
    settle()
    ar(0, 6, 3)
    settle()
    ar(0, 8, 2)
    settle()
    ar(0, 2, 4)
    settle()
    attention_back(0, 2)
    settle()
    through_back(0)
    settle()
    ag_forward(2, 2, dar)
    settle()
    ar(0, 9, 2)
    settle()
    ar(0, 3, 4)
    settle()
    dx_core(0)
    settle()
    qkv_grad(0)
    settle()
    ar(0, 7, 3)
    settle()
    ar(0, 10, 2)
    settle()
    ar(0, 4, 4)
    settle()
    ar(0, 13, 0)
    settle()
    ar(0, 14, 0)
    settle()
    ar(0, 15, 0)
    settle()
    ar(0, 16, 0)
    settle()
    ar(0, 17, 0)
    settle()
    small_total(0)
    settle()
    ar(0, 18, 0)
    settle()
    ag_done(2, 2, dar)
    settle()
    attention_back(1, 0)
    settle()
    ar(0, 1, 5)
    settle()
    dx_y(0)
    settle()
    attention_back(1, 1)
    settle()
    ar(0, 8, 3)
    settle()
    ar(0, 11, 2)
    settle()
    ar(0, 5, 4)
    settle()
    ar(0, 6, 4)
    settle()
    ag_done(1, 3, dzr)
    settle()
    backward_hidden(2)
    settle()
    weight_grad(1, z_.back0, 0, 256, act, dzr)
    settle()
    ar(0, 9, 3)
    settle()
    ar(1, 0, 0)
    settle()
    ar(1, 1, 0)
    settle()
    weight_grad(1, z_.back0, 256, 256, act, dzr)
    settle()
    ar(1, 2, 0)
    settle()
    ar(1, 3, 0)
    settle()
    weight_grad(1, z_.back0, 512, 256, act, dzr)
    settle()
    ar(1, 4, 0)
    settle()
    ar(1, 5, 0)
    settle()
    rs_core(2, 3)
    settle()
    weight_grad(1, z_.in0, 0, 256, n1r, slope)
    settle()
    ar(0, 10, 3)
    settle()
    ar(1, 6, 0)
    settle()
    ar(1, 7, 0)
    settle()
    ar(0, 7, 4)
    settle()
    weight_grad(1, z_.in0, 256, 256, n1r, slope)
    settle()
    ar(1, 8, 0)
    settle()
    ar(1, 9, 0)
    settle()
    weight_grad(1, z_.in0, 512, 256, n1r, slope)
    settle()
    ar(1, 10, 0)
    settle()
    ar(1, 11, 0)
    settle()
    ar(1, 1, 1)
    settle()
    ar(0, 1, 6)
    settle()
    rs_y(2, 3)
    settle()
    ar(0, 12, 1)
    settle()
    ar(0, 8, 4)
    settle()
    ar(0, 13, 1)
    settle()
    ar(0, 15, 1)
    settle()
    ar(0, 18, 1)
    settle()
    attention_back(1, 2)
    settle()
    ar(0, 11, 3)
    settle()
    through_back(1)
    settle()
    dx_arrived_y(0)
    settle()
    dx_core(1)
    settle()
    ar(1, 3, 1)
    settle()
    ar(1, 1, 2)
    settle()
    dx_relay(0, 3)
    settle()
    ar(0, 9, 4)
    settle()
    ar(0, 14, 1)
    settle()
    ar(0, 16, 1)
    settle()
    ar(0, 17, 1)
    settle()
    backward_rows(3)
    ag_start(2, 3, dar)
    settle()
    ar(0, 15, 2)
    settle()
    small_core(1)
    settle()
    ar(0, 0, 5)
    settle()
    dx_y(1)
    settle()
    ar(0, 10, 4)
    settle()
    small_y(1)
    settle()
    ar(0, 2, 5)
    settle()
    ar(0, 3, 5)
    settle()
    ar(0, 3, 6)
    settle()
    ar(0, 4, 5)
    settle()
    ar(0, 18, 2)
    settle()
    ar(1, 5, 1)
    settle()
    ar(0, 5, 5)
    settle()
    ar(0, 5, 6)
    settle()
    ar(0, 6, 5)
    settle()
    publish(r["outq"], 0, r["out"], 0)
    settle()
    publish(r["outq"], 1, r["out"], 0)
    settle()
    publish(r["outq"], 2, r["out"], 0)
    settle()
    ar(0, 1, 7)
    settle()
    ar(0, 1, 8)
    settle()
    ag_forward(2, 3, dar)
    settle()
    ar(1, 3, 2)
    settle()
    ar(0, 12, 2)
    settle()
    ar(1, 0, 1)
    settle()
    ar(1, 5, 2)
    settle()
    ag_done(2, 3, dar)
    settle()
    attention_back(2, 0)
    settle()
    ar(1, 2, 1)
    settle()
    ar(0, 13, 2)
    settle()
    ar(0, 11, 4)
    settle()
    attention_back(2, 1)
    settle()
    dx_relay(0, 2)
    settle()
    attention_back(2, 2)
    settle()
    ar(1, 4, 1)
    settle()
    ar(0, 12, 3)
    settle()
    ar(0, 15, 3)
    settle()
    ar(0, 14, 2)
    settle()
    qkv_grad(1)
    settle()
    ar(0, 13, 3)
    settle()
    ar(0, 18, 3)
    settle()
    ar(0, 16, 2)
    settle()
    ar(1, 13, 0)
    settle()
    ar(1, 14, 0)
    settle()
    ar(1, 15, 0)
    settle()
    ar(1, 16, 0)
    settle()
    ar(0, 17, 2)
    settle()
    ar(1, 6, 1)
    settle()
    ar(1, 17, 0)
    settle()
    through_back(2)
    settle()
    ar(0, 14, 3)
    settle()
    small_total(1)
    settle()
    ar(1, 18, 0)
    settle()
    ar(1, 7, 1)
    settle()
    ar(1, 0, 2)
    settle()
    dx_core(2)
    settle()
    dx_arrived_y(1)
    settle()
    dx_relay(1, 3)
    settle()
    ar(0, 16, 3)
    settle()
    out_grad(1)
    settle()
    ar(1, 12, 0)
    settle()
    ar(1, 1, 3)
    settle()
    ar(1, 2, 2)
    settle()
    ar(1, 8, 1)
    settle()
    ar(0, 12, 4)
    settle()
    ar(0, 17, 3)
    settle()
    ar(0, 7, 5)
    settle()
    dx_y(2)
    settle()
    ar(0, 13, 4)
    settle()
    ar(1, 9, 1)
    settle()
    dx_relay(0, 1)
    settle()
    ar(1, 0, 3)
    settle()
    ar(0, 14, 4)
    settle()
    ar(1, 4, 2)
    settle()
    ar(1, 10, 1)
    settle()
    ar(0, 8, 5)
    settle()
    ar(1, 2, 3)
    settle()
    ar(1, 15, 1)
    settle()
    ar(0, 16, 4)
    settle()
    ar(1, 11, 1)
    settle()
    ar(1, 6, 2)
    settle()
    ar(0, 17, 4)
    settle()
    ar(0, 9, 5)
    settle()
    ar(1, 4, 3)
    settle()
    ar(1, 18, 1)
    settle()
    ar(1, 15, 2)
    settle()
    ar(1, 3, 3)
    settle()
    ar(1, 7, 2)
    settle()
    ar(1, 5, 3)
    settle()
    ar(1, 6, 3)
    settle()
    ar(0, 10, 5)
    settle()
    dx_relay(1, 2)
    settle()
    ar(1, 18, 2)
    settle()
    ar(1, 8, 2)
    settle()
    ar(1, 3, 4)
    settle()
    ar(1, 9, 2)
    settle()
    ar(1, 7, 3)
    settle()
    ar(1, 0, 4)
    settle()
    ar(0, 11, 5)
    settle()
    ar(0, 15, 4)
    settle()
    dx_final(0)
    settle()
    ar(1, 5, 4)
    settle()
    ar(1, 2, 4)
    settle()
    ar(0, 18, 4)
    settle()
    ar(1, 10, 2)
    settle()
    ar(1, 4, 4)
    settle()
    ar(1, 13, 1)
    settle()
    ar(1, 14, 1)
    settle()
    dx_arrived_y(2)
    settle()
    dx_relay(2, 3)
    settle()
    ar(1, 15, 3)
    settle()
    ar(1, 16, 1)
    settle()
    ar(1, 11, 2)
    settle()
    ar(1, 8, 3)
    settle()
    ar(1, 17, 1)
    settle()
    dx_relay(1, 1)
    settle()
    ar(1, 9, 3)
    settle()
    ar(0, 15, 5)
    settle()
    ar(1, 10, 3)
    settle()
    ar(0, 18, 5)
    settle()
    ar(1, 13, 2)
    settle()
    ar(1, 11, 3)
    settle()
    ar(1, 14, 2)
    settle()
    ar(1, 6, 4)
    settle()
    ar(1, 12, 1)
    settle()
    ar(0, 15, 6)
    settle()
    dx_relay(2, 2)
    settle()
    ar(1, 16, 2)
    settle()
    ar(0, 18, 6)
    settle()
    ar(1, 1, 4)
    settle()
    ar(1, 18, 3)
    settle()
    ar(1, 17, 2)
    settle()
    ar(1, 13, 3)
    settle()
    ar(1, 14, 3)
    settle()
    ar(1, 7, 4)
    settle()
    ar(0, 12, 5)
    settle()
    ar(1, 3, 5)
    settle()
    ar(1, 3, 6)
    settle()
    ar(1, 12, 2)
    settle()
    ar(1, 16, 3)
    settle()
    ar(0, 13, 5)
    settle()
    ar(1, 17, 3)
    settle()
    dx_relay(2, 1)
    settle()
    ar(1, 1, 5)
    settle()
    ar(1, 12, 3)
    settle()
    ar(1, 5, 5)
    settle()
    ar(0, 14, 5)
    settle()
    ar(1, 5, 6)
    settle()
    ar(1, 8, 4)
    settle()
    ar(0, 16, 5)
    settle()
    dx_final(1)
    settle()
    ar(0, 17, 5)
    settle()
    ar(1, 9, 4)
    settle()
    ar(1, 0, 5)
    settle()
    ar(1, 10, 4)
    settle()
    ar(1, 2, 5)
    settle()
    ar(1, 11, 4)
    settle()
    ar(1, 4, 5)
    settle()
    ar(1, 15, 4)
    settle()
    ar(0, 15, 7)
    settle()
    ar(0, 15, 8)
    settle()
    ar(1, 15, 5)
    settle()
    ar(1, 1, 6)
    settle()
    ar(0, 18, 7)
    settle()
    ar(0, 18, 8)
    settle()
    ar(1, 6, 5)
    settle()
    ar(1, 18, 4)
    settle()
    ar(1, 13, 4)
    settle()
    ar(1, 18, 5)
    settle()
    ar(1, 15, 6)
    settle()
    ar(1, 14, 4)
    settle()
    ar(1, 7, 5)
    settle()
    ar(1, 16, 4)
    settle()
    ar(1, 17, 4)
    settle()
    ar(1, 8, 5)
    settle()
    dx_final(2)
    settle()
    ar(1, 9, 5)
    settle()
    ar(1, 18, 6)
    settle()
    ar(1, 12, 4)
    settle()
    ar(1, 10, 5)
    settle()
    ar(1, 11, 5)
    settle()
    ar(1, 1, 7)
    settle()
    ar(1, 1, 8)
    settle()
    ar(1, 13, 5)
    settle()
    ar(1, 15, 7)
    settle()
    ar(1, 14, 5)
    settle()
    ar(1, 15, 8)
    settle()
    ar(1, 18, 7)
    settle()
    ar(1, 16, 5)
    settle()
    ar(1, 17, 5)
    settle()
    ar(1, 18, 8)
    settle()
    ar(1, 12, 5)
    settle()
    for u in (4, 2, 3):
        rs_sent(2, u)
    for finish in sent[settled[0]:] + finals:
        finish()


def layer(sizes, *args):
    anywhere = pl.BlockSpec(memory_space=pl.ANY)
    held = pl.BlockSpec(memory_space=pltpu.VMEM)
    call = pl.pallas_call(
        functools.partial(layer_kernel, sizes),
        out_shape=(
            jax.ShapeDtypeStruct((sizes.ns, sizes.rows, sizes.width), BF16),
            jax.ShapeDtypeStruct((sizes.ns, sizes.rows, sizes.width), BF16),
            jax.ShapeDtypeStruct((2, sizes.total, sizes.width), BF16),
        ),
        in_specs=[anywhere] * 4
        + [pl.BlockSpec(memory_space=pltpu.SMEM)]
        + [anywhere] * 4
        + [held] * 6,
        out_specs=[anywhere] * 3,
        scratch_shapes=list(sizes.scratch().values()),
        compiler_params=pltpu.CompilerParams(
            collective_id=0, has_side_effects=True, vmem_limit_bytes=VMEM_BYTES
        ),
    )
    return call(*args)


def widen_kernel(sizes, out, gin, grad, *refs):
    nt, share, hidden, width = sizes.nt, sizes.share, sizes.hidden, sizes.width
    (
        out_t, out_q, gin_t, gin_q, qkv, qv_bias, out_w, out_bias, in_w, in_bias, back_w,
        back_bias, gains, shifts, low, wide, tail, in_sem, out_sem, tail_sem,
    ) = refs
    t = lax.axis_index("tensor")
    pieces = []
    for src, first, second in ((out, out_t, out_q), (gin, gin_t, gin_q)):
        for s in range(sizes.ns):
            dst = first.at[s] if s < nt else second.at[s - nt]
            pieces.append((src.at[s], dst, sizes.rows))
    for b in range(2):
        for first, count, dst in (
            (sizes.back0, hidden, back_w.at[b]),
            (sizes.in0, width, in_w.at[b]),
            (sizes.out0, share, out_w.at[b]),
            (sizes.qkv0, share, qkv.at[b, 0]),
            (sizes.qkv0 + share, share, qkv.at[b, 1]),
            (sizes.qkv0 + 2 * share, share, qkv.at[b, 2]),
        ):
            size = min(count, WIDEN_ROWS)
            for start in range(0, count, size):
                src = grad.at[b, pl.ds(first + start, size)]
                pieces.append((src, dst.at[pl.ds(start, size)], size))
    tails = [
        pltpu.make_async_copy(
            grad.at[b, pl.ds(sizes.small0, 16)], tail.at[b], tail_sem.at[b]
        )
        for b in range(2)
    ]
    reads, writes, places = [], [], []
    place = 0
    for index, (src, dst, size) in enumerate(pieces):
        here = pl.ds(place, size)
        places.append((place, size))
        reads.append(pltpu.make_async_copy(src, low.at[here], in_sem.at[index]))
        writes.append(pltpu.make_async_copy(wide.at[here], dst, out_sem.at[index]))
        place += size
    for copy in reads + tails:
        copy.start()
    for (place, size), read, write in zip(places, reads, writes):
        read.wait()

        def body(step, carry, place=place):
            at = pl.ds(pl.multiple_of(place + step * 32, 32), 32)
            wide[at, :] = low[at, :].astype(F32)
            return carry

        lax.fori_loop(0, size // 32, body, 0)
        write.start()
    for copy in tails:
        copy.wait()
    rows = tail[...].astype(F32)

    def crop_rows(first, count):
        value = jnp.zeros((2, count, share), F32)
        for k in range(4):
            piece = rows[:, first : first + count, k * share : (k + 1) * share]
            value = jnp.where(t == k, piece, value)
        return value

    gains[...] = crop_rows(0, 2)
    shifts[...] = crop_rows(2, 2)
    out_bias[...] = crop_rows(4, 1)[:, 0]
    back_bias[...] = crop_rows(5, 1)[:, 0]
    in_bias[...] = rows[:, 8]
    qv_bias[...] = rows[:, 9:11, :share]
    for copy in writes:
        copy.wait()


WIDEN_ROWS = 256


def widen(sizes, out, gin, grad):
    nt, nq, rows, share, width, hidden = (
        sizes.nt, sizes.nq, sizes.rows, sizes.share, sizes.width, sizes.hidden,
    )
    anywhere = pl.BlockSpec(memory_space=pl.ANY)
    held = pl.BlockSpec(memory_space=pltpu.VMEM)
    shapes = (
        ((nt, rows, width), anywhere),
        ((nq, rows, width), anywhere),
        ((nt, rows, width), anywhere),
        ((nq, rows, width), anywhere),
        ((2, 3, share, width), anywhere),
        ((2, 2, share), held),
        ((2, share, width), anywhere),
        ((2, share), held),
        ((2, width, hidden), anywhere),
        ((2, hidden), held),
        ((2, hidden, width), anywhere),
        ((2, share), held),
        ((2, 2, share), held),
        ((2, 2, share), held),
    )
    total = 2 * sizes.ns * rows + 2 * (hidden + width + 4 * share)
    count = 2 * sizes.ns + 2 * (hidden // WIDEN_ROWS + width // WIDEN_ROWS + 4)
    return pl.pallas_call(
        functools.partial(widen_kernel, sizes),
        out_shape=tuple(jax.ShapeDtypeStruct(shape, F32) for shape, _ in shapes),
        in_specs=[anywhere] * 3,
        out_specs=tuple(spec for _, spec in shapes),
        scratch_shapes=[
            pltpu.VMEM((total, width), BF16),
            pltpu.VMEM((total, width), F32),
            pltpu.VMEM((2, 16, width), BF16),
            pltpu.SemaphoreType.DMA((count,)),
            pltpu.SemaphoreType.DMA((count,)),
            pltpu.SemaphoreType.DMA((2,)),
        ],
        compiler_params=pltpu.CompilerParams(vmem_limit_bytes=VMEM_BYTES),
    )(out, gin, grad)


VMEM_BYTES = 127 * 2**19


def fused(
    x_train,
    x_quiz,
    cot_train,
    cot_quiz,
    quiz_lengths,
    w_qkv,
    b_qv,
    w_out,
    b_out,
    w_in,
    b_in,
    w_back,
    b_back,
    norm_gains,
    norm_shifts,
):
    nt, rows, width = x_train.shape
    share, hidden = w_out.shape[0], w_in.shape[1]
    sizes = Sizes(
        nt, x_quiz.shape[0], rows, lax.axis_size("blk"), share, width, hidden
    )
    out, grad_in, grad = layer(
        sizes,
        x_train,
        x_quiz,
        cot_train,
        cot_quiz,
        quiz_lengths,
        jnp.swapaxes(w_qkv, 1, 2),
        w_out,
        w_in,
        w_back,
        b_out,
        b_in,
        b_back,
        norm_gains,
        norm_shifts,
        b_qv,
    )
    results = list(widen(sizes, out, grad_in, grad))
    results[4] = jnp.swapaxes(results[4], 2, 3)
    return tuple(results)


def fits(mesh):
    return dict(mesh.shape) == {"dp": 2, "tensor": 4, "blk": 4}


def solution(mesh):
    placed = (
        P("dp", "blk", None),
        P("dp", "blk", None),
        P("dp", "blk", None),
        P("dp", "blk", None),
        P("dp"),
        P(None, None, "tensor"),
        P(None, "tensor"),
        P("tensor", None),
        P(),
        P(None, "tensor"),
        P("tensor"),
        P("tensor", None),
        P(),
        P(),
        P(),
    )
    return jax.shard_map(
        fused if fits(mesh) else shards,
        mesh=mesh,
        in_specs=placed,
        out_specs=(
            P("dp", "blk", None),
            P("dp", "blk", None),
            P("dp", "blk", None),
            P("dp", "blk", None),
            P(None, None, None, "tensor"),
            P(None, None, "tensor"),
            P(None, "tensor", None),
            P(None, "tensor"),
            P(None, None, "tensor"),
            P(None, "tensor"),
            P(None, "tensor", None),
            P(None, "tensor"),
            P(None, None, "tensor"),
            P(None, None, "tensor"),
        ),
        check_vma=False,
    )
```

```python
import functools

import jax
import jax.numpy as jnp
from jax import lax
from jax.experimental import pallas as pl
from jax.experimental.pallas import tpu as pltpu
from jax.sharding import PartitionSpec as P

D = 768
HEAD_DIM = 64


EPSILON = 1e-12
ROOT_HALF = 0.7071067811865476
ROOT_TWO_PI = 2.5066282746310002
NEG_LARGE = -1e30


def layer_norm(hidden, gain, shift):
    center = hidden - jnp.mean(hidden, axis=-1, keepdims=True)
    inverse = lax.rsqrt(jnp.mean(center * center, axis=-1, keepdims=True) + EPSILON)
    normal = center * inverse
    return (normal * gain + shift, normal, inverse)


def norm_back(grad_out, normal, inverse, gain):
    scaled = grad_out * gain
    grad_in = inverse * (
        scaled
        - jnp.mean(scaled, axis=-1, keepdims=True)
        - normal * jnp.mean(scaled * normal, axis=-1, keepdims=True)
    )
    return (grad_in, jnp.sum(grad_out * normal, axis=0), jnp.sum(grad_out, axis=0))


def gelu_exact(values):
    return 0.5 * values * (1.0 + lax.erf(values * ROOT_HALF))


def gelu_slope(values):
    return (
        0.5 * (1.0 + lax.erf(values * ROOT_HALF))
        + values * jnp.exp(-0.5 * values * values) / ROOT_TWO_PI
    )


def across(left, right):
    return lax.dot_general(
        left, right, (((0,), (0,)), ((), ())), preferred_element_type=jnp.float32
    )


def against(left, right):
    return lax.dot_general(
        left, right, (((1,), (1,)), ((), ())), preferred_element_type=jnp.float32
    )


def rounded(values):
    return lax.optimization_barrier(values.astype(jnp.bfloat16)).astype(jnp.float32)


def crop(values, column, share):
    return lax.dynamic_slice_in_dim(values, column, share, axis=values.ndim - 1)


def pair_grads(query_heads, dout_heads, log_total, delta, key_heads, value_heads, visible):
    scale = query_heads.shape[-1] ** (-0.5)
    scores = (
        jnp.einsum("sqhe,skhe->shqk", query_heads, key_heads, preferred_element_type=jnp.float32)
        * scale
    )
    probs = jnp.where(visible[:, None, None, :], jnp.exp(scores - log_total[..., None]), 0.0)
    grad_value = jnp.einsum(
        "shqk,sqhe->skhe",
        probs.astype(jnp.bfloat16),
        dout_heads,
        preferred_element_type=jnp.float32,
    )
    grad_probs = jnp.einsum(
        "sqhe,skhe->shqk", dout_heads, value_heads, preferred_element_type=jnp.float32
    )
    grad_scores = (probs * (grad_probs - delta[..., None])).astype(jnp.bfloat16)
    grad_query = jnp.einsum(
        "shqk,skhe->sqhe", grad_scores, key_heads, preferred_element_type=jnp.float32
    )
    grad_key = jnp.einsum(
        "shqk,sqhe->skhe", grad_scores, query_heads, preferred_element_type=jnp.float32
    )
    return (grad_query, grad_key, grad_value)


def run(tokens, cotangent, lengths, first_row, weights):
    w_qkv, b_qv, w_out, b_out, w_in, b_in, w_back, b_back, norm_gains, norm_shifts = weights
    seq_count, row_count, width = tokens.shape
    seq_len = row_count * lax.axis_size("blk")
    span = min(512, seq_len)
    block_count = seq_len // span
    flat_tokens = tokens.reshape(seq_count * row_count, width)
    low_tokens = flat_tokens.astype(jnp.bfloat16)
    projected = jnp.einsum("nd,tde->tne", low_tokens, w_qkv, preferred_element_type=jnp.float32)
    qv_bias = b_qv.astype(jnp.float32)
    query = (projected[0] + qv_bias[0]).astype(jnp.bfloat16)
    key_rows = projected[1].astype(jnp.bfloat16)
    value_rows = (projected[2] + qv_bias[1]).astype(jnp.bfloat16)
    share = key_rows.shape[-1]
    heads = share // HEAD_DIM
    scale = HEAD_DIM ** (-0.5)
    head_shape = (seq_count, row_count, heads, HEAD_DIM)
    query_heads = query.reshape(head_shape)
    key_three = key_rows.reshape(seq_count, row_count, share)
    value_three = value_rows.reshape(seq_count, row_count, share)
    running_max = jnp.full((seq_count, heads, row_count), NEG_LARGE, jnp.float32)
    running_out = jnp.zeros(head_shape, jnp.float32)
    key_piece = lax.all_gather(key_three, "blk", axis=1, tiled=True)
    value_piece = lax.all_gather(value_three, "blk", axis=1, tiled=True)
    piece_rows = key_piece.shape[1]
    key_heads = key_piece.reshape(seq_count, piece_rows, heads, HEAD_DIM)
    value_heads = value_piece.reshape(seq_count, piece_rows, heads, HEAD_DIM)
    scores = (
        jnp.einsum("sqhe,skhe->shqk", query_heads, key_heads, preferred_element_type=jnp.float32)
        * scale
    )
    visible = (jnp.arange(piece_rows, dtype=jnp.int32)[None, :] < lengths[:, None])[
        :, None, None, :
    ]
    scores = jnp.where(visible, scores, NEG_LARGE)
    new_max = jnp.maximum(running_max, jnp.max(scores, axis=-1))
    factor = jnp.exp(running_max - new_max)
    raised = jnp.where(visible, jnp.exp(scores - new_max[..., None]), 0.0)
    new_sum = jnp.sum(raised, axis=-1)
    added = jnp.einsum(
        "shqk,skhe->sqhe",
        raised.astype(jnp.bfloat16),
        value_heads,
        preferred_element_type=jnp.float32,
    )
    new_out = running_out * jnp.swapaxes(factor, 1, 2)[..., None] + added
    mixed_heads = new_out / jnp.swapaxes(new_sum, 1, 2)[..., None]
    log_total = new_max + jnp.log(new_sum)
    mixed_low = mixed_heads.reshape(seq_count * row_count, share).astype(jnp.bfloat16)
    attention = lax.psum(
        jnp.dot(mixed_low, w_out, preferred_element_type=jnp.float32).astype(jnp.bfloat16), "tensor"
    ).astype(jnp.float32) + b_out.astype(jnp.float32)
    normed, unit_one, inverse_one = layer_norm(
        flat_tokens + attention, norm_gains[0], norm_shifts[0]
    )
    normed_low = normed.astype(jnp.bfloat16)
    before = jnp.dot(normed_low, w_in, preferred_element_type=jnp.float32) + b_in.astype(
        jnp.float32
    )
    active_low = gelu_exact(before).astype(jnp.bfloat16)
    branch = lax.psum(
        jnp.dot(active_low, w_back, preferred_element_type=jnp.float32).astype(jnp.bfloat16),
        "tensor",
    ).astype(jnp.float32) + b_back.astype(jnp.float32)
    final, unit_two, inverse_two = layer_norm(normed + branch, norm_gains[1], norm_shifts[1])
    positions = first_row + jnp.arange(row_count, dtype=jnp.int32)
    keep_rows = (
        (positions[None, :] < lengths[:, None])
        .reshape(seq_count * row_count, 1)
        .astype(jnp.float32)
    )
    outputs = (keep_rows * final).reshape(tokens.shape)
    grad_final = keep_rows * cotangent.reshape(seq_count * row_count, width)
    grad_mid, grad_gain_two, grad_shift_two = norm_back(
        grad_final, unit_two, inverse_two, norm_gains[1]
    )
    grad_branch = grad_mid.astype(jnp.bfloat16)
    grad_b_back = jnp.sum(grad_branch.astype(jnp.float32), axis=0)
    grad_w_back = across(active_low, grad_branch)
    grad_active = against(grad_branch, w_back).astype(jnp.bfloat16).astype(jnp.float32)
    grad_before = (grad_active * gelu_slope(before)).astype(jnp.bfloat16)
    grad_b_in = jnp.sum(grad_before.astype(jnp.float32), axis=0)
    grad_w_in = across(normed_low, grad_before)
    grad_normed = grad_mid + rounded(
        lax.psum(against(grad_before, w_in).astype(jnp.bfloat16), "tensor").astype(jnp.float32)
    )
    grad_hidden, grad_gain_one, grad_shift_one = norm_back(
        grad_normed, unit_one, inverse_one, norm_gains[0]
    )
    grad_attention = grad_hidden.astype(jnp.bfloat16)
    grad_b_out = jnp.sum(grad_attention.astype(jnp.float32), axis=0)
    grad_w_out = across(mixed_low, grad_attention)
    grad_mixed = against(grad_attention, w_out).astype(jnp.bfloat16)
    dout_heads = grad_mixed.reshape(head_shape)
    delta = jnp.swapaxes(jnp.sum(dout_heads.astype(jnp.float32) * mixed_heads, axis=-1), 1, 2)
    key_all, value_all = key_piece, value_piece
    key_blocks = jnp.moveaxis(key_all.reshape(seq_count, block_count, span, heads, HEAD_DIM), 1, 0)
    value_blocks = jnp.moveaxis(
        value_all.reshape(seq_count, block_count, span, heads, HEAD_DIM), 1, 0
    )
    visible_all = jnp.arange(seq_len, dtype=jnp.int32)[None, :] < lengths[:, None]
    visible_blocks = jnp.moveaxis(visible_all.reshape(seq_count, block_count, span), 1, 0)

    def sweep_keys(grad_query, item):
        key_block, value_block, visible_block = item
        part_query, part_key, part_value = pair_grads(
            query_heads, dout_heads, log_total, delta, key_block, value_block, visible_block
        )
        return (grad_query + part_query, (part_key, part_value))

    grad_query, (key_terms, value_terms) = lax.scan(
        sweep_keys, jnp.zeros(head_shape, jnp.float32), (key_blocks, value_blocks, visible_blocks)
    )
    key_terms = jnp.moveaxis(key_terms, 0, 1).reshape(seq_count, seq_len, share)
    value_terms = jnp.moveaxis(value_terms, 0, 1).reshape(seq_count, seq_len, share)
    key_sum, value_sum = (
        lax.psum_scatter(
            key_terms.astype(jnp.bfloat16), "blk", scatter_dimension=1, tiled=True
        ).astype(jnp.float32),
        lax.psum_scatter(
            value_terms.astype(jnp.bfloat16), "blk", scatter_dimension=1, tiled=True
        ).astype(jnp.float32),
    )
    grad_query_low = (grad_query * scale).reshape(seq_count * row_count, share).astype(jnp.bfloat16)
    grad_key_low = (key_sum * scale).reshape(seq_count * row_count, share).astype(jnp.bfloat16)
    grad_value_low = value_sum.reshape(seq_count * row_count, share).astype(jnp.bfloat16)
    grad_stack = jnp.stack([grad_query_low, grad_key_low, grad_value_low])
    grad_w_qkv = jnp.einsum(
        "nd,tne->tde", low_tokens, grad_stack, preferred_element_type=jnp.float32
    )
    grad_b_qv = jnp.stack(
        [
            jnp.sum(grad_query_low.astype(jnp.float32), axis=0),
            jnp.sum(grad_value_low.astype(jnp.float32), axis=0),
        ]
    )
    grad_through = lax.psum(
        jnp.einsum("tne,tde->nd", grad_stack, w_qkv, preferred_element_type=jnp.float32).astype(
            jnp.bfloat16
        ),
        "tensor",
    ).astype(jnp.float32)
    grad_tokens = (grad_hidden + rounded(grad_through)).reshape(tokens.shape)
    grad_gains = jnp.stack([grad_gain_one, grad_gain_two])
    grad_shifts = jnp.stack([grad_shift_one, grad_shift_two])
    grads = (
        grad_w_qkv,
        grad_b_qv,
        grad_w_out,
        grad_b_out,
        grad_w_in,
        grad_b_in,
        grad_w_back,
        grad_b_back,
        grad_gains,
        grad_shifts,
    )
    return (outputs, grad_tokens, grads)


def shards(
    x_train,
    x_quiz,
    cot_train,
    cot_quiz,
    quiz_lengths,
    w_qkv,
    b_qv,
    w_out,
    b_out,
    w_in,
    b_in,
    w_back,
    b_back,
    norm_gains,
    norm_shifts,
):
    row_count = x_train.shape[1]
    seq_len = row_count * lax.axis_size("blk")
    first_row = lax.axis_index("blk") * row_count
    share = D // lax.axis_size("tensor")
    column = lax.axis_index("tensor") * share
    weights = (w_qkv, b_qv, w_out, b_out, w_in, b_in, w_back, b_back, norm_gains, norm_shifts)
    full_lengths = jnp.full((x_train.shape[0],), seq_len, jnp.int32)
    out_train, grad_in_train, train_grads = run(
        x_train, cot_train, full_lengths, first_row, weights
    )
    out_quiz, grad_in_quiz, quiz_grads = run(x_quiz, cot_quiz, quiz_lengths, first_row, weights)
    def total(grads):
        pieces = (
            grads[0],
            grads[1],
            grads[2],
            crop(grads[3], column, share),
            grads[4],
            grads[5],
            grads[6],
            crop(grads[7], column, share),
            crop(grads[8], column, share),
            crop(grads[9], column, share),
        )
        low = tuple(piece.astype(jnp.bfloat16) for piece in pieces)
        return tuple(
            piece.astype(jnp.float32) for piece in lax.psum(low, ("dp", "blk"))
        )

    summed = [jnp.stack(pair) for pair in zip(total(train_grads), total(quiz_grads))]
    return (
        out_train,
        out_quiz,
        grad_in_train,
        grad_in_quiz,
        summed[0],
        summed[1],
        summed[2],
        summed[3],
        summed[4],
        summed[5],
        summed[6],
        summed[7],
        summed[8],
        summed[9],
    )


MESH_ID = pl.DeviceIdType.MESH
F32 = jnp.float32
BF16 = jnp.bfloat16
SMALL = 32
BACK_KINDS = "xwxxwx"
IN_KINDS = "xxxxww"
OUT_KINDS = "x"
QKV_KINDS = "xxzxwx"
INV_ROOT_TWO_PI = 1.0 / ROOT_TWO_PI
SETTLE_AGE = 100
WEIGHT_TILE = 256


def nn(left, right):
    return jnp.dot(left, right, preferred_element_type=F32)


def tile_loop(count, tile, body):
    def step(index, carry):
        body(pl.multiple_of(index * tile, tile))
        return carry

    lax.fori_loop(0, count // tile, step, 0)


def tiles(count, tile, body):
    for start in range(0, count, tile):
        body(start)


def sum_rows(value):
    return jnp.sum(value, axis=0, keepdims=True)


def lanes(count):
    return (count // 128 + 1) * 128


class Sizes:
    def __init__(self, nt, nq, rows, blocks, share, width, hidden):
        self.nt, self.nq, self.rows, self.blocks = nt, nq, rows, blocks
        self.share, self.width, self.hidden = share, width, hidden
        self.ns = nt + nq
        self.quarter = rows // 4
        self.seq_len = rows * blocks
        self.heads = share // HEAD_DIM
        self.back0 = 0
        self.in0 = hidden
        self.out0 = hidden + width
        self.qkv0 = self.out0 + share
        self.small0 = self.qkv0 + 3 * share
        self.total = self.small0 + SMALL
        half = self.quarter // 2
        self.streams = tuple((s, part * half, half) for s in range(nt) for part in range(2))
        self.streams += tuple((s, 0, self.quarter) for s in range(nt, self.ns))
        self.streams += tuple((s, 0, self.quarter) for s in range(nt))
        self.chunks = self.plan()
        self.first_half, self.first_zone, half, zone = [], [], 0, 0
        for _, count, kind in self.chunks:
            self.first_half.append(half)
            self.first_zone.append(zone)
            half += count // 2
            zone += count // 2 if kind == "x" else count
        self.half_rows, self.zone_rows = half, zone

    def plan(self):
        pieces = []
        for first, count, kinds in (
            (self.back0, self.hidden, BACK_KINDS),
            (self.in0, self.width, IN_KINDS),
            (self.out0, self.share, OUT_KINDS),
            (self.qkv0, 3 * self.share, QKV_KINDS),
        ):
            size = count // len(kinds)
            for index, kind in enumerate(kinds):
                pieces.append((first + index * size, size, kind))
        first, count, kind = pieces[-1]
        pieces[-1] = (first, count + SMALL, kind)
        return tuple(pieces)

    def scratch(self):
        ns, rows, share, width = self.ns, self.rows, self.share, self.width
        q, blocks, seq = self.quarter, self.blocks, self.seq_len
        dma = pltpu.SemaphoreType.DMA
        nc, nu = len(self.chunks), len(self.streams)
        return dict(
            xown=pltpu.VMEM((ns, q, width), F32),
            cown=pltpu.VMEM((ns, q, width), F32),
            vec=pltpu.VMEM((16, width), F32),
            xg=pltpu.VMEM((ns, seq, width), BF16),
            wqkv=pltpu.VMEM((3, share, width), BF16),
            wout=pltpu.VMEM((share, width), BF16),
            win=pltpu.VMEM((width, self.hidden), BF16),
            wback=pltpu.VMEM((self.hidden, width), BF16),
            qb=pltpu.VMEM((ns, rows, share), BF16),
            kb=pltpu.VMEM((ns, seq, share), BF16),
            vb=pltpu.VMEM((ns, seq, lanes(share)), BF16),
            probs=pltpu.VMEM((ns, self.heads, rows, seq), BF16),
            of=pltpu.VMEM((rows, lanes(share)), F32),
            invl=pltpu.VMEM((ns, rows, share), F32),
            orb=pltpu.VMEM((ns, rows, share), BF16),
            unit1=pltpu.VMEM((ns, q, width), F32),
            inv1=pltpu.VMEM((ns, q, 128), F32),
            n1r=pltpu.VMEM((ns, 4, q, width), BF16),
            dzr=pltpu.VMEM((ns, 4, q, width), BF16),
            dar=pltpu.VMEM((ns, 4, q, width), BF16),
            act=pltpu.VMEM((ns, 4, q, self.hidden), BF16),
            slope=pltpu.VMEM((ns, 4, q, self.hidden), BF16),
            work=pltpu.VMEM((rows, max(seq, width)), F32),
            dsb=pltpu.VMEM((rows, seq), BF16),
            dqb=pltpu.VMEM((ns, rows, share), BF16),
            dkvt=pltpu.VMEM((ns, 2, share, seq), BF16),
            tq=pltpu.VMEM((share, rows), BF16),
            tm=pltpu.VMEM((share, rows), BF16),
            gm=pltpu.VMEM((rows, share), BF16),
            delta=pltpu.VMEM((rows, 128), F32),
            part=pltpu.VMEM((ns, 2, 2, q, width), BF16),
            crecv=pltpu.VMEM((3, ns, 2, q, width), BF16),
            yrecv=pltpu.VMEM((3, ns, q, width), BF16),
            part4=pltpu.VMEM((ns, blocks, 2, 2, q, width), BF16),
            crecv4=pltpu.VMEM((ns, blocks, 2, q, width), BF16),
            yrecv4=pltpu.VMEM((ns, blocks, q, width), BF16),
            zrecv4=pltpu.VMEM((ns, 2, blocks - 1, q, width), BF16),
            outq=pltpu.VMEM((ns, q, width), BF16),
            ginq=pltpu.VMEM((ns, q, width), BF16),
            gb=pltpu.VMEM((2, self.total, width), BF16),
            xrecv=pltpu.VMEM((2, self.half_rows, width), BF16),
            zr1=pltpu.VMEM((2, self.zone_rows, width), BF16),
            zr2=pltpu.VMEM((2, self.half_rows, width), BF16),
            small=pltpu.VMEM((2, SMALL, width), F32),
            smallc=pltpu.VMEM((2, 8, width), F32),
            smalls=pltpu.VMEM((2, 8, width), F32),
            smally=pltpu.VMEM((2, 8, width), F32),
            load_sem=dma((2 * ns + 5,)),
            xz_s=dma((nu, 2, blocks - 1)),
            xz_r=dma((nu, 2, blocks - 1)),
            xc_s=dma((nu, 2, blocks - 1, 3)),
            xc_r=dma((nu, 2, blocks - 1, 3)),
            ex_s=dma((3, nu, 5)),
            ex_r=dma((3, nu, 5)),
            d4_s=dma((ns, 2)),
            d4_r=dma((ns, 2)),
            z4_s=dma((ns, 2, blocks - 1)),
            z4_r=dma((ns, 2, blocks - 1)),
            og_s=dma((2, ns, 3)),
            og_r=dma((2, ns, 3)),
            ol_s=dma((2, ns)),
            ar_s=dma((2, nc, 13)),
            ar_r=dma((2, nc, 13)),
            al_s=dma((2, nc)),
            sm_s=dma((2, 2)),
            sm_r=dma((2, 2)),
        )


INPUTS = (
    "xt", "xq", "ct", "cq", "lens", "wqkv_in", "wout_in", "win_in", "wback_in",
    "b_out", "b_in", "b_back", "gains", "shifts", "b_qv",
)
OUTPUTS = ("out", "gin", "grad")


def layer_kernel(z_, *refs):
    names = INPUTS + OUTPUTS + tuple(z_.scratch())
    r = dict(zip(names, refs))
    nt, ns, rows, blocks = z_.nt, z_.ns, z_.rows, z_.blocks
    share, width, hidden, quarter = z_.share, z_.width, z_.hidden, z_.quarter
    seq_len, heads = z_.seq_len, z_.heads
    scale = HEAD_DIM ** (-0.5)
    batches = (tuple(range(nt)), tuple(range(nt, ns)))
    lens_ref = r["lens"]
    xg, work, part, gb = r["xg"], r["work"], r["part"], r["gb"]

    x = lax.axis_index("dp")
    t = lax.axis_index("tensor")
    z = lax.axis_index("blk")
    y = t // 2
    c = t % 2
    to_x = (1 - x, t, z)
    to_c = (x, t + 1 - 2 * c, z)
    to_y = (x, (t + 2) % 4, z)
    to_d = (x, 3 - t, z)
    to_right = (x, t, jnp.minimum(z + 1, blocks - 1))
    to_left = (x, t, jnp.maximum(z - 1, 0))
    has_left = z > 0
    has_right = z < blocks - 1
    corner = jnp.logical_or(z == 0, z == blocks - 1)
    interior = jnp.logical_and(z > 0, z < blocks - 1)
    to_inner = (x, t, jnp.where(z == 0, 1, blocks - 2))
    to_mirror = (x, t, blocks - 1 - z)
    to_outer = (x, t, jnp.where(z == 1, 0, blocks - 1))
    finals, sent, ages = [], [], []

    def settle(count=3, age=SETTLE_AGE):
        ages.append(len(sent))
        ready = ages[-age] if len(ages) >= age else 0
        for _ in range(min(count, ready - settled[0])):
            sent[settled[0]]()
            settled[0] += 1

    settled = [0]

    def when(cond, fn):
        if cond is None:
            fn()
        else:
            pl.when(cond)(fn)

    def remote(src, dst, ssem, rsem, dev):
        return pltpu.make_async_remote_copy(
            src_ref=src,
            dst_ref=dst,
            send_sem=ssem,
            recv_sem=rsem,
            device_id=dev,
            device_id_type=MESH_ID,
        )

    def send(src, dst, ssem, rsem, dev, cond=None, final=True):
        when(cond, lambda: remote(src, dst, ssem, rsem, dev).start())
        if final:
            sent.append(
                lambda: when(cond, lambda: remote(src, dst, ssem, rsem, dev).wait_send())
            )

    def arrived(dst, ssem, rsem, dev, cond=None):
        when(cond, lambda: remote(dst, dst, ssem, rsem, dev).wait_recv())

    def local(src, dst, sem):
        copy = pltpu.make_async_copy(src, dst, sem)
        copy.start()
        return copy

    mine = pl.ds(pl.multiple_of(t * quarter, quarter), quarter)
    facing = (t + 2) % 4

    def stream(u):
        s, first, count = z_.streams[u]
        return s, pl.ds(first, count)

    def flat(ref, s, lanes_=slice(None)):
        value = ref[s, :, :, lanes_]
        return value.reshape(rows, value.shape[-1])
    own_block = pl.ds(pl.multiple_of(z * rows, rows), rows)

    vec_ref = r["vec"]

    def vec(row, size=None):
        return vec_ref[row : row + 1, : (size or width)]

    def gather_vectors():
        for row, name in enumerate(("b_out", "b_in", "b_back")):
            vec_ref[row : row + 1, :] = r[name][...].astype(F32).reshape(1, width)
        vec_ref[3:5, :] = r["gains"][...]
        vec_ref[5:7, :] = r["shifts"][...]
        vec_ref[7:9, :share] = r["b_qv"][...].astype(F32)

    gather_vectors()
    loads = {}
    load_sem = r["load_sem"]
    x_src = [r["xt"].at[s] for s in range(nt)] + [r["xq"].at[s] for s in range(ns - nt)]
    c_src = [r["ct"].at[s] for s in range(nt)] + [r["cq"].at[s] for s in range(ns - nt)]
    for s in range(ns):
        loads["x", s] = local(x_src[s].at[mine], r["xown"].at[s], load_sem.at[s])
    for index, name in enumerate(("wqkv", "wout", "win", "wback")):
        loads[name] = local(r[name + "_in"], r[name], load_sem.at[ns + index])
    for s in range(ns):
        loads["c", s] = local(c_src[s].at[mine], r["cown"].at[s], load_sem.at[ns + 4 + s])

    barrier = pltpu.get_barrier_semaphore()

    def greet(dev, cond=None):
        when(
            cond,
            lambda: pl.semaphore_signal(
                barrier, inc=1, device_id=dev, device_id_type=MESH_ID
            ),
        )

    for dev in (to_x, to_c, to_y, to_d):
        greet(dev)
    greet(to_left, has_left)
    greet(to_right, has_right)
    when(corner, lambda: pl.semaphore_wait(barrier, 5))
    when(interior, lambda: pl.semaphore_wait(barrier, 6))

    def block_rows(j, q, within=pl.ds(0, quarter)):
        start = j * rows + q * quarter + within.start
        return pl.ds(pl.multiple_of(start, within.size), within.size)

    def side_valid(side, d):
        return z >= d if side == 0 else z <= blocks - 1 - d

    def side_block(side, d):
        return jnp.maximum(z - d, 0) if side == 0 else jnp.minimum(z + d, blocks - 1)

    xz_s, xz_r, xc_s, xc_r = r["xz_s"], r["xz_r"], r["xc_s"], r["xc_r"]

    def xa_start(u):
        s, within = stream(u)
        if within.start == 0:
            loads["x", s].wait()
        place = block_rows(z, t, within)
        xg[s, place, :] = r["xown"][s, within, :].astype(BF16)
        here = xg.at[s, place]
        send(here, here, xz_s.at[u, 0, 0], xz_r.at[u, 0, 0], to_right, has_right)
        send(here, here, xz_s.at[u, 1, 0], xz_r.at[u, 1, 0], to_left, has_left)

    def xa_step(u, d):
        s, within = stream(u)
        for side in range(2):
            valid = side_valid(side, d)
            here = xg.at[s, block_rows(side_block(side, d), t, within)]
            arrived(here, xz_s.at[u, side, d - 1], xz_r.at[u, side, d - 1], to_c, valid)
            if d < blocks - 1:
                more = has_right if side == 0 else has_left
                send(
                    here,
                    here,
                    xz_s.at[u, side, d],
                    xz_r.at[u, side, d],
                    to_right if side == 0 else to_left,
                    jnp.logical_and(valid, more),
                )
            for kind, dev in ((0, to_y), (1, to_c)):
                pair = xc_s.at[u, side, d - 1, kind], xc_r.at[u, side, d - 1, kind]
                send(here, here, *pair, dev, valid)

    def xa_forward(u, d):
        s, within = stream(u)
        for side in range(2):
            valid = side_valid(side, d)
            here = xg.at[s, block_rows(side_block(side, d), facing, within)]
            pair = xc_s.at[u, side, d - 1, 0], xc_r.at[u, side, d - 1, 0]
            arrived(here, *pair, to_c, valid)
            pair = xc_s.at[u, side, d - 1, 2], xc_r.at[u, side, d - 1, 2]
            send(here, here, *pair, to_c, valid)

    def xa_done(u, d):
        s, within = stream(u)
        for side in range(2):
            for kind in (1, 2):
                here = xg.at[s, block_rows(side_block(side, d), t, within)]
                pair = xc_s.at[u, side, d - 1, kind], xc_r.at[u, side, d - 1, kind]
                arrived(here, *pair, to_c, side_valid(side, d))

    def own_cast(s):
        copy = local(x_src[s], work.at[:, pl.ds(0, width)], load_sem.at[2 * ns + 4])
        copy.wait()
        for q in range(4):

            def cast(q=q):
                xg[s, block_rows(z, q), :] = work[
                    q * quarter : (q + 1) * quarter, :width
                ].astype(BF16)

            when(t != q, cast)

    padded = lanes(share)
    padded_head = lax.broadcasted_iota(jnp.int32, (1, padded), 1) // HEAD_DIM
    head_of_lane = lax.broadcasted_iota(jnp.int32, (1, share), 1) // HEAD_DIM
    invl = r["invl"]
    ex_s, ex_r, crecv, yrecv = r["ex_s"], r["ex_r"], r["crecv"], r["yrecv"]

    def rs_sends(k, u):
        s, within = stream(u)
        return (
            (
                part.at[s, :, 1 - c, within],
                crecv.at[k, s, :, within],
                ex_s.at[k, u, 0],
                ex_r.at[k, u, 0],
                to_c,
            ),
            (
                part.at[s, 1 - y, c, within],
                yrecv.at[k, s, within],
                ex_s.at[k, u, 1],
                ex_r.at[k, u, 1],
                to_y,
            ),
        )

    def rs_core(k, u):
        send(*rs_sends(k, u)[0], final=False)

    def rs_y(k, u):
        s, within = stream(u)
        arrived(*rs_sends(k, u)[0][1:])
        part[s, 1 - y, c, within] = (
            part[s, 1 - y, c, within].astype(F32) + crecv[k, s, 1 - y, within].astype(F32)
        ).astype(BF16)
        send(*rs_sends(k, u)[1], final=False)

    def rs_total(k, u):
        s, within = stream(u)
        arrived(*rs_sends(k, u)[1][1:])
        return (
            part[s, y, c, within].astype(F32)
            + crecv[k, s, y, within].astype(F32)
            + yrecv[k, s, within].astype(F32)
        )

    def rs_sent(k, u):
        for args in rs_sends(k, u):
            remote(*args).wait_send()

    def ag_start(k, u, full):
        s, within = stream(u)
        here = full.at[s, t, within]
        send(here, here, ex_s.at[k, u, 3], ex_r.at[k, u, 3], to_y)
        send(here, here, ex_s.at[k, u, 2], ex_r.at[k, u, 2], to_c)

    def ag_forward(k, u, full):
        s, within = stream(u)
        here = full.at[s, facing, within]
        arrived(here, ex_s.at[k, u, 3], ex_r.at[k, u, 3], to_y)
        send(here, here, ex_s.at[k, u, 4], ex_r.at[k, u, 4], to_c)

    def ag_done(k, u, full):
        s, within = stream(u)
        here = full.at[s, t, within]
        arrived(here, ex_s.at[k, u, 2], ex_r.at[k, u, 2], to_c)
        arrived(here, ex_s.at[k, u, 4], ex_r.at[k, u, 4], to_c)

    def publish(buf, s, target, kind):
        here = target.at[s, mine]
        og_s, og_r = r["og_s"], r["og_r"]
        devices = tuple(enumerate((to_c, to_y, to_d)))
        for index, dev in devices:
            sems = og_s.at[kind, s, index], og_r.at[kind, s, index]
            send(buf.at[s], here, *sems, dev)
        copy = local(buf.at[s], here, r["ol_s"].at[kind, s])
        finals.append(copy.wait)

        def landed():
            for index, dev in devices:
                arrived(here, og_s.at[kind, s, index], og_r.at[kind, s, index], dev)

        finals.append(landed)

    def batch_of(s):
        return 0 if s < nt else 1

    def length(s):
        return jnp.int32(seq_len) if s < nt else lens_ref[s - nt]

    def keep_rows(s, within):
        first = z * rows + t * quarter + within.start
        position = first + lax.broadcasted_iota(jnp.int32, (within.size, 1), 0)
        return jnp.where(position < length(s), 1.0, 0.0)

    qb, kb, vb, probs, of, orb = (r[n] for n in ("qb", "kb", "vb", "probs", "of", "orb"))
    wqkv, wout, win, wback = (r[n] for n in ("wqkv", "wout", "win", "wback"))
    unit1, inv1 = r["unit1"], r["inv1"]
    dh = r["xown"]
    n1r, dzr, dar, act, slope = (r[n] for n in ("n1r", "dzr", "dar", "act", "slope"))
    dsb, dqb, dkvt = (r[n] for n in ("dsb", "dqb", "dkvt"))
    small = r["small"]
    tq, tm, gm, delta = (r[n] for n in ("tq", "tm", "gm", "delta"))

    def add_small(s, row, value, size=None):
        place = (batch_of(s), slice(row, row + 1), slice(0, size or width))
        small[place] += value

    def project_query(s):
        low = (against(xg[s, own_block, :], wqkv[0]) + vec(7, share)).astype(BF16)
        qb[s] = low * jnp.array(scale, BF16)

    def project_block(s, start):
        lane = lax.broadcasted_iota(jnp.int32, (rows, padded - share), 1)
        place = pl.ds(start, rows)
        block = xg[s, place, :]
        kb[s, place, :] = against(block, wqkv[1]).astype(BF16)
        vb[s, place, :share] = (against(block, wqkv[2]) + vec(8, share)).astype(BF16)
        vb[s, place, share:] = jnp.where(lane == 0, 1.0, 0.0).astype(BF16)

    def project_own(s):
        project_block(s, pl.multiple_of(z * rows, rows))

    def project_rest(s):
        def body(j):
            project_block(s, pl.multiple_of(((z + 1 + j) % blocks) * rows, rows))

        repeat = rounds if s < nt else loop
        repeat(blocks - 1, body)

    def store_part(s, cols, value, within=pl.ds(0, quarter)):
        low = value.astype(BF16).reshape(2, 2, within.size, value.shape[-1])
        part[s, :, :, within, cols] = low

    key_tiles = tuple(slice(first, first + 256) for first in range(0, seq_len, 256))

    def folded_max(value, running):
        for first in range(0, value.shape[-1], 128):
            piece = value[:, first : first + 128]
            running = piece if running is None else jnp.maximum(running, piece)
        return running

    def rounds(count, body):
        for index in range(count):
            body(index)

    def loop(count, body):
        def step(index, carry):
            body(index)
            return carry

        lax.fori_loop(0, count, step, 0)

    def attention_heads(s):
        attention_start(s)
        loop(heads, lambda h: attention_head(s, h))

    def attention_start(s):
        of[...] = jnp.zeros((rows, padded), F32)
        invl[s] = jnp.zeros((rows, share), F32)

    def attention(s, h):
        if h == 0:
            attention_start(s)
        attention_head(s, h)

    def attention_head(s, h):
        mask = head_of_lane == h
        query = jnp.where(mask, qb[s], jnp.zeros((), BF16))
        highest = None
        for tile in key_tiles:
            scores = against(query, kb[s, tile, :])
            if s >= nt:
                position = tile.start + lax.broadcasted_iota(jnp.int32, (1, 256), 1)
                scores += jnp.where(position < length(s), 0.0, NEG_LARGE)
            work[:, tile] = scores
            highest = folded_max(scores, highest)
        delta[...] = jnp.broadcast_to(
            jnp.max(highest, axis=-1, keepdims=True), (rows, 128)
        )

        top = delta[...]
        mixed = None
        for tile in key_tiles:
            for first in range(tile.start, tile.stop, 128):
                piece = slice(first, first + 128)
                probs[s, h, :, piece] = jnp.exp(work[:, piece] - top).astype(BF16)
            term = nn(probs[s, h, :, tile], vb[s, tile, :])
            mixed = term if mixed is None else mixed + term
        inverse = 1.0 / mixed[:, share : share + 1]
        of[...] = jnp.where(padded_head == h, mixed * inverse, of[...])
        invl[s] = jnp.where(mask, inverse, invl[s])

    def attention_out(s):
        orb[s] = of[:, :share].astype(BF16)

        def body(start):
            cols = pl.ds(start, 256)
            store_part(s, cols, nn(orb[s], wout[:, cols]))

        tiles(width, 256, body)

    def forward_rows(u):
        s, within = stream(u)
        summed = r["xown"][s, within] + (rs_total(0, u) + vec(0))
        center = summed - jnp.mean(summed, axis=-1, keepdims=True)
        inverse = lax.rsqrt(jnp.mean(center * center, axis=-1, keepdims=True) + EPSILON)
        normal = center * inverse
        unit1[s, within] = normal
        inv1[s, within] = jnp.broadcast_to(inverse, (within.size, 128))
        n1r[s, t, within] = (normal * vec(3) + vec(5)).astype(BF16)

    def feed_forward(u):
        s, within = stream(u)
        count = 4 * within.size

        def up(start):
            cols = pl.ds(start, 256)
            left = n1r[s, :, within, :].reshape(count, width)
            before = nn(left, win[:, cols]) + vec_ref[1:2, cols]
            phi = 0.5 * (1.0 + lax.erf(before * ROOT_HALF))
            low = (before * phi).astype(BF16)
            act[s, :, within, cols] = low.reshape(4, within.size, 256)
            bell = jnp.exp(-0.5 * before * before) * INV_ROOT_TWO_PI
            low = (phi + before * bell).astype(BF16)
            slope[s, :, within, cols] = low.reshape(4, within.size, 256)

        (tiles if s < nt else tile_loop)(hidden, 256, up)
        rs_sent(0, u)

        def down(start):
            cols = pl.ds(start, 256)
            left = act[s, :, within, :].reshape(count, hidden)
            store_part(s, cols, nn(left, wback[:, cols]), within)

        (tiles if s < nt else tile_loop)(width, 256, down)

    def norm_back_rows(grad_out, normal, inverse, gain):
        scaled = grad_out * gain
        return inverse * (
            scaled
            - jnp.mean(scaled, axis=-1, keepdims=True)
            - normal * jnp.mean(scaled * normal, axis=-1, keepdims=True)
        )

    def middle_rows(u):
        s, within = stream(u)
        normed = unit1[s, within] * vec(3) + vec(5)
        summed = normed + (rs_total(1, u) + vec(2))
        center = summed - jnp.mean(summed, axis=-1, keepdims=True)
        inverse = lax.rsqrt(jnp.mean(center * center, axis=-1, keepdims=True) + EPSILON)
        normal = center * inverse
        keep = keep_rows(s, within)
        r["outq"][s, within] = (keep * (normal * vec(4) + vec(6))).astype(BF16)
        grad_out = keep * r["cown"][s, within]
        grad = norm_back_rows(grad_out, normal, inverse, vec(4))
        dh[s, within] = grad
        low = grad.astype(BF16)
        dzr[s, t, within] = low
        add_small(s, 1, sum_rows(grad_out * normal))
        add_small(s, 3, sum_rows(grad_out))
        add_small(s, 5, sum_rows(low.astype(F32)))

    def backward_hidden(s):
        b = batch_of(s)

        def up(start):
            cols = pl.ds(start, 256)
            grad = against(flat(dzr, s), wback[cols, :]).astype(BF16).astype(F32)
            low = (grad * flat(slope, s, cols).astype(F32)).astype(BF16)
            slope[s, :, :, cols] = low.reshape(4, quarter, 256)
            small[b, 8:9, cols] += sum_rows(low.astype(F32))

        tiles(hidden, 256, up)
        for u, (sequence, first, count) in enumerate(z_.streams):
            if sequence == s and (s >= nt or count < quarter):
                rs_sent(1, u)

        def down(start):
            cols = pl.ds(start, 256)
            store_part(s, cols, against(flat(slope, s), win[cols, :]))

        tiles(width, 256, down)

    def weight_grad(b, base, first, count, left, right):
        def body(start):
            total = None
            for s in batches[b]:
                term = across(flat(left, s, pl.ds(first + start, WEIGHT_TILE)), flat(right, s))
                total = term if total is None else total + term
            place = pl.ds(pl.multiple_of(base + first + start, 64), WEIGHT_TILE)
            gb[b, place, :] = total.astype(BF16)

        if count > WEIGHT_TILE:
            tile_loop(count, WEIGHT_TILE, body)
        else:
            body(0)

    def backward_rows(u):
        s, within = stream(u)
        grad_out = dh[s] + rs_total(2, u).astype(BF16).astype(F32)
        normal = unit1[s]
        grad = norm_back_rows(grad_out, normal, inv1[s, :, 0:1], vec(3))
        dh[s] = grad
        low = grad.astype(BF16)
        dar[s, t] = low
        add_small(s, 0, sum_rows(grad_out * normal))
        add_small(s, 2, sum_rows(grad_out))
        add_small(s, 4, sum_rows(low.astype(F32)))

    def out_grad(b):
        total = None
        for s in batches[b]:
            term = across(orb[s], flat(dar, s))
            total = term if total is None else total + term
        gb[b, z_.out0 : z_.out0 + share, :] = total.astype(BF16)


    def mixed_back(s):
        grad_mixed = against(flat(dar, s), wout[...]).astype(BF16).astype(F32)
        grad_mixed = (grad_mixed * invl[s]).astype(BF16)
        gm[...] = grad_mixed
        tm[...] = grad_mixed.T
        tq[...] = qb[s].T
        of[:, :share] = grad_mixed.astype(F32) * orb[s].astype(F32)

    def attention_back_heads(s):
        mixed_back(s)
        dqb[s] = jnp.zeros((rows, share), BF16)
        loop(heads, lambda h: attention_back_head(s, h))

    def attention_back(s, h):
        if h == 0:
            mixed_back(s)
            dqb[s] = jnp.zeros((rows, share), BF16)
        attention_back_head(s, h)

    def attention_back_head(s, h):
        mask = head_of_lane == h
        summed = jnp.sum(jnp.where(mask, of[:, :share], 0.0), axis=-1, keepdims=True)
        grad_head = jnp.where(mask, gm[...], jnp.zeros((), BF16))
        for tile in key_tiles:
            grads = against(grad_head, vb[s, tile, :share]) - summed
            dsb[:, tile] = (probs[s, h, :, tile].astype(F32) * grads).astype(BF16)
        grad_query = (nn(dsb[...], kb[s]) * scale).astype(BF16)
        dqb[s] = jnp.where(mask, grad_query, dqb[s])
        place = pl.ds(pl.multiple_of(h * HEAD_DIM, HEAD_DIM), HEAD_DIM)
        dkvt[s, 0, place, :] = nn(tq[place, :], dsb[...]).astype(BF16)
        dkvt[s, 1, place, :] = nn(tm[place, :], probs[s, h]).astype(BF16)

    def through_back(s):
        add_small(s, 9, sum_rows(dqb[s].astype(F32)), share)
        ones = jnp.ones((8, seq_len), BF16)
        add_small(s, 10, against(ones, dkvt[s, 1])[0:1], share)

        work[:, :width] = nn(dqb[s], wqkv[0])
        def body(pair):
            for j in (2 * pair, 2 * pair + 1):
                place = pl.ds(pl.multiple_of(j * rows, rows), rows)
                terms = dkvt[s, :, :, place].reshape(2 * share, rows)
                total = across(terms, wqkv[1:3].reshape(2 * share, width))
                total += jnp.where(j == z, work[:, :width], 0.0)
                r["part4"][s, j] = total.astype(BF16).reshape(2, 2, quarter, width)

        loop(blocks // 2, body)

    def qkv_grad(b):
        query = other = None
        for s in batches[b]:
            term = across(dqb[s], xg[s, own_block, :])
            query = term if query is None else query + term
            term = nn(dkvt[s].reshape(2 * share, seq_len), xg[s])
            other = term if other is None else other + term
        first = z_.qkv0
        gb[b, first : first + share, :] = query.astype(BF16)
        gb[b, first + share : first + 3 * share, :] = other.astype(BF16)

    part4, crecv4, yrecv4, zrecv4 = (r[n] for n in ("part4", "crecv4", "yrecv4", "zrecv4"))
    d4_s, d4_r, z4_s, z4_r = (r[n] for n in ("d4_s", "d4_r", "z4_s", "z4_r"))

    def dx_core(s):
        send(part4.at[s, :, :, 1 - c], crecv4.at[s], d4_s.at[s, 0], d4_r.at[s, 0], to_c)

        def clear(side):
            zrecv4[s, side] = jnp.zeros(zrecv4.shape[2:], BF16)

        when(z == 0, lambda: clear(0))
        when(z == blocks - 1, lambda: clear(1))

    def dx_y(s):
        arrived(crecv4.at[s], d4_s.at[s, 0], d4_r.at[s, 0], to_c)

        def body(j, carry):
            part4[s, j, 1 - y, c] = (
                part4[s, j, 1 - y, c].astype(F32) + crecv4[s, j, 1 - y].astype(F32)
            ).astype(BF16)
            return carry

        lax.fori_loop(0, blocks, body, 0)
        send(part4.at[s, :, 1 - y, c], yrecv4.at[s], d4_s.at[s, 1], d4_r.at[s, 1], to_y)

    def dx_partial(s, j):
        return (
            part4[s, j, y, c].astype(F32)
            + crecv4[s, j, y].astype(F32)
            + yrecv4[s, j].astype(F32)
        )

    def dx_arrived_y(s):
        arrived(yrecv4.at[s], d4_s.at[s, 1], d4_r.at[s, 1], to_y)

    def dx_relay(s, d):
        for side in range(2):
            target = z + d if side == 0 else z - d
            valid = target <= blocks - 1 if side == 0 else target >= 0
            block = jnp.clip(target, 0, blocks - 1)
            has_source = has_left if side == 0 else has_right
            dev = to_right if side == 0 else to_left

            def go(side=side, block=block, has_source=has_source):
                if d < blocks - 1:
                    arrived(
                        zrecv4.at[s, side, d],
                        z4_s.at[s, side, d],
                        z4_r.at[s, side, d],
                        to_c,
                        has_source,
                    )
                    value = dx_partial(s, block) + zrecv4[s, side, d].astype(F32)
                else:
                    value = dx_partial(s, block)
                part4[s, block, y, c] = value.astype(BF16)

            when(valid, go)
            send(
                part4.at[s, block, y, c],
                zrecv4.at[s, side, d - 1],
                z4_s.at[s, side, d - 1],
                z4_r.at[s, side, d - 1],
                dev,
                valid,
            )

    def dx_final(s):
        for side, has_source in ((0, has_left), (1, has_right)):
            arrived(
                zrecv4.at[s, side, 0],
                z4_s.at[s, side, 0],
                z4_r.at[s, side, 0],
                to_c,
                has_source,
            )
        total = (
            dx_partial(s, z)
            + zrecv4[s, 0, 0].astype(F32)
            + zrecv4[s, 1, 0].astype(F32)
        )
        r["ginq"][s] = (dh[s] + total.astype(BF16).astype(F32)).astype(BF16)
        publish(r["ginq"], s, r["gin"], 1)

    xrecv, zr1, zr2, grad_ref = r["xrecv"], r["zr1"], r["zr2"], r["grad"]
    ar_s, ar_r, al_s = r["ar_s"], r["ar_r"], r["al_s"]

    def ar_places(i):
        first, count, kind = z_.chunks[i]
        half = count // 2
        index = x if kind == "x" else jnp.where(z == 1, 0, 1)
        own = pl.ds(pl.multiple_of(first + index * half, 16), half)
        other = pl.ds(pl.multiple_of(first + (1 - index) * half, 16), half)
        return own, other, pl.ds(z_.first_half[i], half), pl.ds(z_.first_zone[i], half)

    def zone_places(i):
        first, count, kind = z_.chunks[i]
        half, base = count // 2, z_.first_zone[i]
        index = jnp.where(z == 1, 0, 1)
        own = pl.ds(pl.multiple_of(base + index * half, 16), half)
        other = pl.ds(pl.multiple_of(base + (1 - index) * half, 16), half)
        return own, other, pl.ds(base, count), pl.ds(first, count)

    def add_into(b, dst, dst_first, left, left_first, right, right_first, count):
        tile = next(size for size in (64, 48, 32, 16) if count % size == 0)

        def body(start):
            at = lambda first: pl.ds(pl.multiple_of(first + start, 16), tile)
            dst[b, at(dst_first), :] = (
                left[b, at(left_first), :].astype(F32)
                + right[b, at(right_first), :].astype(F32)
            ).astype(BF16)

        tile_loop(count, tile, body)

    def sems(b, i, index):
        return ar_s.at[b, i, index], ar_r.at[b, i, index]

    def x0(b, i):
        own, other, half, zone = ar_places(i)
        send(gb.at[b, other], xrecv.at[b, half], *sems(b, i, 0), to_x)

    def x1(b, i):
        own, other, half, zone = ar_places(i)
        arrived(xrecv.at[b, half], *sems(b, i, 0), to_x)
        add_into(b, gb, own.start, gb, own.start, xrecv, half.start, half.size)
        send(gb.at[b, own], zr1.at[b, zone], *sems(b, i, 1), to_inner, corner)

    def x2(b, i):
        own, other, half, zone = ar_places(i)

        def add():
            arrived(zr1.at[b, zone], *sems(b, i, 1), to_x)
            add_into(b, gb, own.start, gb, own.start, zr1, zone.start, half.size)

        when(interior, add)
        send(gb.at[b, own], zr2.at[b, half], *sems(b, i, 2), to_mirror, interior)

    def x_share(b, i, cond):
        own, other, half, zone = ar_places(i)
        src, dst = zr1.at[b, zone], grad_ref.at[b, own]
        send(src, dst, *sems(b, i, 4), to_x, cond, final=False)
        when(cond, lambda: pltpu.make_async_copy(src, dst, al_s.at[b, i]).start())

    def x3(b, i):
        own, other, half, zone = ar_places(i)

        def add():
            arrived(zr2.at[b, half], *sems(b, i, 2), to_x)
            add_into(b, zr1, zone.start, gb, own.start, zr2, half.start, half.size)

        when(interior, add)
        send(zr1.at[b, zone], zr1.at[b, zone], *sems(b, i, 3), to_outer, interior)
        x_share(b, i, interior)

    def x4(b, i):
        own, other, half, zone = ar_places(i)
        arrived(zr1.at[b, zone], *sems(b, i, 3), to_x, corner)
        x_share(b, i, corner)

    def x5(b, i):
        own, other, half, zone = ar_places(i)
        src, dst = zr1.at[b, zone], grad_ref.at[b, own]
        remote(src, dst, *sems(b, i, 4), to_x).wait_send()
        pltpu.make_async_copy(src, dst, al_s.at[b, i]).wait()
        arrived(grad_ref.at[b, other], *sems(b, i, 4), to_x)

    def z0(b, i):
        whole, rows_of = zone_places(i)[2:]
        send(gb.at[b, rows_of], zr1.at[b, whole], *sems(b, i, 0), to_inner, corner)

    def z1(b, i):
        own, other, half, zone = ar_places(i)
        whole, rows_of = zone_places(i)[2:]

        def add():
            arrived(zr1.at[b, whole], *sems(b, i, 0), to_x)
            add_into(b, gb, rows_of.start, gb, rows_of.start, zr1, whole.start, whole.size)

        when(interior, add)
        send(gb.at[b, other], zr2.at[b, half], *sems(b, i, 1), to_mirror, interior)

    def z2(b, i):
        own, other, half, zone = ar_places(i)

        def add():
            arrived(zr2.at[b, half], *sems(b, i, 1), to_x)
            add_into(b, gb, own.start, gb, own.start, zr2, half.start, half.size)

        when(interior, add)
        send(gb.at[b, own], xrecv.at[b, half], *sems(b, i, 2), to_x, interior)

    def z3(b, i):
        own, other, half, zone = ar_places(i)
        zone_own = zone_places(i)[0]

        def add():
            arrived(xrecv.at[b, half], *sems(b, i, 2), to_x)
            add_into(b, zr1, zone_own.start, gb, own.start, xrecv, half.start, half.size)

        when(interior, add)
        here = zr1.at[b, zone_own]
        send(here, here, *sems(b, i, 3), to_mirror, interior)
        send(here, here, *sems(b, i, 4), to_outer, interior)

    def z4(b, i):
        there = zr1.at[b, zone_places(i)[1]]
        arrived(there, *sems(b, i, 3), to_x, interior)
        send(there, there, *sems(b, i, 5), to_outer, interior)

    def z5(b, i):
        there = zr1.at[b, zone_places(i)[1]]
        arrived(there, *sems(b, i, 4), to_x, corner)
        arrived(there, *sems(b, i, 5), to_x, corner)
        z_copy(b, i)

    def z_copy(b, i):
        whole, rows_of = zone_places(i)[2:]
        pltpu.make_async_copy(
            zr1.at[b, whole], grad_ref.at[b, rows_of], al_s.at[b, i]
        ).start()

    def z6(b, i):
        whole, rows_of = zone_places(i)[2:]
        pltpu.make_async_copy(
            zr1.at[b, whole], grad_ref.at[b, rows_of], al_s.at[b, i]
        ).wait()

    def w_halves(i):
        first, count, kind = z_.chunks[i]
        half, base = count // 2, z_.first_zone[i]
        return (
            (pl.ds(first, half), pl.ds(base, half), blocks - 1 - z, to_left, to_right),
            (pl.ds(first + half, half), pl.ds(base + half, half), z, to_right, to_left),
        )

    def w_in(step):
        def go(b, i):
            for index, (here, zone, place, down, up) in enumerate(w_halves(i)):
                at = place == step
                into = sems(b, i, 2 * (step - 1) + index) if step else None

                def add(here=here, zone=zone, into=into):
                    arrived(zr1.at[b, zone], *into, to_x)
                    add_into(b, gb, here.start, gb, here.start, zr1, zone.start, zone.size)

                if step:
                    when(at, add)
                if step < blocks - 1:
                    send(gb.at[b, here], zr1.at[b, zone], *sems(b, i, 2 * step + index), down, at)
                else:
                    half = pl.ds(z_.first_half[i], here.size)
                    send(gb.at[b, here], xrecv.at[b, half], *sems(b, i, 6), to_x, at)

        return go

    def w_out(step):
        def go(b, i):
            for index, (here, zone, place, down, up) in enumerate(w_halves(i)):
                at = place == blocks - 1 - step
                into = sems(b, i, 7 + 2 * (step - 1) + index) if step else None

                def add(here=here, zone=zone):
                    half = pl.ds(z_.first_half[i], here.size)
                    arrived(xrecv.at[b, half], *sems(b, i, 6), to_x)
                    add_into(b, zr1, zone.start, gb, here.start, xrecv, half.start, half.size)

                if step:
                    arrived(zr1.at[b, zone], *into, to_x, at)
                else:
                    when(at, add)
                if step < blocks - 1:
                    src = zr1.at[b, zone]
                    send(src, src, *sems(b, i, 7 + 2 * step + index), up, at)

        return go

    def w7(b, i):
        w_out(3)(b, i)
        z_copy(b, i)

    stages = dict(
        x=(x0, x1, x2, x3, x4, x5),
        z=(z0, z1, z2, z3, z4, z5, z6),
        w=(w_in(0), w_in(1), w_in(2), w_in(3), w_out(0), w_out(1), w_out(2), w7, z6),
    )

    def ar(b, i, stage):
        stages[z_.chunks[i][2]][stage](b, i)

    smallc, smalls, smally = r["smallc"], r["smalls"], r["smally"]
    sm_s, sm_r = r["sm_s"], r["sm_r"]
    top = pl.ds(0, 8)

    def small_core(b):
        send(small.at[b, top], smallc.at[b], sm_s.at[b, 0], sm_r.at[b, 0], to_c)

    def small_y(b):
        arrived(smallc.at[b], sm_s.at[b, 0], sm_r.at[b, 0], to_c)
        smalls[b] = small[b, 0:8, :] + smallc[b]
        send(smalls.at[b], smally.at[b], sm_s.at[b, 1], sm_r.at[b, 1], to_y)

    def small_total(b):
        arrived(smally.at[b], sm_s.at[b, 1], sm_r.at[b, 1], to_y)
        first = z_.small0
        gb[b, first : first + 16, :] = jnp.concatenate(
            [smalls[b] + smally[b], small[b, 8:16, :]], axis=0
        ).astype(BF16)
        gb[b, first + 16 : first + SMALL, :] = jnp.zeros((SMALL - 16, width), BF16)

    small[...] = jnp.zeros(small.shape, F32)
    xa_start(0)
    settle()
    xa_start(1)
    settle()
    loads["wqkv"].wait()
    settle()
    loads["wout"].wait()
    settle()
    loads["win"].wait()
    loads["wback"].wait()
    for s in range(ns):
        loads["c", s].wait()
    settle()
    own_cast(0)
    settle()
    project_query(0)
    settle()
    project_own(0)
    settle()
    xa_step(0, 1)
    settle()
    xa_step(1, 1)
    settle()
    xa_step(0, 2)
    settle()
    xa_step(1, 2)
    settle()
    xa_forward(0, 1)
    settle()
    xa_step(0, 3)
    settle()
    xa_step(1, 3)
    settle()
    xa_start(2)
    settle()
    own_cast(1)
    settle()
    project_own(1)
    settle()
    xa_forward(1, 1)
    settle()
    project_query(1)
    settle()
    xa_forward(0, 2)
    settle()
    xa_forward(0, 3)
    settle()
    xa_forward(1, 2)
    settle()
    xa_forward(1, 3)
    settle()
    xa_done(0, 1)
    xa_done(0, 2)
    xa_done(0, 3)
    xa_done(1, 1)
    xa_done(1, 2)
    xa_done(1, 3)
    settle()
    project_rest(0)
    settle()
    attention(0, 0)
    settle()
    attention(0, 1)
    settle()
    attention(0, 2)
    settle()
    xa_step(2, 1)
    settle()
    attention_out(0)
    settle()
    rs_core(0, 0)
    settle()
    rs_core(0, 1)
    settle()
    rs_y(0, 0)
    settle()
    rs_y(0, 1)
    settle()
    xa_step(2, 2)
    settle()
    xa_forward(2, 1)
    settle()
    forward_rows(0)
    ag_start(0, 0, n1r)
    settle()
    forward_rows(1)
    ag_start(0, 1, n1r)
    settle()
    xa_step(2, 3)
    settle()
    xa_start(3)
    settle()
    own_cast(2)
    settle()
    project_query(2)
    settle()
    project_own(2)
    settle()
    xa_forward(2, 2)
    settle()
    ag_forward(0, 0, n1r)
    settle()
    ag_forward(0, 1, n1r)
    settle()
    ag_done(0, 0, n1r)
    settle()
    feed_forward(0)
    settle()
    rs_core(1, 0)
    settle()
    xa_step(3, 1)
    settle()
    ag_done(0, 1, n1r)
    settle()
    feed_forward(1)
    settle()
    rs_core(1, 1)
    settle()
    rs_y(1, 0)
    settle()
    xa_forward(2, 3)
    settle()
    rs_y(1, 1)
    settle()
    xa_done(2, 1)
    xa_done(2, 2)
    xa_done(2, 3)
    settle()
    project_rest(1)
    settle()
    attention_heads(1)
    settle()
    middle_rows(0)
    ag_start(1, 0, dzr)
    settle()
    xa_forward(3, 1)
    settle()
    attention_out(1)
    settle()
    rs_core(0, 2)
    settle()
    xa_step(3, 2)
    settle()
    middle_rows(1)
    ag_start(1, 1, dzr)
    settle()
    rs_y(0, 2)
    settle()
    ag_forward(1, 0, dzr)
    settle()
    ag_done(1, 0, dzr)
    settle()
    xa_forward(3, 2)
    settle()
    xa_step(3, 3)
    settle()
    ag_forward(1, 1, dzr)
    settle()
    ag_done(1, 1, dzr)
    settle()
    weight_grad(0, z_.back0, 0, 256, act, dzr)
    settle()
    ar(0, 0, 0)
    settle()
    ar(0, 1, 0)
    settle()
    weight_grad(0, z_.back0, 256, 256, act, dzr)
    settle()
    ar(0, 2, 0)
    settle()
    ar(0, 3, 0)
    settle()
    weight_grad(0, z_.back0, 512, 256, act, dzr)
    settle()
    ar(0, 4, 0)
    settle()
    ar(0, 5, 0)
    settle()
    forward_rows(2)
    ag_start(0, 2, n1r)
    settle()
    backward_hidden(0)
    settle()
    weight_grad(0, z_.in0, 0, 256, n1r, slope)
    settle()
    weight_grad(0, z_.in0, 256, 256, n1r, slope)
    settle()
    weight_grad(0, z_.in0, 512, 256, n1r, slope)
    settle()
    ar(0, 6, 0)
    settle()
    ar(0, 7, 0)
    settle()
    ar(0, 8, 0)
    settle()
    ar(0, 9, 0)
    settle()
    ar(0, 10, 0)
    settle()
    ar(0, 11, 0)
    settle()
    rs_core(2, 4)
    settle()
    xa_forward(3, 3)
    settle()
    ar(0, 0, 1)
    settle()
    ar(0, 1, 1)
    settle()
    ar(0, 4, 1)
    settle()
    ag_forward(0, 2, n1r)
    settle()
    rs_y(2, 4)
    settle()
    xa_done(3, 1)
    xa_done(3, 2)
    xa_done(3, 3)
    settle()
    project_rest(2)
    settle()
    attention_heads(2)
    settle()
    attention_out(2)
    settle()
    rs_core(0, 3)
    settle()
    backward_rows(4)
    ag_start(2, 4, dar)
    settle()
    small_core(0)
    settle()
    ar(0, 1, 2)
    settle()
    ar(0, 4, 2)
    settle()
    ar(0, 0, 2)
    settle()
    ar(0, 2, 1)
    settle()
    rs_y(0, 3)
    settle()
    small_y(0)
    settle()
    ar(0, 3, 1)
    settle()
    ar(0, 5, 1)
    settle()
    ar(0, 6, 1)
    settle()
    ar(0, 10, 1)
    settle()
    ar(0, 11, 1)
    settle()
    ag_done(0, 2, n1r)
    settle()
    feed_forward(2)
    settle()
    rs_core(1, 2)
    settle()
    ag_forward(2, 4, dar)
    settle()
    ar(0, 2, 2)
    settle()
    ar(0, 7, 1)
    settle()
    ar(0, 0, 3)
    settle()
    ar(0, 1, 3)
    settle()
    ar(0, 8, 1)
    settle()
    forward_rows(3)
    ag_start(0, 3, n1r)
    settle()
    ag_done(2, 4, dar)
    settle()
    attention_back(0, 0)
    settle()
    out_grad(0)
    settle()
    ar(0, 12, 0)
    settle()
    attention_back(0, 1)
    settle()
    attention_back(0, 2)
    settle()
    through_back(0)
    settle()
    dx_core(0)
    settle()
    ag_forward(0, 3, n1r)
    settle()
    small_total(0)
    settle()
    qkv_grad(0)
    settle()
    ar(0, 13, 0)
    settle()
    ar(0, 14, 0)
    settle()
    ar(0, 15, 0)
    settle()
    ar(0, 16, 0)
    settle()
    ar(0, 17, 0)
    settle()
    ar(0, 18, 0)
    settle()
    ar(0, 3, 2)
    settle()
    ar(0, 5, 2)
    settle()
    ar(0, 6, 2)
    settle()
    ar(0, 7, 2)
    settle()
    dx_y(0)
    settle()
    ag_done(0, 3, n1r)
    settle()
    ar(0, 10, 2)
    settle()
    ar(0, 8, 2)
    settle()
    ar(0, 11, 2)
    settle()
    ar(0, 0, 4)
    settle()
    ar(0, 1, 4)
    settle()
    feed_forward(3)
    settle()
    rs_core(1, 3)
    settle()
    ar(0, 9, 1)
    settle()
    ar(0, 12, 1)
    settle()
    ar(0, 13, 1)
    settle()
    ar(0, 14, 1)
    settle()
    ar(0, 15, 1)
    settle()
    ar(0, 16, 1)
    settle()
    ar(0, 2, 3)
    settle()
    ar(0, 3, 3)
    settle()
    ar(0, 4, 3)
    settle()
    ar(0, 17, 1)
    settle()
    ar(0, 5, 3)
    settle()
    ar(0, 10, 3)
    settle()
    rs_y(1, 2)
    settle()
    rs_y(1, 3)
    settle()
    ar(0, 18, 1)
    settle()
    ar(0, 6, 3)
    settle()
    ar(0, 11, 3)
    settle()
    ar(0, 1, 5)
    settle()
    ar(0, 7, 3)
    settle()
    ar(0, 9, 2)
    settle()
    ar(0, 8, 3)
    settle()
    ar(0, 2, 4)
    settle()
    ar(0, 0, 5)
    settle()
    dx_arrived_y(0)
    settle()
    dx_relay(0, 3)
    settle()
    ar(0, 4, 4)
    settle()
    ar(0, 15, 2)
    settle()
    ar(0, 12, 2)
    settle()
    ar(0, 3, 4)
    settle()
    middle_rows(2)
    ag_start(1, 2, dzr)
    settle()
    ar(0, 10, 4)
    settle()
    ar(0, 17, 2)
    settle()
    ar(0, 13, 2)
    settle()
    ar(0, 5, 4)
    settle()
    middle_rows(3)
    ag_start(1, 3, dzr)
    settle()
    ar(0, 11, 4)
    settle()
    ar(0, 1, 6)
    settle()
    ar(0, 14, 2)
    settle()
    ar(0, 6, 4)
    settle()
    ag_forward(1, 2, dzr)
    settle()
    ar(0, 16, 2)
    settle()
    ar(0, 2, 5)
    settle()
    ar(0, 9, 3)
    settle()
    ar(0, 7, 4)
    settle()
    ag_done(1, 2, dzr)
    settle()
    backward_hidden(1)
    settle()
    rs_core(2, 2)
    settle()
    ag_forward(1, 3, dzr)
    settle()
    ar(0, 18, 2)
    settle()
    ar(0, 3, 5)
    settle()
    ar(0, 8, 4)
    settle()
    ar(0, 15, 3)
    settle()
    rs_y(2, 2)
    settle()
    ag_done(1, 3, dzr)
    settle()
    weight_grad(1, z_.back0, 0, 768, act, dzr)
    settle()
    backward_hidden(2)
    settle()
    weight_grad(1, z_.in0, 0, 768, n1r, slope)
    settle()
    ar(0, 1, 7)
    settle()
    ar(0, 4, 5)
    settle()
    ar(1, 0, 0)
    settle()
    ar(1, 1, 0)
    settle()
    ar(1, 2, 0)
    settle()
    ar(1, 3, 0)
    settle()
    ar(1, 4, 0)
    settle()
    ar(1, 5, 0)
    settle()
    ar(1, 6, 0)
    settle()
    ar(1, 7, 0)
    settle()
    ar(1, 8, 0)
    settle()
    ar(0, 10, 5)
    settle()
    ar(1, 9, 0)
    settle()
    ar(1, 10, 0)
    settle()
    ar(1, 11, 0)
    settle()
    rs_core(2, 3)
    settle()
    ar(0, 9, 4)
    settle()
    dx_relay(0, 2)
    settle()
    ar(0, 12, 3)
    settle()
    ar(0, 13, 3)
    settle()
    ar(0, 14, 3)
    settle()
    ar(0, 16, 3)
    settle()
    rs_y(2, 3)
    settle()
    ar(0, 11, 5)
    settle()
    ar(0, 17, 3)
    settle()
    ar(0, 18, 3)
    settle()
    backward_rows(2)
    ag_start(2, 2, dar)
    settle()
    ar(0, 1, 8)
    settle()
    ar(0, 5, 5)
    settle()
    ar(0, 6, 5)
    settle()
    ar(0, 7, 5)
    settle()
    ar(0, 8, 5)
    settle()
    ar(0, 15, 4)
    settle()
    ar(1, 1, 1)
    settle()
    ar(1, 0, 1)
    settle()
    ar(0, 4, 6)
    settle()
    ar(1, 4, 1)
    settle()
    backward_rows(3)
    ag_start(2, 3, dar)
    settle()
    small_core(1)
    settle()
    publish(r["outq"], 0, r["out"], 0)
    settle()
    publish(r["outq"], 1, r["out"], 0)
    settle()
    ar(1, 2, 1)
    settle()
    publish(r["outq"], 2, r["out"], 0)
    settle()
    ar(0, 10, 6)
    settle()
    ar(1, 10, 1)
    settle()
    ag_forward(2, 2, dar)
    settle()
    ar(0, 12, 4)
    settle()
    small_y(1)
    settle()
    ar(1, 3, 1)
    settle()
    ar(0, 13, 4)
    settle()
    ag_done(2, 2, dar)
    settle()
    attention_back_heads(1)
    settle()
    ar(0, 11, 6)
    settle()
    ar(1, 5, 1)
    settle()
    ar(1, 11, 1)
    settle()
    ag_forward(2, 3, dar)
    settle()
    through_back(1)
    settle()
    ar(1, 1, 2)
    settle()
    ar(1, 0, 2)
    settle()
    ar(1, 6, 1)
    settle()
    ag_done(2, 3, dar)
    settle()
    attention_back_heads(2)
    settle()
    ar(1, 2, 2)
    settle()
    ar(1, 4, 2)
    settle()
    ar(1, 7, 1)
    settle()
    ar(1, 10, 2)
    settle()
    ar(1, 8, 1)
    settle()
    ar(0, 4, 7)
    settle()
    ar(1, 3, 2)
    settle()
    through_back(2)
    settle()
    dx_core(2)
    settle()
    ar(1, 11, 2)
    settle()
    ar(0, 10, 7)
    settle()
    ar(1, 5, 2)
    settle()
    ar(1, 9, 1)
    settle()
    out_grad(1)
    settle()
    ar(1, 12, 0)
    settle()
    qkv_grad(1)
    settle()
    ar(0, 11, 7)
    settle()
    ar(1, 6, 2)
    settle()
    dx_y(2)
    settle()
    ar(1, 13, 0)
    settle()
    ar(1, 14, 0)
    settle()
    ar(1, 15, 0)
    settle()
    ar(1, 16, 0)
    settle()
    ar(1, 17, 0)
    settle()
    dx_core(1)
    settle()
    ar(1, 7, 2)
    settle()
    small_total(1)
    settle()
    ar(1, 18, 0)
    settle()
    ar(0, 14, 4)
    settle()
    ar(0, 16, 4)
    settle()
    ar(0, 17, 4)
    settle()
    ar(0, 18, 4)
    settle()
    dx_relay(0, 1)
    settle()
    ar(1, 0, 3)
    settle()
    ar(1, 1, 3)
    settle()
    ar(1, 2, 3)
    settle()
    ar(1, 8, 2)
    settle()
    ar(1, 3, 3)
    settle()
    ar(1, 4, 3)
    settle()
    dx_y(1)
    settle()
    ar(0, 4, 8)
    settle()
    ar(1, 5, 3)
    settle()
    ar(0, 9, 5)
    settle()
    ar(1, 9, 2)
    settle()
    ar(0, 10, 8)
    settle()
    ar(1, 10, 3)
    settle()
    ar(0, 11, 8)
    settle()
    ar(0, 12, 5)
    settle()
    ar(0, 13, 5)
    settle()
    ar(0, 15, 5)
    settle()
    ar(0, 15, 6)
    settle()
    ar(1, 6, 3)
    settle()
    ar(1, 12, 1)
    settle()
    ar(1, 11, 3)
    settle()
    ar(1, 15, 1)
    settle()
    ar(1, 7, 3)
    settle()
    ar(1, 13, 1)
    settle()
    ar(1, 17, 1)
    settle()
    dx_arrived_y(2)
    settle()
    dx_relay(2, 3)
    settle()
    ar(1, 14, 1)
    settle()
    ar(1, 0, 4)
    settle()
    ar(1, 16, 1)
    settle()
    ar(0, 17, 5)
    settle()
    ar(1, 2, 4)
    settle()
    ar(1, 18, 1)
    settle()
    dx_final(0)
    settle()
    ar(1, 8, 3)
    settle()
    ar(1, 3, 4)
    settle()
    ar(0, 14, 5)
    settle()
    ar(1, 9, 3)
    settle()
    ar(1, 12, 2)
    settle()
    ar(1, 15, 2)
    settle()
    ar(1, 13, 2)
    settle()
    ar(1, 17, 2)
    settle()
    ar(1, 5, 4)
    settle()
    ar(0, 16, 5)
    settle()
    dx_arrived_y(1)
    settle()
    dx_relay(1, 3)
    settle()
    ar(0, 17, 6)
    settle()
    dx_relay(2, 2)
    settle()
    ar(0, 18, 5)
    settle()
    ar(1, 6, 4)
    settle()
    ar(1, 14, 2)
    settle()
    ar(1, 1, 4)
    settle()
    ar(1, 7, 4)
    settle()
    ar(1, 16, 2)
    settle()
    ar(1, 12, 3)
    settle()
    ar(1, 4, 4)
    settle()
    ar(1, 8, 4)
    settle()
    ar(1, 13, 3)
    settle()
    ar(1, 18, 2)
    settle()
    ar(1, 10, 4)
    settle()
    ar(1, 9, 4)
    settle()
    ar(1, 11, 4)
    settle()
    ar(1, 17, 3)
    settle()
    ar(0, 17, 7)
    settle()
    ar(0, 17, 8)
    settle()
    dx_relay(1, 2)
    settle()
    ar(1, 14, 3)
    settle()
    ar(1, 0, 5)
    settle()
    dx_relay(2, 1)
    settle()
    ar(1, 16, 3)
    settle()
    ar(1, 1, 5)
    settle()
    ar(1, 15, 3)
    settle()
    ar(1, 18, 3)
    settle()
    ar(1, 12, 4)
    settle()
    ar(1, 2, 5)
    settle()
    ar(1, 13, 4)
    settle()
    ar(1, 3, 5)
    settle()
    ar(1, 4, 5)
    settle()
    ar(1, 14, 4)
    settle()
    ar(1, 10, 5)
    settle()
    ar(1, 11, 5)
    settle()
    ar(1, 1, 6)
    settle()
    ar(1, 15, 4)
    settle()
    ar(1, 5, 5)
    settle()
    dx_relay(1, 1)
    settle()
    ar(1, 4, 6)
    settle()
    dx_final(2)
    settle()
    ar(1, 16, 4)
    settle()
    ar(1, 6, 5)
    settle()
    ar(1, 10, 6)
    settle()
    ar(1, 11, 6)
    settle()
    ar(1, 18, 4)
    settle()
    ar(1, 7, 5)
    settle()
    ar(1, 8, 5)
    settle()
    ar(1, 1, 7)
    settle()
    ar(1, 1, 8)
    settle()
    ar(1, 9, 5)
    settle()
    ar(1, 17, 4)
    settle()
    ar(1, 17, 5)
    settle()
    ar(1, 15, 5)
    settle()
    ar(1, 15, 6)
    settle()
    dx_final(1)
    settle()
    ar(1, 4, 7)
    settle()
    ar(1, 4, 8)
    settle()
    ar(1, 12, 5)
    settle()
    ar(1, 13, 5)
    settle()
    ar(1, 17, 6)
    settle()
    ar(1, 10, 7)
    settle()
    ar(1, 10, 8)
    settle()
    ar(1, 14, 5)
    settle()
    ar(1, 11, 7)
    settle()
    ar(1, 11, 8)
    settle()
    ar(1, 16, 5)
    settle()
    ar(1, 17, 7)
    settle()
    ar(1, 17, 8)
    settle()
    ar(1, 18, 5)
    settle()
    for u in (4, 2, 3):
        rs_sent(2, u)
    for finish in sent[settled[0]:] + finals:
        finish()


def layer(sizes, *args):
    anywhere = pl.BlockSpec(memory_space=pl.ANY)
    held = pl.BlockSpec(memory_space=pltpu.VMEM)
    call = pl.pallas_call(
        functools.partial(layer_kernel, sizes),
        out_shape=(
            jax.ShapeDtypeStruct((sizes.ns, sizes.rows, sizes.width), BF16),
            jax.ShapeDtypeStruct((sizes.ns, sizes.rows, sizes.width), BF16),
            jax.ShapeDtypeStruct((2, sizes.total, sizes.width), BF16),
        ),
        in_specs=[anywhere] * 4
        + [pl.BlockSpec(memory_space=pltpu.SMEM)]
        + [anywhere] * 4
        + [held] * 6,
        out_specs=[anywhere] * 3,
        scratch_shapes=list(sizes.scratch().values()),
        compiler_params=pltpu.CompilerParams(
            collective_id=0, has_side_effects=True, vmem_limit_bytes=VMEM_BYTES
        ),
    )
    return call(*args)


def widen_kernel(sizes, out, gin, grad, *refs):
    nt, share, hidden, width = sizes.nt, sizes.share, sizes.hidden, sizes.width
    (
        out_t, out_q, gin_t, gin_q, qkv, qv_bias, out_w, out_bias, in_w, in_bias, back_w,
        back_bias, gains, shifts, low, wide, tail, in_sem, out_sem, tail_sem,
    ) = refs
    t = lax.axis_index("tensor")
    pieces = []
    for src, first, second in ((out, out_t, out_q), (gin, gin_t, gin_q)):
        for s in range(sizes.ns):
            dst = first.at[s] if s < nt else second.at[s - nt]
            pieces.append((src.at[s], dst, sizes.rows))
    for b in range(2):
        for first, count, dst in (
            (sizes.back0, hidden, back_w.at[b]),
            (sizes.in0, width, in_w.at[b]),
            (sizes.out0, share, out_w.at[b]),
            (sizes.qkv0, share, qkv.at[b, 0]),
            (sizes.qkv0 + share, share, qkv.at[b, 1]),
            (sizes.qkv0 + 2 * share, share, qkv.at[b, 2]),
        ):
            size = min(count, WIDEN_ROWS)
            for start in range(0, count, size):
                src = grad.at[b, pl.ds(first + start, size)]
                pieces.append((src, dst.at[pl.ds(start, size)], size))
    tails = [
        pltpu.make_async_copy(
            grad.at[b, pl.ds(sizes.small0, 16)], tail.at[b], tail_sem.at[b]
        )
        for b in range(2)
    ]
    reads, writes, places = [], [], []
    place = 0
    for index, (src, dst, size) in enumerate(pieces):
        here = pl.ds(place, size)
        places.append((place, size))
        reads.append(pltpu.make_async_copy(src, low.at[here], in_sem.at[index]))
        writes.append(pltpu.make_async_copy(wide.at[here], dst, out_sem.at[index]))
        place += size
    for copy in reads + tails:
        copy.start()
    for (place, size), read, write in zip(places, reads, writes):
        read.wait()

        def body(step, carry, place=place):
            at = pl.ds(pl.multiple_of(place + step * 32, 32), 32)
            wide[at, :] = low[at, :].astype(F32)
            return carry

        lax.fori_loop(0, size // 32, body, 0)
        write.start()
    for copy in tails:
        copy.wait()
    rows = tail[...].astype(F32)

    def crop_rows(first, count):
        value = jnp.zeros((2, count, share), F32)
        for k in range(4):
            piece = rows[:, first : first + count, k * share : (k + 1) * share]
            value = jnp.where(t == k, piece, value)
        return value

    gains[...] = crop_rows(0, 2)
    shifts[...] = crop_rows(2, 2)
    out_bias[...] = crop_rows(4, 1)[:, 0]
    back_bias[...] = crop_rows(5, 1)[:, 0]
    in_bias[...] = rows[:, 8]
    qv_bias[...] = rows[:, 9:11, :share]
    for copy in writes:
        copy.wait()


WIDEN_ROWS = 256


def widen(sizes, out, gin, grad):
    nt, nq, rows, share, width, hidden = (
        sizes.nt, sizes.nq, sizes.rows, sizes.share, sizes.width, sizes.hidden,
    )
    anywhere = pl.BlockSpec(memory_space=pl.ANY)
    held = pl.BlockSpec(memory_space=pltpu.VMEM)
    shapes = (
        ((nt, rows, width), anywhere),
        ((nq, rows, width), anywhere),
        ((nt, rows, width), anywhere),
        ((nq, rows, width), anywhere),
        ((2, 3, share, width), anywhere),
        ((2, 2, share), held),
        ((2, share, width), anywhere),
        ((2, share), held),
        ((2, width, hidden), anywhere),
        ((2, hidden), held),
        ((2, hidden, width), anywhere),
        ((2, share), held),
        ((2, 2, share), held),
        ((2, 2, share), held),
    )
    total = 2 * sizes.ns * rows + 2 * (hidden + width + 4 * share)
    count = 2 * sizes.ns + 2 * (hidden // WIDEN_ROWS + width // WIDEN_ROWS + 4)
    return pl.pallas_call(
        functools.partial(widen_kernel, sizes),
        out_shape=tuple(jax.ShapeDtypeStruct(shape, F32) for shape, _ in shapes),
        in_specs=[anywhere] * 3,
        out_specs=tuple(spec for _, spec in shapes),
        scratch_shapes=[
            pltpu.VMEM((total, width), BF16),
            pltpu.VMEM((total, width), F32),
            pltpu.VMEM((2, 16, width), BF16),
            pltpu.SemaphoreType.DMA((count,)),
            pltpu.SemaphoreType.DMA((count,)),
            pltpu.SemaphoreType.DMA((2,)),
        ],
        compiler_params=pltpu.CompilerParams(vmem_limit_bytes=VMEM_BYTES),
    )(out, gin, grad)


VMEM_BYTES = 127 * 2**19


def fused(
    x_train,
    x_quiz,
    cot_train,
    cot_quiz,
    quiz_lengths,
    w_qkv,
    b_qv,
    w_out,
    b_out,
    w_in,
    b_in,
    w_back,
    b_back,
    norm_gains,
    norm_shifts,
):
    nt, rows, width = x_train.shape
    share, hidden = w_out.shape[0], w_in.shape[1]
    sizes = Sizes(
        nt, x_quiz.shape[0], rows, lax.axis_size("blk"), share, width, hidden
    )
    out, grad_in, grad = layer(
        sizes,
        x_train,
        x_quiz,
        cot_train,
        cot_quiz,
        quiz_lengths,
        jnp.swapaxes(w_qkv, 1, 2),
        w_out,
        w_in,
        w_back,
        b_out,
        b_in,
        b_back,
        norm_gains,
        norm_shifts,
        b_qv,
    )
    results = list(widen(sizes, out, grad_in, grad))
    results[4] = jnp.swapaxes(results[4], 2, 3)
    return tuple(results)


def fits(mesh):
    return dict(mesh.shape) == {"dp": 2, "tensor": 4, "blk": 4}


def solution(mesh):
    placed = (
        P("dp", "blk", None),
        P("dp", "blk", None),
        P("dp", "blk", None),
        P("dp", "blk", None),
        P("dp"),
        P(None, None, "tensor"),
        P(None, "tensor"),
        P("tensor", None),
        P(),
        P(None, "tensor"),
        P("tensor"),
        P("tensor", None),
        P(),
        P(),
        P(),
    )
    return jax.shard_map(
        fused if fits(mesh) else shards,
        mesh=mesh,
        in_specs=placed,
        out_specs=(
            P("dp", "blk", None),
            P("dp", "blk", None),
            P("dp", "blk", None),
            P("dp", "blk", None),
            P(None, None, None, "tensor"),
            P(None, None, "tensor"),
            P(None, "tensor", None),
            P(None, "tensor"),
            P(None, None, "tensor"),
            P(None, "tensor"),
            P(None, "tensor", None),
            P(None, "tensor"),
            P(None, None, "tensor"),
            P(None, None, "tensor"),
        ),
        check_vma=False,
    )
```

```python
import functools

import jax
import jax.numpy as jnp
from jax import lax
from jax.experimental import pallas as pl
from jax.experimental.pallas import tpu as pltpu
from jax.sharding import PartitionSpec as P

D = 768
HEAD_DIM = 64


EPSILON = 1e-12
ROOT_HALF = 0.7071067811865476
ROOT_TWO_PI = 2.5066282746310002
NEG_LARGE = -1e30


def layer_norm(hidden, gain, shift):
    center = hidden - jnp.mean(hidden, axis=-1, keepdims=True)
    inverse = lax.rsqrt(jnp.mean(center * center, axis=-1, keepdims=True) + EPSILON)
    normal = center * inverse
    return (normal * gain + shift, normal, inverse)


def norm_back(grad_out, normal, inverse, gain):
    scaled = grad_out * gain
    grad_in = inverse * (
        scaled
        - jnp.mean(scaled, axis=-1, keepdims=True)
        - normal * jnp.mean(scaled * normal, axis=-1, keepdims=True)
    )
    return (grad_in, jnp.sum(grad_out * normal, axis=0), jnp.sum(grad_out, axis=0))


def gelu_exact(values):
    return 0.5 * values * (1.0 + lax.erf(values * ROOT_HALF))


def gelu_slope(values):
    return (
        0.5 * (1.0 + lax.erf(values * ROOT_HALF))
        + values * jnp.exp(-0.5 * values * values) / ROOT_TWO_PI
    )


def across(left, right):
    return lax.dot_general(
        left, right, (((0,), (0,)), ((), ())), preferred_element_type=jnp.float32
    )


def against(left, right):
    return lax.dot_general(
        left, right, (((1,), (1,)), ((), ())), preferred_element_type=jnp.float32
    )


def rounded(values):
    return lax.optimization_barrier(values.astype(jnp.bfloat16)).astype(jnp.float32)


def crop(values, column, share):
    return lax.dynamic_slice_in_dim(values, column, share, axis=values.ndim - 1)


def pair_grads(query_heads, dout_heads, log_total, delta, key_heads, value_heads, visible):
    scale = query_heads.shape[-1] ** (-0.5)
    scores = (
        jnp.einsum("sqhe,skhe->shqk", query_heads, key_heads, preferred_element_type=jnp.float32)
        * scale
    )
    probs = jnp.where(visible[:, None, None, :], jnp.exp(scores - log_total[..., None]), 0.0)
    grad_value = jnp.einsum(
        "shqk,sqhe->skhe",
        probs.astype(jnp.bfloat16),
        dout_heads,
        preferred_element_type=jnp.float32,
    )
    grad_probs = jnp.einsum(
        "sqhe,skhe->shqk", dout_heads, value_heads, preferred_element_type=jnp.float32
    )
    grad_scores = (probs * (grad_probs - delta[..., None])).astype(jnp.bfloat16)
    grad_query = jnp.einsum(
        "shqk,skhe->sqhe", grad_scores, key_heads, preferred_element_type=jnp.float32
    )
    grad_key = jnp.einsum(
        "shqk,sqhe->skhe", grad_scores, query_heads, preferred_element_type=jnp.float32
    )
    return (grad_query, grad_key, grad_value)


def run(tokens, cotangent, lengths, first_row, weights):
    w_qkv, b_qv, w_out, b_out, w_in, b_in, w_back, b_back, norm_gains, norm_shifts = weights
    seq_count, row_count, width = tokens.shape
    seq_len = row_count * lax.axis_size("blk")
    span = min(512, seq_len)
    block_count = seq_len // span
    flat_tokens = tokens.reshape(seq_count * row_count, width)
    low_tokens = flat_tokens.astype(jnp.bfloat16)
    projected = jnp.einsum("nd,tde->tne", low_tokens, w_qkv, preferred_element_type=jnp.float32)
    qv_bias = b_qv.astype(jnp.float32)
    query = (projected[0] + qv_bias[0]).astype(jnp.bfloat16)
    key_rows = projected[1].astype(jnp.bfloat16)
    value_rows = (projected[2] + qv_bias[1]).astype(jnp.bfloat16)
    share = key_rows.shape[-1]
    heads = share // HEAD_DIM
    scale = HEAD_DIM ** (-0.5)
    head_shape = (seq_count, row_count, heads, HEAD_DIM)
    query_heads = query.reshape(head_shape)
    key_three = key_rows.reshape(seq_count, row_count, share)
    value_three = value_rows.reshape(seq_count, row_count, share)
    running_max = jnp.full((seq_count, heads, row_count), NEG_LARGE, jnp.float32)
    running_out = jnp.zeros(head_shape, jnp.float32)
    key_piece = lax.all_gather(key_three, "blk", axis=1, tiled=True)
    value_piece = lax.all_gather(value_three, "blk", axis=1, tiled=True)
    piece_rows = key_piece.shape[1]
    key_heads = key_piece.reshape(seq_count, piece_rows, heads, HEAD_DIM)
    value_heads = value_piece.reshape(seq_count, piece_rows, heads, HEAD_DIM)
    scores = (
        jnp.einsum("sqhe,skhe->shqk", query_heads, key_heads, preferred_element_type=jnp.float32)
        * scale
    )
    visible = (jnp.arange(piece_rows, dtype=jnp.int32)[None, :] < lengths[:, None])[
        :, None, None, :
    ]
    scores = jnp.where(visible, scores, NEG_LARGE)
    new_max = jnp.maximum(running_max, jnp.max(scores, axis=-1))
    factor = jnp.exp(running_max - new_max)
    raised = jnp.where(visible, jnp.exp(scores - new_max[..., None]), 0.0)
    new_sum = jnp.sum(raised, axis=-1)
    added = jnp.einsum(
        "shqk,skhe->sqhe",
        raised.astype(jnp.bfloat16),
        value_heads,
        preferred_element_type=jnp.float32,
    )
    new_out = running_out * jnp.swapaxes(factor, 1, 2)[..., None] + added
    mixed_heads = new_out / jnp.swapaxes(new_sum, 1, 2)[..., None]
    log_total = new_max + jnp.log(new_sum)
    mixed_low = mixed_heads.reshape(seq_count * row_count, share).astype(jnp.bfloat16)
    attention = lax.psum(
        jnp.dot(mixed_low, w_out, preferred_element_type=jnp.float32).astype(jnp.bfloat16), "tensor"
    ).astype(jnp.float32) + b_out.astype(jnp.float32)
    normed, unit_one, inverse_one = layer_norm(
        flat_tokens + attention, norm_gains[0], norm_shifts[0]
    )
    normed_low = normed.astype(jnp.bfloat16)
    before = jnp.dot(normed_low, w_in, preferred_element_type=jnp.float32) + b_in.astype(
        jnp.float32
    )
    active_low = gelu_exact(before).astype(jnp.bfloat16)
    branch = lax.psum(
        jnp.dot(active_low, w_back, preferred_element_type=jnp.float32).astype(jnp.bfloat16),
        "tensor",
    ).astype(jnp.float32) + b_back.astype(jnp.float32)
    final, unit_two, inverse_two = layer_norm(normed + branch, norm_gains[1], norm_shifts[1])
    positions = first_row + jnp.arange(row_count, dtype=jnp.int32)
    keep_rows = (
        (positions[None, :] < lengths[:, None])
        .reshape(seq_count * row_count, 1)
        .astype(jnp.float32)
    )
    outputs = (keep_rows * final).reshape(tokens.shape)
    grad_final = keep_rows * cotangent.reshape(seq_count * row_count, width)
    grad_mid, grad_gain_two, grad_shift_two = norm_back(
        grad_final, unit_two, inverse_two, norm_gains[1]
    )
    grad_branch = grad_mid.astype(jnp.bfloat16)
    grad_b_back = jnp.sum(grad_branch.astype(jnp.float32), axis=0)
    grad_w_back = across(active_low, grad_branch)
    grad_active = against(grad_branch, w_back).astype(jnp.bfloat16).astype(jnp.float32)
    grad_before = (grad_active * gelu_slope(before)).astype(jnp.bfloat16)
    grad_b_in = jnp.sum(grad_before.astype(jnp.float32), axis=0)
    grad_w_in = across(normed_low, grad_before)
    grad_normed = grad_mid + rounded(
        lax.psum(against(grad_before, w_in).astype(jnp.bfloat16), "tensor").astype(jnp.float32)
    )
    grad_hidden, grad_gain_one, grad_shift_one = norm_back(
        grad_normed, unit_one, inverse_one, norm_gains[0]
    )
    grad_attention = grad_hidden.astype(jnp.bfloat16)
    grad_b_out = jnp.sum(grad_attention.astype(jnp.float32), axis=0)
    grad_w_out = across(mixed_low, grad_attention)
    grad_mixed = against(grad_attention, w_out).astype(jnp.bfloat16)
    dout_heads = grad_mixed.reshape(head_shape)
    delta = jnp.swapaxes(jnp.sum(dout_heads.astype(jnp.float32) * mixed_heads, axis=-1), 1, 2)
    key_all, value_all = key_piece, value_piece
    key_blocks = jnp.moveaxis(key_all.reshape(seq_count, block_count, span, heads, HEAD_DIM), 1, 0)
    value_blocks = jnp.moveaxis(
        value_all.reshape(seq_count, block_count, span, heads, HEAD_DIM), 1, 0
    )
    visible_all = jnp.arange(seq_len, dtype=jnp.int32)[None, :] < lengths[:, None]
    visible_blocks = jnp.moveaxis(visible_all.reshape(seq_count, block_count, span), 1, 0)

    def sweep_keys(grad_query, item):
        key_block, value_block, visible_block = item
        part_query, part_key, part_value = pair_grads(
            query_heads, dout_heads, log_total, delta, key_block, value_block, visible_block
        )
        return (grad_query + part_query, (part_key, part_value))

    grad_query, (key_terms, value_terms) = lax.scan(
        sweep_keys, jnp.zeros(head_shape, jnp.float32), (key_blocks, value_blocks, visible_blocks)
    )
    key_terms = jnp.moveaxis(key_terms, 0, 1).reshape(seq_count, seq_len, share)
    value_terms = jnp.moveaxis(value_terms, 0, 1).reshape(seq_count, seq_len, share)
    key_sum, value_sum = (
        lax.psum_scatter(
            key_terms.astype(jnp.bfloat16), "blk", scatter_dimension=1, tiled=True
        ).astype(jnp.float32),
        lax.psum_scatter(
            value_terms.astype(jnp.bfloat16), "blk", scatter_dimension=1, tiled=True
        ).astype(jnp.float32),
    )
    grad_query_low = (grad_query * scale).reshape(seq_count * row_count, share).astype(jnp.bfloat16)
    grad_key_low = (key_sum * scale).reshape(seq_count * row_count, share).astype(jnp.bfloat16)
    grad_value_low = value_sum.reshape(seq_count * row_count, share).astype(jnp.bfloat16)
    grad_stack = jnp.stack([grad_query_low, grad_key_low, grad_value_low])
    grad_w_qkv = jnp.einsum(
        "nd,tne->tde", low_tokens, grad_stack, preferred_element_type=jnp.float32
    )
    grad_b_qv = jnp.stack(
        [
            jnp.sum(grad_query_low.astype(jnp.float32), axis=0),
            jnp.sum(grad_value_low.astype(jnp.float32), axis=0),
        ]
    )
    grad_through = lax.psum(
        jnp.einsum("tne,tde->nd", grad_stack, w_qkv, preferred_element_type=jnp.float32).astype(
            jnp.bfloat16
        ),
        "tensor",
    ).astype(jnp.float32)
    grad_tokens = (grad_hidden + rounded(grad_through)).reshape(tokens.shape)
    grad_gains = jnp.stack([grad_gain_one, grad_gain_two])
    grad_shifts = jnp.stack([grad_shift_one, grad_shift_two])
    grads = (
        grad_w_qkv,
        grad_b_qv,
        grad_w_out,
        grad_b_out,
        grad_w_in,
        grad_b_in,
        grad_w_back,
        grad_b_back,
        grad_gains,
        grad_shifts,
    )
    return (outputs, grad_tokens, grads)


def shards(
    x_train,
    x_quiz,
    cot_train,
    cot_quiz,
    quiz_lengths,
    w_qkv,
    b_qv,
    w_out,
    b_out,
    w_in,
    b_in,
    w_back,
    b_back,
    norm_gains,
    norm_shifts,
):
    row_count = x_train.shape[1]
    seq_len = row_count * lax.axis_size("blk")
    first_row = lax.axis_index("blk") * row_count
    share = D // lax.axis_size("tensor")
    column = lax.axis_index("tensor") * share
    weights = (w_qkv, b_qv, w_out, b_out, w_in, b_in, w_back, b_back, norm_gains, norm_shifts)
    full_lengths = jnp.full((x_train.shape[0],), seq_len, jnp.int32)
    out_train, grad_in_train, train_grads = run(
        x_train, cot_train, full_lengths, first_row, weights
    )
    out_quiz, grad_in_quiz, quiz_grads = run(x_quiz, cot_quiz, quiz_lengths, first_row, weights)
    def total(grads):
        pieces = (
            grads[0],
            grads[1],
            grads[2],
            crop(grads[3], column, share),
            grads[4],
            grads[5],
            grads[6],
            crop(grads[7], column, share),
            crop(grads[8], column, share),
            crop(grads[9], column, share),
        )
        low = tuple(piece.astype(jnp.bfloat16) for piece in pieces)
        return tuple(
            piece.astype(jnp.float32) for piece in lax.psum(low, ("dp", "blk"))
        )

    summed = [jnp.stack(pair) for pair in zip(total(train_grads), total(quiz_grads))]
    return (
        out_train,
        out_quiz,
        grad_in_train,
        grad_in_quiz,
        summed[0],
        summed[1],
        summed[2],
        summed[3],
        summed[4],
        summed[5],
        summed[6],
        summed[7],
        summed[8],
        summed[9],
    )


MESH_ID = pl.DeviceIdType.MESH
F32 = jnp.float32
BF16 = jnp.bfloat16
SMALL = 32
BACK_KINDS = "zxxxxx"
IN_KINDS = "wxzxxx"
OUT_KINDS = "x"
QKV_KINDS = "xxxxzw"
INV_ROOT_TWO_PI = 1.0 / ROOT_TWO_PI
SETTLE_AGE = 100
WEIGHT_TILE = 256


def nn(left, right):
    return jnp.dot(left, right, preferred_element_type=F32)


def tile_loop(count, tile, body):
    def step(index, carry):
        body(pl.multiple_of(index * tile, tile))
        return carry

    lax.fori_loop(0, count // tile, step, 0)


def tiles(count, tile, body):
    for start in range(0, count, tile):
        body(start)


def sum_rows(value):
    return jnp.sum(value, axis=0, keepdims=True)


def lanes(count):
    return (count // 128 + 1) * 128


class Sizes:
    def __init__(self, nt, nq, rows, blocks, share, width, hidden):
        self.nt, self.nq, self.rows, self.blocks = nt, nq, rows, blocks
        self.share, self.width, self.hidden = share, width, hidden
        self.ns = nt + nq
        self.quarter = rows // 4
        self.seq_len = rows * blocks
        self.heads = share // HEAD_DIM
        self.back0 = 0
        self.in0 = hidden
        self.out0 = hidden + width
        self.qkv0 = self.out0 + share
        self.small0 = self.qkv0 + 3 * share
        self.total = self.small0 + SMALL
        half = self.quarter // 2
        self.streams = tuple((s, part * half, half) for s in range(nt) for part in range(2))
        self.streams += tuple((s, 0, self.quarter) for s in range(nt, self.ns))
        self.streams += tuple((s, 0, self.quarter) for s in range(nt))
        self.chunks = self.plan()
        self.first_half, self.first_zone, half, zone = [], [], 0, 0
        for _, count, kind in self.chunks:
            self.first_half.append(half)
            self.first_zone.append(zone)
            half += count // 2
            zone += count // 2 if kind == "x" else count
        self.half_rows, self.zone_rows = half, zone

    def plan(self):
        pieces = []
        for first, count, kinds in (
            (self.back0, self.hidden, BACK_KINDS),
            (self.in0, self.width, IN_KINDS),
            (self.out0, self.share, OUT_KINDS),
            (self.qkv0, 3 * self.share, QKV_KINDS),
        ):
            size = count // len(kinds)
            for index, kind in enumerate(kinds):
                pieces.append((first + index * size, size, kind))
        first, count, kind = pieces[-1]
        pieces[-1] = (first, count + SMALL, kind)
        return tuple(pieces)

    def scratch(self):
        ns, rows, share, width = self.ns, self.rows, self.share, self.width
        q, blocks, seq = self.quarter, self.blocks, self.seq_len
        dma = pltpu.SemaphoreType.DMA
        nc, nu = len(self.chunks), len(self.streams)
        return dict(
            xown=pltpu.VMEM((ns, q, width), F32),
            cown=pltpu.VMEM((ns, q, width), F32),
            vec=pltpu.VMEM((16, width), F32),
            raw0=pltpu.VMEM((width,), BF16),
            raw1=pltpu.VMEM((self.hidden,), BF16),
            raw2=pltpu.VMEM((width,), BF16),
            raw_gains=pltpu.VMEM((2, width), F32),
            raw_shifts=pltpu.VMEM((2, width), F32),
            raw_qv=pltpu.VMEM((2, share), BF16),
            lengths=pltpu.SMEM((self.nq,), jnp.int32),
            xg=pltpu.VMEM((ns, seq, width), BF16),
            wqkv=pltpu.VMEM((3, share, width), BF16),
            wout=pltpu.VMEM((share, width), BF16),
            win=pltpu.VMEM((width, self.hidden), BF16),
            wback=pltpu.VMEM((self.hidden, width), BF16),
            qb=pltpu.VMEM((ns, rows, share), BF16),
            kb=pltpu.VMEM((ns, seq, share), BF16),
            vb=pltpu.VMEM((ns, seq, lanes(share)), BF16),
            probs=pltpu.VMEM((ns, self.heads, rows, seq), BF16),
            of=pltpu.VMEM((rows, lanes(share)), F32),
            invl=pltpu.VMEM((ns, rows, share), F32),
            orb=pltpu.VMEM((ns, rows, share), BF16),
            unit1=pltpu.VMEM((ns, q, width), F32),
            inv1=pltpu.VMEM((ns, q, 128), F32),
            n1r=pltpu.VMEM((ns, 4, q, width), BF16),
            dzr=pltpu.VMEM((ns, 4, q, width), BF16),
            dar=pltpu.VMEM((ns, 4, q, width), BF16),
            act=pltpu.VMEM((ns, 4, q, self.hidden), BF16),
            slope=pltpu.VMEM((ns, 4, q, self.hidden), BF16),
            work=pltpu.VMEM((rows, max(seq, width)), F32),
            dsb=pltpu.VMEM((rows, seq), BF16),
            dqb=pltpu.VMEM((ns, rows, share), BF16),
            dkvt=pltpu.VMEM((ns, 2, share, seq), BF16),
            tq=pltpu.VMEM((share, rows), BF16),
            tm=pltpu.VMEM((share, rows), BF16),
            gm=pltpu.VMEM((rows, share), BF16),
            delta=pltpu.VMEM((rows, 128), F32),
            part=pltpu.VMEM((ns, 2, 2, q, width), BF16),
            crecv=pltpu.VMEM((3, ns, 2, q, width), BF16),
            yrecv=pltpu.VMEM((3, ns, q, width), BF16),
            part4=pltpu.VMEM((ns, blocks, 2, 2, q, width), BF16),
            crecv4=pltpu.VMEM((ns, blocks, 2, q, width), BF16),
            yrecv4=pltpu.VMEM((ns, blocks, q, width), BF16),
            zrecv4=pltpu.VMEM((ns, 2, blocks - 1, q, width), BF16),
            outq=pltpu.VMEM((ns, q, width), BF16),
            ginq=pltpu.VMEM((ns, q, width), BF16),
            gb=pltpu.VMEM((2, self.total, width), BF16),
            xrecv=pltpu.VMEM((2, self.half_rows, width), BF16),
            zr1=pltpu.VMEM((2, self.zone_rows, width), BF16),
            zr2=pltpu.VMEM((2, self.half_rows, width), BF16),
            small=pltpu.VMEM((2, SMALL, width), F32),
            smallc=pltpu.VMEM((2, 8, width), F32),
            smalls=pltpu.VMEM((2, 8, width), F32),
            smally=pltpu.VMEM((2, 8, width), F32),
            load_sem=dma((2 * ns + 5,)),
            vec_sem=dma((7,)),
            xz_s=dma((nu - self.nt, 2, blocks - 1)),
            xz_r=dma((nu - self.nt, 2, blocks - 1)),
            xc_s=dma((nu - self.nt, 2, blocks - 1, 3)),
            xc_r=dma((nu - self.nt, 2, blocks - 1, 3)),
            ex_s=dma((3, nu - self.nt, 5)),
            ex_r=dma((3, nu - self.nt, 5)),
            d4_s=dma((ns, 2)),
            d4_r=dma((ns, 2)),
            z4_s=dma((ns, 2, blocks - 1)),
            z4_r=dma((ns, 2, blocks - 1)),
            og_s=dma((2, ns, 3)),
            og_r=dma((2, ns, 3)),
            ol_s=dma((2, ns)),
            ar_s=dma((2, nc, 5)),
            ar_r=dma((2, nc, 5)),
            al_s=dma((2, nc)),
            sm_s=dma((2, 2)),
            sm_r=dma((2, 2)),
        )


INPUTS = (
    "xt", "xq", "ct", "cq", "lens", "wqkv_in", "wout_in", "win_in", "wback_in",
    "b_out", "b_in", "b_back", "gains", "shifts", "b_qv",
)
OUTPUTS = ("out", "gin", "grad")


def layer_kernel(z_, *refs):
    names = INPUTS + OUTPUTS + tuple(z_.scratch())
    r = dict(zip(names, refs))
    nt, ns, rows, blocks = z_.nt, z_.ns, z_.rows, z_.blocks
    share, width, hidden, quarter = z_.share, z_.width, z_.hidden, z_.quarter
    seq_len, heads = z_.seq_len, z_.heads
    scale = HEAD_DIM ** (-0.5)
    batches = (tuple(range(nt)), tuple(range(nt, ns)))
    lens_ref = r["lengths"]
    xg, work, part, gb = r["xg"], r["work"], r["part"], r["gb"]

    x = lax.axis_index("dp")
    t = lax.axis_index("tensor")
    z = lax.axis_index("blk")
    y = t // 2
    c = t % 2
    to_x = (1 - x, t, z)
    to_c = (x, t + 1 - 2 * c, z)
    to_y = (x, (t + 2) % 4, z)
    to_d = (x, 3 - t, z)
    to_right = (x, t, jnp.minimum(z + 1, blocks - 1))
    to_left = (x, t, jnp.maximum(z - 1, 0))
    has_left = z > 0
    has_right = z < blocks - 1
    corner = jnp.logical_or(z == 0, z == blocks - 1)
    interior = jnp.logical_and(z > 0, z < blocks - 1)
    to_inner = (x, t, jnp.where(z == 0, 1, blocks - 2))
    to_mirror = (x, t, blocks - 1 - z)
    to_outer = (x, t, jnp.where(z == 1, 0, blocks - 1))
    finals, sent, ages = [], [], []

    def settle(count=3, age=SETTLE_AGE):
        ages.append(len(sent))
        ready = ages[-age] if len(ages) >= age else 0
        for _ in range(min(count, ready - settled[0])):
            sent[settled[0]]()
            settled[0] += 1

    settled = [0]

    def when(cond, fn):
        if cond is None:
            fn()
        else:
            pl.when(cond)(fn)

    def remote(src, dst, ssem, rsem, dev):
        return pltpu.make_async_remote_copy(
            src_ref=src,
            dst_ref=dst,
            send_sem=ssem,
            recv_sem=rsem,
            device_id=dev,
            device_id_type=MESH_ID,
        )

    def send(src, dst, ssem, rsem, dev, cond=None, final=True):
        when(cond, lambda: remote(src, dst, ssem, rsem, dev).start())
        if final:
            sent.append(
                lambda: when(cond, lambda: remote(src, dst, ssem, rsem, dev).wait_send())
            )

    def arrived(dst, ssem, rsem, dev, cond=None):
        when(cond, lambda: remote(dst, dst, ssem, rsem, dev).wait_recv())

    def local(src, dst, sem):
        copy = pltpu.make_async_copy(src, dst, sem)
        copy.start()
        return copy

    mine = pl.ds(pl.multiple_of(t * quarter, quarter), quarter)
    facing = (t + 2) % 4

    def stream(u):
        s, first, count = z_.streams[u]
        return s, pl.ds(first, count)

    def flat(ref, s, lanes_=slice(None)):
        value = ref[s, :, :, lanes_]
        return value.reshape(rows, value.shape[-1])
    own_block = pl.ds(pl.multiple_of(z * rows, rows), rows)

    vec_ref = r["vec"]

    def vec(row, size=None):
        return vec_ref[row : row + 1, : (size or width)]

    vector_loads = (
        (r["b_out"], r["raw0"]),
        (r["b_in"], r["raw1"]),
        (r["b_back"], r["raw2"]),
        (r["gains"], r["raw_gains"]),
        (r["shifts"], r["raw_shifts"]),
        (r["b_qv"], r["raw_qv"]),
        (r["lens"], r["lengths"]),
    )

    def load_vectors():
        return [
            local(src, dst, r["vec_sem"].at[index])
            for index, (src, dst) in enumerate(vector_loads)
        ]

    def gather_vectors():
        for copy in loads["vectors"]:
            copy.wait()
        for row, name in enumerate(("raw0", "raw1", "raw2")):
            vec_ref[row : row + 1, :] = r[name][...].astype(F32).reshape(1, width)
        vec_ref[3:5, :] = r["raw_gains"][...]
        vec_ref[5:7, :] = r["raw_shifts"][...]
        vec_ref[7:9, :share] = r["raw_qv"][...].astype(F32)

    loads = {}
    load_sem = r["load_sem"]
    x_src = [r["xt"].at[s] for s in range(nt)] + [r["xq"].at[s] for s in range(ns - nt)]
    c_src = [r["ct"].at[s] for s in range(nt)] + [r["cq"].at[s] for s in range(ns - nt)]
    for s in range(ns):
        loads["x", s] = local(x_src[s].at[mine], r["xown"].at[s], load_sem.at[s])
    loads["vectors"] = load_vectors()
    for index, name in enumerate(("wqkv", "wout", "win", "wback")):
        loads[name] = local(r[name + "_in"], r[name], load_sem.at[ns + index])
    for s in range(ns):
        loads["c", s] = local(c_src[s].at[mine], r["cown"].at[s], load_sem.at[ns + 4 + s])

    barrier = pltpu.get_barrier_semaphore()

    def greet(dev, cond=None):
        when(
            cond,
            lambda: pl.semaphore_signal(
                barrier, inc=1, device_id=dev, device_id_type=MESH_ID
            ),
        )

    for dev in (to_x, to_c, to_y, to_d):
        greet(dev)
    greet(to_left, has_left)
    greet(to_right, has_right)
    when(corner, lambda: pl.semaphore_wait(barrier, 5))
    when(interior, lambda: pl.semaphore_wait(barrier, 6))

    def block_rows(j, q, within=pl.ds(0, quarter)):
        start = j * rows + q * quarter + within.start
        return pl.ds(pl.multiple_of(start, within.size), within.size)

    def side_valid(side, d):
        return z >= d if side == 0 else z <= blocks - 1 - d

    def side_block(side, d):
        return jnp.maximum(z - d, 0) if side == 0 else jnp.minimum(z + d, blocks - 1)

    xz_s, xz_r, xc_s, xc_r = r["xz_s"], r["xz_r"], r["xc_s"], r["xc_r"]

    def xa_start(u):
        s, within = stream(u)
        if within.start == 0:
            loads["x", s].wait()
        place = block_rows(z, t, within)
        xg[s, place, :] = r["xown"][s, within, :].astype(BF16)
        here = xg.at[s, place]
        send(here, here, xz_s.at[u, 0, 0], xz_r.at[u, 0, 0], to_right, has_right)
        send(here, here, xz_s.at[u, 1, 0], xz_r.at[u, 1, 0], to_left, has_left)

    def xa_step(u, d):
        s, within = stream(u)
        for side in range(2):
            valid = side_valid(side, d)
            here = xg.at[s, block_rows(side_block(side, d), t, within)]
            arrived(here, xz_s.at[u, side, d - 1], xz_r.at[u, side, d - 1], to_c, valid)
            if d < blocks - 1:
                more = has_right if side == 0 else has_left
                send(
                    here,
                    here,
                    xz_s.at[u, side, d],
                    xz_r.at[u, side, d],
                    to_right if side == 0 else to_left,
                    jnp.logical_and(valid, more),
                )
            for kind, dev in ((0, to_y), (1, to_c)):
                pair = xc_s.at[u, side, d - 1, kind], xc_r.at[u, side, d - 1, kind]
                send(here, here, *pair, dev, valid)

    def xa_forward(u, d):
        s, within = stream(u)
        for side in range(2):
            valid = side_valid(side, d)
            here = xg.at[s, block_rows(side_block(side, d), facing, within)]
            pair = xc_s.at[u, side, d - 1, 0], xc_r.at[u, side, d - 1, 0]
            arrived(here, *pair, to_c, valid)
            pair = xc_s.at[u, side, d - 1, 2], xc_r.at[u, side, d - 1, 2]
            send(here, here, *pair, to_c, valid)

    def xa_done(u, d):
        s, within = stream(u)
        for side in range(2):
            for kind in (1, 2):
                here = xg.at[s, block_rows(side_block(side, d), t, within)]
                pair = xc_s.at[u, side, d - 1, kind], xc_r.at[u, side, d - 1, kind]
                arrived(here, *pair, to_c, side_valid(side, d))

    def own_cast(s):
        copy = local(x_src[s], work.at[:, pl.ds(0, width)], load_sem.at[2 * ns + 4])
        copy.wait()
        for q in range(4):

            def cast(q=q):
                xg[s, block_rows(z, q), :] = work[
                    q * quarter : (q + 1) * quarter, :width
                ].astype(BF16)

            when(t != q, cast)

    padded = lanes(share)
    padded_head = lax.broadcasted_iota(jnp.int32, (1, padded), 1) // HEAD_DIM
    head_of_lane = lax.broadcasted_iota(jnp.int32, (1, share), 1) // HEAD_DIM
    invl = r["invl"]
    crecv, yrecv = r["crecv"], r["yrecv"]
    first_whole = len(z_.streams) - nt

    class Pairs:
        def __init__(self, ref):
            self.at = self
            self.ref = ref

        def __getitem__(self, key):
            k, u, index = key
            return self.ref.at[k, 2 * (u - first_whole) if u >= first_whole else u, index]

    ex_s, ex_r = Pairs(r["ex_s"]), Pairs(r["ex_r"])

    def rs_sends(k, u):
        s, within = stream(u)
        return (
            (
                part.at[s, :, 1 - c, within],
                crecv.at[k, s, :, within],
                ex_s.at[k, u, 0],
                ex_r.at[k, u, 0],
                to_c,
            ),
            (
                part.at[s, 1 - y, c, within],
                yrecv.at[k, s, within],
                ex_s.at[k, u, 1],
                ex_r.at[k, u, 1],
                to_y,
            ),
        )

    def rs_core(k, u):
        send(*rs_sends(k, u)[0], final=False)

    def rs_y(k, u):
        s, within = stream(u)
        arrived(*rs_sends(k, u)[0][1:])
        part[s, 1 - y, c, within] = (
            part[s, 1 - y, c, within].astype(F32) + crecv[k, s, 1 - y, within].astype(F32)
        ).astype(BF16)
        send(*rs_sends(k, u)[1], final=False)

    def rs_total(k, u):
        s, within = stream(u)
        arrived(*rs_sends(k, u)[1][1:])
        return (
            part[s, y, c, within].astype(F32)
            + crecv[k, s, y, within].astype(F32)
            + yrecv[k, s, within].astype(F32)
        )

    def rs_sent(k, u):
        for args in rs_sends(k, u):
            remote(*args).wait_send()

    def ag_start(k, u, full):
        s, within = stream(u)
        here = full.at[s, t, within]
        send(here, here, ex_s.at[k, u, 3], ex_r.at[k, u, 3], to_y)
        send(here, here, ex_s.at[k, u, 2], ex_r.at[k, u, 2], to_c)

    def ag_forward(k, u, full):
        s, within = stream(u)
        here = full.at[s, facing, within]
        arrived(here, ex_s.at[k, u, 3], ex_r.at[k, u, 3], to_y)
        send(here, here, ex_s.at[k, u, 4], ex_r.at[k, u, 4], to_c)

    def ag_done(k, u, full):
        s, within = stream(u)
        here = full.at[s, t, within]
        arrived(here, ex_s.at[k, u, 2], ex_r.at[k, u, 2], to_c)
        arrived(here, ex_s.at[k, u, 4], ex_r.at[k, u, 4], to_c)

    def publish(buf, s, target, kind):
        here = target.at[s, mine]
        og_s, og_r = r["og_s"], r["og_r"]
        devices = tuple(enumerate((to_c, to_y, to_d)))
        for index, dev in devices:
            sems = og_s.at[kind, s, index], og_r.at[kind, s, index]
            send(buf.at[s], here, *sems, dev)
        copy = local(buf.at[s], here, r["ol_s"].at[kind, s])
        finals.append(copy.wait)

        def landed():
            for index, dev in devices:
                arrived(here, og_s.at[kind, s, index], og_r.at[kind, s, index], dev)

        finals.append(landed)

    def batch_of(s):
        return 0 if s < nt else 1

    def length(s):
        return jnp.int32(seq_len) if s < nt else lens_ref[s - nt]

    def keep_rows(s, within):
        first = z * rows + t * quarter + within.start
        position = first + lax.broadcasted_iota(jnp.int32, (within.size, 1), 0)
        return jnp.where(position < length(s), 1.0, 0.0)

    qb, kb, vb, probs, of, orb = (r[n] for n in ("qb", "kb", "vb", "probs", "of", "orb"))
    wqkv, wout, win, wback = (r[n] for n in ("wqkv", "wout", "win", "wback"))
    unit1, inv1 = r["unit1"], r["inv1"]
    dh = r["xown"]
    n1r, dzr, dar, act, slope = (r[n] for n in ("n1r", "dzr", "dar", "act", "slope"))
    dsb, dqb, dkvt = (r[n] for n in ("dsb", "dqb", "dkvt"))
    small = r["small"]
    tq, tm, gm, delta = (r[n] for n in ("tq", "tm", "gm", "delta"))

    def add_small(s, row, value, size=None):
        place = (batch_of(s), slice(row, row + 1), slice(0, size or width))
        small[place] += value

    def project_query(s):
        low = (against(xg[s, own_block, :], wqkv[0]) + vec(7, share)).astype(BF16)
        qb[s] = low * jnp.array(scale, BF16)

    def project_block(s, start):
        lane = lax.broadcasted_iota(jnp.int32, (rows, padded - share), 1)
        place = pl.ds(start, rows)
        block = xg[s, place, :]
        kb[s, place, :] = against(block, wqkv[1]).astype(BF16)
        vb[s, place, :share] = (against(block, wqkv[2]) + vec(8, share)).astype(BF16)
        vb[s, place, share:] = jnp.where(lane == 0, 1.0, 0.0).astype(BF16)

    def project_own(s):
        project_block(s, pl.multiple_of(z * rows, rows))

    def project_rest(s):
        def body(j):
            project_block(s, pl.multiple_of(((z + 1 + j) % blocks) * rows, rows))

        repeat = rounds if s < nt else loop
        repeat(blocks - 1, body)

    def store_part(s, cols, value, within=pl.ds(0, quarter)):
        low = value.astype(BF16).reshape(2, 2, within.size, value.shape[-1])
        part[s, :, :, within, cols] = low

    key_tiles = tuple(slice(first, first + 256) for first in range(0, seq_len, 256))

    def folded_max(value, running):
        for first in range(0, value.shape[-1], 128):
            piece = value[:, first : first + 128]
            running = piece if running is None else jnp.maximum(running, piece)
        return running

    def rounds(count, body):
        for index in range(count):
            body(index)

    def loop(count, body):
        def step(index, carry):
            body(index)
            return carry

        lax.fori_loop(0, count, step, 0)

    def attention_heads(s):
        attention_start(s)
        loop(heads, lambda h: attention_head(s, h))

    def attention_start(s):
        of[...] = jnp.zeros((rows, padded), F32)
        invl[s] = jnp.zeros((rows, share), F32)

    def attention(s, h):
        if h == 0:
            attention_start(s)
        attention_head(s, h)

    def attention_head(s, h):
        mask = head_of_lane == h
        query = jnp.where(mask, qb[s], jnp.zeros((), BF16))
        highest = None
        for tile in key_tiles:
            scores = against(query, kb[s, tile, :])
            if s >= nt:
                position = tile.start + lax.broadcasted_iota(jnp.int32, (1, 256), 1)
                scores += jnp.where(position < length(s), 0.0, NEG_LARGE)
            work[:, tile] = scores
            highest = folded_max(scores, highest)
        delta[...] = jnp.broadcast_to(
            jnp.max(highest, axis=-1, keepdims=True), (rows, 128)
        )

        top = delta[...]
        mixed = None
        for tile in key_tiles:
            for first in range(tile.start, tile.stop, 128):
                piece = slice(first, first + 128)
                probs[s, h, :, piece] = jnp.exp(work[:, piece] - top).astype(BF16)
            term = nn(probs[s, h, :, tile], vb[s, tile, :])
            mixed = term if mixed is None else mixed + term
        inverse = 1.0 / mixed[:, share : share + 1]
        of[...] = jnp.where(padded_head == h, mixed * inverse, of[...])
        invl[s] = jnp.where(mask, inverse, invl[s])

    def attention_out(s):
        orb[s] = of[:, :share].astype(BF16)

        def body(start):
            cols = pl.ds(start, 256)
            store_part(s, cols, nn(orb[s], wout[:, cols]))

        tiles(width, 256, body)

    def forward_rows(u):
        s, within = stream(u)
        summed = r["xown"][s, within] + (rs_total(0, u) + vec(0))
        center = summed - jnp.mean(summed, axis=-1, keepdims=True)
        inverse = lax.rsqrt(jnp.mean(center * center, axis=-1, keepdims=True) + EPSILON)
        normal = center * inverse
        unit1[s, within] = normal
        inv1[s, within] = jnp.broadcast_to(inverse, (within.size, 128))
        n1r[s, t, within] = (normal * vec(3) + vec(5)).astype(BF16)

    def feed_forward(u):
        s, within = stream(u)
        count = 4 * within.size

        def up(start):
            cols = pl.ds(start, 256)
            left = n1r[s, :, within, :].reshape(count, width)
            before = nn(left, win[:, cols]) + vec_ref[1:2, cols]
            phi = 0.5 * (1.0 + lax.erf(before * ROOT_HALF))
            low = (before * phi).astype(BF16)
            act[s, :, within, cols] = low.reshape(4, within.size, 256)
            bell = jnp.exp(-0.5 * before * before) * INV_ROOT_TWO_PI
            low = (phi + before * bell).astype(BF16)
            slope[s, :, within, cols] = low.reshape(4, within.size, 256)

        (tiles if s < nt else tile_loop)(hidden, 256, up)
        rs_sent(0, u)

        def down(start):
            cols = pl.ds(start, 256)
            left = act[s, :, within, :].reshape(count, hidden)
            store_part(s, cols, nn(left, wback[:, cols]), within)

        (tiles if s < nt else tile_loop)(width, 256, down)

    def norm_back_rows(grad_out, normal, inverse, gain):
        scaled = grad_out * gain
        return inverse * (
            scaled
            - jnp.mean(scaled, axis=-1, keepdims=True)
            - normal * jnp.mean(scaled * normal, axis=-1, keepdims=True)
        )

    def middle_rows(u):
        s, within = stream(u)
        normed = unit1[s, within] * vec(3) + vec(5)
        summed = normed + (rs_total(1, u) + vec(2))
        center = summed - jnp.mean(summed, axis=-1, keepdims=True)
        inverse = lax.rsqrt(jnp.mean(center * center, axis=-1, keepdims=True) + EPSILON)
        normal = center * inverse
        keep = keep_rows(s, within)
        r["outq"][s, within] = (keep * (normal * vec(4) + vec(6))).astype(BF16)
        grad_out = keep * r["cown"][s, within]
        grad = norm_back_rows(grad_out, normal, inverse, vec(4))
        dh[s, within] = grad
        low = grad.astype(BF16)
        dzr[s, t, within] = low
        add_small(s, 1, sum_rows(grad_out * normal))
        add_small(s, 3, sum_rows(grad_out))
        add_small(s, 5, sum_rows(low.astype(F32)))

    def backward_hidden(s):
        b = batch_of(s)

        def up(start):
            cols = pl.ds(start, 256)
            grad = against(flat(dzr, s), wback[cols, :]).astype(BF16).astype(F32)
            low = (grad * flat(slope, s, cols).astype(F32)).astype(BF16)
            slope[s, :, :, cols] = low.reshape(4, quarter, 256)
            small[b, 8:9, cols] += sum_rows(low.astype(F32))

        tiles(hidden, 256, up)
        for u, (sequence, first, count) in enumerate(z_.streams):
            if sequence == s and (s >= nt or count < quarter):
                rs_sent(1, u)

        def down(start):
            cols = pl.ds(start, 256)
            store_part(s, cols, against(flat(slope, s), win[cols, :]))

        tiles(width, 256, down)

    def weight_grad(b, base, first, count, left, right):
        def body(start):
            total = None
            for s in batches[b]:
                term = across(flat(left, s, pl.ds(first + start, WEIGHT_TILE)), flat(right, s))
                total = term if total is None else total + term
            place = pl.ds(pl.multiple_of(base + first + start, 64), WEIGHT_TILE)
            gb[b, place, :] = total.astype(BF16)

        if count > WEIGHT_TILE:
            tile_loop(count, WEIGHT_TILE, body)
        else:
            body(0)

    def backward_rows(u):
        s, within = stream(u)
        grad_out = dh[s] + rs_total(2, u).astype(BF16).astype(F32)
        normal = unit1[s]
        grad = norm_back_rows(grad_out, normal, inv1[s, :, 0:1], vec(3))
        dh[s] = grad
        low = grad.astype(BF16)
        dar[s, t] = low
        add_small(s, 0, sum_rows(grad_out * normal))
        add_small(s, 2, sum_rows(grad_out))
        add_small(s, 4, sum_rows(low.astype(F32)))

    def out_grad(b):
        total = None
        for s in batches[b]:
            term = across(orb[s], flat(dar, s))
            total = term if total is None else total + term
        gb[b, z_.out0 : z_.out0 + share, :] = total.astype(BF16)


    def mixed_back(s):
        grad_mixed = against(flat(dar, s), wout[...]).astype(BF16).astype(F32)
        grad_mixed = (grad_mixed * invl[s]).astype(BF16)
        gm[...] = grad_mixed
        tm[...] = grad_mixed.T
        tq[...] = qb[s].T
        of[:, :share] = grad_mixed.astype(F32) * orb[s].astype(F32)

    def attention_back_heads(s):
        mixed_back(s)
        dqb[s] = jnp.zeros((rows, share), BF16)
        loop(heads, lambda h: attention_back_head(s, h))

    def attention_back(s, h):
        if h == 0:
            mixed_back(s)
            dqb[s] = jnp.zeros((rows, share), BF16)
        attention_back_head(s, h)

    def attention_back_head(s, h):
        mask = head_of_lane == h
        summed = jnp.sum(jnp.where(mask, of[:, :share], 0.0), axis=-1, keepdims=True)
        grad_head = jnp.where(mask, gm[...], jnp.zeros((), BF16))
        for tile in key_tiles:
            grads = against(grad_head, vb[s, tile, :share]) - summed
            dsb[:, tile] = (probs[s, h, :, tile].astype(F32) * grads).astype(BF16)
        grad_query = (nn(dsb[...], kb[s]) * scale).astype(BF16)
        dqb[s] = jnp.where(mask, grad_query, dqb[s])
        place = pl.ds(pl.multiple_of(h * HEAD_DIM, HEAD_DIM), HEAD_DIM)
        dkvt[s, 0, place, :] = nn(tq[place, :], dsb[...]).astype(BF16)
        dkvt[s, 1, place, :] = nn(tm[place, :], probs[s, h]).astype(BF16)

    def through_back(s):
        add_small(s, 9, sum_rows(dqb[s].astype(F32)), share)
        ones = jnp.ones((8, seq_len), BF16)
        add_small(s, 10, against(ones, dkvt[s, 1])[0:1], share)

        work[:, :width] = nn(dqb[s], wqkv[0])
        def body(pair):
            for j in (2 * pair, 2 * pair + 1):
                place = pl.ds(pl.multiple_of(j * rows, rows), rows)
                terms = dkvt[s, :, :, place].reshape(2 * share, rows)
                total = across(terms, wqkv[1:3].reshape(2 * share, width))
                total += jnp.where(j == z, work[:, :width], 0.0)
                r["part4"][s, j] = total.astype(BF16).reshape(2, 2, quarter, width)

        loop(blocks // 2, body)

    def qkv_grad(b):
        query = other = None
        for s in batches[b]:
            term = across(dqb[s], xg[s, own_block, :])
            query = term if query is None else query + term
            term = nn(dkvt[s].reshape(2 * share, seq_len), xg[s])
            other = term if other is None else other + term
        first = z_.qkv0
        gb[b, first : first + share, :] = query.astype(BF16)
        gb[b, first + share : first + 3 * share, :] = other.astype(BF16)

    part4, crecv4, yrecv4, zrecv4 = (r[n] for n in ("part4", "crecv4", "yrecv4", "zrecv4"))
    d4_s, d4_r, z4_s, z4_r = (r[n] for n in ("d4_s", "d4_r", "z4_s", "z4_r"))

    def dx_core(s):
        send(part4.at[s, :, :, 1 - c], crecv4.at[s], d4_s.at[s, 0], d4_r.at[s, 0], to_c)

        def clear(side):
            zrecv4[s, side] = jnp.zeros(zrecv4.shape[2:], BF16)

        when(z == 0, lambda: clear(0))
        when(z == blocks - 1, lambda: clear(1))

    def dx_y(s):
        arrived(crecv4.at[s], d4_s.at[s, 0], d4_r.at[s, 0], to_c)

        def body(j, carry):
            part4[s, j, 1 - y, c] = (
                part4[s, j, 1 - y, c].astype(F32) + crecv4[s, j, 1 - y].astype(F32)
            ).astype(BF16)
            return carry

        lax.fori_loop(0, blocks, body, 0)
        send(part4.at[s, :, 1 - y, c], yrecv4.at[s], d4_s.at[s, 1], d4_r.at[s, 1], to_y)

    def dx_partial(s, j):
        return (
            part4[s, j, y, c].astype(F32)
            + crecv4[s, j, y].astype(F32)
            + yrecv4[s, j].astype(F32)
        )

    def dx_arrived_y(s):
        arrived(yrecv4.at[s], d4_s.at[s, 1], d4_r.at[s, 1], to_y)

    def dx_relay(s, d):
        for side in range(2):
            target = z + d if side == 0 else z - d
            valid = target <= blocks - 1 if side == 0 else target >= 0
            block = jnp.clip(target, 0, blocks - 1)
            has_source = has_left if side == 0 else has_right
            dev = to_right if side == 0 else to_left

            def go(side=side, block=block, has_source=has_source):
                if d < blocks - 1:
                    arrived(
                        zrecv4.at[s, side, d],
                        z4_s.at[s, side, d],
                        z4_r.at[s, side, d],
                        to_c,
                        has_source,
                    )
                    value = dx_partial(s, block) + zrecv4[s, side, d].astype(F32)
                else:
                    value = dx_partial(s, block)
                part4[s, block, y, c] = value.astype(BF16)

            when(valid, go)
            send(
                part4.at[s, block, y, c],
                zrecv4.at[s, side, d - 1],
                z4_s.at[s, side, d - 1],
                z4_r.at[s, side, d - 1],
                dev,
                valid,
            )

    def dx_final(s):
        for side, has_source in ((0, has_left), (1, has_right)):
            arrived(
                zrecv4.at[s, side, 0],
                z4_s.at[s, side, 0],
                z4_r.at[s, side, 0],
                to_c,
                has_source,
            )
        total = (
            dx_partial(s, z)
            + zrecv4[s, 0, 0].astype(F32)
            + zrecv4[s, 1, 0].astype(F32)
        )
        r["ginq"][s] = (dh[s] + total.astype(BF16).astype(F32)).astype(BF16)
        publish(r["ginq"], s, r["gin"], 1)

    xrecv, zr1, zr2, grad_ref = r["xrecv"], r["zr1"], r["zr2"], r["grad"]
    ar_s, ar_r, al_s = r["ar_s"], r["ar_r"], r["al_s"]

    def ar_places(i):
        first, count, kind = z_.chunks[i]
        half = count // 2
        index = x if kind == "x" else jnp.where(z == 1, 0, 1)
        own = pl.ds(pl.multiple_of(first + index * half, 16), half)
        other = pl.ds(pl.multiple_of(first + (1 - index) * half, 16), half)
        return own, other, pl.ds(z_.first_half[i], half), pl.ds(z_.first_zone[i], half)

    def zone_places(i):
        first, count, kind = z_.chunks[i]
        half, base = count // 2, z_.first_zone[i]
        index = jnp.where(z == 1, 0, 1)
        own = pl.ds(pl.multiple_of(base + index * half, 16), half)
        other = pl.ds(pl.multiple_of(base + (1 - index) * half, 16), half)
        return own, other, pl.ds(base, count), pl.ds(first, count)

    def add_into(b, dst, dst_first, left, left_first, right, right_first, count):
        tile = next(size for size in (64, 48, 32, 16) if count % size == 0)

        def body(start):
            at = lambda first: pl.ds(pl.multiple_of(first + start, 16), tile)
            dst[b, at(dst_first), :] = (
                left[b, at(left_first), :].astype(F32)
                + right[b, at(right_first), :].astype(F32)
            ).astype(BF16)

        tile_loop(count, tile, body)

    def sems(b, i, index):
        return ar_s.at[b, i, index], ar_r.at[b, i, index]

    def x0(b, i):
        own, other, half, zone = ar_places(i)
        send(gb.at[b, other], xrecv.at[b, half], *sems(b, i, 0), to_x)

    def x1(b, i):
        own, other, half, zone = ar_places(i)
        arrived(xrecv.at[b, half], *sems(b, i, 0), to_x)
        add_into(b, gb, own.start, gb, own.start, xrecv, half.start, half.size)
        send(gb.at[b, own], zr1.at[b, zone], *sems(b, i, 1), to_inner, corner)

    def x2(b, i):
        own, other, half, zone = ar_places(i)

        def add():
            arrived(zr1.at[b, zone], *sems(b, i, 1), to_x)
            add_into(b, gb, own.start, gb, own.start, zr1, zone.start, half.size)

        when(interior, add)
        send(gb.at[b, own], zr2.at[b, half], *sems(b, i, 2), to_mirror, interior)

    def x_share(b, i, cond):
        own, other, half, zone = ar_places(i)
        src, dst = zr1.at[b, zone], grad_ref.at[b, own]
        send(src, dst, *sems(b, i, 3), to_x, cond, final=False)
        when(cond, lambda: pltpu.make_async_copy(src, dst, al_s.at[b, i]).start())

    def x3(b, i):
        own, other, half, zone = ar_places(i)

        def add():
            arrived(zr2.at[b, half], *sems(b, i, 2), to_x)
            add_into(b, zr1, zone.start, gb, own.start, zr2, half.start, half.size)

        when(interior, add)
        send(zr1.at[b, zone], zr1.at[b, zone], *sems(b, i, 1), to_outer, interior)
        x_share(b, i, interior)

    def x4(b, i):
        own, other, half, zone = ar_places(i)
        arrived(zr1.at[b, zone], *sems(b, i, 1), to_x, corner)
        x_share(b, i, corner)

    def x5(b, i):
        own, other, half, zone = ar_places(i)
        src, dst = zr1.at[b, zone], grad_ref.at[b, own]
        remote(src, dst, *sems(b, i, 3), to_x).wait_send()
        pltpu.make_async_copy(src, dst, al_s.at[b, i]).wait()
        arrived(grad_ref.at[b, other], *sems(b, i, 3), to_x)

    def z0(b, i):
        whole, rows_of = zone_places(i)[2:]
        send(gb.at[b, rows_of], zr1.at[b, whole], *sems(b, i, 0), to_inner, corner)

    def z1(b, i):
        own, other, half, zone = ar_places(i)
        whole, rows_of = zone_places(i)[2:]

        def add():
            arrived(zr1.at[b, whole], *sems(b, i, 0), to_x)
            add_into(b, gb, rows_of.start, gb, rows_of.start, zr1, whole.start, whole.size)

        when(interior, add)
        send(gb.at[b, other], zr2.at[b, half], *sems(b, i, 1), to_mirror, interior)

    def z2(b, i):
        own, other, half, zone = ar_places(i)

        def add():
            arrived(zr2.at[b, half], *sems(b, i, 1), to_x)
            add_into(b, gb, own.start, gb, own.start, zr2, half.start, half.size)

        when(interior, add)
        send(gb.at[b, own], xrecv.at[b, half], *sems(b, i, 2), to_x, interior)

    def z3(b, i):
        own, other, half, zone = ar_places(i)
        zone_own = zone_places(i)[0]

        def add():
            arrived(xrecv.at[b, half], *sems(b, i, 2), to_x)
            add_into(b, zr1, zone_own.start, gb, own.start, xrecv, half.start, half.size)

        when(interior, add)
        here = zr1.at[b, zone_own]
        send(here, here, *sems(b, i, 3), to_mirror, interior)
        send(here, here, *sems(b, i, 0), to_outer, interior)

    def z4(b, i):
        there = zr1.at[b, zone_places(i)[1]]
        arrived(there, *sems(b, i, 3), to_x, interior)
        send(there, there, *sems(b, i, 4), to_outer, interior)

    def z5(b, i):
        there = zr1.at[b, zone_places(i)[1]]
        arrived(there, *sems(b, i, 0), to_x, corner)
        arrived(there, *sems(b, i, 4), to_x, corner)
        z_copy(b, i)

    def z_copy(b, i):
        whole, rows_of = zone_places(i)[2:]
        pltpu.make_async_copy(
            zr1.at[b, whole], grad_ref.at[b, rows_of], al_s.at[b, i]
        ).start()

    def z6(b, i):
        whole, rows_of = zone_places(i)[2:]
        pltpu.make_async_copy(
            zr1.at[b, whole], grad_ref.at[b, rows_of], al_s.at[b, i]
        ).wait()

    def w_halves(i):
        first, count, kind = z_.chunks[i]
        half, base = count // 2, z_.first_zone[i]
        return (
            (pl.ds(first, half), pl.ds(base, half), blocks - 1 - z, to_left, to_right),
            (pl.ds(first + half, half), pl.ds(base + half, half), z, to_right, to_left),
        )

    def w_in(step):
        def go(b, i):
            for index, (here, zone, place, down, up) in enumerate(w_halves(i)):
                at = place == step
                into = sems(b, i, index) if step else None

                def add(here=here, zone=zone, into=into):
                    arrived(zr1.at[b, zone], *into, to_x)
                    add_into(b, gb, here.start, gb, here.start, zr1, zone.start, zone.size)

                if step:
                    when(at, add)
                if step < blocks - 1:
                    send(gb.at[b, here], zr1.at[b, zone], *sems(b, i, index), down, at)
                else:
                    half = pl.ds(z_.first_half[i], here.size)
                    send(gb.at[b, here], xrecv.at[b, half], *sems(b, i, 2), to_x, at)

        return go

    def w_out(step):
        def go(b, i):
            for index, (here, zone, place, down, up) in enumerate(w_halves(i)):
                at = place == blocks - 1 - step
                into = sems(b, i, 3 + index) if step else None

                def add(here=here, zone=zone):
                    half = pl.ds(z_.first_half[i], here.size)
                    arrived(xrecv.at[b, half], *sems(b, i, 2), to_x)
                    add_into(b, zr1, zone.start, gb, here.start, xrecv, half.start, half.size)

                if step:
                    arrived(zr1.at[b, zone], *into, to_x, at)
                else:
                    when(at, add)
                if step < blocks - 1:
                    src = zr1.at[b, zone]
                    send(src, src, *sems(b, i, 3 + index), up, at)

        return go

    def w7(b, i):
        w_out(3)(b, i)
        z_copy(b, i)

    stages = dict(
        x=(x0, x1, x2, x3, x4, x5),
        z=(z0, z1, z2, z3, z4, z5, z6),
        w=(w_in(0), w_in(1), w_in(2), w_in(3), w_out(0), w_out(1), w_out(2), w7, z6),
    )

    def ar(b, i, stage):
        stages[z_.chunks[i][2]][stage](b, i)

    smallc, smalls, smally = r["smallc"], r["smalls"], r["smally"]
    sm_s, sm_r = r["sm_s"], r["sm_r"]
    top = pl.ds(0, 8)

    def small_core(b):
        send(small.at[b, top], smallc.at[b], sm_s.at[b, 0], sm_r.at[b, 0], to_c)

    def small_y(b):
        arrived(smallc.at[b], sm_s.at[b, 0], sm_r.at[b, 0], to_c)
        smalls[b] = small[b, 0:8, :] + smallc[b]
        send(smalls.at[b], smally.at[b], sm_s.at[b, 1], sm_r.at[b, 1], to_y)

    def small_total(b):
        arrived(smally.at[b], sm_s.at[b, 1], sm_r.at[b, 1], to_y)
        first = z_.small0
        gb[b, first : first + 16, :] = jnp.concatenate(
            [smalls[b] + smally[b], small[b, 8:16, :]], axis=0
        ).astype(BF16)
        gb[b, first + 16 : first + SMALL, :] = jnp.zeros((SMALL - 16, width), BF16)

    small[...] = jnp.zeros(small.shape, F32)
    xa_start(0)
    settle()
    xa_start(1)
    settle()
    gather_vectors()
    loads["wqkv"].wait()
    settle()
    own_cast(0)
    settle()
    project_query(0)
    settle()
    project_own(0)
    settle()
    loads["wout"].wait()
    settle()
    xa_step(0, 1)
    settle()
    loads["win"].wait()
    loads["wback"].wait()
    for s in range(ns):
        loads["c", s].wait()
    settle()
    xa_step(1, 1)
    settle()
    xa_step(0, 2)
    settle()
    xa_forward(0, 1)
    settle()
    xa_step(1, 2)
    settle()
    xa_start(2)
    settle()
    own_cast(1)
    settle()
    project_query(1)
    settle()
    xa_step(0, 3)
    settle()
    xa_forward(1, 1)
    settle()
    project_own(1)
    settle()
    xa_forward(0, 2)
    settle()
    xa_step(1, 3)
    settle()
    xa_forward(1, 2)
    settle()
    xa_forward(0, 3)
    settle()
    xa_forward(1, 3)
    settle()
    xa_step(2, 1)
    settle()
    xa_done(0, 1)
    xa_done(0, 2)
    xa_done(0, 3)
    xa_done(1, 1)
    xa_done(1, 2)
    xa_done(1, 3)
    settle()
    project_rest(0)
    settle()
    attention(0, 0)
    settle()
    attention(0, 1)
    settle()
    attention(0, 2)
    settle()
    attention_out(0)
    settle()
    rs_core(0, 1)
    settle()
    rs_core(0, 0)
    settle()
    xa_step(2, 2)
    settle()
    rs_y(0, 1)
    settle()
    rs_y(0, 0)
    settle()
    xa_forward(2, 1)
    settle()
    xa_step(2, 3)
    settle()
    xa_start(3)
    settle()
    own_cast(2)
    settle()
    project_own(2)
    settle()
    project_query(2)
    settle()
    xa_forward(2, 2)
    settle()
    forward_rows(1)
    ag_start(0, 1, n1r)
    settle()
    forward_rows(0)
    ag_start(0, 0, n1r)
    settle()
    xa_step(3, 1)
    settle()
    ag_forward(0, 1, n1r)
    settle()
    xa_forward(2, 3)
    settle()
    ag_forward(0, 0, n1r)
    settle()
    ag_done(0, 1, n1r)
    settle()
    feed_forward(1)
    settle()
    rs_core(1, 1)
    settle()
    xa_done(2, 1)
    xa_done(2, 2)
    xa_done(2, 3)
    settle()
    ag_done(0, 0, n1r)
    settle()
    feed_forward(0)
    settle()
    rs_core(1, 0)
    settle()
    project_rest(1)
    settle()
    rs_y(1, 1)
    settle()
    rs_y(1, 0)
    settle()
    xa_step(3, 2)
    settle()
    attention_heads(1)
    settle()
    middle_rows(1)
    ag_start(1, 1, dzr)
    settle()
    middle_rows(0)
    ag_start(1, 0, dzr)
    settle()
    xa_step(3, 3)
    settle()
    attention_out(1)
    settle()
    xa_forward(3, 1)
    settle()
    rs_core(0, 2)
    settle()
    xa_forward(3, 2)
    settle()
    ag_forward(1, 1, dzr)
    settle()
    rs_y(0, 2)
    settle()
    ag_forward(1, 0, dzr)
    settle()
    ag_done(1, 1, dzr)
    settle()
    ag_done(1, 0, dzr)
    settle()
    weight_grad(0, z_.back0, 0, 256, act, dzr)
    settle()
    ar(0, 0, 0)
    settle()
    ar(0, 1, 0)
    settle()
    weight_grad(0, z_.back0, 256, 256, act, dzr)
    settle()
    ar(0, 2, 0)
    settle()
    ar(0, 3, 0)
    settle()
    weight_grad(0, z_.back0, 512, 256, act, dzr)
    settle()
    ar(0, 4, 0)
    settle()
    ar(0, 5, 0)
    settle()
    backward_hidden(0)
    settle()
    weight_grad(0, z_.in0, 0, 256, n1r, slope)
    settle()
    ar(0, 6, 0)
    settle()
    ar(0, 7, 0)
    settle()
    weight_grad(0, z_.in0, 256, 256, n1r, slope)
    settle()
    ar(0, 8, 0)
    settle()
    ar(0, 9, 0)
    settle()
    weight_grad(0, z_.in0, 512, 256, n1r, slope)
    settle()
    rs_core(2, 4)
    settle()
    xa_forward(3, 3)
    settle()
    forward_rows(2)
    ag_start(0, 2, n1r)
    settle()
    ar(0, 1, 1)
    settle()
    ar(0, 10, 0)
    settle()
    rs_y(2, 4)
    settle()
    xa_done(3, 1)
    xa_done(3, 2)
    xa_done(3, 3)
    settle()
    project_rest(2)
    settle()
    ar(0, 2, 1)
    settle()
    ar(0, 11, 0)
    settle()
    attention_heads(2)
    settle()
    backward_rows(4)
    ag_start(2, 4, dar)
    settle()
    small_core(0)
    settle()
    ag_forward(0, 2, n1r)
    settle()
    attention_out(2)
    settle()
    rs_core(0, 3)
    settle()
    ar(0, 0, 1)
    settle()
    ar(0, 3, 1)
    settle()
    small_y(0)
    settle()
    ag_done(0, 2, n1r)
    settle()
    feed_forward(2)
    settle()
    rs_core(1, 2)
    settle()
    rs_y(0, 3)
    settle()
    ag_forward(2, 4, dar)
    settle()
    ar(0, 4, 1)
    settle()
    ar(0, 5, 1)
    settle()
    ar(0, 6, 1)
    settle()
    ar(0, 0, 2)
    settle()
    rs_y(1, 2)
    settle()
    ag_done(2, 4, dar)
    settle()
    attention_back(0, 0)
    settle()
    ar(0, 1, 2)
    settle()
    out_grad(0)
    settle()
    ar(0, 12, 0)
    settle()
    attention_back(0, 1)
    settle()
    forward_rows(3)
    ag_start(0, 3, n1r)
    settle()
    ar(0, 6, 2)
    settle()
    ar(0, 2, 2)
    settle()
    attention_back(0, 2)
    settle()
    qkv_grad(0)
    settle()
    ar(0, 13, 0)
    settle()
    ar(0, 14, 0)
    settle()
    ar(0, 15, 0)
    settle()
    ar(0, 16, 0)
    settle()
    ar(0, 17, 0)
    settle()
    ar(0, 1, 3)
    settle()
    ar(0, 6, 3)
    settle()
    ar(0, 3, 2)
    settle()
    through_back(0)
    settle()
    ag_forward(0, 3, n1r)
    settle()
    ar(0, 0, 3)
    settle()
    ar(0, 2, 3)
    settle()
    ar(0, 4, 2)
    settle()
    ar(0, 1, 4)
    settle()
    dx_core(0)
    settle()
    middle_rows(2)
    ag_start(1, 2, dzr)
    settle()
    small_total(0)
    settle()
    ar(0, 18, 0)
    settle()
    ar(0, 7, 1)
    settle()
    ar(0, 5, 2)
    settle()
    ar(0, 3, 3)
    settle()
    ar(0, 8, 1)
    settle()
    ar(0, 9, 1)
    settle()
    ar(0, 10, 1)
    settle()
    ar(0, 11, 1)
    settle()
    ar(0, 12, 1)
    settle()
    dx_y(0)
    settle()
    ar(0, 0, 4)
    settle()
    ar(0, 2, 4)
    settle()
    ar(0, 13, 1)
    settle()
    ag_done(0, 3, n1r)
    settle()
    feed_forward(3)
    settle()
    ar(0, 4, 3)
    settle()
    ar(0, 3, 4)
    settle()
    rs_core(1, 3)
    settle()
    ag_forward(1, 2, dzr)
    settle()
    ar(0, 14, 1)
    settle()
    ar(0, 17, 1)
    settle()
    ar(0, 15, 1)
    settle()
    ar(0, 18, 1)
    settle()
    ar(0, 0, 5)
    settle()
    ar(0, 0, 6)
    settle()
    rs_y(1, 3)
    settle()
    ar(0, 5, 3)
    settle()
    ag_done(1, 2, dzr)
    settle()
    backward_hidden(1)
    settle()
    ar(0, 7, 2)
    settle()
    ar(0, 4, 4)
    settle()
    ar(0, 6, 4)
    settle()
    ar(0, 8, 2)
    settle()
    rs_core(2, 2)
    settle()
    ar(0, 16, 1)
    settle()
    ar(0, 9, 2)
    settle()
    ar(0, 17, 2)
    settle()
    ar(0, 1, 5)
    settle()
    ar(0, 5, 4)
    settle()
    rs_y(2, 2)
    settle()
    ar(0, 10, 2)
    settle()
    ar(0, 18, 2)
    settle()
    ar(0, 11, 2)
    settle()
    ar(0, 7, 3)
    settle()
    ar(0, 2, 5)
    settle()
    dx_arrived_y(0)
    settle()
    dx_relay(0, 3)
    settle()
    ar(0, 18, 3)
    settle()
    middle_rows(3)
    ag_start(1, 3, dzr)
    settle()
    ar(0, 3, 5)
    settle()
    ar(0, 9, 3)
    settle()
    ar(0, 12, 2)
    settle()
    ar(0, 7, 4)
    settle()
    ar(0, 4, 5)
    settle()
    backward_rows(2)
    ag_start(2, 2, dar)
    settle()
    ar(0, 10, 3)
    settle()
    ar(0, 13, 2)
    settle()
    ar(0, 8, 3)
    settle()
    ar(0, 14, 2)
    settle()
    ar(0, 5, 5)
    settle()
    ar(0, 9, 4)
    settle()
    ar(0, 11, 3)
    settle()
    ag_forward(1, 3, dzr)
    settle()
    ar(0, 17, 3)
    settle()
    ar(0, 15, 2)
    settle()
    ar(0, 18, 4)
    settle()
    ar(0, 10, 4)
    settle()
    ag_done(1, 3, dzr)
    settle()
    backward_hidden(2)
    settle()
    weight_grad(1, z_.in0, 0, 768, n1r, slope)
    settle()
    ar(0, 12, 3)
    settle()
    ar(0, 6, 5)
    settle()
    ar(1, 6, 0)
    settle()
    ar(1, 7, 0)
    settle()
    ar(1, 8, 0)
    settle()
    ar(1, 9, 0)
    settle()
    ar(0, 16, 2)
    settle()
    ar(0, 13, 3)
    settle()
    weight_grad(1, z_.back0, 0, 768, act, dzr)
    settle()
    ar(0, 11, 4)
    settle()
    ar(1, 0, 0)
    settle()
    ar(1, 1, 0)
    settle()
    dx_relay(0, 2)
    settle()
    ar(0, 8, 4)
    settle()
    ag_forward(2, 2, dar)
    settle()
    rs_core(2, 3)
    settle()
    ar(0, 7, 5)
    settle()
    ar(0, 9, 5)
    settle()
    ar(0, 10, 5)
    settle()
    ar(0, 14, 3)
    settle()
    ar(0, 18, 5)
    settle()
    ag_done(2, 2, dar)
    settle()
    attention_back_heads(1)
    settle()
    rs_y(2, 3)
    settle()
    ar(0, 15, 3)
    settle()
    ar(1, 6, 1)
    settle()
    ar(0, 12, 4)
    settle()
    ar(0, 17, 4)
    settle()
    through_back(1)
    settle()
    ar(0, 13, 4)
    settle()
    ar(1, 2, 0)
    settle()
    ar(1, 3, 0)
    settle()
    ar(0, 6, 6)
    settle()
    dx_core(1)
    settle()
    ar(1, 7, 1)
    settle()
    ar(0, 11, 5)
    settle()
    ar(0, 8, 5)
    settle()
    ar(0, 8, 6)
    settle()
    ar(0, 16, 3)
    settle()
    ar(1, 8, 1)
    settle()
    backward_rows(3)
    ag_start(2, 3, dar)
    settle()
    small_core(1)
    settle()
    ar(1, 9, 1)
    settle()
    ar(0, 14, 4)
    settle()
    publish(r["outq"], 0, r["out"], 0)
    settle()
    publish(r["outq"], 1, r["out"], 0)
    settle()
    dx_y(1)
    settle()
    ar(1, 4, 0)
    settle()
    small_y(1)
    settle()
    ar(0, 15, 4)
    settle()
    ar(1, 0, 1)
    settle()
    ar(0, 18, 6)
    settle()
    ar(1, 1, 1)
    settle()
    ar(1, 5, 0)
    settle()
    ag_forward(2, 3, dar)
    settle()
    ar(0, 12, 5)
    settle()
    ar(0, 17, 5)
    settle()
    ar(0, 17, 6)
    settle()
    dx_relay(0, 1)
    settle()
    ar(1, 6, 2)
    settle()
    ag_done(2, 3, dar)
    settle()
    attention_back_heads(2)
    settle()
    ar(1, 7, 2)
    settle()
    ar(1, 8, 2)
    settle()
    ar(1, 2, 1)
    settle()
    ar(1, 0, 2)
    settle()
    ar(1, 9, 2)
    settle()
    ar(0, 16, 4)
    settle()
    qkv_grad(1)
    settle()
    ar(1, 1, 2)
    settle()
    ar(1, 3, 1)
    settle()
    ar(0, 6, 7)
    settle()
    ar(0, 18, 7)
    settle()
    ar(1, 10, 0)
    settle()
    ar(1, 11, 0)
    settle()
    ar(1, 17, 0)
    settle()
    out_grad(1)
    settle()
    through_back(2)
    settle()
    dx_core(2)
    settle()
    dx_final(0)
    settle()
    ar(1, 7, 3)
    settle()
    ar(1, 4, 1)
    settle()
    ar(1, 6, 3)
    settle()
    publish(r["outq"], 2, r["out"], 0)
    settle()
    ar(0, 6, 8)
    settle()
    ar(0, 13, 5)
    settle()
    ar(1, 2, 2)
    settle()
    ar(1, 9, 3)
    settle()
    ar(0, 14, 5)
    settle()
    ar(0, 15, 5)
    settle()
    ar(0, 18, 8)
    settle()
    dx_y(2)
    settle()
    ar(1, 3, 2)
    settle()
    ar(1, 1, 3)
    settle()
    ar(1, 5, 1)
    settle()
    ar(1, 8, 3)
    settle()
    ar(1, 2, 3)
    settle()
    ar(1, 17, 1)
    settle()
    ar(1, 0, 3)
    settle()
    ar(1, 3, 3)
    settle()
    ar(0, 16, 5)
    settle()
    ar(1, 7, 4)
    settle()
    ar(1, 4, 2)
    settle()
    ar(1, 8, 4)
    settle()
    ar(1, 12, 0)
    settle()
    ar(1, 5, 2)
    settle()
    ar(1, 17, 2)
    settle()
    ar(1, 10, 1)
    settle()
    small_total(1)
    settle()
    ar(1, 18, 0)
    settle()
    ar(1, 9, 4)
    settle()
    dx_arrived_y(1)
    settle()
    dx_relay(1, 3)
    settle()
    ar(1, 10, 2)
    settle()
    ar(1, 0, 4)
    settle()
    ar(1, 11, 1)
    settle()
    ar(1, 1, 4)
    settle()
    ar(1, 13, 0)
    settle()
    ar(1, 18, 1)
    settle()
    ar(1, 4, 3)
    settle()
    ar(1, 6, 4)
    settle()
    dx_relay(1, 2)
    settle()
    ar(1, 5, 3)
    settle()
    ar(1, 11, 2)
    settle()
    ar(1, 10, 3)
    settle()
    ar(1, 2, 4)
    settle()
    ar(1, 7, 5)
    settle()
    ar(1, 6, 5)
    settle()
    ar(1, 18, 2)
    settle()
    ar(1, 14, 0)
    settle()
    dx_relay(1, 1)
    settle()
    ar(1, 15, 0)
    settle()
    ar(1, 12, 1)
    settle()
    ar(1, 16, 0)
    settle()
    ar(1, 11, 3)
    settle()
    ar(1, 17, 3)
    settle()
    ar(1, 3, 4)
    settle()
    ar(1, 6, 6)
    settle()
    ar(1, 9, 5)
    settle()
    ar(1, 12, 2)
    settle()
    ar(1, 17, 4)
    settle()
    ar(1, 12, 3)
    settle()
    ar(1, 13, 1)
    settle()
    ar(1, 13, 2)
    settle()
    ar(1, 0, 5)
    settle()
    ar(1, 0, 6)
    settle()
    ar(1, 1, 5)
    settle()
    ar(1, 8, 5)
    settle()
    ar(1, 8, 6)
    settle()
    dx_arrived_y(2)
    settle()
    dx_relay(2, 3)
    settle()
    ar(1, 4, 4)
    settle()
    dx_relay(2, 2)
    settle()
    ar(1, 2, 5)
    settle()
    ar(1, 14, 1)
    settle()
    ar(1, 14, 2)
    settle()
    ar(1, 5, 4)
    settle()
    ar(1, 15, 1)
    settle()
    ar(1, 15, 2)
    settle()
    ar(1, 13, 3)
    settle()
    ar(1, 10, 4)
    settle()
    ar(1, 16, 1)
    settle()
    ar(1, 16, 2)
    settle()
    ar(1, 18, 3)
    settle()
    ar(1, 3, 5)
    settle()
    dx_relay(2, 1)
    settle()
    ar(1, 14, 3)
    settle()
    dx_final(1)
    settle()
    ar(1, 4, 5)
    settle()
    ar(1, 15, 3)
    settle()
    ar(1, 11, 4)
    settle()
    ar(1, 16, 3)
    settle()
    ar(1, 5, 5)
    settle()
    ar(1, 6, 7)
    settle()
    ar(1, 6, 8)
    settle()
    ar(1, 10, 5)
    settle()
    ar(1, 18, 4)
    settle()
    ar(1, 18, 5)
    settle()
    ar(1, 12, 4)
    settle()
    ar(1, 11, 5)
    settle()
    ar(1, 17, 5)
    settle()
    ar(1, 17, 6)
    settle()
    ar(1, 13, 4)
    settle()
    dx_final(2)
    settle()
    ar(1, 14, 4)
    settle()
    ar(1, 12, 5)
    settle()
    ar(1, 15, 4)
    settle()
    ar(1, 13, 5)
    settle()
    ar(1, 16, 4)
    settle()
    ar(1, 14, 5)
    settle()
    ar(1, 18, 6)
    settle()
    ar(1, 18, 7)
    settle()
    ar(1, 15, 5)
    settle()
    ar(1, 16, 5)
    settle()
    ar(1, 18, 8)
    settle()
    for u in (4, 2, 3):
        rs_sent(2, u)
    for finish in sent[settled[0]:] + finals:
        finish()


def layer(sizes, *args):
    anywhere = pl.BlockSpec(memory_space=pl.ANY)
    call = pl.pallas_call(
        functools.partial(layer_kernel, sizes),
        out_shape=(
            jax.ShapeDtypeStruct((sizes.ns, sizes.rows, sizes.width), BF16),
            jax.ShapeDtypeStruct((sizes.ns, sizes.rows, sizes.width), BF16),
            jax.ShapeDtypeStruct((2, sizes.total, sizes.width), BF16),
        ),
        in_specs=[anywhere] * 15,
        out_specs=[anywhere] * 3,
        scratch_shapes=list(sizes.scratch().values()),
        compiler_params=pltpu.CompilerParams(
            collective_id=0, has_side_effects=True, vmem_limit_bytes=VMEM_BYTES
        ),
    )
    return call(*args)


def widen_kernel(sizes, out, gin, grad, *refs):
    nt, share, hidden, width = sizes.nt, sizes.share, sizes.hidden, sizes.width
    (
        out_t, out_q, gin_t, gin_q, qkv, qv_bias, out_w, out_bias, in_w, in_bias, back_w,
        back_bias, gains, shifts, low, wide, tail, in_sem, out_sem, tail_sem,
    ) = refs
    t = lax.axis_index("tensor")
    pieces = []
    for src, first, second in ((out, out_t, out_q), (gin, gin_t, gin_q)):
        for s in range(sizes.ns):
            dst = first.at[s] if s < nt else second.at[s - nt]
            pieces.append((src.at[s], dst, sizes.rows))
    for b in range(2):
        for first, count, dst in (
            (sizes.back0, hidden, back_w.at[b]),
            (sizes.in0, width, in_w.at[b]),
            (sizes.out0, share, out_w.at[b]),
            (sizes.qkv0, share, qkv.at[b, 0]),
            (sizes.qkv0 + share, share, qkv.at[b, 1]),
            (sizes.qkv0 + 2 * share, share, qkv.at[b, 2]),
        ):
            size = min(count, WIDEN_ROWS)
            for start in range(0, count, size):
                src = grad.at[b, pl.ds(first + start, size)]
                pieces.append((src, dst.at[pl.ds(start, size)], size))
    tails = [
        pltpu.make_async_copy(
            grad.at[b, pl.ds(sizes.small0, 16)], tail.at[b], tail_sem.at[b]
        )
        for b in range(2)
    ]
    reads, writes, places = [], [], []
    place = 0
    for index, (src, dst, size) in enumerate(pieces):
        here = pl.ds(place, size)
        places.append((place, size))
        reads.append(pltpu.make_async_copy(src, low.at[here], in_sem.at[index]))
        writes.append(pltpu.make_async_copy(wide.at[here], dst, out_sem.at[index]))
        place += size
    for copy in reads + tails:
        copy.start()
    for (place, size), read, write in zip(places, reads, writes):
        read.wait()

        def body(step, carry, place=place):
            at = pl.ds(pl.multiple_of(place + step * 32, 32), 32)
            wide[at, :] = low[at, :].astype(F32)
            return carry

        lax.fori_loop(0, size // 32, body, 0)
        write.start()
    for copy in tails:
        copy.wait()
    rows = tail[...].astype(F32)

    def crop_rows(first, count):
        value = jnp.zeros((2, count, share), F32)
        for k in range(4):
            piece = rows[:, first : first + count, k * share : (k + 1) * share]
            value = jnp.where(t == k, piece, value)
        return value

    gains[...] = crop_rows(0, 2)
    shifts[...] = crop_rows(2, 2)
    out_bias[...] = crop_rows(4, 1)[:, 0]
    back_bias[...] = crop_rows(5, 1)[:, 0]
    in_bias[...] = rows[:, 8]
    qv_bias[...] = rows[:, 9:11, :share]
    for copy in writes:
        copy.wait()


WIDEN_ROWS = 256


def widen(sizes, out, gin, grad):
    nt, nq, rows, share, width, hidden = (
        sizes.nt, sizes.nq, sizes.rows, sizes.share, sizes.width, sizes.hidden,
    )
    anywhere = pl.BlockSpec(memory_space=pl.ANY)
    held = pl.BlockSpec(memory_space=pltpu.VMEM)
    shapes = (
        ((nt, rows, width), anywhere),
        ((nq, rows, width), anywhere),
        ((nt, rows, width), anywhere),
        ((nq, rows, width), anywhere),
        ((2, 3, share, width), anywhere),
        ((2, 2, share), held),
        ((2, share, width), anywhere),
        ((2, share), held),
        ((2, width, hidden), anywhere),
        ((2, hidden), held),
        ((2, hidden, width), anywhere),
        ((2, share), held),
        ((2, 2, share), held),
        ((2, 2, share), held),
    )
    total = 2 * sizes.ns * rows + 2 * (hidden + width + 4 * share)
    count = 2 * sizes.ns + 2 * (hidden // WIDEN_ROWS + width // WIDEN_ROWS + 4)
    return pl.pallas_call(
        functools.partial(widen_kernel, sizes),
        out_shape=tuple(jax.ShapeDtypeStruct(shape, F32) for shape, _ in shapes),
        in_specs=[anywhere] * 3,
        out_specs=tuple(spec for _, spec in shapes),
        scratch_shapes=[
            pltpu.VMEM((total, width), BF16),
            pltpu.VMEM((total, width), F32),
            pltpu.VMEM((2, 16, width), BF16),
            pltpu.SemaphoreType.DMA((count,)),
            pltpu.SemaphoreType.DMA((count,)),
            pltpu.SemaphoreType.DMA((2,)),
        ],
        compiler_params=pltpu.CompilerParams(vmem_limit_bytes=VMEM_BYTES),
    )(out, gin, grad)


VMEM_BYTES = 127 * 2**19


def fused(
    x_train,
    x_quiz,
    cot_train,
    cot_quiz,
    quiz_lengths,
    w_qkv,
    b_qv,
    w_out,
    b_out,
    w_in,
    b_in,
    w_back,
    b_back,
    norm_gains,
    norm_shifts,
):
    nt, rows, width = x_train.shape
    share, hidden = w_out.shape[0], w_in.shape[1]
    sizes = Sizes(
        nt, x_quiz.shape[0], rows, lax.axis_size("blk"), share, width, hidden
    )
    out, grad_in, grad = layer(
        sizes,
        x_train,
        x_quiz,
        cot_train,
        cot_quiz,
        quiz_lengths,
        jnp.swapaxes(w_qkv, 1, 2),
        w_out,
        w_in,
        w_back,
        b_out,
        b_in,
        b_back,
        norm_gains,
        norm_shifts,
        b_qv,
    )
    results = list(widen(sizes, out, grad_in, grad))
    results[4] = jnp.swapaxes(results[4], 2, 3)
    return tuple(results)


def fits(mesh):
    return dict(mesh.shape) == {"dp": 2, "tensor": 4, "blk": 4}


def solution(mesh):
    placed = (
        P("dp", "blk", None),
        P("dp", "blk", None),
        P("dp", "blk", None),
        P("dp", "blk", None),
        P("dp"),
        P(None, None, "tensor"),
        P(None, "tensor"),
        P("tensor", None),
        P(),
        P(None, "tensor"),
        P("tensor"),
        P("tensor", None),
        P(),
        P(),
        P(),
    )
    return jax.shard_map(
        fused if fits(mesh) else shards,
        mesh=mesh,
        in_specs=placed,
        out_specs=(
            P("dp", "blk", None),
            P("dp", "blk", None),
            P("dp", "blk", None),
            P("dp", "blk", None),
            P(None, None, None, "tensor"),
            P(None, None, "tensor"),
            P(None, "tensor", None),
            P(None, "tensor"),
            P(None, None, "tensor"),
            P(None, "tensor"),
            P(None, "tensor", None),
            P(None, "tensor"),
            P(None, None, "tensor"),
            P(None, None, "tensor"),
        ),
        check_vma=False,
    )
```

```python
import functools

import jax
import jax.numpy as jnp
from jax import lax
from jax.experimental import pallas as pl
from jax.experimental.pallas import tpu as pltpu
from jax.sharding import PartitionSpec as P

D = 768
HEAD_DIM = 64


EPSILON = 1e-12
ROOT_HALF = 0.7071067811865476
ROOT_TWO_PI = 2.5066282746310002
NEG_LARGE = -1e30


def layer_norm(hidden, gain, shift):
    center = hidden - jnp.mean(hidden, axis=-1, keepdims=True)
    inverse = lax.rsqrt(jnp.mean(center * center, axis=-1, keepdims=True) + EPSILON)
    normal = center * inverse
    return (normal * gain + shift, normal, inverse)


def norm_back(grad_out, normal, inverse, gain):
    scaled = grad_out * gain
    grad_in = inverse * (
        scaled
        - jnp.mean(scaled, axis=-1, keepdims=True)
        - normal * jnp.mean(scaled * normal, axis=-1, keepdims=True)
    )
    return (grad_in, jnp.sum(grad_out * normal, axis=0), jnp.sum(grad_out, axis=0))


def gelu_exact(values):
    return 0.5 * values * (1.0 + lax.erf(values * ROOT_HALF))


def gelu_slope(values):
    return (
        0.5 * (1.0 + lax.erf(values * ROOT_HALF))
        + values * jnp.exp(-0.5 * values * values) / ROOT_TWO_PI
    )


def across(left, right):
    return lax.dot_general(
        left, right, (((0,), (0,)), ((), ())), preferred_element_type=jnp.float32
    )


def against(left, right):
    return lax.dot_general(
        left, right, (((1,), (1,)), ((), ())), preferred_element_type=jnp.float32
    )


def rounded(values):
    return lax.optimization_barrier(values.astype(jnp.bfloat16)).astype(jnp.float32)


def crop(values, column, share):
    return lax.dynamic_slice_in_dim(values, column, share, axis=values.ndim - 1)


def pair_grads(query_heads, dout_heads, log_total, delta, key_heads, value_heads, visible):
    scale = query_heads.shape[-1] ** (-0.5)
    scores = (
        jnp.einsum("sqhe,skhe->shqk", query_heads, key_heads, preferred_element_type=jnp.float32)
        * scale
    )
    probs = jnp.where(visible[:, None, None, :], jnp.exp(scores - log_total[..., None]), 0.0)
    grad_value = jnp.einsum(
        "shqk,sqhe->skhe",
        probs.astype(jnp.bfloat16),
        dout_heads,
        preferred_element_type=jnp.float32,
    )
    grad_probs = jnp.einsum(
        "sqhe,skhe->shqk", dout_heads, value_heads, preferred_element_type=jnp.float32
    )
    grad_scores = (probs * (grad_probs - delta[..., None])).astype(jnp.bfloat16)
    grad_query = jnp.einsum(
        "shqk,skhe->sqhe", grad_scores, key_heads, preferred_element_type=jnp.float32
    )
    grad_key = jnp.einsum(
        "shqk,sqhe->skhe", grad_scores, query_heads, preferred_element_type=jnp.float32
    )
    return (grad_query, grad_key, grad_value)


def run(tokens, cotangent, lengths, first_row, weights):
    w_qkv, b_qv, w_out, b_out, w_in, b_in, w_back, b_back, norm_gains, norm_shifts = weights
    seq_count, row_count, width = tokens.shape
    seq_len = row_count * lax.axis_size("blk")
    span = min(512, seq_len)
    block_count = seq_len // span
    flat_tokens = tokens.reshape(seq_count * row_count, width)
    low_tokens = flat_tokens.astype(jnp.bfloat16)
    projected = jnp.einsum("nd,tde->tne", low_tokens, w_qkv, preferred_element_type=jnp.float32)
    qv_bias = b_qv.astype(jnp.float32)
    query = (projected[0] + qv_bias[0]).astype(jnp.bfloat16)
    key_rows = projected[1].astype(jnp.bfloat16)
    value_rows = (projected[2] + qv_bias[1]).astype(jnp.bfloat16)
    share = key_rows.shape[-1]
    heads = share // HEAD_DIM
    scale = HEAD_DIM ** (-0.5)
    head_shape = (seq_count, row_count, heads, HEAD_DIM)
    query_heads = query.reshape(head_shape)
    key_three = key_rows.reshape(seq_count, row_count, share)
    value_three = value_rows.reshape(seq_count, row_count, share)
    running_max = jnp.full((seq_count, heads, row_count), NEG_LARGE, jnp.float32)
    running_out = jnp.zeros(head_shape, jnp.float32)
    key_piece = lax.all_gather(key_three, "blk", axis=1, tiled=True)
    value_piece = lax.all_gather(value_three, "blk", axis=1, tiled=True)
    piece_rows = key_piece.shape[1]
    key_heads = key_piece.reshape(seq_count, piece_rows, heads, HEAD_DIM)
    value_heads = value_piece.reshape(seq_count, piece_rows, heads, HEAD_DIM)
    scores = (
        jnp.einsum("sqhe,skhe->shqk", query_heads, key_heads, preferred_element_type=jnp.float32)
        * scale
    )
    visible = (jnp.arange(piece_rows, dtype=jnp.int32)[None, :] < lengths[:, None])[
        :, None, None, :
    ]
    scores = jnp.where(visible, scores, NEG_LARGE)
    new_max = jnp.maximum(running_max, jnp.max(scores, axis=-1))
    factor = jnp.exp(running_max - new_max)
    raised = jnp.where(visible, jnp.exp(scores - new_max[..., None]), 0.0)
    new_sum = jnp.sum(raised, axis=-1)
    added = jnp.einsum(
        "shqk,skhe->sqhe",
        raised.astype(jnp.bfloat16),
        value_heads,
        preferred_element_type=jnp.float32,
    )
    new_out = running_out * jnp.swapaxes(factor, 1, 2)[..., None] + added
    mixed_heads = new_out / jnp.swapaxes(new_sum, 1, 2)[..., None]
    log_total = new_max + jnp.log(new_sum)
    mixed_low = mixed_heads.reshape(seq_count * row_count, share).astype(jnp.bfloat16)
    attention = lax.psum(
        jnp.dot(mixed_low, w_out, preferred_element_type=jnp.float32).astype(jnp.bfloat16), "tensor"
    ).astype(jnp.float32) + b_out.astype(jnp.float32)
    normed, unit_one, inverse_one = layer_norm(
        flat_tokens + attention, norm_gains[0], norm_shifts[0]
    )
    normed_low = normed.astype(jnp.bfloat16)
    before = jnp.dot(normed_low, w_in, preferred_element_type=jnp.float32) + b_in.astype(
        jnp.float32
    )
    active_low = gelu_exact(before).astype(jnp.bfloat16)
    branch = lax.psum(
        jnp.dot(active_low, w_back, preferred_element_type=jnp.float32).astype(jnp.bfloat16),
        "tensor",
    ).astype(jnp.float32) + b_back.astype(jnp.float32)
    final, unit_two, inverse_two = layer_norm(normed + branch, norm_gains[1], norm_shifts[1])
    positions = first_row + jnp.arange(row_count, dtype=jnp.int32)
    keep_rows = (
        (positions[None, :] < lengths[:, None])
        .reshape(seq_count * row_count, 1)
        .astype(jnp.float32)
    )
    outputs = (keep_rows * final).reshape(tokens.shape)
    grad_final = keep_rows * cotangent.reshape(seq_count * row_count, width)
    grad_mid, grad_gain_two, grad_shift_two = norm_back(
        grad_final, unit_two, inverse_two, norm_gains[1]
    )
    grad_branch = grad_mid.astype(jnp.bfloat16)
    grad_b_back = jnp.sum(grad_branch.astype(jnp.float32), axis=0)
    grad_w_back = across(active_low, grad_branch)
    grad_active = against(grad_branch, w_back).astype(jnp.bfloat16).astype(jnp.float32)
    grad_before = (grad_active * gelu_slope(before)).astype(jnp.bfloat16)
    grad_b_in = jnp.sum(grad_before.astype(jnp.float32), axis=0)
    grad_w_in = across(normed_low, grad_before)
    grad_normed = grad_mid + rounded(
        lax.psum(against(grad_before, w_in).astype(jnp.bfloat16), "tensor").astype(jnp.float32)
    )
    grad_hidden, grad_gain_one, grad_shift_one = norm_back(
        grad_normed, unit_one, inverse_one, norm_gains[0]
    )
    grad_attention = grad_hidden.astype(jnp.bfloat16)
    grad_b_out = jnp.sum(grad_attention.astype(jnp.float32), axis=0)
    grad_w_out = across(mixed_low, grad_attention)
    grad_mixed = against(grad_attention, w_out).astype(jnp.bfloat16)
    dout_heads = grad_mixed.reshape(head_shape)
    delta = jnp.swapaxes(jnp.sum(dout_heads.astype(jnp.float32) * mixed_heads, axis=-1), 1, 2)
    key_all, value_all = key_piece, value_piece
    key_blocks = jnp.moveaxis(key_all.reshape(seq_count, block_count, span, heads, HEAD_DIM), 1, 0)
    value_blocks = jnp.moveaxis(
        value_all.reshape(seq_count, block_count, span, heads, HEAD_DIM), 1, 0
    )
    visible_all = jnp.arange(seq_len, dtype=jnp.int32)[None, :] < lengths[:, None]
    visible_blocks = jnp.moveaxis(visible_all.reshape(seq_count, block_count, span), 1, 0)

    def sweep_keys(grad_query, item):
        key_block, value_block, visible_block = item
        part_query, part_key, part_value = pair_grads(
            query_heads, dout_heads, log_total, delta, key_block, value_block, visible_block
        )
        return (grad_query + part_query, (part_key, part_value))

    grad_query, (key_terms, value_terms) = lax.scan(
        sweep_keys, jnp.zeros(head_shape, jnp.float32), (key_blocks, value_blocks, visible_blocks)
    )
    key_terms = jnp.moveaxis(key_terms, 0, 1).reshape(seq_count, seq_len, share)
    value_terms = jnp.moveaxis(value_terms, 0, 1).reshape(seq_count, seq_len, share)
    key_sum, value_sum = (
        lax.psum_scatter(
            key_terms.astype(jnp.bfloat16), "blk", scatter_dimension=1, tiled=True
        ).astype(jnp.float32),
        lax.psum_scatter(
            value_terms.astype(jnp.bfloat16), "blk", scatter_dimension=1, tiled=True
        ).astype(jnp.float32),
    )
    grad_query_low = (grad_query * scale).reshape(seq_count * row_count, share).astype(jnp.bfloat16)
    grad_key_low = (key_sum * scale).reshape(seq_count * row_count, share).astype(jnp.bfloat16)
    grad_value_low = value_sum.reshape(seq_count * row_count, share).astype(jnp.bfloat16)
    grad_stack = jnp.stack([grad_query_low, grad_key_low, grad_value_low])
    grad_w_qkv = jnp.einsum(
        "nd,tne->tde", low_tokens, grad_stack, preferred_element_type=jnp.float32
    )
    grad_b_qv = jnp.stack(
        [
            jnp.sum(grad_query_low.astype(jnp.float32), axis=0),
            jnp.sum(grad_value_low.astype(jnp.float32), axis=0),
        ]
    )
    grad_through = lax.psum(
        jnp.einsum("tne,tde->nd", grad_stack, w_qkv, preferred_element_type=jnp.float32).astype(
            jnp.bfloat16
        ),
        "tensor",
    ).astype(jnp.float32)
    grad_tokens = (grad_hidden + rounded(grad_through)).reshape(tokens.shape)
    grad_gains = jnp.stack([grad_gain_one, grad_gain_two])
    grad_shifts = jnp.stack([grad_shift_one, grad_shift_two])
    grads = (
        grad_w_qkv,
        grad_b_qv,
        grad_w_out,
        grad_b_out,
        grad_w_in,
        grad_b_in,
        grad_w_back,
        grad_b_back,
        grad_gains,
        grad_shifts,
    )
    return (outputs, grad_tokens, grads)


def shards(
    x_train,
    x_quiz,
    cot_train,
    cot_quiz,
    quiz_lengths,
    w_qkv,
    b_qv,
    w_out,
    b_out,
    w_in,
    b_in,
    w_back,
    b_back,
    norm_gains,
    norm_shifts,
):
    row_count = x_train.shape[1]
    seq_len = row_count * lax.axis_size("blk")
    first_row = lax.axis_index("blk") * row_count
    share = D // lax.axis_size("tensor")
    column = lax.axis_index("tensor") * share
    weights = (w_qkv, b_qv, w_out, b_out, w_in, b_in, w_back, b_back, norm_gains, norm_shifts)
    full_lengths = jnp.full((x_train.shape[0],), seq_len, jnp.int32)
    out_train, grad_in_train, train_grads = run(
        x_train, cot_train, full_lengths, first_row, weights
    )
    out_quiz, grad_in_quiz, quiz_grads = run(x_quiz, cot_quiz, quiz_lengths, first_row, weights)
    def total(grads):
        pieces = (
            grads[0],
            grads[1],
            grads[2],
            crop(grads[3], column, share),
            grads[4],
            grads[5],
            grads[6],
            crop(grads[7], column, share),
            crop(grads[8], column, share),
            crop(grads[9], column, share),
        )
        low = tuple(piece.astype(jnp.bfloat16) for piece in pieces)
        return tuple(
            piece.astype(jnp.float32) for piece in lax.psum(low, ("dp", "blk"))
        )

    summed = [jnp.stack(pair) for pair in zip(total(train_grads), total(quiz_grads))]
    return (
        out_train,
        out_quiz,
        grad_in_train,
        grad_in_quiz,
        summed[0],
        summed[1],
        summed[2],
        summed[3],
        summed[4],
        summed[5],
        summed[6],
        summed[7],
        summed[8],
        summed[9],
    )


MESH_ID = pl.DeviceIdType.MESH
F32 = jnp.float32
BF16 = jnp.bfloat16
SMALL = 32
BACK_KINDS = "zxxxwx"
IN_KINDS = "xwzxwx"
OUT_KINDS = "x"
QKV_KINDS = "xxxxxx"
INV_ROOT_TWO_PI = 1.0 / ROOT_TWO_PI
SETTLE_AGE = 100
WEIGHT_TILE = 256


def nn(left, right):
    return jnp.dot(left, right, preferred_element_type=F32)


def tile_loop(count, tile, body):
    def step(index, carry):
        body(pl.multiple_of(index * tile, tile))
        return carry

    lax.fori_loop(0, count // tile, step, 0)


def tiles(count, tile, body):
    for start in range(0, count, tile):
        body(start)


def sum_rows(value):
    return jnp.sum(value, axis=0, keepdims=True)


def lanes(count):
    return (count // 128 + 1) * 128


class Sizes:
    def __init__(self, nt, nq, rows, blocks, share, width, hidden):
        self.nt, self.nq, self.rows, self.blocks = nt, nq, rows, blocks
        self.share, self.width, self.hidden = share, width, hidden
        self.ns = nt + nq
        self.quarter = rows // 4
        self.seq_len = rows * blocks
        self.heads = share // HEAD_DIM
        self.back0 = 0
        self.in0 = hidden
        self.out0 = hidden + width
        self.qkv0 = self.out0 + share
        self.small0 = self.qkv0 + 3 * share
        self.total = self.small0 + SMALL
        half = self.quarter // 2
        self.streams = tuple((s, part * half, half) for s in range(nt) for part in range(2))
        self.streams += tuple((s, 0, self.quarter) for s in range(nt, self.ns))
        self.streams += tuple((s, 0, self.quarter) for s in range(nt))
        self.chunks = self.plan()
        self.first_half, self.first_zone, half, zone = [], [], 0, 0
        for _, count, kind in self.chunks:
            self.first_half.append(half)
            self.first_zone.append(zone)
            half += count // 2
            zone += count // 2 if kind == "x" else count
        self.half_rows, self.zone_rows = half, zone

    def plan(self):
        pieces = []
        for first, count, kinds in (
            (self.back0, self.hidden, BACK_KINDS),
            (self.in0, self.width, IN_KINDS),
            (self.out0, self.share, OUT_KINDS),
            (self.qkv0, 3 * self.share, QKV_KINDS),
        ):
            size = count // len(kinds)
            for index, kind in enumerate(kinds):
                pieces.append((first + index * size, size, kind))
        first, count, kind = pieces[-1]
        pieces[-1] = (first, count + SMALL, kind)
        return tuple(pieces)

    def scratch(self):
        ns, rows, share, width = self.ns, self.rows, self.share, self.width
        q, blocks, seq = self.quarter, self.blocks, self.seq_len
        dma = pltpu.SemaphoreType.DMA
        nc, nu = len(self.chunks), len(self.streams)
        return dict(
            xown=pltpu.VMEM((ns, q, width), F32),
            cown=pltpu.VMEM((ns, q, width), F32),
            vec=pltpu.VMEM((16, width), F32),
            raw0=pltpu.VMEM((width,), BF16),
            raw1=pltpu.VMEM((self.hidden,), BF16),
            raw2=pltpu.VMEM((width,), BF16),
            raw_gains=pltpu.VMEM((2, width), F32),
            raw_shifts=pltpu.VMEM((2, width), F32),
            raw_qv=pltpu.VMEM((2, share), BF16),
            lengths=pltpu.SMEM((self.nq,), jnp.int32),
            xg=pltpu.VMEM((ns, seq, width), BF16),
            wqkv=pltpu.VMEM((3, share, width), BF16),
            wout=pltpu.VMEM((share, width), BF16),
            win=pltpu.VMEM((width, self.hidden), BF16),
            wback=pltpu.VMEM((self.hidden, width), BF16),
            qb=pltpu.VMEM((ns, rows, share), BF16),
            kb=pltpu.VMEM((ns, seq, share), BF16),
            vb=pltpu.VMEM((ns, seq, lanes(share)), BF16),
            probs=pltpu.VMEM((ns, self.heads, rows, seq), BF16),
            of=pltpu.VMEM((rows, lanes(share)), F32),
            invl=pltpu.VMEM((ns, rows, share), F32),
            orb=pltpu.VMEM((ns, rows, share), BF16),
            unit1=pltpu.VMEM((ns, q, width), F32),
            inv1=pltpu.VMEM((ns, q, 128), F32),
            n1r=pltpu.VMEM((ns, 4, q, width), BF16),
            dzr=pltpu.VMEM((ns, 4, q, width), BF16),
            dar=pltpu.VMEM((ns, 4, q, width), BF16),
            act=pltpu.VMEM((ns, 4, q, self.hidden), BF16),
            slope=pltpu.VMEM((ns, 4, q, self.hidden), BF16),
            work=pltpu.VMEM((rows, max(seq, width)), F32),
            dsb=pltpu.VMEM((rows, seq), BF16),
            dqb=pltpu.VMEM((ns, rows, share), BF16),
            dkvt=pltpu.VMEM((ns, 2, share, seq), BF16),
            tq=pltpu.VMEM((share, rows), BF16),
            tm=pltpu.VMEM((share, rows), BF16),
            gm=pltpu.VMEM((rows, share), BF16),
            delta=pltpu.VMEM((rows, 128), F32),
            part=pltpu.VMEM((ns, 2, 2, q, width), BF16),
            crecv=pltpu.VMEM((3, ns, 2, q, width), BF16),
            yrecv=pltpu.VMEM((3, ns, q, width), BF16),
            part4=pltpu.VMEM((ns, blocks, 2, 2, q, width), BF16),
            crecv4=pltpu.VMEM((ns, blocks, 2, q, width), BF16),
            yrecv4=pltpu.VMEM((ns, blocks, q, width), BF16),
            zrecv4=pltpu.VMEM((ns, 2, blocks - 1, q, width), BF16),
            outq=pltpu.VMEM((ns, q, width), BF16),
            ginq=pltpu.VMEM((ns, q, width), BF16),
            gb=pltpu.VMEM((2, self.total, width), BF16),
            xrecv=pltpu.VMEM((2, self.half_rows, width), BF16),
            zr1=pltpu.VMEM((2, self.zone_rows, width), BF16),
            zr2=pltpu.VMEM((2, self.half_rows, width), BF16),
            small=pltpu.VMEM((2, SMALL, width), F32),
            smallc=pltpu.VMEM((2, 8, width), F32),
            smalls=pltpu.VMEM((2, 8, width), F32),
            smally=pltpu.VMEM((2, 8, width), F32),
            load_sem=dma((2 * ns + 5,)),
            vec_sem=dma((7,)),
            xz_s=dma((nu - self.nt, 2, blocks - 1)),
            xz_r=dma((nu - self.nt, 2, blocks - 1)),
            xc_s=dma((nu - self.nt, 2, blocks - 1, 3)),
            xc_r=dma((nu - self.nt, 2, blocks - 1, 3)),
            ex_s=dma((3, nu - self.nt, 5)),
            ex_r=dma((3, nu - self.nt, 5)),
            d4_s=dma((ns, 2)),
            d4_r=dma((ns, 2)),
            z4_s=dma((ns, 2, blocks - 1)),
            z4_r=dma((ns, 2, blocks - 1)),
            og_s=dma((2, ns, 3)),
            og_r=dma((2, ns, 3)),
            ol_s=dma((2, ns)),
            ar_s=dma((2, nc, 5)),
            ar_r=dma((2, nc, 5)),
            al_s=dma((2, nc)),
            sm_s=dma((2, 2)),
            sm_r=dma((2, 2)),
        )


INPUTS = (
    "xt", "xq", "ct", "cq", "lens", "wqkv_in", "wout_in", "win_in", "wback_in",
    "b_out", "b_in", "b_back", "gains", "shifts", "b_qv",
)
OUTPUTS = ("out", "gin", "grad")


def layer_kernel(z_, *refs):
    names = INPUTS + OUTPUTS + tuple(z_.scratch())
    r = dict(zip(names, refs))
    nt, ns, rows, blocks = z_.nt, z_.ns, z_.rows, z_.blocks
    share, width, hidden, quarter = z_.share, z_.width, z_.hidden, z_.quarter
    seq_len, heads = z_.seq_len, z_.heads
    scale = HEAD_DIM ** (-0.5)
    batches = (tuple(range(nt)), tuple(range(nt, ns)))
    lens_ref = r["lengths"]
    xg, work, part, gb = r["xg"], r["work"], r["part"], r["gb"]

    x = lax.axis_index("dp")
    t = lax.axis_index("tensor")
    z = lax.axis_index("blk")
    y = t // 2
    c = t % 2
    to_x = (1 - x, t, z)
    to_c = (x, t + 1 - 2 * c, z)
    to_y = (x, (t + 2) % 4, z)
    to_d = (x, 3 - t, z)
    to_right = (x, t, jnp.minimum(z + 1, blocks - 1))
    to_left = (x, t, jnp.maximum(z - 1, 0))
    has_left = z > 0
    has_right = z < blocks - 1
    corner = jnp.logical_or(z == 0, z == blocks - 1)
    interior = jnp.logical_and(z > 0, z < blocks - 1)
    to_inner = (x, t, jnp.where(z == 0, 1, blocks - 2))
    to_mirror = (x, t, blocks - 1 - z)
    to_outer = (x, t, jnp.where(z == 1, 0, blocks - 1))
    finals, sent, ages = [], [], []

    def settle(count=3, age=SETTLE_AGE):
        ages.append(len(sent))
        ready = ages[-age] if len(ages) >= age else 0
        for _ in range(min(count, ready - settled[0])):
            sent[settled[0]]()
            settled[0] += 1

    settled = [0]

    def when(cond, fn):
        if cond is None:
            fn()
        else:
            pl.when(cond)(fn)

    def remote(src, dst, ssem, rsem, dev):
        return pltpu.make_async_remote_copy(
            src_ref=src,
            dst_ref=dst,
            send_sem=ssem,
            recv_sem=rsem,
            device_id=dev,
            device_id_type=MESH_ID,
        )

    def send(src, dst, ssem, rsem, dev, cond=None, final=True):
        when(cond, lambda: remote(src, dst, ssem, rsem, dev).start())
        if final:
            sent.append(
                lambda: when(cond, lambda: remote(src, dst, ssem, rsem, dev).wait_send())
            )

    def arrived(dst, ssem, rsem, dev, cond=None):
        when(cond, lambda: remote(dst, dst, ssem, rsem, dev).wait_recv())

    def local(src, dst, sem):
        copy = pltpu.make_async_copy(src, dst, sem)
        copy.start()
        return copy

    mine = pl.ds(pl.multiple_of(t * quarter, quarter), quarter)
    facing = (t + 2) % 4

    def stream(u):
        s, first, count = z_.streams[u]
        return s, pl.ds(first, count)

    def flat(ref, s, lanes_=slice(None)):
        value = ref[s, :, :, lanes_]
        return value.reshape(rows, value.shape[-1])
    own_block = pl.ds(pl.multiple_of(z * rows, rows), rows)

    vec_ref = r["vec"]

    def vec(row, size=None):
        return vec_ref[row : row + 1, : (size or width)]

    vector_loads = (
        (r["b_out"], r["raw0"]),
        (r["b_in"], r["raw1"]),
        (r["b_back"], r["raw2"]),
        (r["gains"], r["raw_gains"]),
        (r["shifts"], r["raw_shifts"]),
        (r["b_qv"], r["raw_qv"]),
        (r["lens"], r["lengths"]),
    )

    def load_vectors():
        return [
            local(src, dst, r["vec_sem"].at[index])
            for index, (src, dst) in enumerate(vector_loads)
        ]

    def gather_vectors():
        for copy in loads["vectors"]:
            copy.wait()
        for row, name in enumerate(("raw0", "raw1", "raw2")):
            vec_ref[row : row + 1, :] = r[name][...].astype(F32).reshape(1, width)
        vec_ref[3:5, :] = r["raw_gains"][...]
        vec_ref[5:7, :] = r["raw_shifts"][...]
        vec_ref[7:9, :share] = r["raw_qv"][...].astype(F32)

    loads = {}
    load_sem = r["load_sem"]
    x_src = [r["xt"].at[s] for s in range(nt)] + [r["xq"].at[s] for s in range(ns - nt)]
    c_src = [r["ct"].at[s] for s in range(nt)] + [r["cq"].at[s] for s in range(ns - nt)]
    for s in range(ns):
        loads["x", s] = local(x_src[s].at[mine], r["xown"].at[s], load_sem.at[s])
    loads["vectors"] = load_vectors()
    for index, name in enumerate(("wqkv", "wout", "win", "wback")):
        loads[name] = local(r[name + "_in"], r[name], load_sem.at[ns + index])
    for s in range(ns):
        loads["c", s] = local(c_src[s].at[mine], r["cown"].at[s], load_sem.at[ns + 4 + s])

    barrier = pltpu.get_barrier_semaphore()

    def greet(dev, cond=None):
        when(
            cond,
            lambda: pl.semaphore_signal(
                barrier, inc=1, device_id=dev, device_id_type=MESH_ID
            ),
        )

    for dev in (to_x, to_c, to_y, to_d):
        greet(dev)
    greet(to_left, has_left)
    greet(to_right, has_right)
    when(corner, lambda: pl.semaphore_wait(barrier, 5))
    when(interior, lambda: pl.semaphore_wait(barrier, 6))

    def block_rows(j, q, within=pl.ds(0, quarter)):
        start = j * rows + q * quarter + within.start
        return pl.ds(pl.multiple_of(start, within.size), within.size)

    def side_valid(side, d):
        return z >= d if side == 0 else z <= blocks - 1 - d

    def side_block(side, d):
        return jnp.maximum(z - d, 0) if side == 0 else jnp.minimum(z + d, blocks - 1)

    xz_s, xz_r, xc_s, xc_r = r["xz_s"], r["xz_r"], r["xc_s"], r["xc_r"]

    def xa_start(u):
        s, within = stream(u)
        if within.start == 0:
            loads["x", s].wait()
        place = block_rows(z, t, within)
        xg[s, place, :] = r["xown"][s, within, :].astype(BF16)
        here = xg.at[s, place]
        send(here, here, xz_s.at[u, 0, 0], xz_r.at[u, 0, 0], to_right, has_right)
        send(here, here, xz_s.at[u, 1, 0], xz_r.at[u, 1, 0], to_left, has_left)

    def xa_step(u, d):
        s, within = stream(u)
        for side in range(2):
            valid = side_valid(side, d)
            here = xg.at[s, block_rows(side_block(side, d), t, within)]
            arrived(here, xz_s.at[u, side, d - 1], xz_r.at[u, side, d - 1], to_c, valid)
            if d < blocks - 1:
                more = has_right if side == 0 else has_left
                send(
                    here,
                    here,
                    xz_s.at[u, side, d],
                    xz_r.at[u, side, d],
                    to_right if side == 0 else to_left,
                    jnp.logical_and(valid, more),
                )
            for kind, dev in ((0, to_y), (1, to_c)):
                pair = xc_s.at[u, side, d - 1, kind], xc_r.at[u, side, d - 1, kind]
                send(here, here, *pair, dev, valid)

    def xa_forward(u, d):
        s, within = stream(u)
        for side in range(2):
            valid = side_valid(side, d)
            here = xg.at[s, block_rows(side_block(side, d), facing, within)]
            pair = xc_s.at[u, side, d - 1, 0], xc_r.at[u, side, d - 1, 0]
            arrived(here, *pair, to_c, valid)
            pair = xc_s.at[u, side, d - 1, 2], xc_r.at[u, side, d - 1, 2]
            send(here, here, *pair, to_c, valid)

    def xa_done(u, d):
        s, within = stream(u)
        for side in range(2):
            for kind in (1, 2):
                here = xg.at[s, block_rows(side_block(side, d), t, within)]
                pair = xc_s.at[u, side, d - 1, kind], xc_r.at[u, side, d - 1, kind]
                arrived(here, *pair, to_c, side_valid(side, d))

    def own_cast(s):
        copy = local(x_src[s], work.at[:, pl.ds(0, width)], load_sem.at[2 * ns + 4])
        copy.wait()
        for q in range(4):

            def cast(q=q):
                xg[s, block_rows(z, q), :] = work[
                    q * quarter : (q + 1) * quarter, :width
                ].astype(BF16)

            when(t != q, cast)

    padded = lanes(share)
    padded_head = lax.broadcasted_iota(jnp.int32, (1, padded), 1) // HEAD_DIM
    head_of_lane = lax.broadcasted_iota(jnp.int32, (1, share), 1) // HEAD_DIM
    invl = r["invl"]
    crecv, yrecv = r["crecv"], r["yrecv"]
    first_whole = len(z_.streams) - nt

    class Pairs:
        def __init__(self, ref):
            self.at = self
            self.ref = ref

        def __getitem__(self, key):
            k, u, index = key
            return self.ref.at[k, 2 * (u - first_whole) if u >= first_whole else u, index]

    ex_s, ex_r = Pairs(r["ex_s"]), Pairs(r["ex_r"])

    def rs_sends(k, u):
        s, within = stream(u)
        return (
            (
                part.at[s, :, 1 - c, within],
                crecv.at[k, s, :, within],
                ex_s.at[k, u, 0],
                ex_r.at[k, u, 0],
                to_c,
            ),
            (
                part.at[s, 1 - y, c, within],
                yrecv.at[k, s, within],
                ex_s.at[k, u, 1],
                ex_r.at[k, u, 1],
                to_y,
            ),
        )

    def rs_core(k, u):
        send(*rs_sends(k, u)[0], final=False)

    def rs_y(k, u):
        s, within = stream(u)
        arrived(*rs_sends(k, u)[0][1:])
        part[s, 1 - y, c, within] = (
            part[s, 1 - y, c, within].astype(F32) + crecv[k, s, 1 - y, within].astype(F32)
        ).astype(BF16)
        send(*rs_sends(k, u)[1], final=False)

    def rs_total(k, u):
        s, within = stream(u)
        arrived(*rs_sends(k, u)[1][1:])
        return (
            part[s, y, c, within].astype(F32)
            + crecv[k, s, y, within].astype(F32)
            + yrecv[k, s, within].astype(F32)
        )

    def rs_sent(k, u):
        for args in rs_sends(k, u):
            remote(*args).wait_send()

    def ag_start(k, u, full):
        s, within = stream(u)
        here = full.at[s, t, within]
        send(here, here, ex_s.at[k, u, 3], ex_r.at[k, u, 3], to_y)
        send(here, here, ex_s.at[k, u, 2], ex_r.at[k, u, 2], to_c)

    def ag_forward(k, u, full):
        s, within = stream(u)
        here = full.at[s, facing, within]
        arrived(here, ex_s.at[k, u, 3], ex_r.at[k, u, 3], to_y)
        send(here, here, ex_s.at[k, u, 4], ex_r.at[k, u, 4], to_c)

    def ag_done(k, u, full):
        s, within = stream(u)
        here = full.at[s, t, within]
        arrived(here, ex_s.at[k, u, 2], ex_r.at[k, u, 2], to_c)
        arrived(here, ex_s.at[k, u, 4], ex_r.at[k, u, 4], to_c)

    def publish(buf, s, target, kind):
        here = target.at[s, mine]
        og_s, og_r = r["og_s"], r["og_r"]
        devices = tuple(enumerate((to_c, to_y, to_d)))
        for index, dev in devices:
            sems = og_s.at[kind, s, index], og_r.at[kind, s, index]
            send(buf.at[s], here, *sems, dev)
        copy = local(buf.at[s], here, r["ol_s"].at[kind, s])
        finals.append(copy.wait)

        def landed():
            for index, dev in devices:
                arrived(here, og_s.at[kind, s, index], og_r.at[kind, s, index], dev)

        finals.append(landed)

    def batch_of(s):
        return 0 if s < nt else 1

    def length(s):
        return jnp.int32(seq_len) if s < nt else lens_ref[s - nt]

    def keep_rows(s, within):
        first = z * rows + t * quarter + within.start
        position = first + lax.broadcasted_iota(jnp.int32, (within.size, 1), 0)
        return jnp.where(position < length(s), 1.0, 0.0)

    qb, kb, vb, probs, of, orb = (r[n] for n in ("qb", "kb", "vb", "probs", "of", "orb"))
    wqkv, wout, win, wback = (r[n] for n in ("wqkv", "wout", "win", "wback"))
    unit1, inv1 = r["unit1"], r["inv1"]
    dh = r["xown"]
    n1r, dzr, dar, act, slope = (r[n] for n in ("n1r", "dzr", "dar", "act", "slope"))
    dsb, dqb, dkvt = (r[n] for n in ("dsb", "dqb", "dkvt"))
    small = r["small"]
    tq, tm, gm, delta = (r[n] for n in ("tq", "tm", "gm", "delta"))

    def add_small(s, row, value, size=None):
        place = (batch_of(s), slice(row, row + 1), slice(0, size or width))
        small[place] += value

    def project_query(s):
        low = (against(xg[s, own_block, :], wqkv[0]) + vec(7, share)).astype(BF16)
        qb[s] = low * jnp.array(scale, BF16)

    def project_block(s, start):
        lane = lax.broadcasted_iota(jnp.int32, (rows, padded - share), 1)
        place = pl.ds(start, rows)
        block = xg[s, place, :]
        kb[s, place, :] = against(block, wqkv[1]).astype(BF16)
        vb[s, place, :share] = (against(block, wqkv[2]) + vec(8, share)).astype(BF16)
        vb[s, place, share:] = jnp.where(lane == 0, 1.0, 0.0).astype(BF16)

    def project_own(s):
        project_block(s, pl.multiple_of(z * rows, rows))

    def project_rest(s):
        def body(j):
            project_block(s, pl.multiple_of(((z + 1 + j) % blocks) * rows, rows))

        repeat = rounds if s < nt else loop
        repeat(blocks - 1, body)

    def store_part(s, cols, value, within=pl.ds(0, quarter)):
        low = value.astype(BF16).reshape(2, 2, within.size, value.shape[-1])
        part[s, :, :, within, cols] = low

    key_tiles = tuple(slice(first, first + 256) for first in range(0, seq_len, 256))

    def folded_max(value, running):
        for first in range(0, value.shape[-1], 128):
            piece = value[:, first : first + 128]
            running = piece if running is None else jnp.maximum(running, piece)
        return running

    def rounds(count, body):
        for index in range(count):
            body(index)

    def loop(count, body):
        def step(index, carry):
            body(index)
            return carry

        lax.fori_loop(0, count, step, 0)

    def attention_heads(s):
        attention_start(s)
        loop(heads, lambda h: attention_head(s, h))

    def attention_start(s):
        of[...] = jnp.zeros((rows, padded), F32)
        invl[s] = jnp.zeros((rows, share), F32)

    def attention(s, h):
        if h == 0:
            attention_start(s)
        attention_head(s, h)

    def attention_head(s, h):
        mask = head_of_lane == h
        query = jnp.where(mask, qb[s], jnp.zeros((), BF16))
        highest = None
        for tile in key_tiles:
            scores = against(query, kb[s, tile, :])
            if s >= nt:
                position = tile.start + lax.broadcasted_iota(jnp.int32, (1, 256), 1)
                scores += jnp.where(position < length(s), 0.0, NEG_LARGE)
            work[:, tile] = scores
            highest = folded_max(scores, highest)
        delta[...] = jnp.broadcast_to(
            jnp.max(highest, axis=-1, keepdims=True), (rows, 128)
        )

        top = delta[...]
        mixed = None
        for tile in key_tiles:
            for first in range(tile.start, tile.stop, 128):
                piece = slice(first, first + 128)
                probs[s, h, :, piece] = jnp.exp(work[:, piece] - top).astype(BF16)
            term = nn(probs[s, h, :, tile], vb[s, tile, :])
            mixed = term if mixed is None else mixed + term
        inverse = 1.0 / mixed[:, share : share + 1]
        of[...] = jnp.where(padded_head == h, mixed * inverse, of[...])
        invl[s] = jnp.where(mask, inverse, invl[s])

    def attention_out(s):
        orb[s] = of[:, :share].astype(BF16)

        def body(start):
            cols = pl.ds(start, 256)
            store_part(s, cols, nn(orb[s], wout[:, cols]))

        tiles(width, 256, body)

    def forward_rows(u):
        s, within = stream(u)
        summed = r["xown"][s, within] + (rs_total(0, u) + vec(0))
        center = summed - jnp.mean(summed, axis=-1, keepdims=True)
        inverse = lax.rsqrt(jnp.mean(center * center, axis=-1, keepdims=True) + EPSILON)
        normal = center * inverse
        unit1[s, within] = normal
        inv1[s, within] = jnp.broadcast_to(inverse, (within.size, 128))
        n1r[s, t, within] = (normal * vec(3) + vec(5)).astype(BF16)

    def feed_forward(u):
        s, within = stream(u)
        count = 4 * within.size

        def up(start):
            cols = pl.ds(start, 256)
            left = n1r[s, :, within, :].reshape(count, width)
            before = nn(left, win[:, cols]) + vec_ref[1:2, cols]
            phi = 0.5 * (1.0 + lax.erf(before * ROOT_HALF))
            low = (before * phi).astype(BF16)
            act[s, :, within, cols] = low.reshape(4, within.size, 256)
            bell = jnp.exp(-0.5 * before * before) * INV_ROOT_TWO_PI
            low = (phi + before * bell).astype(BF16)
            slope[s, :, within, cols] = low.reshape(4, within.size, 256)

        (tiles if s < nt else tile_loop)(hidden, 256, up)
        rs_sent(0, u)

        def down(start):
            cols = pl.ds(start, 256)
            left = act[s, :, within, :].reshape(count, hidden)
            store_part(s, cols, nn(left, wback[:, cols]), within)

        (tiles if s < nt else tile_loop)(width, 256, down)

    def norm_back_rows(grad_out, normal, inverse, gain):
        scaled = grad_out * gain
        return inverse * (
            scaled
            - jnp.mean(scaled, axis=-1, keepdims=True)
            - normal * jnp.mean(scaled * normal, axis=-1, keepdims=True)
        )

    def middle_rows(u):
        s, within = stream(u)
        normed = unit1[s, within] * vec(3) + vec(5)
        summed = normed + (rs_total(1, u) + vec(2))
        center = summed - jnp.mean(summed, axis=-1, keepdims=True)
        inverse = lax.rsqrt(jnp.mean(center * center, axis=-1, keepdims=True) + EPSILON)
        normal = center * inverse
        keep = keep_rows(s, within)
        r["outq"][s, within] = (keep * (normal * vec(4) + vec(6))).astype(BF16)
        grad_out = keep * r["cown"][s, within]
        grad = norm_back_rows(grad_out, normal, inverse, vec(4))
        dh[s, within] = grad
        low = grad.astype(BF16)
        dzr[s, t, within] = low
        add_small(s, 1, sum_rows(grad_out * normal))
        add_small(s, 3, sum_rows(grad_out))
        add_small(s, 5, sum_rows(low.astype(F32)))

    def backward_hidden(s):
        b = batch_of(s)

        def up(start):
            cols = pl.ds(start, 256)
            grad = against(flat(dzr, s), wback[cols, :]).astype(BF16).astype(F32)
            low = (grad * flat(slope, s, cols).astype(F32)).astype(BF16)
            slope[s, :, :, cols] = low.reshape(4, quarter, 256)
            small[b, 8:9, cols] += sum_rows(low.astype(F32))

        tiles(hidden, 256, up)
        for u, (sequence, first, count) in enumerate(z_.streams):
            if sequence == s and (s >= nt or count < quarter):
                rs_sent(1, u)

        def down(start):
            cols = pl.ds(start, 256)
            store_part(s, cols, against(flat(slope, s), win[cols, :]))

        tiles(width, 256, down)

    def weight_grad(b, base, first, count, left, right):
        def body(start):
            total = None
            for s in batches[b]:
                term = across(flat(left, s, pl.ds(first + start, WEIGHT_TILE)), flat(right, s))
                total = term if total is None else total + term
            place = pl.ds(pl.multiple_of(base + first + start, 64), WEIGHT_TILE)
            gb[b, place, :] = total.astype(BF16)

        if count > WEIGHT_TILE:
            tile_loop(count, WEIGHT_TILE, body)
        else:
            body(0)

    def backward_rows(u):
        s, within = stream(u)
        grad_out = dh[s] + rs_total(2, u).astype(BF16).astype(F32)
        normal = unit1[s]
        grad = norm_back_rows(grad_out, normal, inv1[s, :, 0:1], vec(3))
        dh[s] = grad
        low = grad.astype(BF16)
        dar[s, t] = low
        add_small(s, 0, sum_rows(grad_out * normal))
        add_small(s, 2, sum_rows(grad_out))
        add_small(s, 4, sum_rows(low.astype(F32)))

    def out_grad(b):
        total = None
        for s in batches[b]:
            term = across(orb[s], flat(dar, s))
            total = term if total is None else total + term
        gb[b, z_.out0 : z_.out0 + share, :] = total.astype(BF16)


    def mixed_back(s):
        grad_mixed = against(flat(dar, s), wout[...]).astype(BF16).astype(F32)
        grad_mixed = (grad_mixed * invl[s]).astype(BF16)
        gm[...] = grad_mixed
        tm[...] = grad_mixed.T
        tq[...] = qb[s].T
        of[:, :share] = grad_mixed.astype(F32) * orb[s].astype(F32)

    def attention_back_heads(s):
        mixed_back(s)
        dqb[s] = jnp.zeros((rows, share), BF16)
        loop(heads, lambda h: attention_back_head(s, h))

    def attention_back(s, h):
        if h == 0:
            mixed_back(s)
            dqb[s] = jnp.zeros((rows, share), BF16)
        attention_back_head(s, h)

    def attention_back_head(s, h):
        mask = head_of_lane == h
        summed = jnp.sum(jnp.where(mask, of[:, :share], 0.0), axis=-1, keepdims=True)
        grad_head = jnp.where(mask, gm[...], jnp.zeros((), BF16))
        for tile in key_tiles:
            grads = against(grad_head, vb[s, tile, :share]) - summed
            dsb[:, tile] = (probs[s, h, :, tile].astype(F32) * grads).astype(BF16)
        grad_query = (nn(dsb[...], kb[s]) * scale).astype(BF16)
        dqb[s] = jnp.where(mask, grad_query, dqb[s])
        place = pl.ds(pl.multiple_of(h * HEAD_DIM, HEAD_DIM), HEAD_DIM)
        dkvt[s, 0, place, :] = nn(tq[place, :], dsb[...]).astype(BF16)
        dkvt[s, 1, place, :] = nn(tm[place, :], probs[s, h]).astype(BF16)

    def through_back(s):
        add_small(s, 9, sum_rows(dqb[s].astype(F32)), share)
        ones = jnp.ones((8, seq_len), BF16)
        add_small(s, 10, against(ones, dkvt[s, 1])[0:1], share)

        work[:, :width] = nn(dqb[s], wqkv[0])
        def body(pair):
            for j in (2 * pair, 2 * pair + 1):
                place = pl.ds(pl.multiple_of(j * rows, rows), rows)
                terms = dkvt[s, :, :, place].reshape(2 * share, rows)
                total = across(terms, wqkv[1:3].reshape(2 * share, width))
                total += jnp.where(j == z, work[:, :width], 0.0)
                r["part4"][s, j] = total.astype(BF16).reshape(2, 2, quarter, width)

        loop(blocks // 2, body)

    def qkv_grad(b):
        query = other = None
        for s in batches[b]:
            term = across(dqb[s], xg[s, own_block, :])
            query = term if query is None else query + term
            term = nn(dkvt[s].reshape(2 * share, seq_len), xg[s])
            other = term if other is None else other + term
        first = z_.qkv0
        gb[b, first : first + share, :] = query.astype(BF16)
        gb[b, first + share : first + 3 * share, :] = other.astype(BF16)

    part4, crecv4, yrecv4, zrecv4 = (r[n] for n in ("part4", "crecv4", "yrecv4", "zrecv4"))
    d4_s, d4_r, z4_s, z4_r = (r[n] for n in ("d4_s", "d4_r", "z4_s", "z4_r"))

    def dx_core(s):
        send(part4.at[s, :, :, 1 - c], crecv4.at[s], d4_s.at[s, 0], d4_r.at[s, 0], to_c)

        def clear(side):
            zrecv4[s, side] = jnp.zeros(zrecv4.shape[2:], BF16)

        when(z == 0, lambda: clear(0))
        when(z == blocks - 1, lambda: clear(1))

    def dx_y(s):
        arrived(crecv4.at[s], d4_s.at[s, 0], d4_r.at[s, 0], to_c)

        def body(j, carry):
            part4[s, j, 1 - y, c] = (
                part4[s, j, 1 - y, c].astype(F32) + crecv4[s, j, 1 - y].astype(F32)
            ).astype(BF16)
            return carry

        lax.fori_loop(0, blocks, body, 0)
        send(part4.at[s, :, 1 - y, c], yrecv4.at[s], d4_s.at[s, 1], d4_r.at[s, 1], to_y)

    def dx_partial(s, j):
        return (
            part4[s, j, y, c].astype(F32)
            + crecv4[s, j, y].astype(F32)
            + yrecv4[s, j].astype(F32)
        )

    def dx_arrived_y(s):
        arrived(yrecv4.at[s], d4_s.at[s, 1], d4_r.at[s, 1], to_y)

    def dx_relay(s, d):
        for side in range(2):
            target = z + d if side == 0 else z - d
            valid = target <= blocks - 1 if side == 0 else target >= 0
            block = jnp.clip(target, 0, blocks - 1)
            has_source = has_left if side == 0 else has_right
            dev = to_right if side == 0 else to_left

            def go(side=side, block=block, has_source=has_source):
                if d < blocks - 1:
                    arrived(
                        zrecv4.at[s, side, d],
                        z4_s.at[s, side, d],
                        z4_r.at[s, side, d],
                        to_c,
                        has_source,
                    )
                    value = dx_partial(s, block) + zrecv4[s, side, d].astype(F32)
                else:
                    value = dx_partial(s, block)
                part4[s, block, y, c] = value.astype(BF16)

            when(valid, go)
            send(
                part4.at[s, block, y, c],
                zrecv4.at[s, side, d - 1],
                z4_s.at[s, side, d - 1],
                z4_r.at[s, side, d - 1],
                dev,
                valid,
            )

    def dx_final(s):
        for side, has_source in ((0, has_left), (1, has_right)):
            arrived(
                zrecv4.at[s, side, 0],
                z4_s.at[s, side, 0],
                z4_r.at[s, side, 0],
                to_c,
                has_source,
            )
        total = (
            dx_partial(s, z)
            + zrecv4[s, 0, 0].astype(F32)
            + zrecv4[s, 1, 0].astype(F32)
        )
        r["ginq"][s] = (dh[s] + total.astype(BF16).astype(F32)).astype(BF16)
        publish(r["ginq"], s, r["gin"], 1)

    xrecv, zr1, zr2, grad_ref = r["xrecv"], r["zr1"], r["zr2"], r["grad"]
    ar_s, ar_r, al_s = r["ar_s"], r["ar_r"], r["al_s"]

    def ar_places(i):
        first, count, kind = z_.chunks[i]
        half = count // 2
        index = x if kind == "x" else jnp.where(z == 1, 0, 1)
        own = pl.ds(pl.multiple_of(first + index * half, 16), half)
        other = pl.ds(pl.multiple_of(first + (1 - index) * half, 16), half)
        return own, other, pl.ds(z_.first_half[i], half), pl.ds(z_.first_zone[i], half)

    def zone_places(i):
        first, count, kind = z_.chunks[i]
        half, base = count // 2, z_.first_zone[i]
        index = jnp.where(z == 1, 0, 1)
        own = pl.ds(pl.multiple_of(base + index * half, 16), half)
        other = pl.ds(pl.multiple_of(base + (1 - index) * half, 16), half)
        return own, other, pl.ds(base, count), pl.ds(first, count)

    def add_into(b, dst, dst_first, left, left_first, right, right_first, count):
        tile = next(size for size in (64, 48, 32, 16) if count % size == 0)

        def body(start):
            at = lambda first: pl.ds(pl.multiple_of(first + start, 16), tile)
            dst[b, at(dst_first), :] = (
                left[b, at(left_first), :].astype(F32)
                + right[b, at(right_first), :].astype(F32)
            ).astype(BF16)

        tile_loop(count, tile, body)

    def sems(b, i, index):
        return ar_s.at[b, i, index], ar_r.at[b, i, index]

    def x0(b, i):
        own, other, half, zone = ar_places(i)
        send(gb.at[b, other], xrecv.at[b, half], *sems(b, i, 0), to_x)

    def x1(b, i):
        own, other, half, zone = ar_places(i)
        arrived(xrecv.at[b, half], *sems(b, i, 0), to_x)
        add_into(b, gb, own.start, gb, own.start, xrecv, half.start, half.size)
        send(gb.at[b, own], zr1.at[b, zone], *sems(b, i, 1), to_inner, corner)

    def x2(b, i):
        own, other, half, zone = ar_places(i)

        def add():
            arrived(zr1.at[b, zone], *sems(b, i, 1), to_x)
            add_into(b, gb, own.start, gb, own.start, zr1, zone.start, half.size)

        when(interior, add)
        send(gb.at[b, own], zr2.at[b, half], *sems(b, i, 2), to_mirror, interior)

    def x_share(b, i, cond):
        own, other, half, zone = ar_places(i)
        src, dst = zr1.at[b, zone], grad_ref.at[b, own]
        send(src, dst, *sems(b, i, 3), to_x, cond, final=False)
        when(cond, lambda: pltpu.make_async_copy(src, dst, al_s.at[b, i]).start())

    def x3(b, i):
        own, other, half, zone = ar_places(i)

        def add():
            arrived(zr2.at[b, half], *sems(b, i, 2), to_x)
            add_into(b, zr1, zone.start, gb, own.start, zr2, half.start, half.size)

        when(interior, add)
        send(zr1.at[b, zone], zr1.at[b, zone], *sems(b, i, 1), to_outer, interior)
        x_share(b, i, interior)

    def x4(b, i):
        own, other, half, zone = ar_places(i)
        arrived(zr1.at[b, zone], *sems(b, i, 1), to_x, corner)
        x_share(b, i, corner)

    def x5(b, i):
        own, other, half, zone = ar_places(i)
        src, dst = zr1.at[b, zone], grad_ref.at[b, own]
        remote(src, dst, *sems(b, i, 3), to_x).wait_send()
        pltpu.make_async_copy(src, dst, al_s.at[b, i]).wait()
        arrived(grad_ref.at[b, other], *sems(b, i, 3), to_x)

    def z0(b, i):
        whole, rows_of = zone_places(i)[2:]
        send(gb.at[b, rows_of], zr1.at[b, whole], *sems(b, i, 0), to_inner, corner)

    def z1(b, i):
        own, other, half, zone = ar_places(i)
        whole, rows_of = zone_places(i)[2:]

        def add():
            arrived(zr1.at[b, whole], *sems(b, i, 0), to_x)
            add_into(b, gb, rows_of.start, gb, rows_of.start, zr1, whole.start, whole.size)

        when(interior, add)
        send(gb.at[b, other], zr2.at[b, half], *sems(b, i, 1), to_mirror, interior)

    def z2(b, i):
        own, other, half, zone = ar_places(i)

        def add():
            arrived(zr2.at[b, half], *sems(b, i, 1), to_x)
            add_into(b, gb, own.start, gb, own.start, zr2, half.start, half.size)

        when(interior, add)
        send(gb.at[b, own], xrecv.at[b, half], *sems(b, i, 2), to_x, interior)

    def z3(b, i):
        own, other, half, zone = ar_places(i)
        zone_own = zone_places(i)[0]

        def add():
            arrived(xrecv.at[b, half], *sems(b, i, 2), to_x)
            add_into(b, zr1, zone_own.start, gb, own.start, xrecv, half.start, half.size)

        when(interior, add)
        here = zr1.at[b, zone_own]
        send(here, here, *sems(b, i, 3), to_mirror, interior)
        send(here, here, *sems(b, i, 0), to_outer, interior)

    def z4(b, i):
        there = zr1.at[b, zone_places(i)[1]]
        arrived(there, *sems(b, i, 3), to_x, interior)
        send(there, there, *sems(b, i, 4), to_outer, interior)

    def z5(b, i):
        there = zr1.at[b, zone_places(i)[1]]
        arrived(there, *sems(b, i, 0), to_x, corner)
        arrived(there, *sems(b, i, 4), to_x, corner)
        z_copy(b, i)

    def z_copy(b, i):
        whole, rows_of = zone_places(i)[2:]
        pltpu.make_async_copy(
            zr1.at[b, whole], grad_ref.at[b, rows_of], al_s.at[b, i]
        ).start()

    def z6(b, i):
        whole, rows_of = zone_places(i)[2:]
        pltpu.make_async_copy(
            zr1.at[b, whole], grad_ref.at[b, rows_of], al_s.at[b, i]
        ).wait()

    def w_halves(i):
        first, count, kind = z_.chunks[i]
        half, base = count // 2, z_.first_zone[i]
        return (
            (pl.ds(first, half), pl.ds(base, half), blocks - 1 - z, to_left, to_right),
            (pl.ds(first + half, half), pl.ds(base + half, half), z, to_right, to_left),
        )

    def w_in(step):
        def go(b, i):
            for index, (here, zone, place, down, up) in enumerate(w_halves(i)):
                at = place == step
                into = sems(b, i, index) if step else None

                def add(here=here, zone=zone, into=into):
                    arrived(zr1.at[b, zone], *into, to_x)
                    add_into(b, gb, here.start, gb, here.start, zr1, zone.start, zone.size)

                if step:
                    when(at, add)
                if step < blocks - 1:
                    send(gb.at[b, here], zr1.at[b, zone], *sems(b, i, index), down, at)
                else:
                    half = pl.ds(z_.first_half[i], here.size)
                    send(gb.at[b, here], xrecv.at[b, half], *sems(b, i, 2), to_x, at)

        return go

    def w_out(step):
        def go(b, i):
            for index, (here, zone, place, down, up) in enumerate(w_halves(i)):
                at = place == blocks - 1 - step
                into = sems(b, i, 3 + index) if step else None

                def add(here=here, zone=zone):
                    half = pl.ds(z_.first_half[i], here.size)
                    arrived(xrecv.at[b, half], *sems(b, i, 2), to_x)
                    add_into(b, zr1, zone.start, gb, here.start, xrecv, half.start, half.size)

                if step:
                    arrived(zr1.at[b, zone], *into, to_x, at)
                else:
                    when(at, add)
                if step < blocks - 1:
                    src = zr1.at[b, zone]
                    send(src, src, *sems(b, i, 3 + index), up, at)

        return go

    def w7(b, i):
        w_out(3)(b, i)
        z_copy(b, i)

    stages = dict(
        x=(x0, x1, x2, x3, x4, x5),
        z=(z0, z1, z2, z3, z4, z5, z6),
        w=(w_in(0), w_in(1), w_in(2), w_in(3), w_out(0), w_out(1), w_out(2), w7, z6),
    )

    def ar(b, i, stage):
        stages[z_.chunks[i][2]][stage](b, i)

    smallc, smalls, smally = r["smallc"], r["smalls"], r["smally"]
    sm_s, sm_r = r["sm_s"], r["sm_r"]
    top = pl.ds(0, 8)

    def small_core(b):
        send(small.at[b, top], smallc.at[b], sm_s.at[b, 0], sm_r.at[b, 0], to_c)

    def small_y(b):
        arrived(smallc.at[b], sm_s.at[b, 0], sm_r.at[b, 0], to_c)
        smalls[b] = small[b, 0:8, :] + smallc[b]
        send(smalls.at[b], smally.at[b], sm_s.at[b, 1], sm_r.at[b, 1], to_y)

    def small_total(b):
        arrived(smally.at[b], sm_s.at[b, 1], sm_r.at[b, 1], to_y)
        first = z_.small0
        gb[b, first : first + 16, :] = jnp.concatenate(
            [smalls[b] + smally[b], small[b, 8:16, :]], axis=0
        ).astype(BF16)
        gb[b, first + 16 : first + SMALL, :] = jnp.zeros((SMALL - 16, width), BF16)

    small[...] = jnp.zeros(small.shape, F32)
    xa_start(0)
    settle()
    xa_start(1)
    settle()
    gather_vectors()
    loads["wqkv"].wait()
    settle()
    own_cast(0)
    settle()
    project_query(0)
    settle()
    loads["wout"].wait()
    settle()
    project_own(0)
    settle()
    xa_step(0, 1)
    settle()
    loads["win"].wait()
    loads["wback"].wait()
    for s in range(ns):
        loads["c", s].wait()
    settle()
    xa_step(1, 1)
    settle()
    xa_step(0, 2)
    settle()
    xa_forward(0, 1)
    settle()
    xa_step(1, 2)
    settle()
    xa_start(2)
    settle()
    own_cast(1)
    settle()
    project_query(1)
    settle()
    xa_step(0, 3)
    settle()
    xa_forward(1, 1)
    settle()
    project_own(1)
    settle()
    xa_step(1, 3)
    settle()
    xa_forward(0, 2)
    settle()
    xa_forward(0, 3)
    settle()
    xa_forward(1, 2)
    settle()
    xa_forward(1, 3)
    settle()
    xa_step(2, 1)
    settle()
    xa_done(0, 1)
    xa_done(0, 2)
    xa_done(0, 3)
    xa_done(1, 1)
    xa_done(1, 2)
    xa_done(1, 3)
    settle()
    project_rest(0)
    settle()
    attention(0, 0)
    settle()
    attention(0, 1)
    settle()
    attention(0, 2)
    settle()
    attention_out(0)
    settle()
    rs_core(0, 0)
    settle()
    rs_core(0, 1)
    settle()
    xa_step(2, 2)
    settle()
    rs_y(0, 0)
    settle()
    rs_y(0, 1)
    settle()
    xa_forward(2, 1)
    settle()
    xa_step(2, 3)
    settle()
    xa_start(3)
    settle()
    own_cast(2)
    settle()
    project_query(2)
    settle()
    project_own(2)
    settle()
    xa_forward(2, 2)
    settle()
    forward_rows(0)
    ag_start(0, 0, n1r)
    settle()
    forward_rows(1)
    ag_start(0, 1, n1r)
    settle()
    ag_forward(0, 0, n1r)
    settle()
    xa_forward(2, 3)
    settle()
    xa_step(3, 1)
    settle()
    ag_forward(0, 1, n1r)
    settle()
    ag_done(0, 0, n1r)
    settle()
    feed_forward(0)
    settle()
    rs_core(1, 0)
    settle()
    xa_done(2, 1)
    xa_done(2, 2)
    xa_done(2, 3)
    settle()
    ag_done(0, 1, n1r)
    settle()
    feed_forward(1)
    settle()
    rs_core(1, 1)
    settle()
    rs_y(1, 0)
    settle()
    project_rest(1)
    settle()
    rs_y(1, 1)
    settle()
    xa_step(3, 2)
    settle()
    attention_heads(1)
    settle()
    middle_rows(0)
    ag_start(1, 0, dzr)
    settle()
    middle_rows(1)
    ag_start(1, 1, dzr)
    settle()
    attention_out(1)
    settle()
    rs_core(0, 2)
    settle()
    xa_forward(3, 1)
    settle()
    xa_step(3, 3)
    settle()
    rs_y(0, 2)
    settle()
    xa_forward(3, 2)
    settle()
    ag_forward(1, 0, dzr)
    settle()
    ag_forward(1, 1, dzr)
    settle()
    ag_done(1, 0, dzr)
    settle()
    ag_done(1, 1, dzr)
    settle()
    weight_grad(0, z_.back0, 0, 256, act, dzr)
    settle()
    ar(0, 0, 0)
    settle()
    ar(0, 1, 0)
    settle()
    weight_grad(0, z_.back0, 256, 256, act, dzr)
    settle()
    ar(0, 2, 0)
    settle()
    ar(0, 3, 0)
    settle()
    weight_grad(0, z_.back0, 512, 256, act, dzr)
    settle()
    ar(0, 4, 0)
    settle()
    ar(0, 5, 0)
    settle()
    backward_hidden(0)
    settle()
    weight_grad(0, z_.in0, 0, 256, n1r, slope)
    settle()
    ar(0, 6, 0)
    settle()
    ar(0, 7, 0)
    settle()
    weight_grad(0, z_.in0, 256, 256, n1r, slope)
    settle()
    ar(0, 8, 0)
    settle()
    ar(0, 9, 0)
    settle()
    weight_grad(0, z_.in0, 512, 256, n1r, slope)
    settle()
    ar(0, 10, 0)
    settle()
    ar(0, 11, 0)
    settle()
    xa_forward(3, 3)
    settle()
    ar(0, 1, 1)
    settle()
    rs_core(2, 4)
    settle()
    forward_rows(2)
    ag_start(0, 2, n1r)
    settle()
    xa_done(3, 1)
    xa_done(3, 2)
    xa_done(3, 3)
    settle()
    project_rest(2)
    settle()
    rs_y(2, 4)
    settle()
    attention_heads(2)
    settle()
    attention_out(2)
    settle()
    ag_forward(0, 2, n1r)
    settle()
    rs_core(0, 3)
    settle()
    ar(0, 0, 1)
    settle()
    ar(0, 2, 1)
    settle()
    backward_rows(4)
    ag_start(2, 4, dar)
    settle()
    ag_done(0, 2, n1r)
    settle()
    feed_forward(2)
    settle()
    rs_y(0, 3)
    settle()
    rs_core(1, 2)
    settle()
    ar(0, 3, 1)
    settle()
    ar(0, 4, 1)
    settle()
    ar(0, 5, 1)
    settle()
    ar(0, 0, 2)
    settle()
    ar(0, 6, 1)
    settle()
    ar(0, 7, 1)
    settle()
    ag_forward(2, 4, dar)
    settle()
    ar(0, 9, 1)
    settle()
    small_core(0)
    settle()
    rs_y(1, 2)
    settle()
    ag_done(2, 4, dar)
    settle()
    out_grad(0)
    settle()
    ar(0, 12, 0)
    settle()
    small_y(0)
    settle()
    attention_back(0, 0)
    settle()
    attention_back(0, 1)
    settle()
    attention_back(0, 2)
    settle()
    qkv_grad(0)
    settle()
    ar(0, 13, 0)
    settle()
    ar(0, 14, 0)
    settle()
    ar(0, 15, 0)
    settle()
    ar(0, 16, 0)
    settle()
    ar(0, 17, 0)
    settle()
    middle_rows(2)
    ag_start(1, 2, dzr)
    settle()
    ar(0, 0, 3)
    settle()
    ar(0, 1, 2)
    settle()
    ar(0, 4, 2)
    settle()
    ar(0, 7, 2)
    settle()
    forward_rows(3)
    ag_start(0, 3, n1r)
    settle()
    through_back(0)
    settle()
    dx_core(0)
    settle()
    small_total(0)
    settle()
    ar(0, 18, 0)
    settle()
    ar(0, 2, 2)
    settle()
    ar(0, 8, 1)
    settle()
    ar(0, 4, 3)
    settle()
    ar(0, 10, 1)
    settle()
    ar(0, 11, 1)
    settle()
    ar(0, 12, 1)
    settle()
    ar(0, 3, 2)
    settle()
    ar(0, 13, 1)
    settle()
    ar(0, 14, 1)
    settle()
    ag_forward(1, 2, dzr)
    settle()
    ar(0, 0, 4)
    settle()
    dx_y(0)
    settle()
    ar(0, 1, 3)
    settle()
    ar(0, 7, 3)
    settle()
    ar(0, 5, 2)
    settle()
    ag_forward(0, 3, n1r)
    settle()
    ar(0, 15, 1)
    settle()
    ag_done(1, 2, dzr)
    settle()
    backward_hidden(1)
    settle()
    ag_done(0, 3, n1r)
    settle()
    feed_forward(3)
    settle()
    rs_core(1, 3)
    settle()
    ar(0, 2, 3)
    settle()
    ar(0, 6, 2)
    settle()
    ar(0, 8, 2)
    settle()
    ar(0, 9, 2)
    settle()
    rs_core(2, 2)
    settle()
    ar(0, 16, 1)
    settle()
    ar(0, 17, 1)
    settle()
    rs_y(1, 3)
    settle()
    ar(0, 18, 1)
    settle()
    ar(0, 1, 4)
    settle()
    ar(0, 2, 4)
    settle()
    ar(0, 10, 2)
    settle()
    rs_y(2, 2)
    settle()
    ar(0, 11, 2)
    settle()
    ar(0, 4, 4)
    settle()
    ar(0, 0, 5)
    settle()
    ar(0, 0, 6)
    settle()
    ar(0, 10, 3)
    settle()
    ar(0, 3, 3)
    settle()
    ar(0, 7, 4)
    settle()
    dx_arrived_y(0)
    settle()
    dx_relay(0, 3)
    settle()
    ar(0, 5, 3)
    settle()
    ar(0, 12, 2)
    settle()
    ar(0, 3, 4)
    settle()
    ar(0, 1, 5)
    settle()
    ar(0, 8, 3)
    settle()
    ar(0, 13, 2)
    settle()
    middle_rows(3)
    ag_start(1, 3, dzr)
    settle()
    ar(0, 6, 3)
    settle()
    ar(0, 5, 4)
    settle()
    ar(0, 2, 5)
    settle()
    ar(0, 14, 2)
    settle()
    backward_rows(2)
    ag_start(2, 2, dar)
    settle()
    ar(0, 9, 3)
    settle()
    ar(0, 15, 2)
    settle()
    ar(0, 10, 4)
    settle()
    ag_forward(1, 3, dzr)
    settle()
    ar(0, 16, 2)
    settle()
    ar(0, 11, 3)
    settle()
    ar(0, 6, 4)
    settle()
    ar(0, 17, 2)
    settle()
    ar(0, 3, 5)
    settle()
    ag_done(1, 3, dzr)
    settle()
    weight_grad(1, z_.back0, 0, 768, act, dzr)
    settle()
    ar(1, 0, 0)
    settle()
    ar(1, 1, 0)
    settle()
    ar(1, 2, 0)
    settle()
    ar(0, 12, 3)
    settle()
    ar(0, 18, 2)
    settle()
    ar(1, 3, 0)
    settle()
    ar(1, 4, 0)
    settle()
    ar(1, 5, 0)
    settle()
    ag_forward(2, 2, dar)
    settle()
    ar(0, 9, 4)
    settle()
    backward_hidden(2)
    settle()
    rs_core(2, 3)
    settle()
    weight_grad(1, z_.in0, 0, 768, n1r, slope)
    settle()
    rs_y(2, 3)
    settle()
    ar(0, 13, 3)
    settle()
    ar(0, 4, 5)
    settle()
    ar(1, 6, 0)
    settle()
    ar(0, 7, 5)
    settle()
    ar(1, 7, 0)
    settle()
    ar(1, 8, 0)
    settle()
    ar(1, 1, 1)
    settle()
    ar(1, 9, 0)
    settle()
    ar(1, 10, 0)
    settle()
    ar(1, 11, 0)
    settle()
    ar(0, 8, 4)
    settle()
    ar(0, 14, 3)
    settle()
    ar(0, 11, 4)
    settle()
    ar(0, 12, 4)
    settle()
    ag_done(2, 2, dar)
    settle()
    attention_back_heads(1)
    settle()
    backward_rows(3)
    ag_start(2, 3, dar)
    settle()
    through_back(1)
    settle()
    dx_core(1)
    settle()
    small_core(1)
    settle()
    ar(1, 2, 1)
    settle()
    dx_relay(0, 2)
    settle()
    ar(0, 15, 3)
    settle()
    ar(0, 16, 3)
    settle()
    ar(0, 17, 3)
    settle()
    ar(0, 10, 5)
    settle()
    ar(0, 13, 4)
    settle()
    ar(1, 3, 1)
    settle()
    ar(0, 14, 4)
    settle()
    ar(0, 18, 3)
    settle()
    ag_forward(2, 3, dar)
    settle()
    ar(0, 15, 4)
    settle()
    ar(1, 0, 1)
    settle()
    small_y(1)
    settle()
    dx_y(1)
    settle()
    ar(1, 5, 1)
    settle()
    ar(0, 4, 6)
    settle()
    ag_done(2, 3, dar)
    settle()
    out_grad(1)
    settle()
    ar(1, 4, 1)
    settle()
    attention_back_heads(2)
    settle()
    ar(1, 6, 1)
    settle()
    ar(1, 7, 1)
    settle()
    ar(0, 7, 6)
    settle()
    through_back(2)
    settle()
    small_total(1)
    settle()
    ar(1, 9, 1)
    settle()
    dx_core(2)
    settle()
    qkv_grad(1)
    settle()
    ar(1, 8, 1)
    settle()
    ar(1, 11, 1)
    settle()
    ar(0, 10, 6)
    settle()
    ar(0, 4, 7)
    settle()
    ar(0, 7, 7)
    settle()
    dx_y(2)
    settle()
    ar(1, 0, 2)
    settle()
    ar(1, 1, 2)
    settle()
    ar(1, 12, 0)
    settle()
    ar(1, 13, 0)
    settle()
    ar(1, 14, 0)
    settle()
    ar(1, 15, 0)
    settle()
    ar(1, 16, 0)
    settle()
    ar(1, 17, 0)
    settle()
    ar(1, 18, 0)
    settle()
    ar(0, 16, 4)
    settle()
    ar(0, 17, 4)
    settle()
    ar(0, 18, 4)
    settle()
    ar(1, 4, 2)
    settle()
    ar(0, 10, 7)
    settle()
    dx_arrived_y(1)
    settle()
    dx_relay(1, 3)
    settle()
    ar(1, 10, 1)
    settle()
    ar(0, 4, 8)
    settle()
    ar(0, 5, 5)
    settle()
    ar(0, 6, 5)
    settle()
    ar(0, 7, 8)
    settle()
    ar(0, 8, 5)
    settle()
    ar(0, 8, 6)
    settle()
    ar(0, 9, 5)
    settle()
    ar(0, 10, 8)
    settle()
    ar(0, 11, 5)
    settle()
    ar(0, 12, 5)
    settle()
    ar(1, 7, 2)
    settle()
    ar(0, 13, 5)
    settle()
    publish(r["outq"], 0, r["out"], 0)
    settle()
    ar(1, 2, 2)
    settle()
    publish(r["outq"], 1, r["out"], 0)
    settle()
    ar(1, 4, 3)
    settle()
    publish(r["outq"], 2, r["out"], 0)
    settle()
    ar(1, 8, 2)
    settle()
    dx_relay(0, 1)
    settle()
    ar(0, 14, 5)
    settle()
    ar(1, 1, 3)
    settle()
    ar(1, 3, 2)
    settle()
    ar(1, 0, 3)
    settle()
    ar(1, 7, 3)
    settle()
    ar(0, 15, 5)
    settle()
    ar(1, 10, 2)
    settle()
    ar(1, 5, 2)
    settle()
    ar(1, 2, 3)
    settle()
    ar(1, 6, 2)
    settle()
    ar(1, 9, 2)
    settle()
    ar(1, 3, 3)
    settle()
    ar(1, 11, 2)
    settle()
    ar(1, 0, 4)
    settle()
    dx_relay(1, 2)
    settle()
    ar(1, 5, 3)
    settle()
    dx_final(0)
    settle()
    ar(1, 12, 1)
    settle()
    dx_arrived_y(2)
    settle()
    dx_relay(2, 3)
    settle()
    ar(1, 6, 3)
    settle()
    ar(1, 1, 4)
    settle()
    ar(1, 13, 1)
    settle()
    ar(1, 8, 3)
    settle()
    ar(1, 9, 3)
    settle()
    ar(1, 14, 1)
    settle()
    ar(1, 12, 2)
    settle()
    ar(1, 11, 3)
    settle()
    ar(1, 15, 1)
    settle()
    ar(1, 10, 3)
    settle()
    ar(1, 16, 1)
    settle()
    dx_relay(1, 1)
    settle()
    dx_relay(2, 2)
    settle()
    ar(1, 13, 2)
    settle()
    ar(1, 2, 4)
    settle()
    ar(1, 17, 1)
    settle()
    ar(1, 8, 4)
    settle()
    ar(1, 14, 2)
    settle()
    ar(1, 3, 4)
    settle()
    ar(1, 18, 1)
    settle()
    ar(1, 15, 2)
    settle()
    ar(1, 12, 3)
    settle()
    ar(1, 16, 2)
    settle()
    ar(1, 5, 4)
    settle()
    ar(0, 16, 5)
    settle()
    ar(0, 17, 5)
    settle()
    ar(1, 0, 5)
    settle()
    ar(1, 0, 6)
    settle()
    ar(1, 6, 4)
    settle()
    ar(0, 18, 5)
    settle()
    ar(1, 4, 4)
    settle()
    ar(1, 7, 4)
    settle()
    ar(1, 9, 4)
    settle()
    ar(1, 11, 4)
    settle()
    ar(1, 1, 5)
    settle()
    ar(1, 10, 4)
    settle()
    dx_final(1)
    settle()
    dx_relay(2, 1)
    settle()
    ar(1, 13, 3)
    settle()
    ar(1, 2, 5)
    settle()
    ar(1, 17, 2)
    settle()
    ar(1, 14, 3)
    settle()
    ar(1, 18, 2)
    settle()
    ar(1, 15, 3)
    settle()
    ar(1, 8, 5)
    settle()
    ar(1, 8, 6)
    settle()
    ar(1, 16, 3)
    settle()
    ar(1, 4, 5)
    settle()
    ar(1, 7, 5)
    settle()
    ar(1, 17, 3)
    settle()
    ar(1, 10, 5)
    settle()
    ar(1, 18, 3)
    settle()
    ar(1, 3, 5)
    settle()
    ar(1, 4, 6)
    settle()
    ar(1, 12, 4)
    settle()
    ar(1, 5, 5)
    settle()
    ar(1, 7, 6)
    settle()
    dx_final(2)
    settle()
    ar(1, 6, 5)
    settle()
    ar(1, 13, 4)
    settle()
    ar(1, 10, 6)
    settle()
    ar(1, 14, 4)
    settle()
    ar(1, 9, 5)
    settle()
    ar(1, 15, 4)
    settle()
    ar(1, 11, 5)
    settle()
    ar(1, 16, 4)
    settle()
    ar(1, 17, 4)
    settle()
    ar(1, 12, 5)
    settle()
    ar(1, 13, 5)
    settle()
    ar(1, 18, 4)
    settle()
    ar(1, 14, 5)
    settle()
    ar(1, 4, 7)
    settle()
    ar(1, 4, 8)
    settle()
    ar(1, 15, 5)
    settle()
    ar(1, 16, 5)
    settle()
    ar(1, 7, 7)
    settle()
    ar(1, 7, 8)
    settle()
    ar(1, 17, 5)
    settle()
    ar(1, 10, 7)
    settle()
    ar(1, 10, 8)
    settle()
    ar(1, 18, 5)
    settle()
    for u in (4, 2, 3):
        rs_sent(2, u)
    for finish in sent[settled[0]:] + finals:
        finish()


def layer(sizes, *args):
    anywhere = pl.BlockSpec(memory_space=pl.ANY)
    call = pl.pallas_call(
        functools.partial(layer_kernel, sizes),
        out_shape=(
            jax.ShapeDtypeStruct((sizes.ns, sizes.rows, sizes.width), BF16),
            jax.ShapeDtypeStruct((sizes.ns, sizes.rows, sizes.width), BF16),
            jax.ShapeDtypeStruct((2, sizes.total, sizes.width), BF16),
        ),
        in_specs=[anywhere] * 15,
        out_specs=[anywhere] * 3,
        scratch_shapes=list(sizes.scratch().values()),
        compiler_params=pltpu.CompilerParams(
            collective_id=0, has_side_effects=True, vmem_limit_bytes=VMEM_BYTES
        ),
    )
    return call(*args)


def widen_kernel(sizes, out, gin, grad, *refs):
    nt, share, hidden, width = sizes.nt, sizes.share, sizes.hidden, sizes.width
    (
        out_t, out_q, gin_t, gin_q, qkv, qv_bias, out_w, out_bias, in_w, in_bias, back_w,
        back_bias, gains, shifts, low, wide, tail, in_sem, out_sem, tail_sem,
    ) = refs
    t = lax.axis_index("tensor")
    pieces = []
    for src, first, second in ((out, out_t, out_q), (gin, gin_t, gin_q)):
        for s in range(sizes.ns):
            dst = first.at[s] if s < nt else second.at[s - nt]
            pieces.append((src.at[s], dst, sizes.rows))
    for b in range(2):
        for first, count, dst in (
            (sizes.back0, hidden, back_w.at[b]),
            (sizes.in0, width, in_w.at[b]),
            (sizes.out0, share, out_w.at[b]),
            (sizes.qkv0, share, qkv.at[b, 0]),
            (sizes.qkv0 + share, share, qkv.at[b, 1]),
            (sizes.qkv0 + 2 * share, share, qkv.at[b, 2]),
        ):
            size = min(count, WIDEN_ROWS)
            for start in range(0, count, size):
                src = grad.at[b, pl.ds(first + start, size)]
                pieces.append((src, dst.at[pl.ds(start, size)], size))
    tails = [
        pltpu.make_async_copy(
            grad.at[b, pl.ds(sizes.small0, 16)], tail.at[b], tail_sem.at[b]
        )
        for b in range(2)
    ]
    reads, writes, places = [], [], []
    place = 0
    for index, (src, dst, size) in enumerate(pieces):
        here = pl.ds(place, size)
        places.append((place, size))
        reads.append(pltpu.make_async_copy(src, low.at[here], in_sem.at[index]))
        writes.append(pltpu.make_async_copy(wide.at[here], dst, out_sem.at[index]))
        place += size
    for copy in reads + tails:
        copy.start()
    for (place, size), read, write in zip(places, reads, writes):
        read.wait()

        def body(step, carry, place=place):
            at = pl.ds(pl.multiple_of(place + step * 32, 32), 32)
            wide[at, :] = low[at, :].astype(F32)
            return carry

        lax.fori_loop(0, size // 32, body, 0)
        write.start()
    for copy in tails:
        copy.wait()
    rows = tail[...].astype(F32)

    def crop_rows(first, count):
        value = jnp.zeros((2, count, share), F32)
        for k in range(4):
            piece = rows[:, first : first + count, k * share : (k + 1) * share]
            value = jnp.where(t == k, piece, value)
        return value

    gains[...] = crop_rows(0, 2)
    shifts[...] = crop_rows(2, 2)
    out_bias[...] = crop_rows(4, 1)[:, 0]
    back_bias[...] = crop_rows(5, 1)[:, 0]
    in_bias[...] = rows[:, 8]
    qv_bias[...] = rows[:, 9:11, :share]
    for copy in writes:
        copy.wait()


WIDEN_ROWS = 256


def widen(sizes, out, gin, grad):
    nt, nq, rows, share, width, hidden = (
        sizes.nt, sizes.nq, sizes.rows, sizes.share, sizes.width, sizes.hidden,
    )
    anywhere = pl.BlockSpec(memory_space=pl.ANY)
    held = pl.BlockSpec(memory_space=pltpu.VMEM)
    shapes = (
        ((nt, rows, width), anywhere),
        ((nq, rows, width), anywhere),
        ((nt, rows, width), anywhere),
        ((nq, rows, width), anywhere),
        ((2, 3, share, width), anywhere),
        ((2, 2, share), held),
        ((2, share, width), anywhere),
        ((2, share), held),
        ((2, width, hidden), anywhere),
        ((2, hidden), held),
        ((2, hidden, width), anywhere),
        ((2, share), held),
        ((2, 2, share), held),
        ((2, 2, share), held),
    )
    total = 2 * sizes.ns * rows + 2 * (hidden + width + 4 * share)
    count = 2 * sizes.ns + 2 * (hidden // WIDEN_ROWS + width // WIDEN_ROWS + 4)
    return pl.pallas_call(
        functools.partial(widen_kernel, sizes),
        out_shape=tuple(jax.ShapeDtypeStruct(shape, F32) for shape, _ in shapes),
        in_specs=[anywhere] * 3,
        out_specs=tuple(spec for _, spec in shapes),
        scratch_shapes=[
            pltpu.VMEM((total, width), BF16),
            pltpu.VMEM((total, width), F32),
            pltpu.VMEM((2, 16, width), BF16),
            pltpu.SemaphoreType.DMA((count,)),
            pltpu.SemaphoreType.DMA((count,)),
            pltpu.SemaphoreType.DMA((2,)),
        ],
        compiler_params=pltpu.CompilerParams(vmem_limit_bytes=VMEM_BYTES),
    )(out, gin, grad)


VMEM_BYTES = 127 * 2**19


def fused(
    x_train,
    x_quiz,
    cot_train,
    cot_quiz,
    quiz_lengths,
    w_qkv,
    b_qv,
    w_out,
    b_out,
    w_in,
    b_in,
    w_back,
    b_back,
    norm_gains,
    norm_shifts,
):
    nt, rows, width = x_train.shape
    share, hidden = w_out.shape[0], w_in.shape[1]
    sizes = Sizes(
        nt, x_quiz.shape[0], rows, lax.axis_size("blk"), share, width, hidden
    )
    out, grad_in, grad = layer(
        sizes,
        x_train,
        x_quiz,
        cot_train,
        cot_quiz,
        quiz_lengths,
        jnp.swapaxes(w_qkv, 1, 2),
        w_out,
        w_in,
        w_back,
        b_out,
        b_in,
        b_back,
        norm_gains,
        norm_shifts,
        b_qv,
    )
    results = list(widen(sizes, out, grad_in, grad))
    results[4] = jnp.swapaxes(results[4], 2, 3)
    return tuple(results)


def fits(mesh):
    return dict(mesh.shape) == {"dp": 2, "tensor": 4, "blk": 4}


def solution(mesh):
    placed = (
        P("dp", "blk", None),
        P("dp", "blk", None),
        P("dp", "blk", None),
        P("dp", "blk", None),
        P("dp"),
        P(None, None, "tensor"),
        P(None, "tensor"),
        P("tensor", None),
        P(),
        P(None, "tensor"),
        P("tensor"),
        P("tensor", None),
        P(),
        P(),
        P(),
    )
    return jax.shard_map(
        fused if fits(mesh) else shards,
        mesh=mesh,
        in_specs=placed,
        out_specs=(
            P("dp", "blk", None),
            P("dp", "blk", None),
            P("dp", "blk", None),
            P("dp", "blk", None),
            P(None, None, None, "tensor"),
            P(None, None, "tensor"),
            P(None, "tensor", None),
            P(None, "tensor"),
            P(None, None, "tensor"),
            P(None, "tensor"),
            P(None, "tensor", None),
            P(None, "tensor"),
            P(None, None, "tensor"),
            P(None, None, "tensor"),
        ),
        check_vma=False,
    )
```

```python
import functools

import jax
import jax.numpy as jnp
from jax import lax
from jax.experimental import pallas as pl
from jax.experimental.pallas import tpu as pltpu
from jax.sharding import PartitionSpec as P

D = 768
HEAD_DIM = 64


EPSILON = 1e-12
ROOT_HALF = 0.7071067811865476
ROOT_TWO_PI = 2.5066282746310002
NEG_LARGE = -1e30


def layer_norm(hidden, gain, shift):
    center = hidden - jnp.mean(hidden, axis=-1, keepdims=True)
    inverse = lax.rsqrt(jnp.mean(center * center, axis=-1, keepdims=True) + EPSILON)
    normal = center * inverse
    return (normal * gain + shift, normal, inverse)


def norm_back(grad_out, normal, inverse, gain):
    scaled = grad_out * gain
    grad_in = inverse * (
        scaled
        - jnp.mean(scaled, axis=-1, keepdims=True)
        - normal * jnp.mean(scaled * normal, axis=-1, keepdims=True)
    )
    return (grad_in, jnp.sum(grad_out * normal, axis=0), jnp.sum(grad_out, axis=0))


def gelu_exact(values):
    return 0.5 * values * (1.0 + lax.erf(values * ROOT_HALF))


def gelu_slope(values):
    return (
        0.5 * (1.0 + lax.erf(values * ROOT_HALF))
        + values * jnp.exp(-0.5 * values * values) / ROOT_TWO_PI
    )


def across(left, right):
    return lax.dot_general(
        left, right, (((0,), (0,)), ((), ())), preferred_element_type=jnp.float32
    )


def against(left, right):
    return lax.dot_general(
        left, right, (((1,), (1,)), ((), ())), preferred_element_type=jnp.float32
    )


def rounded(values):
    return lax.optimization_barrier(values.astype(jnp.bfloat16)).astype(jnp.float32)


def crop(values, column, share):
    return lax.dynamic_slice_in_dim(values, column, share, axis=values.ndim - 1)


def pair_grads(query_heads, dout_heads, log_total, delta, key_heads, value_heads, visible):
    scale = query_heads.shape[-1] ** (-0.5)
    scores = (
        jnp.einsum("sqhe,skhe->shqk", query_heads, key_heads, preferred_element_type=jnp.float32)
        * scale
    )
    probs = jnp.where(visible[:, None, None, :], jnp.exp(scores - log_total[..., None]), 0.0)
    grad_value = jnp.einsum(
        "shqk,sqhe->skhe",
        probs.astype(jnp.bfloat16),
        dout_heads,
        preferred_element_type=jnp.float32,
    )
    grad_probs = jnp.einsum(
        "sqhe,skhe->shqk", dout_heads, value_heads, preferred_element_type=jnp.float32
    )
    grad_scores = (probs * (grad_probs - delta[..., None])).astype(jnp.bfloat16)
    grad_query = jnp.einsum(
        "shqk,skhe->sqhe", grad_scores, key_heads, preferred_element_type=jnp.float32
    )
    grad_key = jnp.einsum(
        "shqk,sqhe->skhe", grad_scores, query_heads, preferred_element_type=jnp.float32
    )
    return (grad_query, grad_key, grad_value)


def run(tokens, cotangent, lengths, first_row, weights):
    w_qkv, b_qv, w_out, b_out, w_in, b_in, w_back, b_back, norm_gains, norm_shifts = weights
    seq_count, row_count, width = tokens.shape
    seq_len = row_count * lax.axis_size("blk")
    span = min(512, seq_len)
    block_count = seq_len // span
    flat_tokens = tokens.reshape(seq_count * row_count, width)
    low_tokens = flat_tokens.astype(jnp.bfloat16)
    projected = jnp.einsum("nd,tde->tne", low_tokens, w_qkv, preferred_element_type=jnp.float32)
    qv_bias = b_qv.astype(jnp.float32)
    query = (projected[0] + qv_bias[0]).astype(jnp.bfloat16)
    key_rows = projected[1].astype(jnp.bfloat16)
    value_rows = (projected[2] + qv_bias[1]).astype(jnp.bfloat16)
    share = key_rows.shape[-1]
    heads = share // HEAD_DIM
    scale = HEAD_DIM ** (-0.5)
    head_shape = (seq_count, row_count, heads, HEAD_DIM)
    query_heads = query.reshape(head_shape)
    key_three = key_rows.reshape(seq_count, row_count, share)
    value_three = value_rows.reshape(seq_count, row_count, share)
    running_max = jnp.full((seq_count, heads, row_count), NEG_LARGE, jnp.float32)
    running_out = jnp.zeros(head_shape, jnp.float32)
    key_piece = lax.all_gather(key_three, "blk", axis=1, tiled=True)
    value_piece = lax.all_gather(value_three, "blk", axis=1, tiled=True)
    piece_rows = key_piece.shape[1]
    key_heads = key_piece.reshape(seq_count, piece_rows, heads, HEAD_DIM)
    value_heads = value_piece.reshape(seq_count, piece_rows, heads, HEAD_DIM)
    scores = (
        jnp.einsum("sqhe,skhe->shqk", query_heads, key_heads, preferred_element_type=jnp.float32)
        * scale
    )
    visible = (jnp.arange(piece_rows, dtype=jnp.int32)[None, :] < lengths[:, None])[
        :, None, None, :
    ]
    scores = jnp.where(visible, scores, NEG_LARGE)
    new_max = jnp.maximum(running_max, jnp.max(scores, axis=-1))
    factor = jnp.exp(running_max - new_max)
    raised = jnp.where(visible, jnp.exp(scores - new_max[..., None]), 0.0)
    new_sum = jnp.sum(raised, axis=-1)
    added = jnp.einsum(
        "shqk,skhe->sqhe",
        raised.astype(jnp.bfloat16),
        value_heads,
        preferred_element_type=jnp.float32,
    )
    new_out = running_out * jnp.swapaxes(factor, 1, 2)[..., None] + added
    mixed_heads = new_out / jnp.swapaxes(new_sum, 1, 2)[..., None]
    log_total = new_max + jnp.log(new_sum)
    mixed_low = mixed_heads.reshape(seq_count * row_count, share).astype(jnp.bfloat16)
    attention = lax.psum(
        jnp.dot(mixed_low, w_out, preferred_element_type=jnp.float32).astype(jnp.bfloat16), "tensor"
    ).astype(jnp.float32) + b_out.astype(jnp.float32)
    normed, unit_one, inverse_one = layer_norm(
        flat_tokens + attention, norm_gains[0], norm_shifts[0]
    )
    normed_low = normed.astype(jnp.bfloat16)
    before = jnp.dot(normed_low, w_in, preferred_element_type=jnp.float32) + b_in.astype(
        jnp.float32
    )
    active_low = gelu_exact(before).astype(jnp.bfloat16)
    branch = lax.psum(
        jnp.dot(active_low, w_back, preferred_element_type=jnp.float32).astype(jnp.bfloat16),
        "tensor",
    ).astype(jnp.float32) + b_back.astype(jnp.float32)
    final, unit_two, inverse_two = layer_norm(normed + branch, norm_gains[1], norm_shifts[1])
    positions = first_row + jnp.arange(row_count, dtype=jnp.int32)
    keep_rows = (
        (positions[None, :] < lengths[:, None])
        .reshape(seq_count * row_count, 1)
        .astype(jnp.float32)
    )
    outputs = (keep_rows * final).reshape(tokens.shape)
    grad_final = keep_rows * cotangent.reshape(seq_count * row_count, width)
    grad_mid, grad_gain_two, grad_shift_two = norm_back(
        grad_final, unit_two, inverse_two, norm_gains[1]
    )
    grad_branch = grad_mid.astype(jnp.bfloat16)
    grad_b_back = jnp.sum(grad_branch.astype(jnp.float32), axis=0)
    grad_w_back = across(active_low, grad_branch)
    grad_active = against(grad_branch, w_back).astype(jnp.bfloat16).astype(jnp.float32)
    grad_before = (grad_active * gelu_slope(before)).astype(jnp.bfloat16)
    grad_b_in = jnp.sum(grad_before.astype(jnp.float32), axis=0)
    grad_w_in = across(normed_low, grad_before)
    grad_normed = grad_mid + rounded(
        lax.psum(against(grad_before, w_in).astype(jnp.bfloat16), "tensor").astype(jnp.float32)
    )
    grad_hidden, grad_gain_one, grad_shift_one = norm_back(
        grad_normed, unit_one, inverse_one, norm_gains[0]
    )
    grad_attention = grad_hidden.astype(jnp.bfloat16)
    grad_b_out = jnp.sum(grad_attention.astype(jnp.float32), axis=0)
    grad_w_out = across(mixed_low, grad_attention)
    grad_mixed = against(grad_attention, w_out).astype(jnp.bfloat16)
    dout_heads = grad_mixed.reshape(head_shape)
    delta = jnp.swapaxes(jnp.sum(dout_heads.astype(jnp.float32) * mixed_heads, axis=-1), 1, 2)
    key_all, value_all = key_piece, value_piece
    key_blocks = jnp.moveaxis(key_all.reshape(seq_count, block_count, span, heads, HEAD_DIM), 1, 0)
    value_blocks = jnp.moveaxis(
        value_all.reshape(seq_count, block_count, span, heads, HEAD_DIM), 1, 0
    )
    visible_all = jnp.arange(seq_len, dtype=jnp.int32)[None, :] < lengths[:, None]
    visible_blocks = jnp.moveaxis(visible_all.reshape(seq_count, block_count, span), 1, 0)

    def sweep_keys(grad_query, item):
        key_block, value_block, visible_block = item
        part_query, part_key, part_value = pair_grads(
            query_heads, dout_heads, log_total, delta, key_block, value_block, visible_block
        )
        return (grad_query + part_query, (part_key, part_value))

    grad_query, (key_terms, value_terms) = lax.scan(
        sweep_keys, jnp.zeros(head_shape, jnp.float32), (key_blocks, value_blocks, visible_blocks)
    )
    key_terms = jnp.moveaxis(key_terms, 0, 1).reshape(seq_count, seq_len, share)
    value_terms = jnp.moveaxis(value_terms, 0, 1).reshape(seq_count, seq_len, share)
    key_sum, value_sum = (
        lax.psum_scatter(
            key_terms.astype(jnp.bfloat16), "blk", scatter_dimension=1, tiled=True
        ).astype(jnp.float32),
        lax.psum_scatter(
            value_terms.astype(jnp.bfloat16), "blk", scatter_dimension=1, tiled=True
        ).astype(jnp.float32),
    )
    grad_query_low = (grad_query * scale).reshape(seq_count * row_count, share).astype(jnp.bfloat16)
    grad_key_low = (key_sum * scale).reshape(seq_count * row_count, share).astype(jnp.bfloat16)
    grad_value_low = value_sum.reshape(seq_count * row_count, share).astype(jnp.bfloat16)
    grad_stack = jnp.stack([grad_query_low, grad_key_low, grad_value_low])
    grad_w_qkv = jnp.einsum(
        "nd,tne->tde", low_tokens, grad_stack, preferred_element_type=jnp.float32
    )
    grad_b_qv = jnp.stack(
        [
            jnp.sum(grad_query_low.astype(jnp.float32), axis=0),
            jnp.sum(grad_value_low.astype(jnp.float32), axis=0),
        ]
    )
    grad_through = lax.psum(
        jnp.einsum("tne,tde->nd", grad_stack, w_qkv, preferred_element_type=jnp.float32).astype(
            jnp.bfloat16
        ),
        "tensor",
    ).astype(jnp.float32)
    grad_tokens = (grad_hidden + rounded(grad_through)).reshape(tokens.shape)
    grad_gains = jnp.stack([grad_gain_one, grad_gain_two])
    grad_shifts = jnp.stack([grad_shift_one, grad_shift_two])
    grads = (
        grad_w_qkv,
        grad_b_qv,
        grad_w_out,
        grad_b_out,
        grad_w_in,
        grad_b_in,
        grad_w_back,
        grad_b_back,
        grad_gains,
        grad_shifts,
    )
    return (outputs, grad_tokens, grads)


def shards(
    x_train,
    x_quiz,
    cot_train,
    cot_quiz,
    quiz_lengths,
    w_qkv,
    b_qv,
    w_out,
    b_out,
    w_in,
    b_in,
    w_back,
    b_back,
    norm_gains,
    norm_shifts,
):
    row_count = x_train.shape[1]
    seq_len = row_count * lax.axis_size("blk")
    first_row = lax.axis_index("blk") * row_count
    share = D // lax.axis_size("tensor")
    column = lax.axis_index("tensor") * share
    weights = (w_qkv, b_qv, w_out, b_out, w_in, b_in, w_back, b_back, norm_gains, norm_shifts)
    full_lengths = jnp.full((x_train.shape[0],), seq_len, jnp.int32)
    out_train, grad_in_train, train_grads = run(
        x_train, cot_train, full_lengths, first_row, weights
    )
    out_quiz, grad_in_quiz, quiz_grads = run(x_quiz, cot_quiz, quiz_lengths, first_row, weights)
    def total(grads):
        pieces = (
            grads[0],
            grads[1],
            grads[2],
            crop(grads[3], column, share),
            grads[4],
            grads[5],
            grads[6],
            crop(grads[7], column, share),
            crop(grads[8], column, share),
            crop(grads[9], column, share),
        )
        low = tuple(piece.astype(jnp.bfloat16) for piece in pieces)
        return tuple(
            piece.astype(jnp.float32) for piece in lax.psum(low, ("dp", "blk"))
        )

    summed = [jnp.stack(pair) for pair in zip(total(train_grads), total(quiz_grads))]
    return (
        out_train,
        out_quiz,
        grad_in_train,
        grad_in_quiz,
        summed[0],
        summed[1],
        summed[2],
        summed[3],
        summed[4],
        summed[5],
        summed[6],
        summed[7],
        summed[8],
        summed[9],
    )


MESH_ID = pl.DeviceIdType.MESH
F32 = jnp.float32
BF16 = jnp.bfloat16
SMALL = 32
BACK_KINDS = "zxxxwx"
IN_KINDS = "xwzxwx"
OUT_KINDS = "x"
QKV_KINDS = "xxxxxx"
INV_ROOT_TWO_PI = 1.0 / ROOT_TWO_PI
SETTLE_AGE = 100
WEIGHT_TILE = 256


def nn(left, right):
    return jnp.dot(left, right, preferred_element_type=F32)


def tile_loop(count, tile, body):
    def step(index, carry):
        body(pl.multiple_of(index * tile, tile))
        return carry

    lax.fori_loop(0, count // tile, step, 0)


def tiles(count, tile, body):
    for start in range(0, count, tile):
        body(start)


def sum_rows(value):
    return jnp.sum(value, axis=0, keepdims=True)


def lanes(count):
    return (count // 128 + 1) * 128


class Sizes:
    def __init__(self, nt, nq, rows, blocks, share, width, hidden):
        self.nt, self.nq, self.rows, self.blocks = nt, nq, rows, blocks
        self.share, self.width, self.hidden = share, width, hidden
        self.ns = nt + nq
        self.quarter = rows // 4
        self.seq_len = rows * blocks
        self.heads = share // HEAD_DIM
        self.back0 = 0
        self.in0 = hidden
        self.out0 = hidden + width
        self.qkv0 = self.out0 + share
        self.small0 = self.qkv0 + 3 * share
        self.total = self.small0 + SMALL
        half = self.quarter // 2
        self.streams = tuple((s, part * half, half) for s in range(nt) for part in range(2))
        self.streams += tuple((s, 0, self.quarter) for s in range(nt, self.ns))
        self.streams += tuple((s, 0, self.quarter) for s in range(nt))
        self.chunks = self.plan()
        self.first_half, self.first_zone, half, zone = [], [], 0, 0
        for _, count, kind in self.chunks:
            self.first_half.append(half)
            self.first_zone.append(zone)
            half += count // 2
            zone += count // 2 if kind == "x" else count
        self.half_rows, self.zone_rows = half, zone

    def plan(self):
        pieces = []
        for first, count, kinds in (
            (self.back0, self.hidden, BACK_KINDS),
            (self.in0, self.width, IN_KINDS),
            (self.out0, self.share, OUT_KINDS),
            (self.qkv0, 3 * self.share, QKV_KINDS),
        ):
            size = count // len(kinds)
            for index, kind in enumerate(kinds):
                pieces.append((first + index * size, size, kind))
        first, count, kind = pieces[-1]
        pieces[-1] = (first, count + SMALL, kind)
        return tuple(pieces)

    def scratch(self):
        ns, rows, share, width = self.ns, self.rows, self.share, self.width
        q, blocks, seq = self.quarter, self.blocks, self.seq_len
        dma = pltpu.SemaphoreType.DMA
        nc, nu = len(self.chunks), len(self.streams)
        return dict(
            xown=pltpu.VMEM((ns, q, width), F32),
            cown=pltpu.VMEM((ns, q, width), F32),
            vec=pltpu.VMEM((16, width), F32),
            raw0=pltpu.VMEM((width,), BF16),
            raw1=pltpu.VMEM((self.hidden,), BF16),
            raw2=pltpu.VMEM((width,), BF16),
            raw_gains=pltpu.VMEM((2, width), F32),
            raw_shifts=pltpu.VMEM((2, width), F32),
            raw_qv=pltpu.VMEM((2, share), BF16),
            lengths=pltpu.SMEM((self.nq,), jnp.int32),
            xg=pltpu.VMEM((ns, seq, width), BF16),
            wqkv=pltpu.VMEM((3, share, width), BF16),
            wout=pltpu.VMEM((share, width), BF16),
            win=pltpu.VMEM((width, self.hidden), BF16),
            wback=pltpu.VMEM((self.hidden, width), BF16),
            qb=pltpu.VMEM((ns, rows, share), BF16),
            kb=pltpu.VMEM((ns, seq, share), BF16),
            vb=pltpu.VMEM((ns, seq, lanes(share)), BF16),
            probs=pltpu.VMEM((ns, self.heads, rows, seq), BF16),
            of=pltpu.VMEM((rows, lanes(share)), F32),
            invl=pltpu.VMEM((ns, rows, share), F32),
            orb=pltpu.VMEM((ns, rows, share), BF16),
            unit1=pltpu.VMEM((ns, q, width), F32),
            inv1=pltpu.VMEM((ns, q, 128), F32),
            n1r=pltpu.VMEM((ns, 4, q, width), BF16),
            dzr=pltpu.VMEM((ns, 4, q, width), BF16),
            dar=pltpu.VMEM((ns, 4, q, width), BF16),
            act=pltpu.VMEM((ns, 4, q, self.hidden), BF16),
            slope=pltpu.VMEM((ns, 4, q, self.hidden), BF16),
            work=pltpu.VMEM((rows, max(seq, width)), F32),
            dsb=pltpu.VMEM((rows, seq), BF16),
            dqb=pltpu.VMEM((ns, rows, share), BF16),
            dkvt=pltpu.VMEM((ns, 2, share, seq), BF16),
            tq=pltpu.VMEM((share, rows), BF16),
            tm=pltpu.VMEM((share, rows), BF16),
            gm=pltpu.VMEM((rows, share), BF16),
            delta=pltpu.VMEM((rows, 128), F32),
            part=pltpu.VMEM((ns, 2, 2, q, width), BF16),
            crecv=pltpu.VMEM((3, ns, 2, q, width), BF16),
            yrecv=pltpu.VMEM((3, ns, q, width), BF16),
            part4=pltpu.VMEM((ns, blocks, 2, 2, q, width), BF16),
            crecv4=pltpu.VMEM((ns, blocks, 2, q, width), BF16),
            yrecv4=pltpu.VMEM((ns, blocks, q, width), BF16),
            zrecv4=pltpu.VMEM((ns, 2, blocks - 1, q, width), BF16),
            outq=pltpu.VMEM((ns, q, width), BF16),
            ginq=pltpu.VMEM((ns, q, width), BF16),
            gb=pltpu.VMEM((2, self.total, width), BF16),
            xrecv=pltpu.VMEM((2, self.half_rows, width), BF16),
            zr1=pltpu.VMEM((2, self.zone_rows, width), BF16),
            zr2=pltpu.VMEM((2, self.half_rows, width), BF16),
            small=pltpu.VMEM((2, SMALL, width), F32),
            smallc=pltpu.VMEM((2, 8, width), F32),
            smalls=pltpu.VMEM((2, 8, width), F32),
            smally=pltpu.VMEM((2, 8, width), F32),
            load_sem=dma((2 * ns + 5,)),
            vec_sem=dma((7,)),
            xz_s=dma((nu - self.nt, 2, blocks - 1)),
            xz_r=dma((nu - self.nt, blocks - 1)),
            xc_s=dma((nu - self.nt, blocks - 1, 3)),
            xc_r=dma((nu - self.nt, blocks - 1, 3)),
            ex_s=dma((3, nu - self.nt, 5)),
            ex_r=dma((3, nu - self.nt, 5)),
            d4_s=dma((ns, 2)),
            d4_r=dma((ns, 2)),
            z4_s=dma((ns, 2, blocks - 1)),
            z4_r=dma((ns, 2, blocks - 1)),
            og_s=dma((2, ns, 3)),
            og_r=dma((2, ns, 3)),
            ol_s=dma((2, ns)),
            ar_s=dma((2, nc, 5)),
            ar_r=dma((2, nc, 5)),
            al_s=dma((2, nc)),
            sm_s=dma((2, 2)),
            sm_r=dma((2, 2)),
        )


INPUTS = (
    "xt", "xq", "ct", "cq", "lens", "wqkv_in", "wout_in", "win_in", "wback_in",
    "b_out", "b_in", "b_back", "gains", "shifts", "b_qv",
)
OUTPUTS = ("out", "gin", "grad")


def layer_kernel(z_, *refs):
    names = INPUTS + OUTPUTS + tuple(z_.scratch())
    r = dict(zip(names, refs))
    nt, ns, rows, blocks = z_.nt, z_.ns, z_.rows, z_.blocks
    share, width, hidden, quarter = z_.share, z_.width, z_.hidden, z_.quarter
    seq_len, heads = z_.seq_len, z_.heads
    scale = HEAD_DIM ** (-0.5)
    batches = (tuple(range(nt)), tuple(range(nt, ns)))
    lens_ref = r["lengths"]
    xg, work, part, gb = r["xg"], r["work"], r["part"], r["gb"]

    x = lax.axis_index("dp")
    t = lax.axis_index("tensor")
    z = lax.axis_index("blk")
    y = t // 2
    c = t % 2
    to_x = (1 - x, t, z)
    to_c = (x, t + 1 - 2 * c, z)
    to_y = (x, (t + 2) % 4, z)
    to_d = (x, 3 - t, z)
    to_right = (x, t, jnp.minimum(z + 1, blocks - 1))
    to_left = (x, t, jnp.maximum(z - 1, 0))
    has_left = z > 0
    has_right = z < blocks - 1
    corner = jnp.logical_or(z == 0, z == blocks - 1)
    interior = jnp.logical_and(z > 0, z < blocks - 1)
    to_inner = (x, t, jnp.where(z == 0, 1, blocks - 2))
    to_mirror = (x, t, blocks - 1 - z)
    to_outer = (x, t, jnp.where(z == 1, 0, blocks - 1))
    finals, sent, ages = [], [], []

    def settle(count=3, age=SETTLE_AGE):
        ages.append(len(sent))
        ready = ages[-age] if len(ages) >= age else 0
        for _ in range(min(count, ready - settled[0])):
            sent[settled[0]]()
            settled[0] += 1

    settled = [0]

    def when(cond, fn):
        if cond is None:
            fn()
        else:
            pl.when(cond)(fn)

    def remote(src, dst, ssem, rsem, dev):
        return pltpu.make_async_remote_copy(
            src_ref=src,
            dst_ref=dst,
            send_sem=ssem,
            recv_sem=rsem,
            device_id=dev,
            device_id_type=MESH_ID,
        )

    def send(src, dst, ssem, rsem, dev, cond=None, final=True):
        when(cond, lambda: remote(src, dst, ssem, rsem, dev).start())
        if final:
            sent.append(
                lambda: when(cond, lambda: remote(src, dst, ssem, rsem, dev).wait_send())
            )

    def arrived(dst, ssem, rsem, dev, cond=None):
        when(cond, lambda: remote(dst, dst, ssem, rsem, dev).wait_recv())

    def local(src, dst, sem):
        copy = pltpu.make_async_copy(src, dst, sem)
        copy.start()
        return copy

    mine = pl.ds(pl.multiple_of(t * quarter, quarter), quarter)
    facing = (t + 2) % 4

    def stream(u):
        s, first, count = z_.streams[u]
        return s, pl.ds(first, count)

    def flat(ref, s, lanes_=slice(None)):
        value = ref[s, :, :, lanes_]
        return value.reshape(rows, value.shape[-1])
    own_block = pl.ds(pl.multiple_of(z * rows, rows), rows)

    vec_ref = r["vec"]

    def vec(row, size=None):
        return vec_ref[row : row + 1, : (size or width)]

    vector_loads = (
        (r["b_out"], r["raw0"]),
        (r["b_in"], r["raw1"]),
        (r["b_back"], r["raw2"]),
        (r["gains"], r["raw_gains"]),
        (r["shifts"], r["raw_shifts"]),
        (r["b_qv"], r["raw_qv"]),
        (r["lens"], r["lengths"]),
    )

    def load_vectors():
        return [
            local(src, dst, r["vec_sem"].at[index])
            for index, (src, dst) in enumerate(vector_loads)
        ]

    def gather_vectors():
        for copy in loads["vectors"]:
            copy.wait()
        for row, name in enumerate(("raw0", "raw1", "raw2")):
            vec_ref[row : row + 1, :] = r[name][...].astype(F32).reshape(1, width)
        vec_ref[3:5, :] = r["raw_gains"][...]
        vec_ref[5:7, :] = r["raw_shifts"][...]
        vec_ref[7:9, :share] = r["raw_qv"][...].astype(F32)

    loads = {}
    load_sem = r["load_sem"]
    x_src = [r["xt"].at[s] for s in range(nt)] + [r["xq"].at[s] for s in range(ns - nt)]
    c_src = [r["ct"].at[s] for s in range(nt)] + [r["cq"].at[s] for s in range(ns - nt)]
    for s in range(ns):
        loads["x", s] = local(x_src[s].at[mine], r["xown"].at[s], load_sem.at[s])
    loads["vectors"] = load_vectors()
    for index, name in enumerate(("wqkv", "wout", "win", "wback")):
        loads[name] = local(r[name + "_in"], r[name], load_sem.at[ns + index])
    for s in range(ns):
        loads["c", s] = local(c_src[s].at[mine], r["cown"].at[s], load_sem.at[ns + 4 + s])

    barrier = pltpu.get_barrier_semaphore()

    def greet(dev, cond=None):
        when(
            cond,
            lambda: pl.semaphore_signal(
                barrier, inc=1, device_id=dev, device_id_type=MESH_ID
            ),
        )

    for dev in (to_x, to_c, to_y, to_d):
        greet(dev)
    greet(to_left, has_left)
    greet(to_right, has_right)
    when(corner, lambda: pl.semaphore_wait(barrier, 5))
    when(interior, lambda: pl.semaphore_wait(barrier, 6))

    def block_rows(j, q, within=pl.ds(0, quarter)):
        start = j * rows + q * quarter + within.start
        return pl.ds(pl.multiple_of(start, within.size), within.size)

    def side_valid(side, d):
        return z >= d if side == 0 else z <= blocks - 1 - d

    def side_block(side, d):
        return jnp.maximum(z - d, 0) if side == 0 else jnp.minimum(z + d, blocks - 1)

    class Sides:
        def __init__(self, ref):
            self.at = self
            self.ref = ref

        def __getitem__(self, key):
            u, side, step, *kind = key
            slot = step if side == 0 else blocks - 2 - step
            return self.ref.at[(u, slot, *kind)]

    xz_s = r["xz_s"]
    xz_r, xc_s, xc_r = Sides(r["xz_r"]), Sides(r["xc_s"]), Sides(r["xc_r"])

    def xa_start(u):
        s, within = stream(u)
        if within.start == 0:
            loads["x", s].wait()
        place = block_rows(z, t, within)
        xg[s, place, :] = r["xown"][s, within, :].astype(BF16)
        here = xg.at[s, place]
        send(here, here, xz_s.at[u, 0, 0], xz_r.at[u, 0, 0], to_right, has_right)
        send(here, here, xz_s.at[u, 1, 0], xz_r.at[u, 1, 0], to_left, has_left)

    def xa_step(u, d):
        s, within = stream(u)
        for side in range(2):
            valid = side_valid(side, d)
            here = xg.at[s, block_rows(side_block(side, d), t, within)]
            arrived(here, xz_s.at[u, side, d - 1], xz_r.at[u, side, d - 1], to_c, valid)
            if d < blocks - 1:
                more = has_right if side == 0 else has_left
                send(
                    here,
                    here,
                    xz_s.at[u, side, d],
                    xz_r.at[u, side, d],
                    to_right if side == 0 else to_left,
                    jnp.logical_and(valid, more),
                )
            for kind, dev in ((0, to_y), (1, to_c)):
                pair = xc_s.at[u, side, d - 1, kind], xc_r.at[u, side, d - 1, kind]
                send(here, here, *pair, dev, valid)

    def xa_forward(u, d):
        s, within = stream(u)
        for side in range(2):
            valid = side_valid(side, d)
            here = xg.at[s, block_rows(side_block(side, d), facing, within)]
            pair = xc_s.at[u, side, d - 1, 0], xc_r.at[u, side, d - 1, 0]
            arrived(here, *pair, to_c, valid)
            pair = xc_s.at[u, side, d - 1, 2], xc_r.at[u, side, d - 1, 2]
            send(here, here, *pair, to_c, valid)

    def xa_done(u, d):
        s, within = stream(u)
        for side in range(2):
            for kind in (1, 2):
                here = xg.at[s, block_rows(side_block(side, d), t, within)]
                pair = xc_s.at[u, side, d - 1, kind], xc_r.at[u, side, d - 1, kind]
                arrived(here, *pair, to_c, side_valid(side, d))

    def own_cast(s):
        copy = local(x_src[s], work.at[:, pl.ds(0, width)], load_sem.at[2 * ns + 4])
        copy.wait()
        for q in range(4):

            def cast(q=q):
                xg[s, block_rows(z, q), :] = work[
                    q * quarter : (q + 1) * quarter, :width
                ].astype(BF16)

            when(t != q, cast)

    padded = lanes(share)
    padded_head = lax.broadcasted_iota(jnp.int32, (1, padded), 1) // HEAD_DIM
    head_of_lane = lax.broadcasted_iota(jnp.int32, (1, share), 1) // HEAD_DIM
    invl = r["invl"]
    crecv, yrecv = r["crecv"], r["yrecv"]
    first_whole = len(z_.streams) - nt

    class Pairs:
        def __init__(self, ref):
            self.at = self
            self.ref = ref

        def __getitem__(self, key):
            k, u, index = key
            return self.ref.at[k, 2 * (u - first_whole) if u >= first_whole else u, index]

    ex_s, ex_r = Pairs(r["ex_s"]), Pairs(r["ex_r"])

    def rs_sends(k, u):
        s, within = stream(u)
        return (
            (
                part.at[s, :, 1 - c, within],
                crecv.at[k, s, :, within],
                ex_s.at[k, u, 0],
                ex_r.at[k, u, 0],
                to_c,
            ),
            (
                part.at[s, 1 - y, c, within],
                yrecv.at[k, s, within],
                ex_s.at[k, u, 1],
                ex_r.at[k, u, 1],
                to_y,
            ),
        )

    def rs_core(k, u):
        send(*rs_sends(k, u)[0], final=False)

    def rs_y(k, u):
        s, within = stream(u)
        arrived(*rs_sends(k, u)[0][1:])
        part[s, 1 - y, c, within] = (
            part[s, 1 - y, c, within].astype(F32) + crecv[k, s, 1 - y, within].astype(F32)
        ).astype(BF16)
        send(*rs_sends(k, u)[1], final=False)

    def rs_total(k, u):
        s, within = stream(u)
        arrived(*rs_sends(k, u)[1][1:])
        return (
            part[s, y, c, within].astype(F32)
            + crecv[k, s, y, within].astype(F32)
            + yrecv[k, s, within].astype(F32)
        )

    def rs_sent(k, u):
        for args in rs_sends(k, u):
            remote(*args).wait_send()

    def ag_start(k, u, full):
        s, within = stream(u)
        here = full.at[s, t, within]
        send(here, here, ex_s.at[k, u, 3], ex_r.at[k, u, 3], to_y)
        send(here, here, ex_s.at[k, u, 2], ex_r.at[k, u, 2], to_c)

    def ag_forward(k, u, full):
        s, within = stream(u)
        here = full.at[s, facing, within]
        arrived(here, ex_s.at[k, u, 3], ex_r.at[k, u, 3], to_y)
        send(here, here, ex_s.at[k, u, 4], ex_r.at[k, u, 4], to_c)

    def ag_done(k, u, full):
        s, within = stream(u)
        here = full.at[s, t, within]
        arrived(here, ex_s.at[k, u, 2], ex_r.at[k, u, 2], to_c)
        arrived(here, ex_s.at[k, u, 4], ex_r.at[k, u, 4], to_c)

    def publish(buf, s, target, kind):
        here = target.at[s, mine]
        og_s, og_r = r["og_s"], r["og_r"]
        devices = tuple(enumerate((to_c, to_y, to_d)))
        for index, dev in devices:
            sems = og_s.at[kind, s, index], og_r.at[kind, s, index]
            send(buf.at[s], here, *sems, dev)
        copy = local(buf.at[s], here, r["ol_s"].at[kind, s])
        finals.append(copy.wait)

        def landed():
            for index, dev in devices:
                arrived(here, og_s.at[kind, s, index], og_r.at[kind, s, index], dev)

        finals.append(landed)

    def batch_of(s):
        return 0 if s < nt else 1

    def length(s):
        return jnp.int32(seq_len) if s < nt else lens_ref[s - nt]

    def keep_rows(s, within):
        first = z * rows + t * quarter + within.start
        position = first + lax.broadcasted_iota(jnp.int32, (within.size, 1), 0)
        return jnp.where(position < length(s), 1.0, 0.0)

    qb, kb, vb, probs, of, orb = (r[n] for n in ("qb", "kb", "vb", "probs", "of", "orb"))
    wqkv, wout, win, wback = (r[n] for n in ("wqkv", "wout", "win", "wback"))
    unit1, inv1 = r["unit1"], r["inv1"]
    dh = r["xown"]
    n1r, dzr, dar, act, slope = (r[n] for n in ("n1r", "dzr", "dar", "act", "slope"))
    dsb, dqb, dkvt = (r[n] for n in ("dsb", "dqb", "dkvt"))
    small = r["small"]
    tq, tm, gm, delta = (r[n] for n in ("tq", "tm", "gm", "delta"))

    def add_small(s, row, value, size=None):
        place = (batch_of(s), slice(row, row + 1), slice(0, size or width))
        small[place] += value

    def project_query(s):
        low = (against(xg[s, own_block, :], wqkv[0]) + vec(7, share)).astype(BF16)
        qb[s] = low * jnp.array(scale, BF16)

    def project_block(s, start):
        lane = lax.broadcasted_iota(jnp.int32, (rows, padded - share), 1)
        place = pl.ds(start, rows)
        block = xg[s, place, :]
        kb[s, place, :] = against(block, wqkv[1]).astype(BF16)
        vb[s, place, :share] = (against(block, wqkv[2]) + vec(8, share)).astype(BF16)
        vb[s, place, share:] = jnp.where(lane == 0, 1.0, 0.0).astype(BF16)

    def project_own(s):
        project_block(s, pl.multiple_of(z * rows, rows))

    def project_rest(s):
        def body(j):
            project_block(s, pl.multiple_of(((z + 1 + j) % blocks) * rows, rows))

        repeat = rounds if s < nt else loop
        repeat(blocks - 1, body)

    def store_part(s, cols, value, within=pl.ds(0, quarter)):
        low = value.astype(BF16).reshape(2, 2, within.size, value.shape[-1])
        part[s, :, :, within, cols] = low

    key_tiles = tuple(slice(first, first + 256) for first in range(0, seq_len, 256))

    def folded_max(value, running):
        for first in range(0, value.shape[-1], 128):
            piece = value[:, first : first + 128]
            running = piece if running is None else jnp.maximum(running, piece)
        return running

    def rounds(count, body):
        for index in range(count):
            body(index)

    def loop(count, body):
        def step(index, carry):
            body(index)
            return carry

        lax.fori_loop(0, count, step, 0)

    def attention_heads(s):
        attention_start(s)
        loop(heads, lambda h: attention_head(s, h))

    def attention_start(s):
        of[...] = jnp.zeros((rows, padded), F32)
        invl[s] = jnp.zeros((rows, share), F32)

    def attention(s, h):
        if h == 0:
            attention_start(s)
        attention_head(s, h)

    def attention_head(s, h):
        mask = head_of_lane == h
        query = jnp.where(mask, qb[s], jnp.zeros((), BF16))
        highest = None
        for tile in key_tiles:
            scores = against(query, kb[s, tile, :])
            if s >= nt:
                position = tile.start + lax.broadcasted_iota(jnp.int32, (1, 256), 1)
                scores += jnp.where(position < length(s), 0.0, NEG_LARGE)
            work[:, tile] = scores
            highest = folded_max(scores, highest)
        delta[...] = jnp.broadcast_to(
            jnp.max(highest, axis=-1, keepdims=True), (rows, 128)
        )

        top = delta[...]
        mixed = None
        for tile in key_tiles:
            for first in range(tile.start, tile.stop, 128):
                piece = slice(first, first + 128)
                probs[s, h, :, piece] = jnp.exp(work[:, piece] - top).astype(BF16)
            term = nn(probs[s, h, :, tile], vb[s, tile, :])
            mixed = term if mixed is None else mixed + term
        inverse = 1.0 / mixed[:, share : share + 1]
        of[...] = jnp.where(padded_head == h, mixed * inverse, of[...])
        invl[s] = jnp.where(mask, inverse, invl[s])

    def attention_out(s):
        orb[s] = of[:, :share].astype(BF16)

        def body(start):
            cols = pl.ds(start, 256)
            store_part(s, cols, nn(orb[s], wout[:, cols]))

        tiles(width, 256, body)

    def forward_rows(u):
        s, within = stream(u)
        summed = r["xown"][s, within] + (rs_total(0, u) + vec(0))
        center = summed - jnp.mean(summed, axis=-1, keepdims=True)
        inverse = lax.rsqrt(jnp.mean(center * center, axis=-1, keepdims=True) + EPSILON)
        normal = center * inverse
        unit1[s, within] = normal
        inv1[s, within] = jnp.broadcast_to(inverse, (within.size, 128))
        n1r[s, t, within] = (normal * vec(3) + vec(5)).astype(BF16)

    def feed_forward(u):
        s, within = stream(u)
        count = 4 * within.size

        def up(start):
            cols = pl.ds(start, 256)
            left = n1r[s, :, within, :].reshape(count, width)
            before = nn(left, win[:, cols]) + vec_ref[1:2, cols]
            phi = 0.5 * (1.0 + lax.erf(before * ROOT_HALF))
            low = (before * phi).astype(BF16)
            act[s, :, within, cols] = low.reshape(4, within.size, 256)
            bell = jnp.exp(-0.5 * before * before) * INV_ROOT_TWO_PI
            low = (phi + before * bell).astype(BF16)
            slope[s, :, within, cols] = low.reshape(4, within.size, 256)

        (tiles if s < nt else tile_loop)(hidden, 256, up)
        rs_sent(0, u)

        def down(start):
            cols = pl.ds(start, 256)
            left = act[s, :, within, :].reshape(count, hidden)
            store_part(s, cols, nn(left, wback[:, cols]), within)

        (tiles if s < nt else tile_loop)(width, 256, down)

    def norm_back_rows(grad_out, normal, inverse, gain):
        scaled = grad_out * gain
        return inverse * (
            scaled
            - jnp.mean(scaled, axis=-1, keepdims=True)
            - normal * jnp.mean(scaled * normal, axis=-1, keepdims=True)
        )

    def middle_rows(u):
        s, within = stream(u)
        normed = unit1[s, within] * vec(3) + vec(5)
        summed = normed + (rs_total(1, u) + vec(2))
        center = summed - jnp.mean(summed, axis=-1, keepdims=True)
        inverse = lax.rsqrt(jnp.mean(center * center, axis=-1, keepdims=True) + EPSILON)
        normal = center * inverse
        keep = keep_rows(s, within)
        r["outq"][s, within] = (keep * (normal * vec(4) + vec(6))).astype(BF16)
        grad_out = keep * r["cown"][s, within]
        grad = norm_back_rows(grad_out, normal, inverse, vec(4))
        dh[s, within] = grad
        low = grad.astype(BF16)
        dzr[s, t, within] = low
        add_small(s, 1, sum_rows(grad_out * normal))
        add_small(s, 3, sum_rows(grad_out))
        add_small(s, 5, sum_rows(low.astype(F32)))

    def backward_hidden(s):
        b = batch_of(s)

        def up(start):
            cols = pl.ds(start, 256)
            grad = against(flat(dzr, s), wback[cols, :]).astype(BF16).astype(F32)
            low = (grad * flat(slope, s, cols).astype(F32)).astype(BF16)
            slope[s, :, :, cols] = low.reshape(4, quarter, 256)
            small[b, 8:9, cols] += sum_rows(low.astype(F32))

        tiles(hidden, 256, up)
        for u, (sequence, first, count) in enumerate(z_.streams):
            if sequence == s and (s >= nt or count < quarter):
                rs_sent(1, u)

        def down(start):
            cols = pl.ds(start, 256)
            store_part(s, cols, against(flat(slope, s), win[cols, :]))

        tiles(width, 256, down)

    def weight_grad(b, base, first, count, left, right):
        def body(start):
            total = None
            for s in batches[b]:
                term = across(flat(left, s, pl.ds(first + start, WEIGHT_TILE)), flat(right, s))
                total = term if total is None else total + term
            place = pl.ds(pl.multiple_of(base + first + start, 64), WEIGHT_TILE)
            gb[b, place, :] = total.astype(BF16)

        if count > WEIGHT_TILE:
            tile_loop(count, WEIGHT_TILE, body)
        else:
            body(0)

    def backward_rows(u):
        s, within = stream(u)
        grad_out = dh[s] + rs_total(2, u).astype(BF16).astype(F32)
        normal = unit1[s]
        grad = norm_back_rows(grad_out, normal, inv1[s, :, 0:1], vec(3))
        dh[s] = grad
        low = grad.astype(BF16)
        dar[s, t] = low
        add_small(s, 0, sum_rows(grad_out * normal))
        add_small(s, 2, sum_rows(grad_out))
        add_small(s, 4, sum_rows(low.astype(F32)))

    def out_grad(b):
        total = None
        for s in batches[b]:
            term = across(orb[s], flat(dar, s))
            total = term if total is None else total + term
        gb[b, z_.out0 : z_.out0 + share, :] = total.astype(BF16)


    def mixed_back(s):
        grad_mixed = against(flat(dar, s), wout[...]).astype(BF16).astype(F32)
        grad_mixed = (grad_mixed * invl[s]).astype(BF16)
        gm[...] = grad_mixed
        tm[...] = grad_mixed.T
        tq[...] = qb[s].T
        of[:, :share] = grad_mixed.astype(F32) * orb[s].astype(F32)

    def attention_back_heads(s):
        mixed_back(s)
        dqb[s] = jnp.zeros((rows, share), BF16)
        loop(heads, lambda h: attention_back_head(s, h))

    def attention_back(s, h):
        if h == 0:
            mixed_back(s)
            dqb[s] = jnp.zeros((rows, share), BF16)
        attention_back_head(s, h)

    def attention_back_head(s, h):
        mask = head_of_lane == h
        summed = jnp.sum(jnp.where(mask, of[:, :share], 0.0), axis=-1, keepdims=True)
        grad_head = jnp.where(mask, gm[...], jnp.zeros((), BF16))
        for tile in key_tiles:
            grads = against(grad_head, vb[s, tile, :share]) - summed
            dsb[:, tile] = (probs[s, h, :, tile].astype(F32) * grads).astype(BF16)
        grad_query = (nn(dsb[...], kb[s]) * scale).astype(BF16)
        dqb[s] = jnp.where(mask, grad_query, dqb[s])
        place = pl.ds(pl.multiple_of(h * HEAD_DIM, HEAD_DIM), HEAD_DIM)
        dkvt[s, 0, place, :] = nn(tq[place, :], dsb[...]).astype(BF16)
        dkvt[s, 1, place, :] = nn(tm[place, :], probs[s, h]).astype(BF16)

    def through_back(s):
        add_small(s, 9, sum_rows(dqb[s].astype(F32)), share)
        ones = jnp.ones((8, seq_len), BF16)
        add_small(s, 10, against(ones, dkvt[s, 1])[0:1], share)

        work[:, :width] = nn(dqb[s], wqkv[0])
        def body(pair):
            for j in (2 * pair, 2 * pair + 1):
                place = pl.ds(pl.multiple_of(j * rows, rows), rows)
                terms = dkvt[s, :, :, place].reshape(2 * share, rows)
                total = across(terms, wqkv[1:3].reshape(2 * share, width))
                total += jnp.where(j == z, work[:, :width], 0.0)
                r["part4"][s, j] = total.astype(BF16).reshape(2, 2, quarter, width)

        loop(blocks // 2, body)

    def qkv_grad(b):
        query = other = None
        for s in batches[b]:
            term = across(dqb[s], xg[s, own_block, :])
            query = term if query is None else query + term
            term = nn(dkvt[s].reshape(2 * share, seq_len), xg[s])
            other = term if other is None else other + term
        first = z_.qkv0
        gb[b, first : first + share, :] = query.astype(BF16)
        gb[b, first + share : first + 3 * share, :] = other.astype(BF16)

    part4, crecv4, yrecv4, zrecv4 = (r[n] for n in ("part4", "crecv4", "yrecv4", "zrecv4"))
    d4_s, d4_r, z4_s, z4_r = (r[n] for n in ("d4_s", "d4_r", "z4_s", "z4_r"))

    def dx_core(s):
        send(part4.at[s, :, :, 1 - c], crecv4.at[s], d4_s.at[s, 0], d4_r.at[s, 0], to_c)

        def clear(side):
            zrecv4[s, side] = jnp.zeros(zrecv4.shape[2:], BF16)

        when(z == 0, lambda: clear(0))
        when(z == blocks - 1, lambda: clear(1))

    def dx_y(s):
        arrived(crecv4.at[s], d4_s.at[s, 0], d4_r.at[s, 0], to_c)

        def body(j, carry):
            part4[s, j, 1 - y, c] = (
                part4[s, j, 1 - y, c].astype(F32) + crecv4[s, j, 1 - y].astype(F32)
            ).astype(BF16)
            return carry

        lax.fori_loop(0, blocks, body, 0)
        send(part4.at[s, :, 1 - y, c], yrecv4.at[s], d4_s.at[s, 1], d4_r.at[s, 1], to_y)

    def dx_partial(s, j):
        return (
            part4[s, j, y, c].astype(F32)
            + crecv4[s, j, y].astype(F32)
            + yrecv4[s, j].astype(F32)
        )

    def dx_arrived_y(s):
        arrived(yrecv4.at[s], d4_s.at[s, 1], d4_r.at[s, 1], to_y)

    def dx_relay(s, d):
        for side in range(2):
            target = z + d if side == 0 else z - d
            valid = target <= blocks - 1 if side == 0 else target >= 0
            block = jnp.clip(target, 0, blocks - 1)
            has_source = has_left if side == 0 else has_right
            dev = to_right if side == 0 else to_left

            def go(side=side, block=block, has_source=has_source):
                if d < blocks - 1:
                    arrived(
                        zrecv4.at[s, side, d],
                        z4_s.at[s, side, d],
                        z4_r.at[s, side, d],
                        to_c,
                        has_source,
                    )
                    value = dx_partial(s, block) + zrecv4[s, side, d].astype(F32)
                else:
                    value = dx_partial(s, block)
                part4[s, block, y, c] = value.astype(BF16)

            when(valid, go)
            send(
                part4.at[s, block, y, c],
                zrecv4.at[s, side, d - 1],
                z4_s.at[s, side, d - 1],
                z4_r.at[s, side, d - 1],
                dev,
                valid,
            )

    def dx_final(s):
        for side, has_source in ((0, has_left), (1, has_right)):
            arrived(
                zrecv4.at[s, side, 0],
                z4_s.at[s, side, 0],
                z4_r.at[s, side, 0],
                to_c,
                has_source,
            )
        total = (
            dx_partial(s, z)
            + zrecv4[s, 0, 0].astype(F32)
            + zrecv4[s, 1, 0].astype(F32)
        )
        r["ginq"][s] = (dh[s] + total.astype(BF16).astype(F32)).astype(BF16)
        publish(r["ginq"], s, r["gin"], 1)

    xrecv, zr1, zr2, grad_ref = r["xrecv"], r["zr1"], r["zr2"], r["grad"]
    ar_s, ar_r, al_s = r["ar_s"], r["ar_r"], r["al_s"]

    def ar_places(i):
        first, count, kind = z_.chunks[i]
        half = count // 2
        index = x if kind == "x" else jnp.where(z == 1, 0, 1)
        own = pl.ds(pl.multiple_of(first + index * half, 16), half)
        other = pl.ds(pl.multiple_of(first + (1 - index) * half, 16), half)
        return own, other, pl.ds(z_.first_half[i], half), pl.ds(z_.first_zone[i], half)

    def zone_places(i):
        first, count, kind = z_.chunks[i]
        half, base = count // 2, z_.first_zone[i]
        index = jnp.where(z == 1, 0, 1)
        own = pl.ds(pl.multiple_of(base + index * half, 16), half)
        other = pl.ds(pl.multiple_of(base + (1 - index) * half, 16), half)
        return own, other, pl.ds(base, count), pl.ds(first, count)

    def add_into(b, dst, dst_first, left, left_first, right, right_first, count):
        tile = next(size for size in (64, 48, 32, 16) if count % size == 0)

        def body(start):
            at = lambda first: pl.ds(pl.multiple_of(first + start, 16), tile)
            dst[b, at(dst_first), :] = (
                left[b, at(left_first), :].astype(F32)
                + right[b, at(right_first), :].astype(F32)
            ).astype(BF16)

        tile_loop(count, tile, body)

    def sems(b, i, index):
        return ar_s.at[b, i, index], ar_r.at[b, i, index]

    def x0(b, i):
        own, other, half, zone = ar_places(i)
        send(gb.at[b, other], xrecv.at[b, half], *sems(b, i, 0), to_x)

    def x1(b, i):
        own, other, half, zone = ar_places(i)
        arrived(xrecv.at[b, half], *sems(b, i, 0), to_x)
        add_into(b, gb, own.start, gb, own.start, xrecv, half.start, half.size)
        send(gb.at[b, own], zr1.at[b, zone], *sems(b, i, 1), to_inner, corner)

    def x2(b, i):
        own, other, half, zone = ar_places(i)

        def add():
            arrived(zr1.at[b, zone], *sems(b, i, 1), to_x)
            add_into(b, gb, own.start, gb, own.start, zr1, zone.start, half.size)

        when(interior, add)
        send(gb.at[b, own], zr2.at[b, half], *sems(b, i, 2), to_mirror, interior)

    def x_share(b, i, cond):
        own, other, half, zone = ar_places(i)
        src, dst = zr1.at[b, zone], grad_ref.at[b, own]
        send(src, dst, *sems(b, i, 3), to_x, cond, final=False)
        when(cond, lambda: pltpu.make_async_copy(src, dst, al_s.at[b, i]).start())

    def x3(b, i):
        own, other, half, zone = ar_places(i)

        def add():
            arrived(zr2.at[b, half], *sems(b, i, 2), to_x)
            add_into(b, zr1, zone.start, gb, own.start, zr2, half.start, half.size)

        when(interior, add)
        send(zr1.at[b, zone], zr1.at[b, zone], *sems(b, i, 1), to_outer, interior)
        x_share(b, i, interior)

    def x4(b, i):
        own, other, half, zone = ar_places(i)
        arrived(zr1.at[b, zone], *sems(b, i, 1), to_x, corner)
        x_share(b, i, corner)

    def x5(b, i):
        own, other, half, zone = ar_places(i)
        src, dst = zr1.at[b, zone], grad_ref.at[b, own]
        remote(src, dst, *sems(b, i, 3), to_x).wait_send()
        pltpu.make_async_copy(src, dst, al_s.at[b, i]).wait()
        arrived(grad_ref.at[b, other], *sems(b, i, 3), to_x)

    def z0(b, i):
        whole, rows_of = zone_places(i)[2:]
        send(gb.at[b, rows_of], zr1.at[b, whole], *sems(b, i, 0), to_inner, corner)

    def z1(b, i):
        own, other, half, zone = ar_places(i)
        whole, rows_of = zone_places(i)[2:]

        def add():
            arrived(zr1.at[b, whole], *sems(b, i, 0), to_x)
            add_into(b, gb, rows_of.start, gb, rows_of.start, zr1, whole.start, whole.size)

        when(interior, add)
        send(gb.at[b, other], zr2.at[b, half], *sems(b, i, 1), to_mirror, interior)

    def z2(b, i):
        own, other, half, zone = ar_places(i)

        def add():
            arrived(zr2.at[b, half], *sems(b, i, 1), to_x)
            add_into(b, gb, own.start, gb, own.start, zr2, half.start, half.size)

        when(interior, add)
        send(gb.at[b, own], xrecv.at[b, half], *sems(b, i, 2), to_x, interior)

    def z3(b, i):
        own, other, half, zone = ar_places(i)
        zone_own = zone_places(i)[0]

        def add():
            arrived(xrecv.at[b, half], *sems(b, i, 2), to_x)
            add_into(b, zr1, zone_own.start, gb, own.start, xrecv, half.start, half.size)

        when(interior, add)
        here = zr1.at[b, zone_own]
        send(here, here, *sems(b, i, 3), to_mirror, interior)
        send(here, here, *sems(b, i, 0), to_outer, interior)

    def z4(b, i):
        there = zr1.at[b, zone_places(i)[1]]
        arrived(there, *sems(b, i, 3), to_x, interior)
        send(there, there, *sems(b, i, 4), to_outer, interior)

    def z5(b, i):
        there = zr1.at[b, zone_places(i)[1]]
        arrived(there, *sems(b, i, 0), to_x, corner)
        arrived(there, *sems(b, i, 4), to_x, corner)
        z_copy(b, i)

    def z_copy(b, i):
        whole, rows_of = zone_places(i)[2:]
        pltpu.make_async_copy(
            zr1.at[b, whole], grad_ref.at[b, rows_of], al_s.at[b, i]
        ).start()

    def z6(b, i):
        whole, rows_of = zone_places(i)[2:]
        pltpu.make_async_copy(
            zr1.at[b, whole], grad_ref.at[b, rows_of], al_s.at[b, i]
        ).wait()

    def w_halves(i):
        first, count, kind = z_.chunks[i]
        half, base = count // 2, z_.first_zone[i]
        return (
            (pl.ds(first, half), pl.ds(base, half), blocks - 1 - z, to_left, to_right),
            (pl.ds(first + half, half), pl.ds(base + half, half), z, to_right, to_left),
        )

    def w_in(step):
        def go(b, i):
            for index, (here, zone, place, down, up) in enumerate(w_halves(i)):
                at = place == step
                into = sems(b, i, index) if step else None

                def add(here=here, zone=zone, into=into):
                    arrived(zr1.at[b, zone], *into, to_x)
                    add_into(b, gb, here.start, gb, here.start, zr1, zone.start, zone.size)

                if step:
                    when(at, add)
                if step < blocks - 1:
                    send(gb.at[b, here], zr1.at[b, zone], *sems(b, i, index), down, at)
                else:
                    half = pl.ds(z_.first_half[i], here.size)
                    send(gb.at[b, here], xrecv.at[b, half], *sems(b, i, 2), to_x, at)

        return go

    def w_out(step):
        def go(b, i):
            for index, (here, zone, place, down, up) in enumerate(w_halves(i)):
                at = place == blocks - 1 - step
                into = sems(b, i, 3 + index) if step else None

                def add(here=here, zone=zone):
                    half = pl.ds(z_.first_half[i], here.size)
                    arrived(xrecv.at[b, half], *sems(b, i, 2), to_x)
                    add_into(b, zr1, zone.start, gb, here.start, xrecv, half.start, half.size)

                if step:
                    arrived(zr1.at[b, zone], *into, to_x, at)
                else:
                    when(at, add)
                if step < blocks - 1:
                    src = zr1.at[b, zone]
                    send(src, src, *sems(b, i, 3 + index), up, at)

        return go

    def w7(b, i):
        w_out(3)(b, i)
        z_copy(b, i)

    stages = dict(
        x=(x0, x1, x2, x3, x4, x5),
        z=(z0, z1, z2, z3, z4, z5, z6),
        w=(w_in(0), w_in(1), w_in(2), w_in(3), w_out(0), w_out(1), w_out(2), w7, z6),
    )

    def ar(b, i, stage):
        stages[z_.chunks[i][2]][stage](b, i)

    smallc, smalls, smally = r["smallc"], r["smalls"], r["smally"]
    sm_s, sm_r = r["sm_s"], r["sm_r"]
    top = pl.ds(0, 8)

    def small_core(b):
        send(small.at[b, top], smallc.at[b], sm_s.at[b, 0], sm_r.at[b, 0], to_c)

    def small_y(b):
        arrived(smallc.at[b], sm_s.at[b, 0], sm_r.at[b, 0], to_c)
        smalls[b] = small[b, 0:8, :] + smallc[b]
        send(smalls.at[b], smally.at[b], sm_s.at[b, 1], sm_r.at[b, 1], to_y)

    def small_total(b):
        arrived(smally.at[b], sm_s.at[b, 1], sm_r.at[b, 1], to_y)
        first = z_.small0
        gb[b, first : first + 16, :] = jnp.concatenate(
            [smalls[b] + smally[b], small[b, 8:16, :]], axis=0
        ).astype(BF16)
        gb[b, first + 16 : first + SMALL, :] = jnp.zeros((SMALL - 16, width), BF16)

    small[...] = jnp.zeros(small.shape, F32)
    xa_start(0)
    settle()
    xa_start(1)
    settle()
    gather_vectors()
    loads["wqkv"].wait()
    settle()
    own_cast(0)
    settle()
    project_query(0)
    settle()
    loads["wout"].wait()
    settle()
    project_own(0)
    settle()
    xa_step(0, 1)
    settle()
    loads["win"].wait()
    loads["wback"].wait()
    for s in range(ns):
        loads["c", s].wait()
    settle()
    xa_step(1, 1)
    settle()
    xa_step(0, 2)
    settle()
    xa_forward(0, 1)
    settle()
    xa_step(1, 2)
    settle()
    xa_start(2)
    settle()
    own_cast(1)
    settle()
    project_query(1)
    settle()
    xa_step(0, 3)
    settle()
    xa_forward(1, 1)
    settle()
    project_own(1)
    settle()
    xa_step(1, 3)
    settle()
    xa_forward(0, 2)
    settle()
    xa_forward(0, 3)
    settle()
    xa_forward(1, 2)
    settle()
    xa_forward(1, 3)
    settle()
    xa_step(2, 1)
    settle()
    xa_done(0, 1)
    xa_done(0, 2)
    xa_done(0, 3)
    xa_done(1, 1)
    xa_done(1, 2)
    xa_done(1, 3)
    settle()
    project_rest(0)
    settle()
    attention(0, 0)
    settle()
    attention(0, 1)
    settle()
    attention(0, 2)
    settle()
    attention_out(0)
    settle()
    rs_core(0, 0)
    settle()
    rs_core(0, 1)
    settle()
    xa_step(2, 2)
    settle()
    rs_y(0, 0)
    settle()
    rs_y(0, 1)
    settle()
    xa_forward(2, 1)
    settle()
    xa_step(2, 3)
    settle()
    xa_start(3)
    settle()
    own_cast(2)
    settle()
    project_query(2)
    settle()
    project_own(2)
    settle()
    xa_forward(2, 2)
    settle()
    forward_rows(0)
    ag_start(0, 0, n1r)
    settle()
    forward_rows(1)
    ag_start(0, 1, n1r)
    settle()
    ag_forward(0, 0, n1r)
    settle()
    xa_forward(2, 3)
    settle()
    xa_step(3, 1)
    settle()
    ag_forward(0, 1, n1r)
    settle()
    ag_done(0, 0, n1r)
    settle()
    feed_forward(0)
    settle()
    rs_core(1, 0)
    settle()
    xa_done(2, 1)
    xa_done(2, 2)
    xa_done(2, 3)
    settle()
    ag_done(0, 1, n1r)
    settle()
    feed_forward(1)
    settle()
    rs_core(1, 1)
    settle()
    rs_y(1, 0)
    settle()
    project_rest(1)
    settle()
    rs_y(1, 1)
    settle()
    xa_step(3, 2)
    settle()
    attention_heads(1)
    settle()
    middle_rows(0)
    ag_start(1, 0, dzr)
    settle()
    middle_rows(1)
    ag_start(1, 1, dzr)
    settle()
    attention_out(1)
    settle()
    rs_core(0, 2)
    settle()
    xa_forward(3, 1)
    settle()
    xa_step(3, 3)
    settle()
    rs_y(0, 2)
    settle()
    xa_forward(3, 2)
    settle()
    ag_forward(1, 0, dzr)
    settle()
    ag_forward(1, 1, dzr)
    settle()
    ag_done(1, 0, dzr)
    settle()
    ag_done(1, 1, dzr)
    settle()
    weight_grad(0, z_.back0, 0, 256, act, dzr)
    settle()
    ar(0, 0, 0)
    settle()
    ar(0, 1, 0)
    settle()
    weight_grad(0, z_.back0, 256, 256, act, dzr)
    settle()
    ar(0, 2, 0)
    settle()
    ar(0, 3, 0)
    settle()
    weight_grad(0, z_.back0, 512, 256, act, dzr)
    settle()
    ar(0, 4, 0)
    settle()
    ar(0, 5, 0)
    settle()
    backward_hidden(0)
    settle()
    weight_grad(0, z_.in0, 0, 256, n1r, slope)
    settle()
    ar(0, 6, 0)
    settle()
    ar(0, 7, 0)
    settle()
    weight_grad(0, z_.in0, 256, 256, n1r, slope)
    settle()
    ar(0, 8, 0)
    settle()
    ar(0, 9, 0)
    settle()
    weight_grad(0, z_.in0, 512, 256, n1r, slope)
    settle()
    ar(0, 10, 0)
    settle()
    ar(0, 11, 0)
    settle()
    xa_forward(3, 3)
    settle()
    ar(0, 1, 1)
    settle()
    rs_core(2, 4)
    settle()
    forward_rows(2)
    ag_start(0, 2, n1r)
    settle()
    xa_done(3, 1)
    xa_done(3, 2)
    xa_done(3, 3)
    settle()
    project_rest(2)
    settle()
    rs_y(2, 4)
    settle()
    attention_heads(2)
    settle()
    attention_out(2)
    settle()
    ag_forward(0, 2, n1r)
    settle()
    rs_core(0, 3)
    settle()
    ar(0, 0, 1)
    settle()
    ar(0, 2, 1)
    settle()
    backward_rows(4)
    ag_start(2, 4, dar)
    settle()
    ag_done(0, 2, n1r)
    settle()
    feed_forward(2)
    settle()
    rs_y(0, 3)
    settle()
    rs_core(1, 2)
    settle()
    ar(0, 3, 1)
    settle()
    ar(0, 4, 1)
    settle()
    ar(0, 5, 1)
    settle()
    ar(0, 0, 2)
    settle()
    ar(0, 6, 1)
    settle()
    ar(0, 7, 1)
    settle()
    ag_forward(2, 4, dar)
    settle()
    ar(0, 9, 1)
    settle()
    small_core(0)
    settle()
    rs_y(1, 2)
    settle()
    ag_done(2, 4, dar)
    settle()
    out_grad(0)
    settle()
    ar(0, 12, 0)
    settle()
    small_y(0)
    settle()
    attention_back(0, 0)
    settle()
    attention_back(0, 1)
    settle()
    attention_back(0, 2)
    settle()
    qkv_grad(0)
    settle()
    ar(0, 13, 0)
    settle()
    ar(0, 14, 0)
    settle()
    ar(0, 15, 0)
    settle()
    ar(0, 16, 0)
    settle()
    ar(0, 17, 0)
    settle()
    middle_rows(2)
    ag_start(1, 2, dzr)
    settle()
    ar(0, 0, 3)
    settle()
    ar(0, 1, 2)
    settle()
    ar(0, 4, 2)
    settle()
    ar(0, 7, 2)
    settle()
    forward_rows(3)
    ag_start(0, 3, n1r)
    settle()
    through_back(0)
    settle()
    dx_core(0)
    settle()
    small_total(0)
    settle()
    ar(0, 18, 0)
    settle()
    ar(0, 2, 2)
    settle()
    ar(0, 8, 1)
    settle()
    ar(0, 4, 3)
    settle()
    ar(0, 10, 1)
    settle()
    ar(0, 11, 1)
    settle()
    ar(0, 12, 1)
    settle()
    ar(0, 3, 2)
    settle()
    ar(0, 13, 1)
    settle()
    ar(0, 14, 1)
    settle()
    ag_forward(1, 2, dzr)
    settle()
    ar(0, 0, 4)
    settle()
    dx_y(0)
    settle()
    ar(0, 1, 3)
    settle()
    ar(0, 7, 3)
    settle()
    ar(0, 5, 2)
    settle()
    ag_forward(0, 3, n1r)
    settle()
    ar(0, 15, 1)
    settle()
    ag_done(1, 2, dzr)
    settle()
    backward_hidden(1)
    settle()
    ag_done(0, 3, n1r)
    settle()
    feed_forward(3)
    settle()
    rs_core(1, 3)
    settle()
    ar(0, 2, 3)
    settle()
    ar(0, 6, 2)
    settle()
    ar(0, 8, 2)
    settle()
    ar(0, 9, 2)
    settle()
    rs_core(2, 2)
    settle()
    ar(0, 16, 1)
    settle()
    ar(0, 17, 1)
    settle()
    rs_y(1, 3)
    settle()
    ar(0, 18, 1)
    settle()
    ar(0, 1, 4)
    settle()
    ar(0, 2, 4)
    settle()
    ar(0, 10, 2)
    settle()
    rs_y(2, 2)
    settle()
    ar(0, 11, 2)
    settle()
    ar(0, 4, 4)
    settle()
    ar(0, 0, 5)
    settle()
    ar(0, 0, 6)
    settle()
    ar(0, 10, 3)
    settle()
    ar(0, 3, 3)
    settle()
    ar(0, 7, 4)
    settle()
    dx_arrived_y(0)
    settle()
    dx_relay(0, 3)
    settle()
    ar(0, 5, 3)
    settle()
    ar(0, 12, 2)
    settle()
    ar(0, 3, 4)
    settle()
    ar(0, 1, 5)
    settle()
    ar(0, 8, 3)
    settle()
    ar(0, 13, 2)
    settle()
    middle_rows(3)
    ag_start(1, 3, dzr)
    settle()
    ar(0, 6, 3)
    settle()
    ar(0, 5, 4)
    settle()
    ar(0, 2, 5)
    settle()
    ar(0, 14, 2)
    settle()
    backward_rows(2)
    ag_start(2, 2, dar)
    settle()
    ar(0, 9, 3)
    settle()
    ar(0, 15, 2)
    settle()
    ar(0, 10, 4)
    settle()
    ag_forward(1, 3, dzr)
    settle()
    ar(0, 16, 2)
    settle()
    ar(0, 11, 3)
    settle()
    ar(0, 6, 4)
    settle()
    ar(0, 17, 2)
    settle()
    ar(0, 3, 5)
    settle()
    ag_done(1, 3, dzr)
    settle()
    weight_grad(1, z_.back0, 0, 768, act, dzr)
    settle()
    ar(1, 0, 0)
    settle()
    ar(1, 1, 0)
    settle()
    ar(1, 2, 0)
    settle()
    ar(0, 12, 3)
    settle()
    ar(0, 18, 2)
    settle()
    ar(1, 3, 0)
    settle()
    ar(1, 4, 0)
    settle()
    ar(1, 5, 0)
    settle()
    ag_forward(2, 2, dar)
    settle()
    ar(0, 9, 4)
    settle()
    backward_hidden(2)
    settle()
    rs_core(2, 3)
    settle()
    weight_grad(1, z_.in0, 0, 768, n1r, slope)
    settle()
    rs_y(2, 3)
    settle()
    ar(0, 13, 3)
    settle()
    ar(0, 4, 5)
    settle()
    ar(1, 6, 0)
    settle()
    ar(0, 7, 5)
    settle()
    ar(1, 7, 0)
    settle()
    ar(1, 8, 0)
    settle()
    ar(1, 1, 1)
    settle()
    ar(1, 9, 0)
    settle()
    ar(1, 10, 0)
    settle()
    ar(1, 11, 0)
    settle()
    ar(0, 8, 4)
    settle()
    ar(0, 14, 3)
    settle()
    ar(0, 11, 4)
    settle()
    ar(0, 12, 4)
    settle()
    ag_done(2, 2, dar)
    settle()
    attention_back_heads(1)
    settle()
    backward_rows(3)
    ag_start(2, 3, dar)
    settle()
    through_back(1)
    settle()
    dx_core(1)
    settle()
    small_core(1)
    settle()
    ar(1, 2, 1)
    settle()
    dx_relay(0, 2)
    settle()
    ar(0, 15, 3)
    settle()
    ar(0, 16, 3)
    settle()
    ar(0, 17, 3)
    settle()
    ar(0, 10, 5)
    settle()
    ar(0, 13, 4)
    settle()
    ar(1, 3, 1)
    settle()
    ar(0, 14, 4)
    settle()
    ar(0, 18, 3)
    settle()
    ag_forward(2, 3, dar)
    settle()
    ar(0, 15, 4)
    settle()
    ar(1, 0, 1)
    settle()
    small_y(1)
    settle()
    dx_y(1)
    settle()
    ar(1, 5, 1)
    settle()
    ar(0, 4, 6)
    settle()
    ag_done(2, 3, dar)
    settle()
    out_grad(1)
    settle()
    ar(1, 4, 1)
    settle()
    attention_back_heads(2)
    settle()
    ar(1, 6, 1)
    settle()
    ar(1, 7, 1)
    settle()
    ar(0, 7, 6)
    settle()
    through_back(2)
    settle()
    small_total(1)
    settle()
    ar(1, 9, 1)
    settle()
    dx_core(2)
    settle()
    qkv_grad(1)
    settle()
    ar(1, 8, 1)
    settle()
    ar(1, 11, 1)
    settle()
    ar(0, 10, 6)
    settle()
    ar(0, 4, 7)
    settle()
    ar(0, 7, 7)
    settle()
    dx_y(2)
    settle()
    ar(1, 0, 2)
    settle()
    ar(1, 1, 2)
    settle()
    ar(1, 12, 0)
    settle()
    ar(1, 13, 0)
    settle()
    ar(1, 14, 0)
    settle()
    ar(1, 15, 0)
    settle()
    ar(1, 16, 0)
    settle()
    ar(1, 17, 0)
    settle()
    ar(1, 18, 0)
    settle()
    ar(0, 16, 4)
    settle()
    ar(0, 17, 4)
    settle()
    ar(0, 18, 4)
    settle()
    ar(1, 4, 2)
    settle()
    ar(0, 10, 7)
    settle()
    dx_arrived_y(1)
    settle()
    dx_relay(1, 3)
    settle()
    ar(1, 10, 1)
    settle()
    ar(0, 4, 8)
    settle()
    ar(0, 5, 5)
    settle()
    ar(0, 6, 5)
    settle()
    ar(0, 7, 8)
    settle()
    ar(0, 8, 5)
    settle()
    ar(0, 8, 6)
    settle()
    ar(0, 9, 5)
    settle()
    ar(0, 10, 8)
    settle()
    ar(0, 11, 5)
    settle()
    ar(0, 12, 5)
    settle()
    ar(1, 7, 2)
    settle()
    ar(0, 13, 5)
    settle()
    publish(r["outq"], 0, r["out"], 0)
    settle()
    ar(1, 2, 2)
    settle()
    publish(r["outq"], 1, r["out"], 0)
    settle()
    ar(1, 4, 3)
    settle()
    publish(r["outq"], 2, r["out"], 0)
    settle()
    ar(1, 8, 2)
    settle()
    dx_relay(0, 1)
    settle()
    ar(0, 14, 5)
    settle()
    ar(1, 1, 3)
    settle()
    ar(1, 3, 2)
    settle()
    ar(1, 0, 3)
    settle()
    ar(1, 7, 3)
    settle()
    ar(0, 15, 5)
    settle()
    ar(1, 10, 2)
    settle()
    ar(1, 5, 2)
    settle()
    ar(1, 2, 3)
    settle()
    ar(1, 6, 2)
    settle()
    ar(1, 9, 2)
    settle()
    ar(1, 3, 3)
    settle()
    ar(1, 11, 2)
    settle()
    ar(1, 0, 4)
    settle()
    dx_relay(1, 2)
    settle()
    ar(1, 5, 3)
    settle()
    dx_final(0)
    settle()
    ar(1, 12, 1)
    settle()
    dx_arrived_y(2)
    settle()
    dx_relay(2, 3)
    settle()
    ar(1, 6, 3)
    settle()
    ar(1, 1, 4)
    settle()
    ar(1, 13, 1)
    settle()
    ar(1, 8, 3)
    settle()
    ar(1, 9, 3)
    settle()
    ar(1, 14, 1)
    settle()
    ar(1, 12, 2)
    settle()
    ar(1, 11, 3)
    settle()
    ar(1, 15, 1)
    settle()
    ar(1, 10, 3)
    settle()
    ar(1, 16, 1)
    settle()
    dx_relay(1, 1)
    settle()
    dx_relay(2, 2)
    settle()
    ar(1, 13, 2)
    settle()
    ar(1, 2, 4)
    settle()
    ar(1, 17, 1)
    settle()
    ar(1, 8, 4)
    settle()
    ar(1, 14, 2)
    settle()
    ar(1, 3, 4)
    settle()
    ar(1, 18, 1)
    settle()
    ar(1, 15, 2)
    settle()
    ar(1, 12, 3)
    settle()
    ar(1, 16, 2)
    settle()
    ar(1, 5, 4)
    settle()
    ar(0, 16, 5)
    settle()
    ar(0, 17, 5)
    settle()
    ar(1, 0, 5)
    settle()
    ar(1, 0, 6)
    settle()
    ar(1, 6, 4)
    settle()
    ar(0, 18, 5)
    settle()
    ar(1, 4, 4)
    settle()
    ar(1, 7, 4)
    settle()
    ar(1, 9, 4)
    settle()
    ar(1, 11, 4)
    settle()
    ar(1, 1, 5)
    settle()
    ar(1, 10, 4)
    settle()
    dx_final(1)
    settle()
    dx_relay(2, 1)
    settle()
    ar(1, 13, 3)
    settle()
    ar(1, 2, 5)
    settle()
    ar(1, 17, 2)
    settle()
    ar(1, 14, 3)
    settle()
    ar(1, 18, 2)
    settle()
    ar(1, 15, 3)
    settle()
    ar(1, 8, 5)
    settle()
    ar(1, 8, 6)
    settle()
    ar(1, 16, 3)
    settle()
    ar(1, 4, 5)
    settle()
    ar(1, 7, 5)
    settle()
    ar(1, 17, 3)
    settle()
    ar(1, 10, 5)
    settle()
    ar(1, 18, 3)
    settle()
    ar(1, 3, 5)
    settle()
    ar(1, 4, 6)
    settle()
    ar(1, 12, 4)
    settle()
    ar(1, 5, 5)
    settle()
    ar(1, 7, 6)
    settle()
    dx_final(2)
    settle()
    ar(1, 6, 5)
    settle()
    ar(1, 13, 4)
    settle()
    ar(1, 10, 6)
    settle()
    ar(1, 14, 4)
    settle()
    ar(1, 9, 5)
    settle()
    ar(1, 15, 4)
    settle()
    ar(1, 11, 5)
    settle()
    ar(1, 16, 4)
    settle()
    ar(1, 17, 4)
    settle()
    ar(1, 12, 5)
    settle()
    ar(1, 13, 5)
    settle()
    ar(1, 18, 4)
    settle()
    ar(1, 14, 5)
    settle()
    ar(1, 4, 7)
    settle()
    ar(1, 4, 8)
    settle()
    ar(1, 15, 5)
    settle()
    ar(1, 16, 5)
    settle()
    ar(1, 7, 7)
    settle()
    ar(1, 7, 8)
    settle()
    ar(1, 17, 5)
    settle()
    ar(1, 10, 7)
    settle()
    ar(1, 10, 8)
    settle()
    ar(1, 18, 5)
    settle()
    for u in (4, 2, 3):
        rs_sent(2, u)
    for finish in sent[settled[0]:] + finals:
        finish()


def layer(sizes, *args):
    anywhere = pl.BlockSpec(memory_space=pl.ANY)
    call = pl.pallas_call(
        functools.partial(layer_kernel, sizes),
        out_shape=(
            jax.ShapeDtypeStruct((sizes.ns, sizes.rows, sizes.width), BF16),
            jax.ShapeDtypeStruct((sizes.ns, sizes.rows, sizes.width), BF16),
            jax.ShapeDtypeStruct((2, sizes.total, sizes.width), BF16),
        ),
        in_specs=[anywhere] * 15,
        out_specs=[anywhere] * 3,
        scratch_shapes=list(sizes.scratch().values()),
        compiler_params=pltpu.CompilerParams(
            collective_id=0, has_side_effects=True, vmem_limit_bytes=VMEM_BYTES
        ),
    )
    return call(*args)


def widen_kernel(sizes, out, gin, grad, *refs):
    nt, share, hidden, width = sizes.nt, sizes.share, sizes.hidden, sizes.width
    (
        out_t, out_q, gin_t, gin_q, qkv, qv_bias, out_w, out_bias, in_w, in_bias, back_w,
        back_bias, gains, shifts, low, wide, tail, in_sem, out_sem, tail_sem,
    ) = refs
    t = lax.axis_index("tensor")
    pieces = []
    for src, first, second in ((out, out_t, out_q), (gin, gin_t, gin_q)):
        for s in range(sizes.ns):
            dst = first.at[s] if s < nt else second.at[s - nt]
            pieces.append((src.at[s], dst, sizes.rows))
    for b in range(2):
        for first, count, dst in (
            (sizes.back0, hidden, back_w.at[b]),
            (sizes.in0, width, in_w.at[b]),
            (sizes.out0, share, out_w.at[b]),
            (sizes.qkv0, share, qkv.at[b, 0]),
            (sizes.qkv0 + share, share, qkv.at[b, 1]),
            (sizes.qkv0 + 2 * share, share, qkv.at[b, 2]),
        ):
            size = min(count, WIDEN_ROWS)
            for start in range(0, count, size):
                src = grad.at[b, pl.ds(first + start, size)]
                pieces.append((src, dst.at[pl.ds(start, size)], size))
    tails = [
        pltpu.make_async_copy(
            grad.at[b, pl.ds(sizes.small0, 16)], tail.at[b], tail_sem.at[b]
        )
        for b in range(2)
    ]
    reads, writes, places = [], [], []
    place = 0
    for index, (src, dst, size) in enumerate(pieces):
        here = pl.ds(place, size)
        places.append((place, size))
        reads.append(pltpu.make_async_copy(src, low.at[here], in_sem.at[index]))
        writes.append(pltpu.make_async_copy(wide.at[here], dst, out_sem.at[index]))
        place += size
    for copy in reads + tails:
        copy.start()
    for (place, size), read, write in zip(places, reads, writes):
        read.wait()

        def body(step, carry, place=place):
            at = pl.ds(pl.multiple_of(place + step * 32, 32), 32)
            wide[at, :] = low[at, :].astype(F32)
            return carry

        lax.fori_loop(0, size // 32, body, 0)
        write.start()
    for copy in tails:
        copy.wait()
    rows = tail[...].astype(F32)

    def crop_rows(first, count):
        value = jnp.zeros((2, count, share), F32)
        for k in range(4):
            piece = rows[:, first : first + count, k * share : (k + 1) * share]
            value = jnp.where(t == k, piece, value)
        return value

    gains[...] = crop_rows(0, 2)
    shifts[...] = crop_rows(2, 2)
    out_bias[...] = crop_rows(4, 1)[:, 0]
    back_bias[...] = crop_rows(5, 1)[:, 0]
    in_bias[...] = rows[:, 8]
    qv_bias[...] = rows[:, 9:11, :share]
    for copy in writes:
        copy.wait()


WIDEN_ROWS = 768


def widen(sizes, out, gin, grad):
    nt, nq, rows, share, width, hidden = (
        sizes.nt, sizes.nq, sizes.rows, sizes.share, sizes.width, sizes.hidden,
    )
    anywhere = pl.BlockSpec(memory_space=pl.ANY)
    held = pl.BlockSpec(memory_space=pltpu.VMEM)
    shapes = (
        ((nt, rows, width), anywhere),
        ((nq, rows, width), anywhere),
        ((nt, rows, width), anywhere),
        ((nq, rows, width), anywhere),
        ((2, 3, share, width), anywhere),
        ((2, 2, share), held),
        ((2, share, width), anywhere),
        ((2, share), held),
        ((2, width, hidden), anywhere),
        ((2, hidden), held),
        ((2, hidden, width), anywhere),
        ((2, share), held),
        ((2, 2, share), held),
        ((2, 2, share), held),
    )
    total = 2 * sizes.ns * rows + 2 * (hidden + width + 4 * share)
    count = 2 * sizes.ns + 2 * (hidden // WIDEN_ROWS + width // WIDEN_ROWS + 4)
    return pl.pallas_call(
        functools.partial(widen_kernel, sizes),
        out_shape=tuple(jax.ShapeDtypeStruct(shape, F32) for shape, _ in shapes),
        in_specs=[anywhere] * 3,
        out_specs=tuple(spec for _, spec in shapes),
        scratch_shapes=[
            pltpu.VMEM((total, width), BF16),
            pltpu.VMEM((total, width), F32),
            pltpu.VMEM((2, 16, width), BF16),
            pltpu.SemaphoreType.DMA((count,)),
            pltpu.SemaphoreType.DMA((count,)),
            pltpu.SemaphoreType.DMA((2,)),
        ],
        compiler_params=pltpu.CompilerParams(vmem_limit_bytes=VMEM_BYTES),
    )(out, gin, grad)


VMEM_BYTES = 127 * 2**19


def fused(
    x_train,
    x_quiz,
    cot_train,
    cot_quiz,
    quiz_lengths,
    w_qkv,
    b_qv,
    w_out,
    b_out,
    w_in,
    b_in,
    w_back,
    b_back,
    norm_gains,
    norm_shifts,
):
    nt, rows, width = x_train.shape
    share, hidden = w_out.shape[0], w_in.shape[1]
    sizes = Sizes(
        nt, x_quiz.shape[0], rows, lax.axis_size("blk"), share, width, hidden
    )
    out, grad_in, grad = layer(
        sizes,
        x_train,
        x_quiz,
        cot_train,
        cot_quiz,
        quiz_lengths,
        jnp.swapaxes(w_qkv, 1, 2),
        w_out,
        w_in,
        w_back,
        b_out,
        b_in,
        b_back,
        norm_gains,
        norm_shifts,
        b_qv,
    )
    results = list(widen(sizes, out, grad_in, grad))
    results[4] = jnp.swapaxes(results[4], 2, 3)
    return tuple(results)


def fits(mesh):
    return dict(mesh.shape) == {"dp": 2, "tensor": 4, "blk": 4}


def solution(mesh):
    placed = (
        P("dp", "blk", None),
        P("dp", "blk", None),
        P("dp", "blk", None),
        P("dp", "blk", None),
        P("dp"),
        P(None, None, "tensor"),
        P(None, "tensor"),
        P("tensor", None),
        P(),
        P(None, "tensor"),
        P("tensor"),
        P("tensor", None),
        P(),
        P(),
        P(),
    )
    return jax.shard_map(
        fused if fits(mesh) else shards,
        mesh=mesh,
        in_specs=placed,
        out_specs=(
            P("dp", "blk", None),
            P("dp", "blk", None),
            P("dp", "blk", None),
            P("dp", "blk", None),
            P(None, None, None, "tensor"),
            P(None, None, "tensor"),
            P(None, "tensor", None),
            P(None, "tensor"),
            P(None, None, "tensor"),
            P(None, "tensor"),
            P(None, "tensor", None),
            P(None, "tensor"),
            P(None, None, "tensor"),
            P(None, None, "tensor"),
        ),
        check_vma=False,
    )
```
